32 devices in a mesh: cells: 8 (over z, y), genes: 4 (over x, core).
Axes of the slice: x: 2, y: 2, z: 4, core: 2. Of those that a mesh axis runs over, the one named last changes fastest.
Arguments:
- counts: bfloat16 [1024, 16384], P('cells', 'genes'), may hold values from 0 to 254
- occupancy: int32 [8, 128], P('cells', 'genes'), may hold values 0 or 1
- start_basis: bfloat16 [64, 16384], P(None, 'genes'), may hold values from -0.046875 to 0.046875
Outputs:
- new_basis: float32 [64, 16384], P(None, ('genes', 'cells'))
The draws below stay inside these ranges and needn't reach their ends.
All inputs are finite; a program needn't handle non-finite values. No bound on the sum of `occupancy` on one device may be relied on, other than what follows from the above.
Results may differ from the reference program's by a relative error of at most 0.01.
Values sent between devices are 32-bit elements; how exact they have to be, the bound alone decides.
No kernel may reach another device: no remote copies, remote signals or barrier semaphores. Data moves between devices by JAX's collectives and lax.ppermute only.
A program may use at most 64 MiB of HBM per device.

```python
import math
import jax
import jax.numpy as jnp
from jax import lax

GENES = 16384
COMPS = 64
TILE = 128
CELLS = 1024


def draw_counts(key, part):
    key_rows, key_cols, key_cells = jax.random.split(jax.random.fold_in(key, 17), 3)
    row_high = jax.random.randint(key_rows, (CELLS, 1), 2, 18)
    col_high = jax.random.randint(key_cols, (1, GENES), 1, 16)
    whole = jax.random.randint(key_cells, (CELLS, GENES), 0, row_high * col_high)
    return whole.astype(jnp.float32).astype(jnp.bfloat16)


def with_ends(entries, key, smallest, largest):
    index_at = [jax.random.randint(jax.random.fold_in(key, axis), (), 0, length) for axis, length in enumerate(entries.shape)]
    widest = entries.shape.index(max(entries.shape))
    beside = index_at[:widest] + [(index_at[widest] + 1) % entries.shape[widest]] + index_at[widest + 1:]
    return entries.at[tuple(index_at)].set(smallest).at[tuple(beside)].set(largest)


def shard_levels(own_key, extent, shards, smallest, largest):
    def one(axis_at, blocks):
        heights = jax.random.uniform(jax.random.fold_in(jax.random.fold_in(own_key, 6), axis_at), (blocks,), jnp.float32, smallest / len(shards), largest / len(shards))
        return jnp.repeat(jnp.exp(heights), extent[axis_at] // blocks).reshape((-1,) + (1,) * (len(extent) - axis_at - 1))

    gain = one(*shards[0])
    for cut in shards[1:]:
        gain = gain * one(*cut)
    return gain


def normal_values(rng, dims, width, limit, shards=(), held_as=jnp.bfloat16):
    result = width * jax.random.normal(rng, dims, jnp.float32)
    if shards:
        result = result * shard_levels(rng, dims, shards, -0.22, 0.18)
    return jnp.clip(result, -limit, limit).astype(held_as)


def setup_inputs(seed: int = 0) -> dict:
    arg_keys = jax.random.split(jax.random.key(seed), 4)
    counts = draw_counts(jax.random.fold_in(arg_keys[3], 71), 0)
    occupancy = with_ends((jax.random.randint(arg_keys[1], (CELLS // TILE, GENES // TILE), 0, 4) < 3).astype(jnp.int32), jax.random.fold_in(arg_keys[1], 1), 0, 1)
    start_basis = normal_values(arg_keys[2], (COMPS, GENES), GENES ** -0.5, 0.046875, ((1, 4),))
    return {"counts": counts, "occupancy": occupancy, "start_basis": start_basis}


def reference(counts, occupancy, start_basis):
    tile_rows, tile_cols = occupancy.shape
    logged = jnp.log1p(counts.astype(jnp.float32)).reshape(tile_rows, TILE, tile_cols, TILE)
    logged = (logged * occupancy.astype(jnp.float32)[:, None, :, None]).reshape(counts.shape)
    gene_mean = lax.optimization_barrier(jnp.sum(logged, axis=0)) / CELLS
    centered = (logged - gene_mean).astype(jnp.bfloat16)
    scores = lax.dot_general(start_basis.astype(jnp.float32), centered.astype(jnp.float32), (((1,), (1,)), ((), ())), preferred_element_type=jnp.float32)
    score_high = scores.astype(jnp.bfloat16)
    score_low = (scores - score_high.astype(jnp.float32)).astype(jnp.bfloat16)
    stacked = jnp.concatenate([score_high, score_low], axis=0)
    both = jnp.dot(stacked.astype(jnp.float32), centered.astype(jnp.float32), preferred_element_type=jnp.float32)
    spread = both[:COMPS] + both[COMPS:]
    gram_sum = lax.dot_general(spread.astype(jnp.float32), spread.astype(jnp.float32), (((1,), (1,)), ((), ())), precision=lax.Precision.HIGHEST, preferred_element_type=jnp.float32)
    factor = jnp.linalg.cholesky(gram_sum)
    basis_now = jax.scipy.linalg.solve_triangular(factor, spread, lower=True)
    return basis_now * math.sqrt(GENES)
```

```python
import functools
import math

import jax
import jax.numpy as jnp
from jax import lax
from jax.experimental import pallas as pl
from jax.experimental.pallas import tpu as pltpu
from jax.sharding import PartitionSpec as P

F32 = jnp.float32
BF16 = jnp.bfloat16
NN = (((1,), (0,)), ((), ()))
NT = (((1,), (1,)), ((), ()))
WHOLE = pl.BlockSpec(memory_space=pltpu.VMEM)
SCALARS = pl.BlockSpec(memory_space=pltpu.SMEM)
PARAMS = pltpu.CompilerParams(vmem_limit_bytes=48 * 2**20)
MOST_PARTNERS = 8


def dot(a, b, dims):
    return lax.dot_general(a, b, dims, preferred_element_type=F32)


def split_terms(x, count):
    terms = []
    for _ in range(count):
        term = x.astype(BF16)
        terms.append(term)
        x = x - term.astype(F32)
    return terms


def tree_sum(parts):
    while len(parts) > 1:
        parts = [a + b for a, b in zip(parts[::2], parts[1::2])]
    return parts[0]


def log_kernel(tile_rows, tile_edge, occ_ref, counts_ref, basis_ref, high_ref, low_ref, score_ref, sum_ref):
    step = pl.program_id(0)
    rows, cols = counts_ref.shape
    tile_cols = cols // tile_edge

    @pl.when(step == 0)
    def _():
        score_ref[...] = jnp.zeros_like(score_ref)

    for col in range(tile_cols):
        lanes = pl.ds(col * tile_edge, tile_edge)
        total = None
        for row in range(tile_rows):
            subs = pl.ds(row * tile_edge, tile_edge)
            occ = occ_ref[row, step * tile_cols + col].astype(F32)
            logged = jnp.log(1.0 + counts_ref[subs, lanes].astype(F32)) * occ
            high = logged.astype(BF16)
            high_ref[subs, lanes] = high
            low_ref[subs, lanes] = (logged - high.astype(F32)).astype(BF16)
            part = jnp.sum(logged, axis=0, keepdims=True)
            total = part if total is None else total + part
        sum_ref[:, lanes] = total
    basis = basis_ref[...]
    score_ref[...] += dot(basis, high_ref[...], NT) + dot(basis, low_ref[...], NT)


def log_and_scores(counts, occupancy, basis):
    cells, genes = counts.shape
    tile_rows, tile_cols = occupancy.shape
    edge = cells // tile_rows
    comps = basis.shape[0]
    width = genes // 4 if genes % (4 * edge) == 0 else genes
    return pl.pallas_call(
        functools.partial(log_kernel, tile_rows, edge),
        grid=(genes // width,),
        out_shape=(
            jax.ShapeDtypeStruct((cells, genes), BF16),
            jax.ShapeDtypeStruct((cells, genes), BF16),
            jax.ShapeDtypeStruct((comps, cells), F32),
            jax.ShapeDtypeStruct((1, genes), F32),
        ),
        in_specs=[
            SCALARS,
            pl.BlockSpec((cells, width), lambda i: (0, i)),
            pl.BlockSpec((comps, width), lambda i: (0, i)),
        ],
        out_specs=(
            pl.BlockSpec((cells, width), lambda i: (0, i)),
            pl.BlockSpec((cells, width), lambda i: (0, i)),
            pl.BlockSpec((comps, cells), lambda i: (0, 0)),
            pl.BlockSpec((1, width), lambda i: (0, i)),
        ),
        compiler_params=PARAMS,
        name="log_scores",
    )(occupancy, counts, basis)


def spread_piece(terms, high, low):
    comps = terms[0].shape[0]
    on_low = dot(jnp.concatenate(terms[:2], axis=0), low, NN)
    on_high = dot(jnp.concatenate(terms, axis=0), high, NN)
    small = on_low[comps:] + on_high[2 * comps:]
    middle = on_low[:comps] + on_high[comps:2 * comps]
    return (small + middle) + on_high[:comps]


def spread_kernel(count, picks, with_rows, me_ref, *refs):
    score_refs, (high_ref, low_ref), outs = refs[:count], refs[count:count + 2], refs[count + 2:]
    scores = tree_sum([ref[...] for ref in score_refs])
    terms = split_terms(scores, 3)
    for pick, out in zip(picks, outs):
        width = out.shape[1]
        lanes = pl.ds(pl.multiple_of((me_ref[0] ^ pick) * width, width), width)
        out[...] = spread_piece(terms, high_ref[:, lanes], low_ref[:, lanes])
    if with_rows:
        outs[-1][...] = jnp.broadcast_to(jnp.sum(scores, axis=1, keepdims=True), outs[-1].shape)


def spread_pieces(me, score_parts, high, low, picks, width, with_rows):
    comps = score_parts[0].shape[0]
    shapes = [jax.ShapeDtypeStruct((comps, width), F32) for _ in picks]
    if with_rows:
        shapes.append(jax.ShapeDtypeStruct((comps, 128), F32))
    return pl.pallas_call(
        functools.partial(spread_kernel, len(score_parts), picks, with_rows),
        out_shape=shapes,
        in_specs=[SCALARS] + [WHOLE] * (len(score_parts) + 2),
        out_specs=[WHOLE] * len(shapes),
        compiler_params=PARAMS,
        name="spread_rows" if with_rows else "spread",
    )(me, *score_parts, high, low)


def gram_kernel(count, scale, *refs):
    pieces, (sums_ref, rows_ref, spread_ref, gram_ref) = refs[:count], refs[count:]
    mean = sums_ref[...] * scale
    spread = tree_sum([ref[...] for ref in pieces]) - rows_ref[:, :1] * mean
    spread_ref[...] = spread
    gram_ref[...] = lax.dot_general(
        spread, spread, NT, precision=lax.Precision.HIGHEST, preferred_element_type=F32
    )


def centered_gram(pieces, sums, rows, cell_total):
    comps, width = pieces[0].shape
    return pl.pallas_call(
        functools.partial(gram_kernel, len(pieces), 1.0 / cell_total),
        out_shape=(
            jax.ShapeDtypeStruct((comps, width), F32),
            jax.ShapeDtypeStruct((comps, comps), F32),
        ),
        in_specs=[WHOLE] * (len(pieces) + 2),
        out_specs=(WHOLE, WHOLE),
        compiler_params=PARAMS,
        name="gram",
    )(*pieces, sums, rows)


def basis_kernel(count, scale, *refs):
    grams, (spread_ref, out_ref) = refs[:count], refs[count:]
    gram = tree_sum([ref[...] for ref in grams])
    comps = gram.shape[0]
    row_at = lax.broadcasted_iota(jnp.int32, (comps, comps), 0)
    col_at = lax.broadcasted_iota(jnp.int32, (comps, comps), 1)
    eye = row_at == col_at
    both = jnp.concatenate([gram, jnp.where(eye, 1.0, 0.0).astype(F32)], axis=1)
    below = lax.broadcasted_iota(jnp.int32, (comps, 1), 0)
    for j in range(comps):
        row = both[j:j + 1, :] / both[j:j + 1, j:j + 1]
        both = both - jnp.where(below > j, both[:, j:j + 1], 0.0) * row
    pivots = jnp.sum(jnp.where(eye, both[:, :comps], 0.0), axis=1, keepdims=True)
    inverse = both[:, comps:] * (scale / jnp.sqrt(pivots))
    out_ref[...] = lax.dot_general(
        inverse, spread_ref[...], NN, precision=lax.Precision.HIGHEST, preferred_element_type=F32
    )


def orthonormal(grams, spread, scale):
    return pl.pallas_call(
        functools.partial(basis_kernel, len(grams), scale),
        out_shape=jax.ShapeDtypeStruct(spread.shape, F32),
        in_specs=[WHOLE] * (len(grams) + 1),
        out_specs=WHOLE,
        compiler_params=PARAMS,
        name="orthonormal",
    )(*grams, spread)


def few(size):
    return size <= MOST_PARTNERS and size & (size - 1) == 0


def send(x, axis, offset):
    size = lax.axis_size(axis)
    return lax.ppermute(x, axis, [(i, i ^ offset) for i in range(size)])


def from_partners(x, axis):
    if not few(lax.axis_size(axis)):
        return [lax.psum(x, axis)]
    return [x] + [send(x, axis, k) for k in range(1, lax.axis_size(axis))]


def scattered_spread(score_parts, high, low, width):
    size = lax.axis_size("cells")
    me = lax.axis_index("cells").astype(jnp.int32).reshape(1)
    if size == 1 or not few(size) or width % 128:
        whole, rows = spread_pieces(
            jnp.zeros_like(me), score_parts, high, low, [0], high.shape[1], True
        )
        return [lax.psum_scatter(whole, "cells", scatter_dimension=1, tiled=True)], rows
    away = list(range(size - 1, 0, -2))
    sent = spread_pieces(me, score_parts, high, low, away, width, False)
    came = [send(x, "cells", 1) for x in sent]
    *kept, rows = spread_pieces(me, score_parts, high, low, [k ^ 1 for k in away], width, True)
    parts = {k ^ 1: a + b for k, a, b in zip(away, kept, came)}
    return [parts[0]] + [send(parts[k], "cells", k) for k in range(2, size, 2)], rows


def on_device(counts, occupancy, start_basis):
    cell_count, gene_count = counts.shape
    size = lax.axis_size("cells")
    width = gene_count // size
    me = lax.axis_index("cells")
    high, low, scores, sums = log_and_scores(counts, occupancy, start_basis)
    score_parts = from_partners(scores, "genes")
    sums = tree_sum(from_partners(sums, "cells"))
    sums = lax.dynamic_slice_in_dim(sums, me * width, width, 1)
    pieces, rows = scattered_spread(score_parts, high, low, width)
    rows = tree_sum(from_partners(rows, "cells"))
    spread, gram = centered_gram(pieces, sums, rows, cell_count * size)
    gram = tree_sum(from_partners(gram, "genes"))
    scale = math.sqrt(gene_count * lax.axis_size("genes"))
    return orthonormal(from_partners(gram, "cells"), spread, scale)


def solution(mesh):
    in_specs = (P("cells", "genes"), P("cells", "genes"), P(None, "genes"))
    out_specs = P(None, ("genes", "cells"))
    return jax.shard_map(
        on_device, mesh=mesh, in_specs=in_specs, out_specs=out_specs, check_vma=False
    )
```

```python
import functools
import math

import jax
import jax.numpy as jnp
from jax import lax
from jax.experimental import pallas as pl
from jax.experimental.pallas import tpu as pltpu
from jax.sharding import PartitionSpec as P

F32 = jnp.float32
BF16 = jnp.bfloat16
NN = (((1,), (0,)), ((), ()))
NT = (((1,), (1,)), ((), ()))
WHOLE = pl.BlockSpec(memory_space=pltpu.VMEM)
SCALARS = pl.BlockSpec(memory_space=pltpu.SMEM)
PARAMS = pltpu.CompilerParams(vmem_limit_bytes=48 * 2**20)
MOST_PARTNERS = 8


def dot(a, b, dims):
    return lax.dot_general(a, b, dims, preferred_element_type=F32)


def split_terms(x, count):
    terms = []
    for _ in range(count):
        term = x.astype(BF16)
        terms.append(term)
        x = x - term.astype(F32)
    return terms


def tree_sum(parts):
    while len(parts) > 1:
        parts = [a + b for a, b in zip(parts[::2], parts[1::2])]
    return parts[0]


def sum_over(parts):
    return tree_sum([parts[k] for k in range(parts.shape[0])])


def log_kernel(tile_rows, tile_edge, width, occ_hbm, counts_hbm, basis_hbm, high_ref, low_ref, score_ref, sum_ref,
               occ_ref, counts_ref, basis_ref, occ_sem, basis_sem, counts_sem):
    cells, genes = high_ref.shape
    fetch_occ = pltpu.make_async_copy(occ_hbm, occ_ref, occ_sem)
    fetch_basis = pltpu.make_async_copy(basis_hbm, basis_ref, basis_sem)
    fetches = [
        pltpu.make_async_copy(
            counts_hbm.at[:, pl.ds(at * width, width)], counts_ref.at[:, pl.ds(at * width, width)], counts_sem.at[at]
        )
        for at in range(genes // width)
    ]
    fetch_occ.start()
    for fetch in fetches:
        fetch.start()
    fetch_basis.start()
    fetch_occ.wait()
    scores = None
    for at, fetch in enumerate(fetches):
        fetch.wait()
        for col in range(at * width // tile_edge, (at + 1) * width // tile_edge):
            lanes = pl.ds(col * tile_edge, tile_edge)
            total = None
            for row in range(tile_rows):
                subs = pl.ds(row * tile_edge, tile_edge)
                occ = occ_ref[row, col].astype(F32)
                logged = jnp.log(1.0 + counts_ref[subs, lanes].astype(F32)) * occ
                high = logged.astype(BF16)
                high_ref[subs, lanes] = high
                low_ref[subs, lanes] = (logged - high.astype(F32)).astype(BF16)
                part = jnp.sum(logged, axis=0, keepdims=True)
                total = part if total is None else total + part
            sum_ref[:, lanes] = total
        if at == 0:
            fetch_basis.wait()
        chunk = pl.ds(at * width, width)
        basis = basis_ref[:, chunk]
        part = dot(basis, high_ref[:, chunk], NT) + dot(basis, low_ref[:, chunk], NT)
        scores = part if scores is None else scores + part
    for k in range(score_ref.shape[0]):
        score_ref[k] = scores


def log_and_scores(counts, occupancy, basis, copies):
    cells, genes = counts.shape
    tile_rows, tile_cols = occupancy.shape
    edge = cells // tile_rows
    comps = basis.shape[0]
    width = genes // 4 if genes % (4 * edge) == 0 else genes
    hbm = pl.BlockSpec(memory_space=pltpu.HBM)
    return pl.pallas_call(
        functools.partial(log_kernel, tile_rows, edge, width),
        out_shape=(
            jax.ShapeDtypeStruct((cells, genes), BF16),
            jax.ShapeDtypeStruct((cells, genes), BF16),
            jax.ShapeDtypeStruct((copies, comps, cells), F32),
            jax.ShapeDtypeStruct((1, genes), F32),
        ),
        in_specs=[hbm, hbm, hbm],
        out_specs=(WHOLE, WHOLE, WHOLE, WHOLE),
        scratch_shapes=[
            pltpu.SMEM(occupancy.shape, jnp.int32),
            pltpu.VMEM(counts.shape, BF16),
            pltpu.VMEM(basis.shape, BF16),
            pltpu.SemaphoreType.DMA,
            pltpu.SemaphoreType.DMA,
            pltpu.SemaphoreType.DMA((genes // width,)),
        ],
        compiler_params=PARAMS,
        name="log_scores",
    )(occupancy, counts, basis)


def spread_piece(terms, high, low):
    comps = terms[0].shape[0]
    on_low = dot(jnp.concatenate(terms[:2], axis=0), low, NN)
    on_high = dot(jnp.concatenate(terms, axis=0), high, NN)
    small = on_low[comps:] + on_high[2 * comps:]
    middle = on_low[:comps] + on_high[comps:2 * comps]
    return (small + middle) + on_high[:comps]


def spread_kernel(score_ref, high_ref, low_ref, sum_ref, out_ref):
    scores = sum_over(score_ref)
    comps, cells = scores.shape
    terms = split_terms(scores, 3)
    pieces, rows, width = out_ref.shape
    eye = lax.broadcasted_iota(jnp.int32, (comps, comps), 0) == lax.broadcasted_iota(jnp.int32, (comps, comps), 1)
    row_sums = jnp.sum(jnp.where(eye, jnp.sum(scores, axis=1, keepdims=True), 0.0), axis=0, keepdims=True)
    row_sums = [row_sums[:, at:at + width] for at in range(0, comps, width)]
    if width > comps:
        row_sums = [jnp.concatenate(row_sums + [jnp.zeros((1, width - comps), F32)], axis=1)]
    zeros = jnp.zeros((rows - comps - 1 - len(row_sums), width), F32)
    for d in range(pieces):
        lanes = pl.ds(d * width, width)
        out_ref[d, :comps] = spread_piece(terms, high_ref[:, lanes], low_ref[:, lanes])
        out_ref[d, comps:] = jnp.concatenate([sum_ref[:, lanes]] + row_sums + [zeros], axis=0)


def extra_rows(comps, width):
    return -(-(1 - (-comps // width)) // 8) * 8


def spread_pieces(scores, high, low, sums, pieces):
    comps = scores.shape[1]
    width = high.shape[1] // pieces
    return pl.pallas_call(
        spread_kernel,
        out_shape=jax.ShapeDtypeStruct((pieces, comps + extra_rows(comps, width), width), F32),
        in_specs=[WHOLE] * 4,
        out_specs=WHOLE,
        compiler_params=PARAMS,
        name="spread",
    )(scores, high, low, sums)


def gram_kernel(scale, piece_ref, spread_ref, gram_ref):
    total = sum_over(piece_ref)
    comps, width = spread_ref.shape
    mean = total[comps:comps + 1] * scale
    eye = lax.broadcasted_iota(jnp.int32, (comps, comps), 0) == lax.broadcasted_iota(jnp.int32, (comps, comps), 1)
    row_sums = [total[comps + 1 + at:comps + 2 + at, :comps] for at in range(-(-comps // width))]
    row_sums = row_sums[0] if len(row_sums) == 1 else jnp.concatenate(row_sums, axis=1)
    row_sums = jnp.sum(jnp.where(eye, row_sums, 0.0), axis=1, keepdims=True)
    spread = total[:comps] - row_sums * mean
    spread_ref[...] = spread
    gram = lax.dot_general(
        spread, spread, NT, precision=lax.Precision.HIGHEST, preferred_element_type=F32
    )
    half = comps // 2
    gram = jnp.concatenate([gram[:half], gram[half:]], axis=1)
    for k in range(gram_ref.shape[0]):
        gram_ref[k] = gram


def centered_gram(pieces, comps, cell_total, copies):
    width = pieces.shape[2]
    return pl.pallas_call(
        functools.partial(gram_kernel, 1.0 / cell_total),
        out_shape=(
            jax.ShapeDtypeStruct((comps, width), F32),
            jax.ShapeDtypeStruct((copies, comps // 2, comps * 2), F32),
        ),
        in_specs=[WHOLE],
        out_specs=(WHOLE, WHOLE),
        compiler_params=PARAMS,
        name="gram",
    )(pieces)


def add_kernel(part_ref, out_ref):
    total = sum_over(part_ref)
    for k in range(out_ref.shape[0]):
        out_ref[k] = total


def add_and_copy(parts, copies):
    return pl.pallas_call(
        add_kernel,
        out_shape=jax.ShapeDtypeStruct((copies,) + parts.shape[1:], F32),
        in_specs=[WHOLE],
        out_specs=WHOLE,
        compiler_params=PARAMS,
        name="add",
    )(parts)


def basis_kernel(scale, gram_ref, spread_ref, out_ref):
    gram = sum_over(gram_ref)
    comps = spread_ref.shape[0]
    gram = jnp.concatenate([gram[:, :comps], gram[:, comps:]], axis=0)
    row_at = lax.broadcasted_iota(jnp.int32, (comps, comps), 0)
    col_at = lax.broadcasted_iota(jnp.int32, (comps, comps), 1)
    eye = row_at == col_at
    both = jnp.concatenate([gram, jnp.where(eye, 1.0, 0.0).astype(F32)], axis=1)
    below = lax.broadcasted_iota(jnp.int32, (comps, 1), 0)
    for j in range(comps):
        row = both[j:j + 1, :] / both[j:j + 1, j:j + 1]
        both = both - jnp.where(below > j, both[:, j:j + 1], 0.0) * row
    pivots = jnp.sum(jnp.where(eye, both[:, :comps], 0.0), axis=1, keepdims=True)
    inverse = both[:, comps:] * (scale / jnp.sqrt(pivots))
    out_ref[...] = lax.dot_general(
        inverse, spread_ref[...], NN, precision=lax.Precision.HIGHEST, preferred_element_type=F32
    )


def orthonormal(grams, spread, scale):
    return pl.pallas_call(
        functools.partial(basis_kernel, scale),
        out_shape=jax.ShapeDtypeStruct(spread.shape, F32),
        in_specs=[WHOLE, WHOLE],
        out_specs=WHOLE,
        compiler_params=PARAMS,
        name="orthonormal",
    )(grams, spread)


def swap(parts, axis):
    return lax.all_to_all(parts, axis, 0, 0)


def on_device(counts, occupancy, start_basis):
    cell_count, gene_count = counts.shape
    cells, genes = lax.axis_size("cells"), lax.axis_size("genes")
    high, low, scores, sums = log_and_scores(counts, occupancy, start_basis, genes)
    pieces = spread_pieces(swap(scores, "genes"), high, low, sums, cells)
    spread, gram = centered_gram(swap(pieces, "cells"), start_basis.shape[0], cell_count * cells, genes)
    gram = add_and_copy(swap(gram, "genes"), cells)
    return orthonormal(swap(gram, "cells"), spread, math.sqrt(gene_count * genes))


def solution(mesh):
    in_specs = (P("cells", "genes"), P("cells", "genes"), P(None, "genes"))
    out_specs = P(None, ("genes", "cells"))
    return jax.shard_map(
        on_device, mesh=mesh, in_specs=in_specs, out_specs=out_specs, check_vma=False
    )
```

```python
import functools
import math

import jax
import jax.numpy as jnp
from jax import lax
from jax.experimental import pallas as pl
from jax.experimental.pallas import tpu as pltpu
from jax.sharding import PartitionSpec as P

F32 = jnp.float32
BF16 = jnp.bfloat16
NN = (((1,), (0,)), ((), ()))
NT = (((1,), (1,)), ((), ()))
WHOLE = pl.BlockSpec(memory_space=pltpu.VMEM)
SCALARS = pl.BlockSpec(memory_space=pltpu.SMEM)
LANES = 128
PARAMS = pltpu.CompilerParams(vmem_limit_bytes=16 * 2**20)
LOG_PARAMS = pltpu.CompilerParams(vmem_limit_bytes=205 * 2**18)
MOST_PARTNERS = 8


def dot(a, b, dims):
    return lax.dot_general(a, b, dims, preferred_element_type=F32)


def split_terms(x, count):
    terms = []
    for _ in range(count):
        term = x.astype(BF16)
        terms.append(term)
        x = x - term.astype(F32)
    return terms


def tree_sum(parts):
    while len(parts) > 1:
        parts = [sum(parts[at + 1:at + 2], parts[at]) for at in range(0, len(parts), 2)]
    return parts[0]


def log_kernel(tile_rows, tile_edge, width, occ_hbm, counts_hbm, basis_hbm, high_ref, low_ref, score_ref, sum_ref,
               occ_ref, counts_ref, basis_ref, occ_sem, basis_sem, counts_sem):
    cells, genes = high_ref.shape
    fetch_occ = pltpu.make_async_copy(occ_hbm, occ_ref, occ_sem)
    fetch_basis = pltpu.make_async_copy(basis_hbm, basis_ref, basis_sem)
    fetches = [
        pltpu.make_async_copy(
            counts_hbm.at[:, pl.ds(at * width, width)], counts_ref.at[:, pl.ds(at * width, width)], counts_sem.at[at]
        )
        for at in range(genes // width)
    ]
    fetch_occ.start()
    for fetch in fetches:
        fetch.start()
    fetch_basis.start()
    fetch_occ.wait()
    scores = None
    for at, fetch in enumerate(fetches):
        fetch.wait()
        for col in range(at * width // tile_edge, (at + 1) * width // tile_edge):
            lanes = pl.ds(col * tile_edge, tile_edge)
            total = None
            for row in range(tile_rows):
                subs = pl.ds(row * tile_edge, tile_edge)
                occ = occ_ref[row, col].astype(F32)
                logged = jnp.log(1.0 + counts_ref[subs, lanes].astype(F32)) * occ
                high = logged.astype(BF16)
                high_ref[subs, lanes] = high
                low_ref[subs, lanes] = (logged - high.astype(F32)).astype(BF16)
                part = jnp.sum(logged, axis=0, keepdims=True)
                total = part if total is None else total + part
            sum_ref[:, lanes] = total
        if at == 0:
            fetch_basis.wait()
        chunk = pl.ds(at * width, width)
        basis = basis_ref[:, chunk]
        part = dot(basis, high_ref[:, chunk], NT) + dot(basis, low_ref[:, chunk], NT)
        scores = part if scores is None else scores + part
    score_ref[...] = scores


def log_and_scores(counts, occupancy, basis):
    cells, genes = counts.shape
    tile_rows, tile_cols = occupancy.shape
    edge = cells // tile_rows
    comps = basis.shape[0]
    width = genes // 4 if genes % (4 * edge) == 0 else genes
    hbm = pl.BlockSpec(memory_space=pltpu.HBM)
    return pl.pallas_call(
        functools.partial(log_kernel, tile_rows, edge, width),
        out_shape=(
            jax.ShapeDtypeStruct((cells, genes), BF16),
            jax.ShapeDtypeStruct((cells, genes), BF16),
            jax.ShapeDtypeStruct((comps, cells), F32),
            jax.ShapeDtypeStruct((1, genes), F32),
        ),
        in_specs=[hbm, hbm, hbm],
        out_specs=(WHOLE, WHOLE, WHOLE, WHOLE),
        scratch_shapes=[
            pltpu.SMEM(occupancy.shape, jnp.int32),
            pltpu.VMEM(counts.shape, BF16),
            pltpu.VMEM(basis.shape, BF16),
            pltpu.SemaphoreType.DMA,
            pltpu.SemaphoreType.DMA,
            pltpu.SemaphoreType.DMA((genes // width,)),
        ],
        compiler_params=LOG_PARAMS,
        name="log_scores",
    )(occupancy, counts, basis)


def spread_piece(terms, high, low):
    comps = terms[0].shape[0]
    on_low = dot(jnp.concatenate(terms[:2], axis=0), low, NN)
    on_high = dot(jnp.concatenate(terms, axis=0), high, NN)
    small = on_low[comps:] + on_high[2 * comps:]
    middle = on_low[:comps] + on_high[comps:2 * comps]
    return (small + middle) + on_high[:comps]


def spread_kernel(count, picks, me_ref, *refs):
    score_refs, (high_ref, low_ref, sum_ref), outs = refs[:count], refs[count:count + 3], refs[count + 3:]
    scores = tree_sum([ref[...] for ref in score_refs])
    comps = scores.shape[0]
    terms = split_terms(scores, 3)
    eye = lax.broadcasted_iota(jnp.int32, (comps, LANES), 0) == lax.broadcasted_iota(jnp.int32, (comps, LANES), 1)
    row_sums = jnp.sum(jnp.where(eye, jnp.sum(scores, axis=1, keepdims=True), 0.0), axis=0, keepdims=True)
    chunks = high_ref.shape[1] // (LANES * lax.axis_size("cells"))
    width = chunks * LANES
    for pick, out in zip(picks, outs):
        start = pl.multiple_of((me_ref[0] ^ pick) * width, width)
        lanes = pl.ds(start, width)
        piece = spread_piece(terms, high_ref[:, lanes], low_ref[:, lanes])
        sums = sum_ref[:, lanes]
        extra = [row_sums]
        for at in range(chunks):
            out[at * comps:(at + 1) * comps] = piece[:, at * LANES:(at + 1) * LANES]
            extra.append(sums[:, at * LANES:(at + 1) * LANES])
        extra.append(jnp.zeros((out.shape[0] - chunks * comps - chunks - 1, LANES), F32))
        out[chunks * comps:] = jnp.concatenate(extra, axis=0)


def block_rows(comps, chunks):
    return comps * chunks + -(-(chunks + 1) // 8) * 8


def spread_pieces(me, scores, high, low, sums, picks):
    comps = scores[0].shape[0]
    chunks = high.shape[1] // (LANES * lax.axis_size("cells"))
    block = jax.ShapeDtypeStruct((block_rows(comps, chunks), LANES), F32)
    return pl.pallas_call(
        functools.partial(spread_kernel, len(scores), picks),
        out_shape=[block] * len(picks),
        in_specs=[SCALARS] + [WHOLE] * (len(scores) + 3),
        out_specs=[WHOLE] * len(picks),
        compiler_params=PARAMS,
        name="spread",
    )(me, *scores, high, low, sums)


def gram_kernel(scale, chunks, *refs):
    pieces, (spread_ref, gram_ref) = refs[:-2], refs[-2:]
    comps = spread_ref.shape[0]
    total = tree_sum([ref[...] for ref in pieces])
    extra = total[chunks * comps:chunks * comps + chunks + 1]
    eye = lax.broadcasted_iota(jnp.int32, (comps, LANES), 0) == lax.broadcasted_iota(jnp.int32, (comps, LANES), 1)
    row_sums = jnp.sum(jnp.where(eye, extra[:1], 0.0), axis=1, keepdims=True) * scale
    parts = [total[at * comps:(at + 1) * comps] - row_sums * extra[at + 1:at + 2] for at in range(chunks)]
    spread = jnp.concatenate(parts, axis=1)
    spread_ref[...] = spread
    gram_ref[...] = packed_gram(spread)


def packed_gram(spread):
    gram = lax.dot_general(spread, spread, NT, precision=lax.Precision.HIGHEST, preferred_element_type=F32)
    half = spread.shape[0] // 2
    return jnp.concatenate([gram[:half], gram[half:]], axis=1)


def centered_gram(pieces, comps, cell_total):
    chunks = pieces[0].shape[0] // comps
    return pl.pallas_call(
        functools.partial(gram_kernel, 1.0 / cell_total, chunks),
        out_shape=(
            jax.ShapeDtypeStruct((comps, chunks * LANES), F32),
            jax.ShapeDtypeStruct((comps // 2, comps * 2), F32),
        ),
        in_specs=[WHOLE] * len(pieces),
        out_specs=(WHOLE, WHOLE),
        compiler_params=PARAMS,
        name="gram",
    )(*pieces)


def plain_gram_kernel(scale, spread_ref, row_ref, sum_ref, out_ref, gram_ref):
    spread = spread_ref[...] - row_ref[...] * scale * sum_ref[...]
    out_ref[...] = spread
    gram_ref[...] = packed_gram(spread)


def plain_gram(spread, rows, sums, cell_total):
    comps, width = spread.shape
    return pl.pallas_call(
        functools.partial(plain_gram_kernel, 1.0 / cell_total),
        out_shape=(
            jax.ShapeDtypeStruct((comps, width), F32),
            jax.ShapeDtypeStruct((comps // 2, comps * 2), F32),
        ),
        in_specs=[WHOLE] * 3,
        out_specs=(WHOLE, WHOLE),
        compiler_params=PARAMS,
        name="plain_gram",
    )(spread, rows, sums)


def basis_kernel(scale, *refs):
    grams, (spread_ref, out_ref) = refs[:-2], refs[-2:]
    gram = tree_sum([ref[...] for ref in grams])
    comps = spread_ref.shape[0]
    gram = jnp.concatenate([gram[:, :comps], gram[:, comps:]], axis=0)
    row_at = lax.broadcasted_iota(jnp.int32, (comps, comps), 0)
    col_at = lax.broadcasted_iota(jnp.int32, (comps, comps), 1)
    eye = row_at == col_at
    both = jnp.concatenate([gram, jnp.where(eye, 1.0, 0.0).astype(F32)], axis=1)
    below = lax.broadcasted_iota(jnp.int32, (comps, 1), 0)
    for j in range(comps):
        row = both[j:j + 1, :] / both[j:j + 1, j:j + 1]
        both = both - jnp.where(below > j, both[:, j:j + 1], 0.0) * row
    pivots = jnp.sum(jnp.where(eye, both[:, :comps], 0.0), axis=1, keepdims=True)
    inverse = both[:, comps:] * (scale / jnp.sqrt(pivots))
    out_ref[...] = lax.dot_general(
        inverse, spread_ref[...], NN, precision=lax.Precision.HIGHEST, preferred_element_type=F32
    )


def orthonormal(grams, spread, scale):
    return pl.pallas_call(
        functools.partial(basis_kernel, scale),
        out_shape=jax.ShapeDtypeStruct(spread.shape, F32),
        in_specs=[WHOLE] * (len(grams) + 1),
        out_specs=WHOLE,
        compiler_params=PARAMS,
        name="orthonormal",
    )(*grams, spread)


def few(size):
    return size <= MOST_PARTNERS and size & (size - 1) == 0


def send(x, axis, offset):
    return lax.ppermute(x, axis, [(i, i ^ offset) for i in range(lax.axis_size(axis))])


def from_partners(x, axis, offsets):
    return [x] + [send(x, axis, k) for k in offsets]


def sum_in_steps(x, axis):
    size = lax.axis_size(axis)
    if not few(size):
        return [lax.psum(x, axis)]
    if size > 4:
        x = tree_sum(from_partners(x, axis, [1]))
        return from_partners(x, axis, range(2, size, 2))
    return from_partners(x, axis, range(1, size))


def scattered_spread(scores, high, low, sums, cell_total):
    size = lax.axis_size("cells")
    comps = scores[0].shape[0]
    width = high.shape[1] // size
    if size == 1 or not few(size) or width % LANES:
        scores = tree_sum(scores)
        terms = split_terms(scores, 3)
        spread = lax.psum_scatter(spread_piece(terms, high, low), "cells", scatter_dimension=1, tiled=True)
        rows = lax.psum(jnp.sum(scores, axis=1, keepdims=True), "cells")
        sums = lax.psum_scatter(sums, "cells", scatter_dimension=1, tiled=True)
        return plain_gram(spread, rows, sums, cell_total)
    me = lax.axis_index("cells").astype(jnp.int32).reshape(1)
    away = list(range(size - 1, 0, -2))
    came = [send(x, "cells", 1) for x in spread_pieces(me, scores, high, low, sums, away)]
    kept = spread_pieces(me, scores, high, low, sums, [k ^ 1 for k in away])
    own = [kept[-1], came[-1]]
    far = [send(a + b, "cells", k ^ 1) for k, a, b in zip(away[:-1], kept, came)]
    return centered_gram(own + far, comps, cell_total)


def on_device(counts, occupancy, start_basis):
    cell_count, gene_count = counts.shape
    cells, genes = lax.axis_size("cells"), lax.axis_size("genes")
    high, low, scores, sums = log_and_scores(counts, occupancy, start_basis)
    scores = sum_in_steps(scores, "genes")
    spread, gram = scattered_spread(scores, high, low, sums, cell_count * cells)
    gram = tree_sum(sum_in_steps(gram, "genes"))
    return orthonormal(sum_in_steps(gram, "cells"), spread, math.sqrt(gene_count * genes))


def solution(mesh):
    in_specs = (P("cells", "genes"), P("cells", "genes"), P(None, "genes"))
    out_specs = P(None, ("genes", "cells"))
    return jax.shard_map(
        on_device, mesh=mesh, in_specs=in_specs, out_specs=out_specs, check_vma=False
    )
```

```python
import functools
import math

import jax
import jax.numpy as jnp
from jax import lax
from jax.experimental import pallas as pl
from jax.experimental.pallas import tpu as pltpu
from jax.sharding import PartitionSpec as P

F32 = jnp.float32
BF16 = jnp.bfloat16
NN = (((1,), (0,)), ((), ()))
NT = (((1,), (1,)), ((), ()))
WHOLE = pl.BlockSpec(memory_space=pltpu.VMEM)
SCALARS = pl.BlockSpec(memory_space=pltpu.SMEM)
LANES = 128
PARAMS = pltpu.CompilerParams(vmem_limit_bytes=16 * 2**20)
LOG_PARAMS = pltpu.CompilerParams(vmem_limit_bytes=205 * 2**18)
MOST_PARTNERS = 8


def dot(a, b, dims):
    return lax.dot_general(a, b, dims, preferred_element_type=F32)


def split_terms(x, count):
    terms = []
    for _ in range(count):
        term = x.astype(BF16)
        terms.append(term)
        x = x - term.astype(F32)
    return terms


def tree_sum(parts):
    while len(parts) > 1:
        parts = [sum(parts[at + 1:at + 2], parts[at]) for at in range(0, len(parts), 2)]
    return parts[0]


def log_kernel(tile_rows, tile_edge, width, occ_hbm, counts_hbm, basis_hbm, high_ref, low_ref, score_ref, sum_ref,
               occ_ref, counts_ref, basis_ref, occ_sem, basis_sem, counts_sem):
    cells, genes = high_ref.shape
    fetch_occ = pltpu.make_async_copy(occ_hbm, occ_ref, occ_sem)
    fetch_basis = pltpu.make_async_copy(basis_hbm, basis_ref, basis_sem)
    fetches = [
        pltpu.make_async_copy(
            counts_hbm.at[:, pl.ds(at * width, width)], counts_ref.at[:, pl.ds(at * width, width)], counts_sem.at[at]
        )
        for at in range(genes // width)
    ]
    fetch_occ.start()
    for fetch in fetches:
        fetch.start()
    fetch_basis.start()
    fetch_occ.wait()
    scores = None
    for at, fetch in enumerate(fetches):
        fetch.wait()
        for col in range(at * width // tile_edge, (at + 1) * width // tile_edge):
            lanes = pl.ds(col * tile_edge, tile_edge)
            total = None
            for row in range(tile_rows):
                subs = pl.ds(row * tile_edge, tile_edge)
                occ = occ_ref[row, col].astype(F32)
                logged = jnp.log(1.0 + counts_ref[subs, lanes].astype(F32)) * occ
                high = logged.astype(BF16)
                high_ref[subs, lanes] = high
                low_ref[subs, lanes] = (logged - high.astype(F32)).astype(BF16)
                part = jnp.sum(logged, axis=0, keepdims=True)
                total = part if total is None else total + part
            sum_ref[:, lanes] = total
        if at == 0:
            fetch_basis.wait()
        chunk = pl.ds(at * width, width)
        basis = basis_ref[:, chunk]
        part = dot(basis, high_ref[:, chunk], NT) + dot(basis, low_ref[:, chunk], NT)
        scores = part if scores is None else scores + part
    score_ref[...] = scores


def log_and_scores(counts, occupancy, basis):
    cells, genes = counts.shape
    tile_rows, tile_cols = occupancy.shape
    edge = cells // tile_rows
    comps = basis.shape[0]
    width = genes // 4 if genes % (4 * edge) == 0 else genes
    hbm = pl.BlockSpec(memory_space=pltpu.HBM)
    return pl.pallas_call(
        functools.partial(log_kernel, tile_rows, edge, width),
        out_shape=(
            jax.ShapeDtypeStruct((cells, genes), BF16),
            jax.ShapeDtypeStruct((cells, genes), BF16),
            jax.ShapeDtypeStruct((comps, cells), F32),
            jax.ShapeDtypeStruct((1, genes), F32),
        ),
        in_specs=[hbm, hbm, hbm],
        out_specs=(WHOLE, WHOLE, WHOLE, WHOLE),
        scratch_shapes=[
            pltpu.SMEM(occupancy.shape, jnp.int32),
            pltpu.VMEM(counts.shape, BF16),
            pltpu.VMEM(basis.shape, BF16),
            pltpu.SemaphoreType.DMA,
            pltpu.SemaphoreType.DMA,
            pltpu.SemaphoreType.DMA((genes // width,)),
        ],
        compiler_params=LOG_PARAMS,
        name="log_scores",
    )(occupancy, counts, basis)


def spread_piece(terms, high, low):
    comps = terms[0].shape[0]
    on_low = dot(jnp.concatenate(terms[:2], axis=0), low, NN)
    on_high = dot(jnp.concatenate(terms, axis=0), high, NN)
    small = on_low[comps:] + on_high[2 * comps:]
    middle = on_low[:comps] + on_high[comps:2 * comps]
    return (small + middle) + on_high[:comps]


def spread_kernel(count, picks, me_ref, *refs):
    score_refs, (high_ref, low_ref, sum_ref), outs = refs[:count], refs[count:count + 3], refs[count + 3:]
    scores = tree_sum([ref[...] for ref in score_refs])
    comps = scores.shape[0]
    terms = split_terms(scores, 3)
    eye = lax.broadcasted_iota(jnp.int32, (comps, LANES), 0) == lax.broadcasted_iota(jnp.int32, (comps, LANES), 1)
    row_sums = jnp.sum(jnp.where(eye, jnp.sum(scores, axis=1, keepdims=True), 0.0), axis=0, keepdims=True)
    chunks = high_ref.shape[1] // (LANES * lax.axis_size("cells"))
    width = chunks * LANES
    for pick, out in zip(picks, outs):
        start = pl.multiple_of((me_ref[0] ^ pick) * width, width)
        lanes = pl.ds(start, width)
        piece = spread_piece(terms, high_ref[:, lanes], low_ref[:, lanes])
        sums = sum_ref[:, lanes]
        extra = [row_sums]
        for at in range(chunks):
            out[at * comps:(at + 1) * comps] = piece[:, at * LANES:(at + 1) * LANES]
            extra.append(sums[:, at * LANES:(at + 1) * LANES])
        extra.append(jnp.zeros((out.shape[0] - chunks * comps - chunks - 1, LANES), F32))
        out[chunks * comps:] = jnp.concatenate(extra, axis=0)


def block_rows(comps, chunks):
    return comps * chunks + -(-(chunks + 1) // 8) * 8


def spread_pieces(me, scores, high, low, sums, picks):
    comps = scores[0].shape[0]
    chunks = high.shape[1] // (LANES * lax.axis_size("cells"))
    block = jax.ShapeDtypeStruct((block_rows(comps, chunks), LANES), F32)
    return pl.pallas_call(
        functools.partial(spread_kernel, len(scores), picks),
        out_shape=[block] * len(picks),
        in_specs=[SCALARS] + [WHOLE] * (len(scores) + 3),
        out_specs=[WHOLE] * len(picks),
        compiler_params=PARAMS,
        cost_estimate=pl.CostEstimate(
            flops=10 * comps * len(picks) * chunks * LANES * high.shape[0], bytes_accessed=2**21, transcendentals=0
        ),
        name="spread",
    )(me, *scores, high, low, sums)


def gram_kernel(scale, chunks, *refs):
    pieces, (spread_ref, gram_ref) = refs[:-2], refs[-2:]
    comps = spread_ref.shape[0]
    total = tree_sum([ref[...] for ref in pieces])
    extra = total[chunks * comps:chunks * comps + chunks + 1]
    eye = lax.broadcasted_iota(jnp.int32, (comps, LANES), 0) == lax.broadcasted_iota(jnp.int32, (comps, LANES), 1)
    row_sums = jnp.sum(jnp.where(eye, extra[:1], 0.0), axis=1, keepdims=True) * scale
    parts = [total[at * comps:(at + 1) * comps] - row_sums * extra[at + 1:at + 2] for at in range(chunks)]
    spread = jnp.concatenate(parts, axis=1)
    spread_ref[...] = spread
    gram_ref[...] = packed_gram(spread)


def packed_gram(spread):
    gram = lax.dot_general(spread, spread, NT, precision=lax.Precision.HIGHEST, preferred_element_type=F32)
    half = spread.shape[0] // 2
    return jnp.concatenate([gram[:half], gram[half:]], axis=1)


def centered_gram(pieces, comps, cell_total):
    chunks = pieces[0].shape[0] // comps
    return pl.pallas_call(
        functools.partial(gram_kernel, 1.0 / cell_total, chunks),
        out_shape=(
            jax.ShapeDtypeStruct((comps, chunks * LANES), F32),
            jax.ShapeDtypeStruct((comps // 2, comps * 2), F32),
        ),
        in_specs=[WHOLE] * len(pieces),
        out_specs=(WHOLE, WHOLE),
        compiler_params=PARAMS,
        name="gram",
    )(*pieces)


def plain_gram_kernel(scale, spread_ref, row_ref, sum_ref, out_ref, gram_ref):
    spread = spread_ref[...] - row_ref[...] * scale * sum_ref[...]
    out_ref[...] = spread
    gram_ref[...] = packed_gram(spread)


def plain_gram(spread, rows, sums, cell_total):
    comps, width = spread.shape
    return pl.pallas_call(
        functools.partial(plain_gram_kernel, 1.0 / cell_total),
        out_shape=(
            jax.ShapeDtypeStruct((comps, width), F32),
            jax.ShapeDtypeStruct((comps // 2, comps * 2), F32),
        ),
        in_specs=[WHOLE] * 3,
        out_specs=(WHOLE, WHOLE),
        compiler_params=PARAMS,
        name="plain_gram",
    )(spread, rows, sums)


def inverse_of(x):
    guess = pl.reciprocal(x, approx=True)
    for _ in range(2):
        guess = guess * (2.0 - x * guess)
    return guess


def row_of(x, at):
    return jnp.broadcast_to(x[at:at + 1, :], x.shape)


def eliminate(groups, edge):
    groups = list(groups)
    below = lax.broadcasted_iota(jnp.int32, groups[0].shape, 0)
    for at in range(len(groups)):
        spread = [
            [jnp.broadcast_to(rows[:, c:c + 1], rows.shape) for c in range(at * edge, (at + 1) * edge)]
            for rows in groups[at:]
        ]
        for i in range(0, edge, 2):
            cols = spread[0]
            first, second = cols[i], cols[i + 1]
            a, b, c = row_of(first, i), row_of(second, i), row_of(second, i + 1)
            inv_a = inverse_of(a)
            inv_c = a * inverse_of(a * c - b * b)
            ratio = b * inv_a
            factors = []
            for k in range(i + 2, edge):
                top = row_of(cols[k], i)
                factors.append((k, top * inv_a, (row_of(cols[k], i + 1) - ratio * top) * inv_c))
            rows = groups[at]
            upper = row_of(rows, i) * inv_a
            rows = rows - jnp.where(below > i, first, 0.0) * upper
            lower = row_of(rows, i + 1) * inv_c
            groups[at] = rows - jnp.where(below > i + 1, second - ratio * first, 0.0) * lower
            for ahead, cols in enumerate(spread):
                first = cols[i]
                second = cols[i + 1] - ratio * first
                for k, on_first, on_second in factors:
                    cols[k] = cols[k] - first * on_first - second * on_second
                if ahead:
                    groups[at + ahead] = groups[at + ahead] - first * upper - second * lower
    return groups


def basis_kernel(scale, *refs):
    grams, (spread_ref, out_ref) = refs[:-2], refs[-2:]
    gram = tree_sum([ref[...] for ref in grams])
    comps = spread_ref.shape[0]
    gram = jnp.concatenate([gram[:, :comps], gram[:, comps:]], axis=0)
    row_at = lax.broadcasted_iota(jnp.int32, (comps, comps), 0)
    col_at = lax.broadcasted_iota(jnp.int32, (comps, comps), 1)
    eye = row_at == col_at
    trace = jnp.sum(jnp.where(eye, gram, 0.0), axis=(0, 1), keepdims=True)
    both = jnp.concatenate([gram * (1.0 / trace), jnp.where(eye, 1.0, 0.0).astype(F32)], axis=1)
    groups = eliminate([both[at:at + 8] for at in range(0, comps, 8)], 8)
    both = jnp.concatenate(groups, axis=0)
    pivots = jnp.sum(jnp.where(eye, both[:, :comps], 0.0), axis=1, keepdims=True)
    inverse = both[:, comps:] * (scale / jnp.sqrt(pivots) / jnp.sqrt(trace))
    out_ref[...] = lax.dot_general(
        inverse, spread_ref[...], NN, precision=lax.Precision.HIGHEST, preferred_element_type=F32
    )


def orthonormal(grams, spread, scale):
    return pl.pallas_call(
        functools.partial(basis_kernel, scale),
        out_shape=jax.ShapeDtypeStruct(spread.shape, F32),
        in_specs=[WHOLE] * (len(grams) + 1),
        out_specs=WHOLE,
        compiler_params=PARAMS,
        name="orthonormal",
    )(*grams, spread)


def few(size):
    return size <= MOST_PARTNERS and size & (size - 1) == 0


def send(x, axis, offset):
    return lax.ppermute(x, axis, [(i, i ^ offset) for i in range(lax.axis_size(axis))])


def from_partners(x, axis, offsets):
    return [x] + [send(x, axis, k) for k in offsets]


def sum_in_steps(x, axis):
    size = lax.axis_size(axis)
    if not few(size):
        return [lax.psum(x, axis)]
    if size > 4:
        x = tree_sum(from_partners(x, axis, range(1, 4)))
        return from_partners(x, axis, range(4, size, 4))
    return from_partners(x, axis, range(1, size))


def scattered_spread(scores, high, low, sums, cell_total):
    size = lax.axis_size("cells")
    comps = scores[0].shape[0]
    width = high.shape[1] // size
    if size == 1 or not few(size) or width % LANES:
        scores = tree_sum(scores)
        terms = split_terms(scores, 3)
        spread = lax.psum_scatter(spread_piece(terms, high, low), "cells", scatter_dimension=1, tiled=True)
        rows = lax.psum(jnp.sum(scores, axis=1, keepdims=True), "cells")
        sums = lax.psum_scatter(sums, "cells", scatter_dimension=1, tiled=True)
        return plain_gram(spread, rows, sums, cell_total)
    me = lax.axis_index("cells").astype(jnp.int32).reshape(1)
    away = list(range(size - 1, 0, -2))
    kept = [k ^ 1 for k in away]
    sent = list(spread_pieces(me, scores, high, low, sums, away[:2]))
    *late, = spread_pieces(me, scores, high, low, sums, away[2:] + kept)
    sent, kept = sent + late[:len(away) - 2], late[len(away) - 2:]
    came, far = [], []
    for at, k in enumerate(away):
        if at == len(away) - 1 and at >= 2:
            sent[at], far[0] = lax.optimization_barrier((sent[at], far[0]))
        elif at >= 2:
            sent[at], came[at - 1] = lax.optimization_barrier((sent[at], came[at - 1]))
        came.append(send(sent[at], "cells", 1))
        if at < len(away) - 1:
            far.append(send(kept[at] + came[at], "cells", k ^ 1))
    return centered_gram([kept[-1], came[-1]] + far, comps, cell_total)


def on_device(counts, occupancy, start_basis):
    cell_count, gene_count = counts.shape
    cells, genes = lax.axis_size("cells"), lax.axis_size("genes")
    high, low, scores, sums = log_and_scores(counts, occupancy, start_basis)
    scores = sum_in_steps(scores, "genes")
    spread, gram = scattered_spread(scores, high, low, sums, cell_count * cells)
    gram = tree_sum(sum_in_steps(gram, "genes"))
    return orthonormal(sum_in_steps(gram, "cells"), spread, math.sqrt(gene_count * genes))


def solution(mesh):
    in_specs = (P("cells", "genes"), P("cells", "genes"), P(None, "genes"))
    out_specs = P(None, ("genes", "cells"))
    return jax.shard_map(
        on_device, mesh=mesh, in_specs=in_specs, out_specs=out_specs, check_vma=False
    )
```

```python
import functools
import math

import jax
import jax.numpy as jnp
from jax import lax
from jax.experimental import pallas as pl
from jax.experimental.pallas import tpu as pltpu
from jax.sharding import PartitionSpec as P

F32 = jnp.float32
BF16 = jnp.bfloat16
NN = (((1,), (0,)), ((), ()))
NT = (((1,), (1,)), ((), ()))
WHOLE = pl.BlockSpec(memory_space=pltpu.VMEM)
SCALARS = pl.BlockSpec(memory_space=pltpu.SMEM)
LANES = 128
PARAMS = pltpu.CompilerParams(vmem_limit_bytes=16 * 2**20)
LOG_PARAMS = pltpu.CompilerParams(vmem_limit_bytes=205 * 2**18)
MOST_PARTNERS = 8


def dot(a, b, dims):
    return lax.dot_general(a, b, dims, preferred_element_type=F32)


def split_terms(x, count):
    terms = []
    for _ in range(count):
        term = x.astype(BF16)
        terms.append(term)
        x = x - term.astype(F32)
    return terms


def tree_sum(parts):
    while len(parts) > 1:
        parts = [sum(parts[at + 1:at + 2], parts[at]) for at in range(0, len(parts), 2)]
    return parts[0]


def log_kernel(tile_rows, tile_edge, width, occ_hbm, counts_hbm, basis_hbm, high_ref, low_ref, score_ref, sum_ref,
               occ_ref, counts_ref, basis_ref, occ_sem, basis_sem, counts_sem):
    cells, genes = high_ref.shape
    fetch_occ = pltpu.make_async_copy(occ_hbm, occ_ref, occ_sem)
    fetch_basis = pltpu.make_async_copy(basis_hbm, basis_ref, basis_sem)
    fetches = [
        pltpu.make_async_copy(
            counts_hbm.at[:, pl.ds(at * width, width)], counts_ref.at[:, pl.ds(at * width, width)], counts_sem.at[at]
        )
        for at in range(genes // width)
    ]
    fetch_occ.start()
    for fetch in fetches:
        fetch.start()
    fetch_basis.start()
    fetch_occ.wait()
    scores = None
    for at, fetch in enumerate(fetches):
        fetch.wait()
        for col in range(at * width // tile_edge, (at + 1) * width // tile_edge):
            lanes = pl.ds(col * tile_edge, tile_edge)
            total = None
            for row in range(tile_rows):
                subs = pl.ds(row * tile_edge, tile_edge)
                occ = occ_ref[row, col].astype(F32)
                logged = jnp.log(1.0 + counts_ref[subs, lanes].astype(F32)) * occ
                high = logged.astype(BF16)
                high_ref[subs, lanes] = high
                low_ref[subs, lanes] = (logged - high.astype(F32)).astype(BF16)
                part = jnp.sum(logged, axis=0, keepdims=True)
                total = part if total is None else total + part
            sum_ref[:, lanes] = total
        if at == 0:
            fetch_basis.wait()
        chunk = pl.ds(at * width, width)
        basis = basis_ref[:, chunk]
        part = dot(basis, high_ref[:, chunk], NT) + dot(basis, low_ref[:, chunk], NT)
        scores = part if scores is None else scores + part
    score_ref[...] = scores


def log_and_scores(counts, occupancy, basis):
    cells, genes = counts.shape
    tile_rows, tile_cols = occupancy.shape
    edge = cells // tile_rows
    comps = basis.shape[0]
    width = genes // 4 if genes % (4 * edge) == 0 else genes
    hbm = pl.BlockSpec(memory_space=pltpu.HBM)
    return pl.pallas_call(
        functools.partial(log_kernel, tile_rows, edge, width),
        out_shape=(
            jax.ShapeDtypeStruct((cells, genes), BF16),
            jax.ShapeDtypeStruct((cells, genes), BF16),
            jax.ShapeDtypeStruct((comps, cells), F32),
            jax.ShapeDtypeStruct((1, genes), F32),
        ),
        in_specs=[hbm, hbm, hbm],
        out_specs=(WHOLE, WHOLE, WHOLE, WHOLE),
        scratch_shapes=[
            pltpu.SMEM(occupancy.shape, jnp.int32),
            pltpu.VMEM(counts.shape, BF16),
            pltpu.VMEM(basis.shape, BF16),
            pltpu.SemaphoreType.DMA,
            pltpu.SemaphoreType.DMA,
            pltpu.SemaphoreType.DMA((genes // width,)),
        ],
        compiler_params=LOG_PARAMS,
        name="log_scores",
    )(occupancy, counts, basis)


def spread_piece(terms, high, low):
    comps = terms[0].shape[0]
    on_low = dot(jnp.concatenate(terms[:2], axis=0), low, NN)
    on_high = dot(jnp.concatenate(terms, axis=0), high, NN)
    small = on_low[comps:] + on_high[2 * comps:]
    middle = on_low[:comps] + on_high[comps:2 * comps]
    return (small + middle) + on_high[:comps]


def spread_kernel(count, picks, me_ref, *refs):
    score_refs, (high_ref, low_ref, sum_ref), outs = refs[:count], refs[count:count + 3], refs[count + 3:]
    scores = tree_sum([ref[...] for ref in score_refs])
    comps = scores.shape[0]
    half = comps // 2
    terms = split_terms(scores, 3)
    terms = [[term[at:at + half] for term in terms] for at in (0, half)]
    eye = lax.broadcasted_iota(jnp.int32, (comps, LANES), 0) == lax.broadcasted_iota(jnp.int32, (comps, LANES), 1)
    row_sums = jnp.sum(jnp.where(eye, jnp.sum(scores, axis=1, keepdims=True), 0.0), axis=0, keepdims=True)
    chunks = high_ref.shape[1] // (LANES * lax.axis_size("cells"))
    width = chunks * LANES
    for pick, out in zip(picks, outs):
        for i, (offset, which) in enumerate(pick):
            lanes = pl.ds(pl.multiple_of((me_ref[0] ^ offset) * width, width), width)
            piece = spread_piece(terms[which], high_ref[:, lanes], low_ref[:, lanes])
            for at in range(chunks):
                out[i, at * half:(at + 1) * half] = piece[:, at * LANES:(at + 1) * LANES]
            if which == 0:
                sums = sum_ref[:, lanes]
                extra = [row_sums] + [sums[:, at * LANES:(at + 1) * LANES] for at in range(chunks)]
                extra.append(jnp.zeros((out.shape[1] - chunks * half - chunks - 1, LANES), F32))
                out[i, chunks * half:] = jnp.concatenate(extra, axis=0)


def half_rows(comps, chunks, which):
    extra = 0 if which else -(-(chunks + 1) // 8) * 8
    return comps // 2 * chunks + extra


def spread_pieces(me, scores, high, low, sums, picks):
    comps = scores[0].shape[0]
    chunks = high.shape[1] // (LANES * lax.axis_size("cells"))
    rows = [half_rows(comps, chunks, pick[0][1]) for pick in picks]
    pairs = sum(len(pick) for pick in picks)
    return pl.pallas_call(
        functools.partial(spread_kernel, len(scores), picks),
        out_shape=[jax.ShapeDtypeStruct((len(p), r, LANES), F32) for p, r in zip(picks, rows)],
        in_specs=[SCALARS] + [WHOLE] * (len(scores) + 3),
        out_specs=[WHOLE] * len(picks),
        compiler_params=PARAMS,
        cost_estimate=pl.CostEstimate(
            flops=5 * comps * pairs * chunks * LANES * high.shape[0], bytes_accessed=2**21, transcendentals=0
        ),
        name="spread",
    )(me, *scores, high, low, sums)


def gram_kernel(scale, chunks, counts, *refs):
    pieces, (spread_ref, gram_ref) = refs[:-2], refs[-2:]
    comps = spread_ref.shape[0]
    half = comps // 2
    first = tree_sum([ref[...] for ref in pieces[:counts[0]]])
    second = tree_sum([ref[...] for ref in pieces[counts[0]:]])
    extra = first[chunks * half:chunks * half + chunks + 1]
    eye = lax.broadcasted_iota(jnp.int32, (comps, LANES), 0) == lax.broadcasted_iota(jnp.int32, (comps, LANES), 1)
    row_sums = jnp.sum(jnp.where(eye, extra[:1], 0.0), axis=1, keepdims=True) * scale
    parts = []
    for at in range(chunks):
        rows = slice(at * half, (at + 1) * half)
        part = jnp.concatenate([first[rows], second[rows]], axis=0)
        parts.append(part - row_sums * extra[at + 1:at + 2])
    spread = jnp.concatenate(parts, axis=1)
    spread_ref[...] = spread
    gram_ref[...] = packed_gram(spread)


def packed_gram(spread):
    gram = lax.dot_general(spread, spread, NT, precision=lax.Precision.HIGHEST, preferred_element_type=F32)
    half = spread.shape[0] // 2
    return jnp.concatenate([gram[:half], gram[half:]], axis=1)


def centered_gram(halves, comps, cell_total):
    first, second = halves
    chunks = second[0].shape[0] // (comps // 2)
    return pl.pallas_call(
        functools.partial(gram_kernel, 1.0 / cell_total, chunks, [len(first), len(second)]),
        out_shape=(
            jax.ShapeDtypeStruct((comps, chunks * LANES), F32),
            jax.ShapeDtypeStruct((comps // 2, comps * 2), F32),
        ),
        in_specs=[WHOLE] * (len(first) + len(second)),
        out_specs=(WHOLE, WHOLE),
        compiler_params=PARAMS,
        name="gram",
    )(*first, *second)


def plain_gram_kernel(scale, spread_ref, row_ref, sum_ref, out_ref, gram_ref):
    spread = spread_ref[...] - row_ref[...] * scale * sum_ref[...]
    out_ref[...] = spread
    gram_ref[...] = packed_gram(spread)


def plain_gram(spread, rows, sums, cell_total):
    comps, width = spread.shape
    return pl.pallas_call(
        functools.partial(plain_gram_kernel, 1.0 / cell_total),
        out_shape=(
            jax.ShapeDtypeStruct((comps, width), F32),
            jax.ShapeDtypeStruct((comps // 2, comps * 2), F32),
        ),
        in_specs=[WHOLE] * 3,
        out_specs=(WHOLE, WHOLE),
        compiler_params=PARAMS,
        name="plain_gram",
    )(spread, rows, sums)


def inverse_of(x):
    guess = pl.reciprocal(x, approx=True)
    for _ in range(2):
        guess = guess * (2.0 - x * guess)
    return guess


def row_of(x, at):
    return jnp.broadcast_to(x[at:at + 1, :], x.shape)


def eliminate(groups, edge):
    groups = list(groups)
    below = lax.broadcasted_iota(jnp.int32, groups[0].shape, 0)
    for at in range(len(groups)):
        spread = [
            [jnp.broadcast_to(rows[:, c:c + 1], rows.shape) for c in range(at * edge, (at + 1) * edge)]
            for rows in groups[at:]
        ]
        for i in range(0, edge, 2):
            cols = spread[0]
            first, second = cols[i], cols[i + 1]
            a, b, c = row_of(first, i), row_of(second, i), row_of(second, i + 1)
            inv_a = inverse_of(a)
            inv_c = a * inverse_of(a * c - b * b)
            ratio = b * inv_a
            factors = []
            for k in range(i + 2, edge):
                top = row_of(cols[k], i)
                factors.append((k, top * inv_a, (row_of(cols[k], i + 1) - ratio * top) * inv_c))
            rows = groups[at]
            upper = row_of(rows, i) * inv_a
            rows = rows - jnp.where(below > i, first, 0.0) * upper
            lower = row_of(rows, i + 1) * inv_c
            groups[at] = rows - jnp.where(below > i + 1, second - ratio * first, 0.0) * lower
            for ahead, cols in enumerate(spread):
                first = cols[i]
                second = cols[i + 1] - ratio * first
                for k, on_first, on_second in factors:
                    cols[k] = cols[k] - first * on_first - second * on_second
                if ahead:
                    groups[at + ahead] = groups[at + ahead] - first * upper - second * lower
    return groups


def basis_kernel(scale, *refs):
    grams, (spread_ref, out_ref) = refs[:-2], refs[-2:]
    gram = tree_sum([ref[...] for ref in grams])
    comps = spread_ref.shape[0]
    gram = jnp.concatenate([gram[:, :comps], gram[:, comps:]], axis=0)
    row_at = lax.broadcasted_iota(jnp.int32, (comps, comps), 0)
    col_at = lax.broadcasted_iota(jnp.int32, (comps, comps), 1)
    eye = row_at == col_at
    trace = jnp.sum(jnp.where(eye, gram, 0.0), axis=(0, 1), keepdims=True)
    both = jnp.concatenate([gram * (1.0 / trace), jnp.where(eye, 1.0, 0.0).astype(F32)], axis=1)
    groups = eliminate([both[at:at + 8] for at in range(0, comps, 8)], 8)
    both = jnp.concatenate(groups, axis=0)
    pivots = jnp.sum(jnp.where(eye, both[:, :comps], 0.0), axis=1, keepdims=True)
    inverse = both[:, comps:] * (scale / jnp.sqrt(pivots) / jnp.sqrt(trace))
    out_ref[...] = lax.dot_general(
        inverse, spread_ref[...], NN, precision=lax.Precision.HIGHEST, preferred_element_type=F32
    )


def orthonormal(grams, spread, scale):
    return pl.pallas_call(
        functools.partial(basis_kernel, scale),
        out_shape=jax.ShapeDtypeStruct(spread.shape, F32),
        in_specs=[WHOLE] * (len(grams) + 1),
        out_specs=WHOLE,
        compiler_params=PARAMS,
        name="orthonormal",
    )(*grams, spread)


def power_of_two(size):
    return size & (size - 1) == 0


def send(x, axis, offset):
    return lax.ppermute(x, axis, [(i, i ^ offset) for i in range(lax.axis_size(axis))])


def sum_in_steps(x, axis):
    size = lax.axis_size(axis)
    if not power_of_two(size) or size > MOST_PARTNERS:
        return [lax.psum(x, axis)]
    terms = [x]
    offset = 1
    while offset < size:
        x = tree_sum(terms)
        terms = [x, send(x, axis, offset)]
        offset *= 2
    return terms


def scattered_spread(scores, high, low, sums, cell_total):
    size = lax.axis_size("cells")
    comps = scores[0].shape[0]
    width = high.shape[1] // size
    if size.bit_length() != 4 or not power_of_two(size) or width % LANES:
        scores = tree_sum(scores)
        terms = split_terms(scores, 3)
        spread = lax.psum_scatter(spread_piece(terms, high, low), "cells", scatter_dimension=1, tiled=True)
        rows = lax.psum(jnp.sum(scores, axis=1, keepdims=True), "cells")
        sums = lax.psum_scatter(sums, "cells", scatter_dimension=1, tiled=True)
        return plain_gram(spread, rows, sums, cell_total)
    me = lax.axis_index("cells").astype(jnp.int32).reshape(1)
    orders = [(1, 2), (2, 1)]
    last = size // 2
    picks = []
    for base in (last, 0):
        for half, (b, c) in enumerate(orders):
            picks.append([(base + b, half), (base + b + c, half)])
    stay = []
    for base in (last, 0):
        for half, (b, c) in enumerate(orders):
            stay.append([(base, half), (base + c, half)])
    blocks = list(spread_pieces(me, scores, high, low, sums, picks[:2]))
    blocks[0], me = lax.optimization_barrier((blocks[0], me))
    rest = list(spread_pieces(me, scores, high, low, sums, stay + picks[2:]))
    stay, sent = rest[:len(stay)], blocks + rest[len(stay):]
    came = [send(x, "cells", b) for x, (b, c) in zip(sent[:2], orders)]
    came, sent[2:] = lax.optimization_barrier((came, sent[2:]))
    came += [send(x, "cells", b) for x, (b, c) in zip(sent[2:], orders)]
    came = [x + y for x, y in zip(stay, came)]
    ends = []
    for at, x in enumerate(came):
        ends.append([x[0], send(x[1], "cells", orders[at % 2][1])])
    finals = [ends[2 + half] + [send(tree_sum(ends[half]), "cells", last)] for half in range(len(orders))]
    return centered_gram(finals, comps, cell_total)


def on_device(counts, occupancy, start_basis):
    cell_count, gene_count = counts.shape
    cells, genes = lax.axis_size("cells"), lax.axis_size("genes")
    high, low, scores, sums = log_and_scores(counts, occupancy, start_basis)
    scores = sum_in_steps(scores, "genes")
    spread, gram = scattered_spread(scores, high, low, sums, cell_count * cells)
    gram = tree_sum(sum_in_steps(gram, "genes"))
    return orthonormal(sum_in_steps(gram, "cells"), spread, math.sqrt(gene_count * genes))


def solution(mesh):
    in_specs = (P("cells", "genes"), P("cells", "genes"), P(None, "genes"))
    out_specs = P(None, ("genes", "cells"))
    return jax.shard_map(
        on_device, mesh=mesh, in_specs=in_specs, out_specs=out_specs, check_vma=False
    )
```

```python
import functools
import math

import jax
import jax.numpy as jnp
from jax import lax
from jax.experimental import pallas as pl
from jax.experimental.pallas import tpu as pltpu
from jax.sharding import PartitionSpec as P

F32 = jnp.float32
BF16 = jnp.bfloat16
NN = (((1,), (0,)), ((), ()))
NT = (((1,), (1,)), ((), ()))
WHOLE = pl.BlockSpec(memory_space=pltpu.VMEM)
SCALARS = pl.BlockSpec(memory_space=pltpu.SMEM)
LANES = 128
PARAMS = pltpu.CompilerParams(vmem_limit_bytes=16 * 2**20)
LOG_PARAMS = pltpu.CompilerParams(vmem_limit_bytes=205 * 2**18)


def dot(a, b, dims):
    return lax.dot_general(a, b, dims, preferred_element_type=F32)


def split_terms(x, count):
    terms = []
    for _ in range(count):
        term = x.astype(BF16)
        terms.append(term)
        x = x - term.astype(F32)
    return terms


def tree_sum(parts):
    while len(parts) > 1:
        parts = [sum(parts[at + 1:at + 2], parts[at]) for at in range(0, len(parts), 2)]
    return parts[0]


def log_kernel(tile_rows, tile_edge, width, occ_hbm, counts_hbm, basis_hbm, top_ref, bottom_ref, score_ref,
               occ_ref, counts_ref, basis_ref, term_ref, occ_sem, basis_sem, counts_sem):
    cells, genes = counts_ref.shape
    fetch_occ = pltpu.make_async_copy(occ_hbm, occ_ref, occ_sem)
    fetch_basis = pltpu.make_async_copy(basis_hbm, basis_ref, basis_sem)
    fetches = [
        pltpu.make_async_copy(
            counts_hbm.at[:, pl.ds(at * width, width)], counts_ref.at[:, pl.ds(at * width, width)], counts_sem.at[at]
        )
        for at in range(genes // width)
    ]
    fetch_occ.start()
    for fetch in fetches:
        fetch.start()
    fetch_basis.start()
    fetch_occ.wait()
    scores = None
    for at, fetch in enumerate(fetches):
        fetch.wait()
        for col in range(at * width // tile_edge, (at + 1) * width // tile_edge):
            lanes = pl.ds(col * tile_edge, tile_edge)
            for row in range(tile_rows):
                subs = pl.ds(row * tile_edge, tile_edge)
                occ = occ_ref[row, col].astype(F32)
                logged = jnp.log(1.0 + counts_ref[subs, lanes].astype(F32)) * occ
                high = logged.astype(BF16)
                term_ref[0, subs, lanes] = high
                term_ref[1, subs, lanes] = (logged - high.astype(F32)).astype(BF16)
                for begin in range(row * tile_edge, (row + 1) * tile_edge, tile_edge // 2):
                    part = logged[begin - row * tile_edge:begin - row * tile_edge + tile_edge // 2]
                    ref, to = (top_ref, begin) if begin < cells // 2 else (bottom_ref, begin - cells // 2)
                    ref[pl.ds(to, tile_edge // 2), lanes] = part
        if at == 0:
            fetch_basis.wait()
        chunk = pl.ds(at * width, width)
        basis = basis_ref[:, chunk]
        part = dot(basis, term_ref[0, :, chunk], NT) + dot(basis, term_ref[1, :, chunk], NT)
        scores = part if scores is None else scores + part
    score_ref[...] = scores


def log_and_scores(counts, occupancy, basis):
    cells, genes = counts.shape
    tile_rows, tile_cols = occupancy.shape
    edge = cells // tile_rows
    comps = basis.shape[0]
    width = genes // 4 if genes % (4 * edge) == 0 else genes
    hbm = pl.BlockSpec(memory_space=pltpu.HBM)
    return pl.pallas_call(
        functools.partial(log_kernel, tile_rows, edge, width),
        out_shape=(
            jax.ShapeDtypeStruct((cells // 2, genes), F32),
            jax.ShapeDtypeStruct((cells // 2, genes), F32),
            jax.ShapeDtypeStruct((comps, cells), F32),
        ),
        in_specs=[hbm, hbm, hbm],
        out_specs=(WHOLE, WHOLE, WHOLE),
        scratch_shapes=[
            pltpu.SMEM(occupancy.shape, jnp.int32),
            pltpu.VMEM(counts.shape, BF16),
            pltpu.VMEM(basis.shape, BF16),
            pltpu.VMEM((2,) + counts.shape, BF16),
            pltpu.SemaphoreType.DMA,
            pltpu.SemaphoreType.DMA,
            pltpu.SemaphoreType.DMA((genes // width,)),
        ],
        compiler_params=LOG_PARAMS,
        name="log_scores",
    )(occupancy, counts, basis)


def spread_piece(terms, high, low):
    comps = terms[0].shape[0]
    on_low = dot(jnp.concatenate(terms[:2], axis=0), low, NN)
    on_high = dot(jnp.concatenate(terms, axis=0), high, NN)
    small = on_low[comps:] + on_high[2 * comps:]
    middle = on_low[:comps] + on_high[comps:2 * comps]
    return (small + middle) + on_high[:comps]


def spread_kernel(picks, me_ref, score_ref, came_ref, *refs):
    (even, odd), outs = (refs[:2], refs[2:4]), refs[4:]
    scores = score_ref[...] + came_ref[...]
    comps = scores.shape[0]
    half = comps // 2
    terms = split_terms(scores, 3)
    eye = lax.broadcasted_iota(jnp.int32, (comps, LANES), 0) == lax.broadcasted_iota(jnp.int32, (comps, LANES), 1)
    row_sums = jnp.sum(jnp.where(eye, jnp.sum(scores, axis=1, keepdims=True), 0.0), axis=0, keepdims=True)
    chunks = even[0].shape[1] // (LANES * lax.axis_size("cells"))
    width = chunks * LANES
    wanted = {}
    for pick, out in zip(picks, outs):
        for i, (offset, which) in enumerate(pick):
            wanted.setdefault(offset, []).append((which, out, i))
    for offset, places in wanted.items():
        lanes = pl.ds(pl.multiple_of((me_ref[0] ^ offset) * width, width), width)
        halves = sorted(which for which, _, _ in places)
        rows = slice(halves[0] * half, (halves[-1] + 1) * half)
        sums = []
        for part, (top_ref, bottom_ref) in enumerate((even, odd)):
            logged = jnp.concatenate([top_ref[:, lanes], bottom_ref[:, lanes]], axis=0)
            high, low = split_terms(logged, 2)
            piece = spread_piece([term[rows] for term in terms], high, low)
            for which, out, i in places:
                from_row = (which - halves[0]) * half
                for at in range(chunks):
                    to_row = (part * chunks + at) * half
                    out[i, to_row:to_row + half] = piece[from_row:from_row + half, at * LANES:(at + 1) * LANES]
            total = jnp.sum(logged, axis=0, keepdims=True)
            sums += [total[:, at * LANES:(at + 1) * LANES] for at in range(chunks)]
        for which, out, i in places:
            extra = [row_sums] if which else sums
            left = out.shape[1] - 2 * chunks * half - len(extra)
            if left:
                extra = extra + [jnp.zeros((left, LANES), F32)]
            out[i, 2 * chunks * half:] = jnp.concatenate(extra, axis=0)


def spread_pieces(me, scores, logged, picks):
    comps = scores[0].shape[0]
    cells, genes = logged[0].shape
    chunks = genes // (LANES * lax.axis_size("cells"))
    rows = comps * chunks + -(-2 * chunks // 8) * 8
    pairs = sum(len(pick) for pick in picks)
    return pl.pallas_call(
        functools.partial(spread_kernel, picks),
        out_shape=[jax.ShapeDtypeStruct((len(pick), rows, LANES), F32) for pick in picks],
        in_specs=[SCALARS] + [WHOLE] * 6,
        out_specs=[WHOLE] * len(picks),
        compiler_params=PARAMS,
        cost_estimate=pl.CostEstimate(
            flops=20 * comps * pairs * chunks * LANES * cells, bytes_accessed=2**21, transcendentals=0
        ),
        name="spread",
    )(me, *scores, *logged)


def gram_kernel(scale, chunks, counts, *refs):
    pieces, (even_ref, odd_ref, gram_ref) = refs[:-3], refs[-3:]
    comps = even_ref.shape[0]
    half = comps // 2
    first = tree_sum([ref[...] for ref in pieces[:counts[0]]])
    second = tree_sum([ref[...] for ref in pieces[counts[0]:]])
    sums = first[2 * chunks * half:]
    row_sums = second[2 * chunks * half:2 * chunks * half + 1]
    eye = lax.broadcasted_iota(jnp.int32, (comps, LANES), 0) == lax.broadcasted_iota(jnp.int32, (comps, LANES), 1)
    row_sums = jnp.sum(jnp.where(eye, row_sums, 0.0), axis=1, keepdims=True) * scale
    parts = []
    for at in range(2 * chunks):
        rows = slice(at * half, (at + 1) * half)
        part = jnp.concatenate([first[rows], second[rows]], axis=0)
        parts.append(part - row_sums * sums[at:at + 1])
    even_ref[...] = jnp.concatenate(parts[:chunks], axis=1)
    odd_ref[...] = jnp.concatenate(parts[chunks:], axis=1)
    gram_ref[...] = packed_gram(jnp.concatenate(parts, axis=1))


def packed_gram(spread):
    gram = lax.dot_general(spread, spread, NT, precision=lax.Precision.HIGHEST, preferred_element_type=F32)
    half = spread.shape[0] // 2
    return jnp.concatenate([gram[:half], gram[half:]], axis=1)


def centered_gram(halves, comps, cell_total):
    first, second = halves
    chunks = second[0].shape[0] // comps
    return pl.pallas_call(
        functools.partial(gram_kernel, 1.0 / cell_total, chunks, [len(first), len(second)]),
        out_shape=(
            jax.ShapeDtypeStruct((comps, chunks * LANES), F32),
            jax.ShapeDtypeStruct((comps, chunks * LANES), F32),
            jax.ShapeDtypeStruct((comps // 2, comps * 2), F32),
        ),
        in_specs=[WHOLE] * (len(first) + len(second)),
        out_specs=(WHOLE, WHOLE, WHOLE),
        compiler_params=PARAMS,
        name="gram",
    )(*first, *second)


def plain_gram_kernel(scale, spread_ref, row_ref, sum_ref, out_ref, gram_ref):
    spread = spread_ref[...] - row_ref[...] * scale * sum_ref[...]
    out_ref[...] = spread
    gram_ref[...] = packed_gram(spread)


def plain_gram(spread, rows, sums, cell_total):
    comps, width = spread.shape
    return pl.pallas_call(
        functools.partial(plain_gram_kernel, 1.0 / cell_total),
        out_shape=(
            jax.ShapeDtypeStruct((comps, width), F32),
            jax.ShapeDtypeStruct((comps // 2, comps * 2), F32),
        ),
        in_specs=[WHOLE] * 3,
        out_specs=(WHOLE, WHOLE),
        compiler_params=PARAMS,
        name="plain_gram",
    )(spread, rows, sums)


def inverse_of(x):
    guess = pl.reciprocal(x, approx=True)
    for _ in range(2):
        guess = guess * (2.0 - x * guess)
    return guess


def row_of(x, at):
    return jnp.broadcast_to(x[at:at + 1, :], x.shape)


def eliminate(groups, edge):
    groups = list(groups)
    below = lax.broadcasted_iota(jnp.int32, groups[0].shape, 0)
    for at in range(len(groups)):
        spread = [
            [jnp.broadcast_to(rows[:, c:c + 1], rows.shape) for c in range(at * edge, (at + 1) * edge)]
            for rows in groups[at:]
        ]
        for i in range(0, edge, 2):
            cols = spread[0]
            first, second = cols[i], cols[i + 1]
            a, b, c = row_of(first, i), row_of(second, i), row_of(second, i + 1)
            inv_a = inverse_of(a)
            inv_c = a * inverse_of(a * c - b * b)
            ratio = b * inv_a
            factors = []
            for k in range(i + 2, edge):
                top = row_of(cols[k], i)
                factors.append((k, top * inv_a, (row_of(cols[k], i + 1) - ratio * top) * inv_c))
            rows = groups[at]
            upper = row_of(rows, i) * inv_a
            rows = rows - jnp.where(below > i, first, 0.0) * upper
            lower = row_of(rows, i + 1) * inv_c
            groups[at] = rows - jnp.where(below > i + 1, second - ratio * first, 0.0) * lower
            for ahead, cols in enumerate(spread):
                first = cols[i]
                second = cols[i + 1] - ratio * first
                for k, on_first, on_second in factors:
                    cols[k] = cols[k] - first * on_first - second * on_second
                if ahead:
                    groups[at + ahead] = groups[at + ahead] - first * upper - second * lower
    return groups


def basis_kernel(scale, lead_ref, gram_ref, spread_ref, came_gram_ref, came_spread_ref, out_ref):
    lead = lead_ref[0] == 1
    gram = jnp.where(lead, gram_ref[...], came_gram_ref[...])
    spread = jnp.where(lead, spread_ref[...], came_spread_ref[...])
    comps = spread.shape[0]
    gram = jnp.concatenate([gram[:, :comps], gram[:, comps:]], axis=0)
    row_at = lax.broadcasted_iota(jnp.int32, (comps, comps), 0)
    col_at = lax.broadcasted_iota(jnp.int32, (comps, comps), 1)
    eye = row_at == col_at
    trace = jnp.sum(jnp.where(eye, gram, 0.0), axis=(0, 1), keepdims=True)
    both = jnp.concatenate([gram * (1.0 / trace), jnp.where(eye, 1.0, 0.0).astype(F32)], axis=1)
    groups = eliminate([both[at:at + 8] for at in range(0, comps, 8)], 8)
    both = jnp.concatenate(groups, axis=0)
    pivots = jnp.sum(jnp.where(eye, both[:, :comps], 0.0), axis=1, keepdims=True)
    inverse = both[:, comps:] * (scale / jnp.sqrt(pivots) / jnp.sqrt(trace))
    out_ref[...] = lax.dot_general(
        inverse, spread, NN, precision=lax.Precision.HIGHEST, preferred_element_type=F32
    )


def orthonormal(lead, own, came, scale):
    return pl.pallas_call(
        functools.partial(basis_kernel, scale),
        out_shape=jax.ShapeDtypeStruct(own[1].shape, F32),
        in_specs=[SCALARS] + [WHOLE] * 4,
        out_specs=WHOLE,
        compiler_params=PARAMS,
        name="orthonormal",
    )(lead, *own, *came)


def among(x, offset_cells, offset_genes, senders):
    cells, genes = lax.axis_size("cells"), lax.axis_size("genes")
    pairs = [
        (c * genes + g, (c ^ offset_cells) * genes + (g ^ offset_genes))
        for c in range(cells)
        for g in range(senders, genes, 2)
    ]
    return lax.ppermute(x, ("cells", "genes"), pairs)


def doublings(size):
    return [1 << at for at in range(size.bit_length() - 1)]


def lead_scatter(scores, logged, cell_total):
    size = lax.axis_size("cells")
    comps = scores[0].shape[0]
    me = lax.axis_index("cells").astype(jnp.int32).reshape(1)
    orders = [(1, 2), (2, 1)]
    last = size // 2
    picks, stay = [], []
    for base in (last, 0):
        for half, (b, c) in enumerate(orders):
            picks.append([(base + b, half), (base + b + c, half)])
            stay.append([(base, half), (base + c, half)])
    blocks = list(spread_pieces(me, scores, logged, picks[:2]))
    blocks[0], me = lax.optimization_barrier((blocks[0], me))
    rest = list(spread_pieces(me, scores, logged, stay + picks[2:]))
    stay, sent = rest[:len(stay)], blocks + rest[len(stay):]
    came = [among(x, b, 0, 1) for x, (b, c) in zip(sent[:2], orders)]
    came, sent[2:] = lax.optimization_barrier((came, sent[2:]))
    came += [among(x, b, 0, 1) for x, (b, c) in zip(sent[2:], orders)]
    came = [x + y for x, y in zip(stay, came)]
    ends = []
    for at, x in enumerate(came):
        ends.append([x[0], among(x[1], orders[at % 2][1], 0, 1)])
    finals = [ends[2 + half] + [among(tree_sum(ends[half]), last, 0, 1)] for half in range(len(orders))]
    return centered_gram(finals, comps, cell_total)


def in_pairs(logged, scores, cell_total):
    cells, genes = lax.axis_size("cells"), lax.axis_size("genes")
    scores = scores + among(scores, 0, 1, 0)
    scores, logged = lax.optimization_barrier((scores, logged))
    given = [among(x, 0, 1, 0) for x in logged]
    terms = [scores, jnp.zeros_like(scores)]
    for offset in doublings(genes)[1:]:
        terms = [terms[0] + terms[1], None] if offset > 2 else [scores, None]
        terms[1] = among(terms[0], 0, offset, 1)
    even, odd, gram = lead_scatter(terms, given + list(logged), cell_total)
    given_even = among(even, 0, 1, 1)
    for offset in doublings(genes)[1:]:
        gram = gram + among(gram, 0, offset, 1)
    for offset in doublings(cells):
        gram = gram + among(gram, offset, 0, 1)
    return (gram, odd), (among(gram, 0, 1, 1), given_even)


def all_alike(logged, scores, cell_total):
    scores = lax.psum(scores, "genes")
    logged = jnp.concatenate(logged, axis=0)
    spread = lax.psum_scatter(
        spread_piece(split_terms(scores, 3), *split_terms(logged, 2)), "cells", scatter_dimension=1, tiled=True
    )
    rows = lax.psum(jnp.sum(scores, axis=1, keepdims=True), "cells")
    sums = lax.psum_scatter(jnp.sum(logged, axis=0, keepdims=True), "cells", scatter_dimension=1, tiled=True)
    spread, gram = plain_gram(spread, rows, sums, cell_total)
    gram = lax.psum(gram, ("cells", "genes"))
    return (gram, spread), (gram, spread)


def on_device(counts, occupancy, start_basis):
    cell_count, gene_count = counts.shape
    cells, genes = lax.axis_size("cells"), lax.axis_size("genes")
    *logged, scores = log_and_scores(counts, occupancy, start_basis)
    paired = cells == 1 << 3 and genes > 1 and genes & (genes - 1) == 0
    paired = paired and gene_count % (cells * LANES) == 0
    work = in_pairs if paired else all_alike
    own, came = work(logged, scores, cell_count * cells)
    lead = (lax.axis_index("genes") % 2).astype(jnp.int32).reshape(1)
    return orthonormal(lead, own, came, math.sqrt(gene_count * genes))


def solution(mesh):
    in_specs = (P("cells", "genes"), P("cells", "genes"), P(None, "genes"))
    out_specs = P(None, ("genes", "cells"))
    return jax.shard_map(
        on_device, mesh=mesh, in_specs=in_specs, out_specs=out_specs, check_vma=False
    )
```

```python
import functools
import math

import jax
import jax.numpy as jnp
from jax import lax
from jax.experimental import pallas as pl
from jax.experimental.pallas import tpu as pltpu
from jax.sharding import PartitionSpec as P

F32 = jnp.float32
BF16 = jnp.bfloat16
NN = (((1,), (0,)), ((), ()))
NT = (((1,), (1,)), ((), ()))
WHOLE = pl.BlockSpec(memory_space=pltpu.VMEM)
SCALARS = pl.BlockSpec(memory_space=pltpu.SMEM)
LANES = 128
PARAMS = pltpu.CompilerParams(vmem_limit_bytes=16 * 2**20)
LOG_PARAMS = pltpu.CompilerParams(vmem_limit_bytes=205 * 2**18)


def dot(a, b, dims):
    return lax.dot_general(a, b, dims, preferred_element_type=F32)


def split_terms(x, count):
    terms = []
    for _ in range(count):
        term = x.astype(BF16)
        terms.append(term)
        x = x - term.astype(F32)
    return terms


def tree_sum(parts):
    while len(parts) > 1:
        parts = [sum(parts[at + 1:at + 2], parts[at]) for at in range(0, len(parts), 2)]
    return parts[0]


def log_kernel(tile_rows, tile_edge, width, occ_hbm, counts_hbm, basis_hbm, top_ref, bottom_ref, score_ref,
               occ_ref, counts_ref, basis_ref, term_ref, occ_sem, basis_sem, counts_sem):
    cells, genes = counts_ref.shape
    fetch_occ = pltpu.make_async_copy(occ_hbm, occ_ref, occ_sem)
    fetch_basis = pltpu.make_async_copy(basis_hbm, basis_ref, basis_sem)
    fetches = [
        pltpu.make_async_copy(
            counts_hbm.at[:, pl.ds(at * width, width)], counts_ref.at[:, pl.ds(at * width, width)], counts_sem.at[at]
        )
        for at in range(genes // width)
    ]
    fetch_occ.start()
    for fetch in fetches:
        fetch.start()
    fetch_basis.start()
    fetch_occ.wait()
    scores = None
    for at, fetch in enumerate(fetches):
        fetch.wait()
        for col in range(at * width // tile_edge, (at + 1) * width // tile_edge):
            lanes = pl.ds(col * tile_edge, tile_edge)
            for row in range(tile_rows):
                subs = pl.ds(row * tile_edge, tile_edge)
                occ = occ_ref[row, col].astype(F32)
                logged = jnp.log(1.0 + counts_ref[subs, lanes].astype(F32)) * occ
                high = logged.astype(BF16)
                term_ref[0, subs, lanes] = high
                term_ref[1, subs, lanes] = (logged - high.astype(F32)).astype(BF16)
                for begin in range(row * tile_edge, (row + 1) * tile_edge, tile_edge // 2):
                    part = logged[begin - row * tile_edge:begin - row * tile_edge + tile_edge // 2]
                    ref, to = (top_ref, begin) if begin < cells // 2 else (bottom_ref, begin - cells // 2)
                    ref[pl.ds(to, tile_edge // 2), lanes] = part
        if at == 0:
            fetch_basis.wait()
        chunk = pl.ds(at * width, width)
        basis = basis_ref[:, chunk]
        part = dot(basis, term_ref[0, :, chunk], NT) + dot(basis, term_ref[1, :, chunk], NT)
        scores = part if scores is None else scores + part
    score_ref[...] = scores


def log_and_scores(counts, occupancy, basis):
    cells, genes = counts.shape
    tile_rows, tile_cols = occupancy.shape
    edge = cells // tile_rows
    comps = basis.shape[0]
    width = genes // 4 if genes % (4 * edge) == 0 else genes
    hbm = pl.BlockSpec(memory_space=pltpu.HBM)
    return pl.pallas_call(
        functools.partial(log_kernel, tile_rows, edge, width),
        out_shape=(
            jax.ShapeDtypeStruct((cells // 2, genes), F32),
            jax.ShapeDtypeStruct((cells // 2, genes), F32),
            jax.ShapeDtypeStruct((comps, cells), F32),
        ),
        in_specs=[hbm, hbm, hbm],
        out_specs=(WHOLE, WHOLE, WHOLE),
        scratch_shapes=[
            pltpu.SMEM(occupancy.shape, jnp.int32),
            pltpu.VMEM(counts.shape, BF16),
            pltpu.VMEM(basis.shape, BF16),
            pltpu.VMEM((2,) + counts.shape, BF16),
            pltpu.SemaphoreType.DMA,
            pltpu.SemaphoreType.DMA,
            pltpu.SemaphoreType.DMA((genes // width,)),
        ],
        compiler_params=LOG_PARAMS,
        name="log_scores",
    )(occupancy, counts, basis)


def spread_piece(terms, high, low):
    comps = terms[0].shape[0]
    on_low = dot(jnp.concatenate(terms[:2], axis=0), low, NN)
    on_high = dot(jnp.concatenate(terms, axis=0), high, NN)
    small = on_low[comps:] + on_high[2 * comps:]
    middle = on_low[:comps] + on_high[comps:2 * comps]
    return (small + middle) + on_high[:comps]


def spread_kernel(picks, me_ref, score_ref, came_ref, *refs):
    (even, odd), outs = (refs[:2], refs[2:4]), refs[4:]
    scores = score_ref[...] + came_ref[...]
    comps = scores.shape[0]
    half = comps // 2
    terms = split_terms(scores, 3)
    eye = lax.broadcasted_iota(jnp.int32, (comps, LANES), 0) == lax.broadcasted_iota(jnp.int32, (comps, LANES), 1)
    row_sums = jnp.sum(jnp.where(eye, jnp.sum(scores, axis=1, keepdims=True), 0.0), axis=0, keepdims=True)
    chunks = even[0].shape[1] // (LANES * lax.axis_size("cells"))
    width = chunks * LANES
    wanted = {}
    for pick, out in zip(picks, outs):
        for i, (offset, which) in enumerate(pick):
            wanted.setdefault(offset, []).append((which, out, i))
    for offset, places in wanted.items():
        lanes = pl.ds(pl.multiple_of((me_ref[0] ^ offset) * width, width), width)
        halves = sorted(which for which, _, _ in places)
        rows = slice(halves[0] * half, (halves[-1] + 1) * half)
        sums = []
        for part, (top_ref, bottom_ref) in enumerate((even, odd)):
            logged = jnp.concatenate([top_ref[:, lanes], bottom_ref[:, lanes]], axis=0)
            high, low = split_terms(logged, 2)
            piece = spread_piece([term[rows] for term in terms], high, low)
            for which, out, i in places:
                from_row = (which - halves[0]) * half
                for at in range(chunks):
                    to_row = (part * chunks + at) * half
                    out[i, to_row:to_row + half] = piece[from_row:from_row + half, at * LANES:(at + 1) * LANES]
            total = jnp.sum(logged, axis=0, keepdims=True)
            sums += [total[:, at * LANES:(at + 1) * LANES] for at in range(chunks)]
        for which, out, i in places:
            extra = [row_sums] if which else sums
            left = out.shape[1] - 2 * chunks * half - len(extra)
            if left:
                extra = extra + [jnp.zeros((left, LANES), F32)]
            out[i, 2 * chunks * half:] = jnp.concatenate(extra, axis=0)


def spread_pieces(me, scores, logged, picks):
    comps = scores[0].shape[0]
    cells, genes = logged[0].shape
    chunks = genes // (LANES * lax.axis_size("cells"))
    rows = comps * chunks + -(-2 * chunks // 8) * 8
    pairs = sum(len(pick) for pick in picks)
    return pl.pallas_call(
        functools.partial(spread_kernel, picks),
        out_shape=[jax.ShapeDtypeStruct((len(pick), rows, LANES), F32) for pick in picks],
        in_specs=[SCALARS] + [WHOLE] * 6,
        out_specs=[WHOLE] * len(picks),
        compiler_params=PARAMS,
        cost_estimate=pl.CostEstimate(
            flops=20 * comps * pairs * chunks * LANES * cells, bytes_accessed=2**21, transcendentals=0
        ),
        name="spread",
    )(me, *scores, *logged)


def gram_kernel(scale, chunks, counts, *refs):
    pieces, (even_ref, odd_ref, gram_ref) = refs[:-3], refs[-3:]
    comps = even_ref.shape[0]
    half = comps // 2
    first = tree_sum([ref[...] for ref in pieces[:counts[0]]])
    second = tree_sum([ref[...] for ref in pieces[counts[0]:]])
    sums = first[2 * chunks * half:]
    row_sums = second[2 * chunks * half:2 * chunks * half + 1]
    eye = lax.broadcasted_iota(jnp.int32, (comps, LANES), 0) == lax.broadcasted_iota(jnp.int32, (comps, LANES), 1)
    row_sums = jnp.sum(jnp.where(eye, row_sums, 0.0), axis=1, keepdims=True) * scale
    parts = []
    for at in range(2 * chunks):
        rows = slice(at * half, (at + 1) * half)
        part = jnp.concatenate([first[rows], second[rows]], axis=0)
        parts.append(part - row_sums * sums[at:at + 1])
    even_ref[...] = jnp.concatenate(parts[:chunks], axis=1)
    odd_ref[...] = jnp.concatenate(parts[chunks:], axis=1)
    gram_ref[...] = packed_gram(jnp.concatenate(parts, axis=1))


def packed_gram(spread):
    gram = lax.dot_general(spread, spread, NT, precision=lax.Precision.HIGHEST, preferred_element_type=F32)
    half = spread.shape[0] // 2
    return jnp.concatenate([gram[:half], gram[half:]], axis=1)


def centered_gram(halves, comps, cell_total):
    first, second = halves
    chunks = second[0].shape[0] // comps
    return pl.pallas_call(
        functools.partial(gram_kernel, 1.0 / cell_total, chunks, [len(first), len(second)]),
        out_shape=(
            jax.ShapeDtypeStruct((comps, chunks * LANES), F32),
            jax.ShapeDtypeStruct((comps, chunks * LANES), F32),
            jax.ShapeDtypeStruct((comps // 2, comps * 2), F32),
        ),
        in_specs=[WHOLE] * (len(first) + len(second)),
        out_specs=(WHOLE, WHOLE, WHOLE),
        compiler_params=PARAMS,
        name="gram",
    )(*first, *second)


def plain_gram_kernel(scale, spread_ref, row_ref, sum_ref, out_ref, gram_ref):
    spread = spread_ref[...] - row_ref[...] * scale * sum_ref[...]
    out_ref[...] = spread
    gram_ref[...] = packed_gram(spread)


def plain_gram(spread, rows, sums, cell_total):
    comps, width = spread.shape
    return pl.pallas_call(
        functools.partial(plain_gram_kernel, 1.0 / cell_total),
        out_shape=(
            jax.ShapeDtypeStruct((comps, width), F32),
            jax.ShapeDtypeStruct((comps // 2, comps * 2), F32),
        ),
        in_specs=[WHOLE] * 3,
        out_specs=(WHOLE, WHOLE),
        compiler_params=PARAMS,
        name="plain_gram",
    )(spread, rows, sums)


def inverse_of(x):
    guess = pl.reciprocal(x, approx=True)
    for _ in range(2):
        guess = guess * (2.0 - x * guess)
    return guess


def row_of(x, at):
    return jnp.broadcast_to(x[at:at + 1, :], x.shape)


def eliminate(groups, edge):
    groups = list(groups)
    below = lax.broadcasted_iota(jnp.int32, groups[0].shape, 0)
    for at in range(len(groups)):
        spread = [
            [jnp.broadcast_to(rows[:, c:c + 1], rows.shape) for c in range(at * edge, (at + 1) * edge)]
            for rows in groups[at:]
        ]
        for i in range(0, edge, 2):
            cols = spread[0]
            first, second = cols[i], cols[i + 1]
            a, b, c = row_of(first, i), row_of(second, i), row_of(second, i + 1)
            inv_a = inverse_of(a)
            inv_c = a * inverse_of(a * c - b * b)
            ratio = b * inv_a
            factors = []
            for k in range(i + 2, edge):
                top = row_of(cols[k], i)
                factors.append((k, top * inv_a, (row_of(cols[k], i + 1) - ratio * top) * inv_c))
            rows = groups[at]
            upper = row_of(rows, i) * inv_a
            rows = rows - jnp.where(below > i, first, 0.0) * upper
            lower = row_of(rows, i + 1) * inv_c
            groups[at] = rows - jnp.where(below > i + 1, second - ratio * first, 0.0) * lower
            for ahead, cols in enumerate(spread):
                first = cols[i]
                second = cols[i + 1] - ratio * first
                for k, on_first, on_second in factors:
                    cols[k] = cols[k] - first * on_first - second * on_second
                if ahead:
                    groups[at + ahead] = groups[at + ahead] - first * upper - second * lower
    return groups


def basis_kernel(scale, lead_ref, gram_ref, spread_ref, came_gram_ref, came_spread_ref, out_ref):
    lead = lead_ref[0] == 1
    gram = jnp.where(lead, gram_ref[...], came_gram_ref[...])
    spread = jnp.where(lead, spread_ref[...], came_spread_ref[...])
    comps = spread.shape[0]
    gram = jnp.concatenate([gram[:, :comps], gram[:, comps:]], axis=0)
    row_at = lax.broadcasted_iota(jnp.int32, (comps, comps), 0)
    col_at = lax.broadcasted_iota(jnp.int32, (comps, comps), 1)
    eye = row_at == col_at
    trace = jnp.sum(jnp.where(eye, gram, 0.0), axis=(0, 1), keepdims=True)
    both = jnp.concatenate([gram * (1.0 / trace), jnp.where(eye, 1.0, 0.0).astype(F32)], axis=1)
    groups = eliminate([both[at:at + 8] for at in range(0, comps, 8)], 8)
    both = jnp.concatenate(groups, axis=0)
    pivots = jnp.sum(jnp.where(eye, both[:, :comps], 0.0), axis=1, keepdims=True)
    inverse = both[:, comps:] * (scale / jnp.sqrt(pivots) / jnp.sqrt(trace))
    out_ref[...] = lax.dot_general(
        inverse, spread, NN, precision=lax.Precision.HIGHEST, preferred_element_type=F32
    )


def orthonormal(lead, own, came, scale):
    return pl.pallas_call(
        functools.partial(basis_kernel, scale),
        out_shape=jax.ShapeDtypeStruct(own[1].shape, F32),
        in_specs=[SCALARS] + [WHOLE] * 4,
        out_specs=WHOLE,
        compiler_params=PARAMS,
        name="orthonormal",
    )(lead, *own, *came)


def swap(x):
    return lax.ppermute(x, "genes", [(i, i ^ 1) for i in range(lax.axis_size("genes"))])


def lead_swap(x, offset_cells, offset_genes):
    cells, genes = lax.axis_size("cells"), lax.axis_size("genes")
    pairs = []
    for c in range(cells):
        for g in range(genes):
            to = ((c ^ offset_cells) * genes + (g ^ offset_genes)) if g % 2 else c * genes + g
            pairs.append((c * genes + g, to))
    return lax.ppermute(x, ("cells", "genes"), pairs)


def doublings(size):
    return [1 << at for at in range(size.bit_length() - 1)]


def lead_scatter(scores, logged, cell_total):
    size = lax.axis_size("cells")
    comps = scores[0].shape[0]
    me = lax.axis_index("cells").astype(jnp.int32).reshape(1)
    orders = [(1, 2), (2, 1)]
    last = size // 2
    picks, stay = [], []
    for base in (last, 0):
        for half, (b, c) in enumerate(orders):
            picks.append([(base + b, half), (base + b + c, half)])
            stay.append([(base, half), (base + c, half)])
    blocks = list(spread_pieces(me, scores, logged, picks[:2]))
    blocks[0], me = lax.optimization_barrier((blocks[0], me))
    rest = list(spread_pieces(me, scores, logged, stay + picks[2:]))
    stay, sent = rest[:len(stay)], blocks + rest[len(stay):]
    came = [lead_swap(x, b, 0) for x, (b, c) in zip(sent[:2], orders)]
    came, sent[2:] = lax.optimization_barrier((came, sent[2:]))
    came += [lead_swap(x, b, 0) for x, (b, c) in zip(sent[2:], orders)]
    came = [x + y for x, y in zip(stay, came)]
    ends = []
    for at, x in enumerate(came):
        ends.append([x[0], lead_swap(x[1], orders[at % 2][1], 0)])
    finals = [ends[2 + half] + [lead_swap(tree_sum(ends[half]), last, 0)] for half in range(len(orders))]
    return centered_gram(finals, comps, cell_total)


def in_pairs(logged, scores, cell_total):
    cells, genes = lax.axis_size("cells"), lax.axis_size("genes")
    scores = scores + swap(scores)
    scores, logged = lax.optimization_barrier((scores, logged))
    given = [swap(x) for x in logged]
    terms = [scores, jnp.zeros_like(scores)]
    for offset in doublings(genes)[1:]:
        terms = [terms[0] + terms[1], None] if offset > 2 else [scores, None]
        terms[1] = lead_swap(terms[0], 0, offset)
    even, odd, gram = lead_scatter(terms, given + list(logged), cell_total)
    given_even = swap(even)
    for offset in doublings(genes)[1:]:
        gram = gram + lead_swap(gram, 0, offset)
    for offset in doublings(cells):
        gram = gram + lead_swap(gram, offset, 0)
    return (gram, odd), (swap(gram), given_even)


def all_alike(logged, scores, cell_total):
    scores = lax.psum(scores, "genes")
    logged = jnp.concatenate(logged, axis=0)
    spread = lax.psum_scatter(
        spread_piece(split_terms(scores, 3), *split_terms(logged, 2)), "cells", scatter_dimension=1, tiled=True
    )
    rows = lax.psum(jnp.sum(scores, axis=1, keepdims=True), "cells")
    sums = lax.psum_scatter(jnp.sum(logged, axis=0, keepdims=True), "cells", scatter_dimension=1, tiled=True)
    spread, gram = plain_gram(spread, rows, sums, cell_total)
    gram = lax.psum(gram, ("cells", "genes"))
    return (gram, spread), (gram, spread)


def on_device(counts, occupancy, start_basis):
    cell_count, gene_count = counts.shape
    cells, genes = lax.axis_size("cells"), lax.axis_size("genes")
    *logged, scores = log_and_scores(counts, occupancy, start_basis)
    paired = cells == 1 << 3 and genes > 1 and genes & (genes - 1) == 0
    paired = paired and gene_count % (cells * LANES) == 0
    work = in_pairs if paired else all_alike
    own, came = work(logged, scores, cell_count * cells)
    lead = (lax.axis_index("genes") % 2).astype(jnp.int32).reshape(1)
    return orthonormal(lead, own, came, math.sqrt(gene_count * genes))


def solution(mesh):
    in_specs = (P("cells", "genes"), P("cells", "genes"), P(None, "genes"))
    out_specs = P(None, ("genes", "cells"))
    return jax.shard_map(
        on_device, mesh=mesh, in_specs=in_specs, out_specs=out_specs, check_vma=False
    )
```

```python
import functools
import math

import jax
import jax.numpy as jnp
from jax import lax
from jax.experimental import pallas as pl
from jax.experimental.pallas import tpu as pltpu
from jax.sharding import PartitionSpec as P

F32 = jnp.float32
BF16 = jnp.bfloat16
NN = (((1,), (0,)), ((), ()))
NT = (((1,), (1,)), ((), ()))
WHOLE = pl.BlockSpec(memory_space=pltpu.VMEM)
SCALARS = pl.BlockSpec(memory_space=pltpu.SMEM)
LANES = 128
PARAMS = pltpu.CompilerParams(vmem_limit_bytes=16 * 2**20)
LOG_PARAMS = pltpu.CompilerParams(vmem_limit_bytes=205 * 2**18)
MOST_PARTNERS = 8


def dot(a, b, dims):
    return lax.dot_general(a, b, dims, preferred_element_type=F32)


def split_terms(x, count):
    terms = []
    for _ in range(count):
        term = x.astype(BF16)
        terms.append(term)
        x = x - term.astype(F32)
    return terms


def tree_sum(parts):
    while len(parts) > 1:
        parts = [sum(parts[at + 1:at + 2], parts[at]) for at in range(0, len(parts), 2)]
    return parts[0]


def log_kernel(tile_rows, tile_edge, width, occ_hbm, counts_hbm, basis_hbm, high_ref, low_ref, score_ref, sum_ref,
               occ_ref, counts_ref, basis_ref, occ_sem, basis_sem, counts_sem):
    cells, genes = high_ref.shape
    fetch_occ = pltpu.make_async_copy(occ_hbm, occ_ref, occ_sem)
    fetch_basis = pltpu.make_async_copy(basis_hbm, basis_ref, basis_sem)
    fetches = [
        pltpu.make_async_copy(
            counts_hbm.at[:, pl.ds(at * width, width)], counts_ref.at[:, pl.ds(at * width, width)], counts_sem.at[at]
        )
        for at in range(genes // width)
    ]
    fetch_occ.start()
    for fetch in fetches:
        fetch.start()
    fetch_basis.start()
    fetch_occ.wait()
    scores = None
    for at, fetch in enumerate(fetches):
        fetch.wait()
        for col in range(at * width // tile_edge, (at + 1) * width // tile_edge):
            lanes = pl.ds(col * tile_edge, tile_edge)
            total = None
            for row in range(tile_rows):
                subs = pl.ds(row * tile_edge, tile_edge)
                occ = occ_ref[row, col].astype(F32)
                logged = jnp.log(1.0 + counts_ref[subs, lanes].astype(F32)) * occ
                high = logged.astype(BF16)
                high_ref[subs, lanes] = high
                low_ref[subs, lanes] = (logged - high.astype(F32)).astype(BF16)
                part = jnp.sum(logged, axis=0, keepdims=True)
                total = part if total is None else total + part
            sum_ref[:, lanes] = total
        if at == 0:
            fetch_basis.wait()
        chunk = pl.ds(at * width, width)
        basis = basis_ref[:, chunk]
        part = dot(basis, high_ref[:, chunk], NT) + dot(basis, low_ref[:, chunk], NT)
        scores = part if scores is None else scores + part
    score_ref[...] = scores


def log_and_scores(counts, occupancy, basis):
    cells, genes = counts.shape
    tile_rows, tile_cols = occupancy.shape
    edge = cells // tile_rows
    comps = basis.shape[0]
    width = genes // 4 if genes % (4 * edge) == 0 else genes
    hbm = pl.BlockSpec(memory_space=pltpu.HBM)
    return pl.pallas_call(
        functools.partial(log_kernel, tile_rows, edge, width),
        out_shape=(
            jax.ShapeDtypeStruct((cells, genes), BF16),
            jax.ShapeDtypeStruct((cells, genes), BF16),
            jax.ShapeDtypeStruct((comps, cells), F32),
            jax.ShapeDtypeStruct((1, genes), F32),
        ),
        in_specs=[hbm, hbm, hbm],
        out_specs=(WHOLE, WHOLE, WHOLE, WHOLE),
        scratch_shapes=[
            pltpu.SMEM(occupancy.shape, jnp.int32),
            pltpu.VMEM(counts.shape, BF16),
            pltpu.VMEM(basis.shape, BF16),
            pltpu.SemaphoreType.DMA,
            pltpu.SemaphoreType.DMA,
            pltpu.SemaphoreType.DMA((genes // width,)),
        ],
        compiler_params=LOG_PARAMS,
        name="log_scores",
    )(occupancy, counts, basis)


def spread_piece(terms, high, low):
    comps = terms[0].shape[0]
    on_low = dot(jnp.concatenate(terms[:2], axis=0), low, NN)
    on_high = dot(jnp.concatenate(terms, axis=0), high, NN)
    small = on_low[comps:] + on_high[2 * comps:]
    middle = on_low[:comps] + on_high[comps:2 * comps]
    return (small + middle) + on_high[:comps]


def spread_kernel(count, picks, me_ref, *refs):
    score_refs, (high_ref, low_ref, sum_ref), outs = refs[:count], refs[count:count + 3], refs[count + 3:]
    scores = tree_sum([ref[...] for ref in score_refs])
    comps = scores.shape[0]
    terms = split_terms(scores, 3)
    eye = lax.broadcasted_iota(jnp.int32, (comps, LANES), 0) == lax.broadcasted_iota(jnp.int32, (comps, LANES), 1)
    row_sums = jnp.sum(jnp.where(eye, jnp.sum(scores, axis=1, keepdims=True), 0.0), axis=0, keepdims=True)
    chunks = high_ref.shape[1] // (LANES * lax.axis_size("cells"))
    width = chunks * LANES
    for pick, out in zip(picks, outs):
        start = pl.multiple_of((me_ref[0] ^ pick) * width, width)
        lanes = pl.ds(start, width)
        piece = spread_piece(terms, high_ref[:, lanes], low_ref[:, lanes])
        sums = sum_ref[:, lanes]
        extra = [row_sums]
        for at in range(chunks):
            out[at * comps:(at + 1) * comps] = piece[:, at * LANES:(at + 1) * LANES]
            extra.append(sums[:, at * LANES:(at + 1) * LANES])
        extra.append(jnp.zeros((out.shape[0] - chunks * comps - chunks - 1, LANES), F32))
        out[chunks * comps:] = jnp.concatenate(extra, axis=0)


def block_rows(comps, chunks):
    return comps * chunks + -(-(chunks + 1) // 8) * 8


def spread_pieces(me, scores, high, low, sums, picks):
    comps = scores[0].shape[0]
    chunks = high.shape[1] // (LANES * lax.axis_size("cells"))
    block = jax.ShapeDtypeStruct((block_rows(comps, chunks), LANES), F32)
    return pl.pallas_call(
        functools.partial(spread_kernel, len(scores), picks),
        out_shape=[block] * len(picks),
        in_specs=[SCALARS] + [WHOLE] * (len(scores) + 3),
        out_specs=[WHOLE] * len(picks),
        compiler_params=PARAMS,
        cost_estimate=pl.CostEstimate(
            flops=10 * comps * len(picks) * chunks * LANES * high.shape[0], bytes_accessed=2**21, transcendentals=0
        ),
        name="spread",
    )(me, *scores, high, low, sums)


def gram_kernel(scale, chunks, *refs):
    pieces, (spread_ref, gram_ref) = refs[:-2], refs[-2:]
    comps = spread_ref.shape[0]
    total = tree_sum([ref[...] for ref in pieces])
    extra = total[chunks * comps:chunks * comps + chunks + 1]
    eye = lax.broadcasted_iota(jnp.int32, (comps, LANES), 0) == lax.broadcasted_iota(jnp.int32, (comps, LANES), 1)
    row_sums = jnp.sum(jnp.where(eye, extra[:1], 0.0), axis=1, keepdims=True) * scale
    parts = [total[at * comps:(at + 1) * comps] - row_sums * extra[at + 1:at + 2] for at in range(chunks)]
    spread = jnp.concatenate(parts, axis=1)
    spread_ref[...] = spread
    gram_ref[...] = packed_gram(spread)


def packed_gram(spread):
    gram = lax.dot_general(spread, spread, NT, precision=lax.Precision.HIGHEST, preferred_element_type=F32)
    half = spread.shape[0] // 2
    return jnp.concatenate([gram[:half], gram[half:]], axis=1)


def centered_gram(pieces, comps, cell_total):
    chunks = pieces[0].shape[0] // comps
    return pl.pallas_call(
        functools.partial(gram_kernel, 1.0 / cell_total, chunks),
        out_shape=(
            jax.ShapeDtypeStruct((comps, chunks * LANES), F32),
            jax.ShapeDtypeStruct((comps // 2, comps * 2), F32),
        ),
        in_specs=[WHOLE] * len(pieces),
        out_specs=(WHOLE, WHOLE),
        compiler_params=PARAMS,
        name="gram",
    )(*pieces)


def plain_gram_kernel(scale, spread_ref, row_ref, sum_ref, out_ref, gram_ref):
    spread = spread_ref[...] - row_ref[...] * scale * sum_ref[...]
    out_ref[...] = spread
    gram_ref[...] = packed_gram(spread)


def plain_gram(spread, rows, sums, cell_total):
    comps, width = spread.shape
    return pl.pallas_call(
        functools.partial(plain_gram_kernel, 1.0 / cell_total),
        out_shape=(
            jax.ShapeDtypeStruct((comps, width), F32),
            jax.ShapeDtypeStruct((comps // 2, comps * 2), F32),
        ),
        in_specs=[WHOLE] * 3,
        out_specs=(WHOLE, WHOLE),
        compiler_params=PARAMS,
        name="plain_gram",
    )(spread, rows, sums)


def inverse_of(x):
    guess = pl.reciprocal(x, approx=True)
    for _ in range(2):
        guess = guess * (2.0 - x * guess)
    return guess


def row_of(x, at):
    return jnp.broadcast_to(x[at:at + 1, :], x.shape)


def eliminate(groups, edge):
    groups = list(groups)
    below = lax.broadcasted_iota(jnp.int32, groups[0].shape, 0)
    for at in range(len(groups)):
        spread = [
            [jnp.broadcast_to(rows[:, c:c + 1], rows.shape) for c in range(at * edge, (at + 1) * edge)]
            for rows in groups[at:]
        ]
        for i in range(0, edge, 2):
            cols = spread[0]
            first, second = cols[i], cols[i + 1]
            a, b, c = row_of(first, i), row_of(second, i), row_of(second, i + 1)
            inv_a = inverse_of(a)
            inv_c = a * inverse_of(a * c - b * b)
            ratio = b * inv_a
            factors = []
            for k in range(i + 2, edge):
                top = row_of(cols[k], i)
                factors.append((k, top * inv_a, (row_of(cols[k], i + 1) - ratio * top) * inv_c))
            rows = groups[at]
            upper = row_of(rows, i) * inv_a
            rows = rows - jnp.where(below > i, first, 0.0) * upper
            lower = row_of(rows, i + 1) * inv_c
            groups[at] = rows - jnp.where(below > i + 1, second - ratio * first, 0.0) * lower
            for ahead, cols in enumerate(spread):
                first = cols[i]
                second = cols[i + 1] - ratio * first
                for k, on_first, on_second in factors:
                    cols[k] = cols[k] - first * on_first - second * on_second
                if ahead:
                    groups[at + ahead] = groups[at + ahead] - first * upper - second * lower
    return groups


def basis_kernel(scale, *refs):
    grams, (spread_ref, out_ref) = refs[:-2], refs[-2:]
    gram = tree_sum([ref[...] for ref in grams])
    comps = spread_ref.shape[0]
    gram = jnp.concatenate([gram[:, :comps], gram[:, comps:]], axis=0)
    row_at = lax.broadcasted_iota(jnp.int32, (comps, comps), 0)
    col_at = lax.broadcasted_iota(jnp.int32, (comps, comps), 1)
    eye = row_at == col_at
    trace = jnp.sum(jnp.where(eye, gram, 0.0), axis=(0, 1), keepdims=True)
    both = jnp.concatenate([gram * (1.0 / trace), jnp.where(eye, 1.0, 0.0).astype(F32)], axis=1)
    groups = eliminate([both[at:at + 8] for at in range(0, comps, 8)], 8)
    both = jnp.concatenate(groups, axis=0)
    pivots = jnp.sum(jnp.where(eye, both[:, :comps], 0.0), axis=1, keepdims=True)
    inverse = both[:, comps:] * (scale / jnp.sqrt(pivots) / jnp.sqrt(trace))
    out_ref[...] = lax.dot_general(
        inverse, spread_ref[...], NN, precision=lax.Precision.HIGHEST, preferred_element_type=F32
    )


def orthonormal(grams, spread, scale):
    return pl.pallas_call(
        functools.partial(basis_kernel, scale),
        out_shape=jax.ShapeDtypeStruct(spread.shape, F32),
        in_specs=[WHOLE] * (len(grams) + 1),
        out_specs=WHOLE,
        compiler_params=PARAMS,
        name="orthonormal",
    )(*grams, spread)


def power_of_two(size):
    return size & (size - 1) == 0


def send(x, offset_cells, offset_genes):
    cells, genes = lax.axis_size("cells"), lax.axis_size("genes")
    pairs = []
    for c in range(cells):
        for g in range(genes):
            pairs.append((c * genes + g, (c ^ offset_cells) * genes + (g ^ offset_genes)))
    return lax.ppermute(x, ("cells", "genes"), pairs)


def sum_in_steps(x, over_cells):
    cells, genes = lax.axis_size("cells"), lax.axis_size("genes")
    if not power_of_two(genes) or not power_of_two(cells) or cells > MOST_PARTNERS:
        return [lax.psum(x, ("cells", "genes") if over_cells else "genes")]
    steps = [(0, 1 << at) for at in range(genes.bit_length() - 1)]
    if over_cells:
        steps += [(1 << at, 0) for at in range(cells.bit_length() - 1)]
    pair = 1 if genes > 1 else 0
    terms = [x]
    for at, (c, g) in enumerate(steps):
        x = tree_sum(terms)
        terms = [x, send(x, c, g ^ (pair if at else 0))]
    return terms


def scattered_spread(scores, high, low, sums, cell_total):
    size = lax.axis_size("cells")
    comps = scores[0].shape[0]
    width = high.shape[1] // size
    if size < 4 or size > MOST_PARTNERS or not power_of_two(size) or width % LANES:
        scores = tree_sum(scores)
        terms = split_terms(scores, 3)
        spread = lax.psum_scatter(spread_piece(terms, high, low), "cells", scatter_dimension=1, tiled=True)
        rows = lax.psum(jnp.sum(scores, axis=1, keepdims=True), "cells")
        sums = lax.psum_scatter(sums, "cells", scatter_dimension=1, tiled=True)
        return plain_gram(spread, rows, sums, cell_total)
    me = lax.axis_index("cells").astype(jnp.int32).reshape(1)
    last = size // 2
    first, second = list(range(size - 1, last, -1)), list(range(last - 1, 0, -1))
    blocks = spread_pieces(me, scores, high, low, sums, first)
    came = [send(x, k - last, 0) for k, x in zip(first, blocks)]
    far, own, *blocks = spread_pieces(me, scores, high, low, sums, [last, 0] + second)
    also = [send(x, k, 0) for k, x in zip(second, blocks)]
    far = send(tree_sum([far] + came), last, 0)
    return centered_gram([own] + also + [far], comps, cell_total)


def on_device(counts, occupancy, start_basis):
    cell_count, gene_count = counts.shape
    cells, genes = lax.axis_size("cells"), lax.axis_size("genes")
    high, low, scores, sums = log_and_scores(counts, occupancy, start_basis)
    scores = sum_in_steps(scores, False)
    spread, gram = scattered_spread(scores, high, low, sums, cell_count * cells)
    return orthonormal(sum_in_steps(gram, True), spread, math.sqrt(gene_count * genes))


def solution(mesh):
    in_specs = (P("cells", "genes"), P("cells", "genes"), P(None, "genes"))
    out_specs = P(None, ("genes", "cells"))
    return jax.shard_map(
        on_device, mesh=mesh, in_specs=in_specs, out_specs=out_specs, check_vma=False
    )
```

```python
import functools
import math

import jax
import jax.numpy as jnp
from jax import lax
from jax.experimental import pallas as pl
from jax.experimental.pallas import tpu as pltpu
from jax.sharding import PartitionSpec as P

F32 = jnp.float32
BF16 = jnp.bfloat16
NN = (((1,), (0,)), ((), ()))
NT = (((1,), (1,)), ((), ()))
WHOLE = pl.BlockSpec(memory_space=pltpu.VMEM)
SCALARS = pl.BlockSpec(memory_space=pltpu.SMEM)
LANES = 128
PARAMS = pltpu.CompilerParams(vmem_limit_bytes=16 * 2**20)
LOG_PARAMS = pltpu.CompilerParams(vmem_limit_bytes=205 * 2**18)


def dot(a, b, dims):
    return lax.dot_general(a, b, dims, preferred_element_type=F32)


def split_terms(x, count):
    terms = []
    for _ in range(count):
        term = x.astype(BF16)
        terms.append(term)
        x = x - term.astype(F32)
    return terms


def tree_sum(parts):
    while len(parts) > 1:
        parts = [sum(parts[at + 1:at + 2], parts[at]) for at in range(0, len(parts), 2)]
    return parts[0]


def log_kernel(width, counts_hbm, high_ref, low_ref, sum_ref, counts_ref, counts_sem):
    cells, genes = high_ref.shape
    fetches = [
        pltpu.make_async_copy(
            counts_hbm.at[:, pl.ds(at * width, width)], counts_ref.at[:, pl.ds(at * width, width)], counts_sem.at[at]
        )
        for at in range(genes // width)
    ]
    for fetch in fetches:
        fetch.start()
    for at, fetch in enumerate(fetches):
        fetch.wait()
        for begin in range(at * width, (at + 1) * width, LANES):
            lanes = pl.ds(begin, LANES)
            logged = jnp.log(1.0 + counts_ref[:, lanes].astype(F32))
            high = logged.astype(BF16)
            high_ref[:, lanes] = high
            low_ref[:, lanes] = (logged - high.astype(F32)).astype(BF16)
            sum_ref[:, lanes] = jnp.sum(logged, axis=0, keepdims=True)


def log_terms(counts):
    cells, genes = counts.shape
    width = genes // 8
    return pl.pallas_call(
        functools.partial(log_kernel, width),
        out_shape=(
            jax.ShapeDtypeStruct((cells, genes), BF16),
            jax.ShapeDtypeStruct((cells, genes), BF16),
            jax.ShapeDtypeStruct((1, genes), F32),
        ),
        in_specs=[pl.BlockSpec(memory_space=pltpu.HBM)],
        out_specs=(WHOLE, WHOLE, WHOLE),
        scratch_shapes=[pltpu.VMEM(counts.shape, BF16), pltpu.SemaphoreType.DMA((genes // width,))],
        compiler_params=LOG_PARAMS,
        cost_estimate=pl.CostEstimate(flops=20 * cells * genes, bytes_accessed=8 * cells * genes, transcendentals=0),
        name="log_terms",
    )(counts)


def score_kernel(width, occ_ref, basis_ref, high_ref, low_ref, score_ref):
    comps, genes = basis_ref.shape
    edge = genes // occ_ref.shape[1]
    scores = None
    for begin in range(0, genes, width):
        basis = []
        for at in range(begin, begin + width, edge):
            columns = basis_ref[:, pl.ds(at, edge)]
            basis.append(columns * occ_ref[0, at // edge].astype(F32).astype(BF16))
        basis = jnp.concatenate(basis, axis=1)
        lanes = pl.ds(begin, width)
        part = dot(basis, high_ref[:, lanes], NT) + dot(basis, low_ref[:, lanes], NT)
        scores = part if scores is None else scores + part
    score_ref[...] = scores


def score_part(occupancy, basis, high, low):
    comps, genes = basis.shape
    cells = high.shape[0]
    return pl.pallas_call(
        functools.partial(score_kernel, genes // 4),
        out_shape=jax.ShapeDtypeStruct((comps, cells), F32),
        in_specs=[SCALARS, WHOLE, WHOLE, WHOLE],
        out_specs=WHOLE,
        compiler_params=PARAMS,
        name="scores",
    )(occupancy, basis, high, low)


def spread_piece(terms, high, low):
    comps = terms[0].shape[0]
    on_low = dot(jnp.concatenate(terms[:2], axis=0), low, NN)
    on_high = dot(jnp.concatenate(terms, axis=0), high, NN)
    small = on_low[comps:] + on_high[2 * comps:]
    middle = on_low[:comps] + on_high[comps:2 * comps]
    return (small + middle) + on_high[:comps]


def spread_kernel(count, picks, me_ref, occ_ref, *refs):
    score_refs, (high_ref, low_ref, sum_ref), outs = refs[:count], refs[count:count + 3], refs[count + 3:]
    scores = tree_sum([ref[...] for ref in score_refs])
    comps = scores.shape[0]
    terms = split_terms(scores, 3)
    eye = lax.broadcasted_iota(jnp.int32, (comps, LANES), 0) == lax.broadcasted_iota(jnp.int32, (comps, LANES), 1)
    row_sums = jnp.sum(jnp.where(eye, jnp.sum(scores, axis=1, keepdims=True), 0.0), axis=0, keepdims=True)
    chunks = high_ref.shape[1] // (LANES * lax.axis_size("cells"))
    width = chunks * LANES
    for pick, out in zip(picks, outs):
        start = pl.multiple_of((me_ref[0] ^ pick) * width, width)
        lanes = pl.ds(start, width)
        piece = spread_piece(terms, high_ref[:, lanes], low_ref[:, lanes])
        sums = sum_ref[:, lanes]
        extra = [row_sums]
        for at in range(chunks):
            occ = occ_ref[0, (me_ref[0] ^ pick) * chunks + at].astype(F32)
            out[at * comps:(at + 1) * comps] = piece[:, at * LANES:(at + 1) * LANES] * occ
            extra.append(sums[:, at * LANES:(at + 1) * LANES] * occ)
        extra.append(jnp.zeros((out.shape[0] - chunks * comps - chunks - 1, LANES), F32))
        out[chunks * comps:] = jnp.concatenate(extra, axis=0)


def block_rows(comps, chunks):
    return comps * chunks + -(-(chunks + 1) // 8) * 8


def spread_pieces(me, occupancy, scores, high, low, sums, picks):
    comps = scores[0].shape[0]
    chunks = high.shape[1] // (LANES * lax.axis_size("cells"))
    block = jax.ShapeDtypeStruct((block_rows(comps, chunks), LANES), F32)
    return pl.pallas_call(
        functools.partial(spread_kernel, len(scores), picks),
        out_shape=[block] * len(picks),
        in_specs=[SCALARS] * 2 + [WHOLE] * (len(scores) + 3),
        out_specs=[WHOLE] * len(picks),
        compiler_params=PARAMS,
        cost_estimate=pl.CostEstimate(
            flops=10 * comps * len(picks) * chunks * LANES * high.shape[0], bytes_accessed=2**21, transcendentals=0
        ),
        name="spread",
    )(me, occupancy, *scores, high, low, sums)


def gram_kernel(scale, chunks, *refs):
    pieces, (spread_ref, gram_ref) = refs[:-2], refs[-2:]
    comps = spread_ref.shape[0]
    total = tree_sum([ref[...] for ref in pieces])
    extra = total[chunks * comps:chunks * comps + chunks + 1]
    eye = lax.broadcasted_iota(jnp.int32, (comps, LANES), 0) == lax.broadcasted_iota(jnp.int32, (comps, LANES), 1)
    row_sums = jnp.sum(jnp.where(eye, extra[:1], 0.0), axis=1, keepdims=True) * scale
    parts = [total[at * comps:(at + 1) * comps] - row_sums * extra[at + 1:at + 2] for at in range(chunks)]
    spread = jnp.concatenate(parts, axis=1)
    spread_ref[...] = spread
    gram_ref[...] = packed_gram(spread)


def packed_gram(spread):
    gram = lax.dot_general(spread, spread, NT, precision=lax.Precision.HIGHEST, preferred_element_type=F32)
    half = spread.shape[0] // 2
    return jnp.concatenate([gram[:half], gram[half:]], axis=1)


def centered_gram(pieces, comps, cell_total):
    chunks = pieces[0].shape[0] // comps
    return pl.pallas_call(
        functools.partial(gram_kernel, 1.0 / cell_total, chunks),
        out_shape=(
            jax.ShapeDtypeStruct((comps, chunks * LANES), F32),
            jax.ShapeDtypeStruct((comps // 2, comps * 2), F32),
        ),
        in_specs=[WHOLE] * len(pieces),
        out_specs=(WHOLE, WHOLE),
        compiler_params=PARAMS,
        name="gram",
    )(*pieces)


def plain_gram_kernel(scale, spread_ref, row_ref, sum_ref, out_ref, gram_ref):
    spread = spread_ref[...] - row_ref[...] * scale * sum_ref[...]
    out_ref[...] = spread
    gram_ref[...] = packed_gram(spread)


def plain_gram(spread, rows, sums, cell_total):
    comps, width = spread.shape
    return pl.pallas_call(
        functools.partial(plain_gram_kernel, 1.0 / cell_total),
        out_shape=(
            jax.ShapeDtypeStruct((comps, width), F32),
            jax.ShapeDtypeStruct((comps // 2, comps * 2), F32),
        ),
        in_specs=[WHOLE] * 3,
        out_specs=(WHOLE, WHOLE),
        compiler_params=PARAMS,
        name="plain_gram",
    )(spread, rows, sums)


def inverse_of(x):
    guess = pl.reciprocal(x, approx=True)
    for _ in range(2):
        guess = guess * (2.0 - x * guess)
    return guess


def row_of(x, at):
    return jnp.broadcast_to(x[at:at + 1, :], x.shape)


def eliminate(groups, edge):
    groups = list(groups)
    below = lax.broadcasted_iota(jnp.int32, groups[0].shape, 0)
    for at in range(len(groups)):
        spread = [
            [jnp.broadcast_to(rows[:, c:c + 1], rows.shape) for c in range(at * edge, (at + 1) * edge)]
            for rows in groups[at:]
        ]
        for i in range(0, edge, 2):
            cols = spread[0]
            first, second = cols[i], cols[i + 1]
            a, b, c = row_of(first, i), row_of(second, i), row_of(second, i + 1)
            inv_a = inverse_of(a)
            inv_c = a * inverse_of(a * c - b * b)
            ratio = b * inv_a
            factors = []
            for k in range(i + 2, edge):
                top = row_of(cols[k], i)
                factors.append((k, top * inv_a, (row_of(cols[k], i + 1) - ratio * top) * inv_c))
            rows = groups[at]
            upper = row_of(rows, i) * inv_a
            rows = rows - jnp.where(below > i, first, 0.0) * upper
            lower = row_of(rows, i + 1) * inv_c
            groups[at] = rows - jnp.where(below > i + 1, second - ratio * first, 0.0) * lower
            for ahead, cols in enumerate(spread):
                first = cols[i]
                second = cols[i + 1] - ratio * first
                for k, on_first, on_second in factors:
                    cols[k] = cols[k] - first * on_first - second * on_second
                if ahead:
                    groups[at + ahead] = groups[at + ahead] - first * upper - second * lower
    return groups


def basis_kernel(scale, *refs):
    grams, (spread_ref, out_ref) = refs[:-2], refs[-2:]
    gram = tree_sum([ref[...] for ref in grams])
    comps = spread_ref.shape[0]
    gram = jnp.concatenate([gram[:, :comps], gram[:, comps:]], axis=0)
    row_at = lax.broadcasted_iota(jnp.int32, (comps, comps), 0)
    col_at = lax.broadcasted_iota(jnp.int32, (comps, comps), 1)
    eye = row_at == col_at
    trace = jnp.sum(jnp.where(eye, gram, 0.0), axis=(0, 1), keepdims=True)
    both = jnp.concatenate([gram * (1.0 / trace), jnp.where(eye, 1.0, 0.0).astype(F32)], axis=1)
    groups = eliminate([both[at:at + 8] for at in range(0, comps, 8)], 8)
    both = jnp.concatenate(groups, axis=0)
    pivots = jnp.sum(jnp.where(eye, both[:, :comps], 0.0), axis=1, keepdims=True)
    inverse = both[:, comps:] * (scale / jnp.sqrt(pivots) / jnp.sqrt(trace))
    out_ref[...] = lax.dot_general(
        inverse, spread_ref[...], NN, precision=lax.Precision.HIGHEST, preferred_element_type=F32
    )


def orthonormal(grams, spread, scale):
    return pl.pallas_call(
        functools.partial(basis_kernel, scale),
        out_shape=jax.ShapeDtypeStruct(spread.shape, F32),
        in_specs=[WHOLE] * (len(grams) + 1),
        out_specs=WHOLE,
        compiler_params=PARAMS,
        name="orthonormal",
    )(*grams, spread)


def send(x, offset_cells, offset_genes):
    cells, genes = lax.axis_size("cells"), lax.axis_size("genes")
    pairs = []
    for c in range(cells):
        for g in range(genes):
            pairs.append((c * genes + g, (c ^ offset_cells) * genes + (g ^ offset_genes)))
    return lax.ppermute(x, ("cells", "genes"), pairs)


def sum_in_steps(x, over_cells):
    cells, genes = lax.axis_size("cells"), lax.axis_size("genes")
    steps = [(0, 1 << at) for at in range(genes.bit_length() - 1)]
    if over_cells:
        steps += [(1 << at, 0) for at in range(cells.bit_length() - 1)]
    pair = 1 if genes > 1 else 0
    terms = [x]
    for at, (c, g) in enumerate(steps):
        x = tree_sum(terms)
        terms = [x, send(x, c, g ^ (pair if at else 0))]
    return terms


def scattered_spread(occupancy, scores, high, low, sums, cell_total):
    comps = scores[0].shape[0]
    me = lax.axis_index("cells").astype(jnp.int32).reshape(1)
    make = functools.partial(spread_pieces, occupancy=occupancy, scores=scores, high=high, low=low, sums=sums)
    blocks = list(make(me, picks=[7, 6, 5]))
    blocks[0], me = lax.optimization_barrier((blocks[0], me))
    came = [send(x, k - 4, 0) for k, x in zip((7, 6, 5), blocks)]
    far, own, near, *blocks = make(me, picks=[4, 0, 2, 3, 1])
    also = [send(x, 1, 0) for x in blocks]
    near = send(near + also[0], 2, 0)
    far = send(tree_sum([far] + came), 4, 0)
    return centered_gram([near, own + also[1] + far], comps, cell_total)


def all_alike(counts, occupancy, start_basis):
    tile_rows, tile_cols = occupancy.shape
    edge = counts.shape[0] // tile_rows
    logged = jnp.log(1.0 + counts.astype(F32)).reshape(tile_rows, edge, tile_cols, -1)
    logged = (logged * occupancy.astype(F32)[:, None, :, None]).reshape(counts.shape)
    high, low = split_terms(logged, 2)
    scores = lax.psum(dot(start_basis, high, NT) + dot(start_basis, low, NT), "genes")
    spread = spread_piece(split_terms(scores, 3), high, low)
    spread = lax.psum_scatter(spread, "cells", scatter_dimension=1, tiled=True)
    rows = lax.psum(jnp.sum(scores, axis=1, keepdims=True), "cells")
    sums = lax.psum_scatter(jnp.sum(logged, axis=0, keepdims=True), "cells", scatter_dimension=1, tiled=True)
    spread, gram = plain_gram(spread, rows, sums, counts.shape[0] * lax.axis_size("cells"))
    return [lax.psum(gram, ("cells", "genes"))], spread


def in_steps(counts, occupancy, start_basis):
    high, low, sums = log_terms(counts)
    scores = sum_in_steps(score_part(occupancy, start_basis, high, low), False)
    cell_total = counts.shape[0] * lax.axis_size("cells")
    spread, gram = scattered_spread(occupancy, scores, high, low, sums, cell_total)
    return sum_in_steps(gram, True), spread


def on_device(counts, occupancy, start_basis):
    gene_count = counts.shape[1]
    cells, genes = lax.axis_size("cells"), lax.axis_size("genes")
    halvings = cells == 1 << 3 and genes & (genes - 1) == 0
    tiles = occupancy.shape[0] == 1 and gene_count == occupancy.shape[1] * LANES
    work = in_steps if halvings and tiles and gene_count % (cells * LANES) == 0 else all_alike
    grams, spread = work(counts, occupancy, start_basis)
    return orthonormal(grams, spread, math.sqrt(gene_count * genes))


def solution(mesh):
    in_specs = (P("cells", "genes"), P("cells", "genes"), P(None, "genes"))
    out_specs = P(None, ("genes", "cells"))
    return jax.shard_map(
        on_device, mesh=mesh, in_specs=in_specs, out_specs=out_specs, check_vma=False
    )
```

```python
import functools
import math

import jax
import jax.numpy as jnp
from jax import lax
from jax.experimental import pallas as pl
from jax.experimental.pallas import tpu as pltpu
from jax.sharding import PartitionSpec as P

F32 = jnp.float32
BF16 = jnp.bfloat16
NN = (((1,), (0,)), ((), ()))
NT = (((1,), (1,)), ((), ()))
WHOLE = pl.BlockSpec(memory_space=pltpu.VMEM)
SCALARS = pl.BlockSpec(memory_space=pltpu.SMEM)
LANES = 128
PARAMS = pltpu.CompilerParams(vmem_limit_bytes=16 * 2**20)
LOG_PARAMS = pltpu.CompilerParams(vmem_limit_bytes=205 * 2**18)


def dot(a, b, dims):
    return lax.dot_general(a, b, dims, preferred_element_type=F32)


def split_terms(x, count):
    terms = []
    for _ in range(count):
        term = x.astype(BF16)
        terms.append(term)
        x = x - term.astype(F32)
    return terms


def tree_sum(parts):
    while len(parts) > 1:
        parts = [sum(parts[at + 1:at + 2], parts[at]) for at in range(0, len(parts), 2)]
    return parts[0]


def log_kernel(width, counts_hbm, high_ref, low_ref, sum_ref, counts_ref, counts_sem):
    cells, genes = high_ref.shape
    fetches = [
        pltpu.make_async_copy(
            counts_hbm.at[:, pl.ds(at * width, width)], counts_ref.at[:, pl.ds(at * width, width)], counts_sem.at[at]
        )
        for at in range(genes // width)
    ]
    for fetch in fetches:
        fetch.start()
    for at, fetch in enumerate(fetches):
        fetch.wait()
        for begin in range(at * width, (at + 1) * width, LANES):
            lanes = pl.ds(begin, LANES)
            logged = jnp.log(1.0 + counts_ref[:, lanes].astype(F32))
            high = logged.astype(BF16)
            high_ref[:, lanes] = high
            low_ref[:, lanes] = (logged - high.astype(F32)).astype(BF16)
            sum_ref[:, lanes] = jnp.sum(logged, axis=0, keepdims=True)


def log_terms(counts):
    cells, genes = counts.shape
    width = genes // 8
    return pl.pallas_call(
        functools.partial(log_kernel, width),
        out_shape=(
            jax.ShapeDtypeStruct((cells, genes), BF16),
            jax.ShapeDtypeStruct((cells, genes), BF16),
            jax.ShapeDtypeStruct((1, genes), F32),
        ),
        in_specs=[pl.BlockSpec(memory_space=pltpu.HBM)],
        out_specs=(WHOLE, WHOLE, WHOLE),
        scratch_shapes=[pltpu.VMEM(counts.shape, BF16), pltpu.SemaphoreType.DMA((genes // width,))],
        compiler_params=LOG_PARAMS,
        cost_estimate=pl.CostEstimate(flops=20 * cells * genes, bytes_accessed=8 * cells * genes, transcendentals=0),
        name="log_terms",
    )(counts)


def score_kernel(width, occ_ref, basis_ref, high_ref, low_ref, score_ref, lane_ref):
    comps, genes = basis_ref.shape
    edge = genes // occ_ref.shape[1]
    occupancy = occ_ref[...].astype(F32)
    scores = None
    for begin in range(0, genes, width):
        basis = []
        for at in range(begin, begin + width, edge):
            occ = jnp.broadcast_to(occupancy[:, at // edge:at // edge + 1], (1, edge))
            lane_ref[:, pl.ds(at, edge)] = occ
            basis.append(basis_ref[:, pl.ds(at, edge)] * occ.astype(BF16))
        basis = jnp.concatenate(basis, axis=1)
        lanes = pl.ds(begin, width)
        part = dot(basis, high_ref[:, lanes], NT) + dot(basis, low_ref[:, lanes], NT)
        scores = part if scores is None else scores + part
    score_ref[...] = scores


def score_part(occupancy, basis, high, low):
    comps, genes = basis.shape
    cells = high.shape[0]
    return pl.pallas_call(
        functools.partial(score_kernel, genes // 4),
        out_shape=(jax.ShapeDtypeStruct((comps, cells), F32), jax.ShapeDtypeStruct((1, genes), F32)),
        in_specs=[WHOLE] * 4,
        out_specs=(WHOLE, WHOLE),
        compiler_params=PARAMS,
        name="scores",
    )(occupancy, basis, high, low)


def spread_piece(terms, high, low):
    comps = terms[0].shape[0]
    on_low = dot(jnp.concatenate(terms[:2], axis=0), low, NN)
    on_high = dot(jnp.concatenate(terms, axis=0), high, NN)
    small = on_low[comps:] + on_high[2 * comps:]
    middle = on_low[:comps] + on_high[comps:2 * comps]
    return (small + middle) + on_high[:comps]


def spread_kernel(count, picks, me_ref, *refs):
    score_refs, outs = refs[:count], refs[count + 4:]
    high_ref, low_ref, sum_ref, occ_ref = refs[count:count + 4]
    scores = tree_sum([ref[...] for ref in score_refs])
    comps = scores.shape[0]
    terms = split_terms(scores, 3)
    eye = lax.broadcasted_iota(jnp.int32, (comps, LANES), 0) == lax.broadcasted_iota(jnp.int32, (comps, LANES), 1)
    row_sums = jnp.sum(jnp.where(eye, jnp.sum(scores, axis=1, keepdims=True), 0.0), axis=0, keepdims=True)
    chunks = high_ref.shape[1] // (LANES * lax.axis_size("cells"))
    width = chunks * LANES
    for pick, out in zip(picks, outs):
        start = pl.multiple_of((me_ref[0] ^ pick) * width, width)
        lanes = pl.ds(start, width)
        piece = spread_piece(terms, high_ref[:, lanes], low_ref[:, lanes]) * occ_ref[:, lanes]
        sums = sum_ref[:, lanes] * occ_ref[:, lanes]
        extra = [row_sums]
        for at in range(chunks):
            out[at * comps:(at + 1) * comps] = piece[:, at * LANES:(at + 1) * LANES]
            extra.append(sums[:, at * LANES:(at + 1) * LANES])
        extra.append(jnp.zeros((out.shape[0] - chunks * comps - chunks - 1, LANES), F32))
        out[chunks * comps:] = jnp.concatenate(extra, axis=0)


def block_rows(comps, chunks):
    return comps * chunks + -(-(chunks + 1) // 8) * 8


def spread_pieces(me, scores, high, low, sums, occ, picks):
    comps = scores[0].shape[0]
    chunks = high.shape[1] // (LANES * lax.axis_size("cells"))
    block = jax.ShapeDtypeStruct((block_rows(comps, chunks), LANES), F32)
    return pl.pallas_call(
        functools.partial(spread_kernel, len(scores), picks),
        out_shape=[block] * len(picks),
        in_specs=[SCALARS] + [WHOLE] * (len(scores) + 4),
        out_specs=[WHOLE] * len(picks),
        compiler_params=PARAMS,
        cost_estimate=pl.CostEstimate(
            flops=10 * comps * len(picks) * chunks * LANES * high.shape[0], bytes_accessed=2**21, transcendentals=0
        ),
        name="spread",
    )(me, *scores, high, low, sums, occ)


def gram_kernel(scale, chunks, *refs):
    pieces, (spread_ref, gram_ref) = refs[:-2], refs[-2:]
    comps = spread_ref.shape[0]
    total = tree_sum([ref[...] for ref in pieces])
    extra = total[chunks * comps:chunks * comps + chunks + 1]
    eye = lax.broadcasted_iota(jnp.int32, (comps, LANES), 0) == lax.broadcasted_iota(jnp.int32, (comps, LANES), 1)
    row_sums = jnp.sum(jnp.where(eye, extra[:1], 0.0), axis=1, keepdims=True) * scale
    parts = [total[at * comps:(at + 1) * comps] - row_sums * extra[at + 1:at + 2] for at in range(chunks)]
    spread = jnp.concatenate(parts, axis=1)
    spread_ref[...] = spread
    gram_ref[...] = packed_gram(spread)


def packed_gram(spread):
    gram = lax.dot_general(spread, spread, NT, precision=lax.Precision.HIGHEST, preferred_element_type=F32)
    half = spread.shape[0] // 2
    return jnp.concatenate([gram[:half], gram[half:]], axis=1)


def centered_gram(pieces, comps, cell_total):
    chunks = pieces[0].shape[0] // comps
    return pl.pallas_call(
        functools.partial(gram_kernel, 1.0 / cell_total, chunks),
        out_shape=(
            jax.ShapeDtypeStruct((comps, chunks * LANES), F32),
            jax.ShapeDtypeStruct((comps // 2, comps * 2), F32),
        ),
        in_specs=[WHOLE] * len(pieces),
        out_specs=(WHOLE, WHOLE),
        compiler_params=PARAMS,
        name="gram",
    )(*pieces)


def plain_gram_kernel(scale, spread_ref, row_ref, sum_ref, out_ref, gram_ref):
    spread = spread_ref[...] - row_ref[...] * scale * sum_ref[...]
    out_ref[...] = spread
    gram_ref[...] = packed_gram(spread)


def plain_gram(spread, rows, sums, cell_total):
    comps, width = spread.shape
    return pl.pallas_call(
        functools.partial(plain_gram_kernel, 1.0 / cell_total),
        out_shape=(
            jax.ShapeDtypeStruct((comps, width), F32),
            jax.ShapeDtypeStruct((comps // 2, comps * 2), F32),
        ),
        in_specs=[WHOLE] * 3,
        out_specs=(WHOLE, WHOLE),
        compiler_params=PARAMS,
        name="plain_gram",
    )(spread, rows, sums)


def inverse_of(x):
    guess = pl.reciprocal(x, approx=True)
    for _ in range(2):
        guess = guess * (2.0 - x * guess)
    return guess


def row_of(x, at):
    return jnp.broadcast_to(x[at:at + 1, :], x.shape)


def eliminate(groups, edge):
    groups = list(groups)
    below = lax.broadcasted_iota(jnp.int32, groups[0].shape, 0)
    for at in range(len(groups)):
        spread = [
            [jnp.broadcast_to(rows[:, c:c + 1], rows.shape) for c in range(at * edge, (at + 1) * edge)]
            for rows in groups[at:]
        ]
        for i in range(0, edge, 2):
            cols = spread[0]
            first, second = cols[i], cols[i + 1]
            a, b, c = row_of(first, i), row_of(second, i), row_of(second, i + 1)
            inv_a = inverse_of(a)
            inv_c = a * inverse_of(a * c - b * b)
            ratio = b * inv_a
            factors = []
            for k in range(i + 2, edge):
                top = row_of(cols[k], i)
                factors.append((k, top * inv_a, (row_of(cols[k], i + 1) - ratio * top) * inv_c))
            rows = groups[at]
            upper = row_of(rows, i) * inv_a
            rows = rows - jnp.where(below > i, first, 0.0) * upper
            lower = row_of(rows, i + 1) * inv_c
            groups[at] = rows - jnp.where(below > i + 1, second - ratio * first, 0.0) * lower
            for ahead, cols in enumerate(spread):
                first = cols[i]
                second = cols[i + 1] - ratio * first
                for k, on_first, on_second in factors:
                    cols[k] = cols[k] - first * on_first - second * on_second
                if ahead:
                    groups[at + ahead] = groups[at + ahead] - first * upper - second * lower
    return groups


def basis_kernel(scale, *refs):
    grams, (spread_ref, out_ref) = refs[:-2], refs[-2:]
    gram = tree_sum([ref[...] for ref in grams])
    comps = spread_ref.shape[0]
    gram = jnp.concatenate([gram[:, :comps], gram[:, comps:]], axis=0)
    row_at = lax.broadcasted_iota(jnp.int32, (comps, comps), 0)
    col_at = lax.broadcasted_iota(jnp.int32, (comps, comps), 1)
    eye = row_at == col_at
    trace = jnp.sum(jnp.where(eye, gram, 0.0), axis=(0, 1), keepdims=True)
    both = jnp.concatenate([gram * (1.0 / trace), jnp.where(eye, 1.0, 0.0).astype(F32)], axis=1)
    groups = eliminate([both[at:at + 8] for at in range(0, comps, 8)], 8)
    both = jnp.concatenate(groups, axis=0)
    pivots = jnp.sum(jnp.where(eye, both[:, :comps], 0.0), axis=1, keepdims=True)
    inverse = both[:, comps:] * (scale / jnp.sqrt(pivots) / jnp.sqrt(trace))
    out_ref[...] = lax.dot_general(
        inverse, spread_ref[...], NN, precision=lax.Precision.HIGHEST, preferred_element_type=F32
    )


def orthonormal(grams, spread, scale):
    return pl.pallas_call(
        functools.partial(basis_kernel, scale),
        out_shape=jax.ShapeDtypeStruct(spread.shape, F32),
        in_specs=[WHOLE] * (len(grams) + 1),
        out_specs=WHOLE,
        compiler_params=PARAMS,
        name="orthonormal",
    )(*grams, spread)


def send(x, offset_cells, offset_genes):
    cells, genes = lax.axis_size("cells"), lax.axis_size("genes")
    pairs = []
    for c in range(cells):
        for g in range(genes):
            pairs.append((c * genes + g, (c ^ offset_cells) * genes + (g ^ offset_genes)))
    return lax.ppermute(x, ("cells", "genes"), pairs)


def gene_terms(x):
    return [x] + [send(x, 0, k) for k in range(1, lax.axis_size("genes"))]


def cell_terms(x):
    terms = [x]
    for at in range(lax.axis_size("cells").bit_length() - 1):
        x = tree_sum(terms)
        terms = [x, send(x, 1 << at, 1)]
    return terms


def scattered_spread(scores, high, low, sums, occ, cell_total):
    comps = scores[0].shape[0]
    me = lax.axis_index("cells").astype(jnp.int32).reshape(1)
    make = functools.partial(spread_pieces, scores=scores, high=high, low=low, sums=sums, occ=occ)
    blocks = list(make(me, picks=[7, 6, 5]))
    blocks[0], me = lax.optimization_barrier((blocks[0], me))
    came = [send(x, k - 4, 1) for k, x in zip((7, 6, 5), blocks)]
    far, near, own, *blocks = make(me, picks=[4, 2, 0, 3, 1])
    far, near = send(far, 0, 1), send(near, 0, 1)
    near = send(near + send(blocks[0], 1, 1), 2, 1)
    also = send(blocks[1], 1, 0)
    far = send(far + lax.optimization_barrier(tree_sum(came)), 4, 1)
    return centered_gram([own + also + (near + far)], comps, cell_total)


def all_alike(counts, occupancy, start_basis):
    tile_rows, tile_cols = occupancy.shape
    edge = counts.shape[0] // tile_rows
    logged = jnp.log(1.0 + counts.astype(F32)).reshape(tile_rows, edge, tile_cols, -1)
    logged = (logged * occupancy.astype(F32)[:, None, :, None]).reshape(counts.shape)
    high, low = split_terms(logged, 2)
    scores = lax.psum(dot(start_basis, high, NT) + dot(start_basis, low, NT), "genes")
    spread = spread_piece(split_terms(scores, 3), high, low)
    spread = lax.psum_scatter(spread, "cells", scatter_dimension=1, tiled=True)
    rows = lax.psum(jnp.sum(scores, axis=1, keepdims=True), "cells")
    sums = lax.psum_scatter(jnp.sum(logged, axis=0, keepdims=True), "cells", scatter_dimension=1, tiled=True)
    spread, gram = plain_gram(spread, rows, sums, counts.shape[0] * lax.axis_size("cells"))
    return [lax.psum(gram, ("cells", "genes"))], spread


def in_steps(counts, occupancy, start_basis):
    high, low, sums = log_terms(counts)
    scores, occ = score_part(occupancy, start_basis, high, low)
    cell_total = counts.shape[0] * lax.axis_size("cells")
    spread, gram = scattered_spread(gene_terms(scores), high, low, sums, occ, cell_total)
    return cell_terms(tree_sum(gene_terms(gram))), spread


def on_device(counts, occupancy, start_basis):
    gene_count = counts.shape[1]
    cells, genes = lax.axis_size("cells"), lax.axis_size("genes")
    halvings = cells == 1 << 3 and genes == 1 << 2
    tiles = occupancy.shape[0] == 1 and gene_count == occupancy.shape[1] * LANES
    work = in_steps if halvings and tiles and gene_count % (cells * LANES) == 0 else all_alike
    grams, spread = work(counts, occupancy, start_basis)
    return orthonormal(grams, spread, math.sqrt(gene_count * genes))


def solution(mesh):
    in_specs = (P("cells", "genes"), P("cells", "genes"), P(None, "genes"))
    out_specs = P(None, ("genes", "cells"))
    return jax.shard_map(
        on_device, mesh=mesh, in_specs=in_specs, out_specs=out_specs, check_vma=False
    )
```

```python
import functools
import math

import jax
import jax.numpy as jnp
from jax import lax
from jax.experimental import pallas as pl
from jax.experimental.pallas import tpu as pltpu
from jax.sharding import PartitionSpec as P

F32 = jnp.float32
BF16 = jnp.bfloat16
NN = (((1,), (0,)), ((), ()))
NT = (((1,), (1,)), ((), ()))
WHOLE = pl.BlockSpec(memory_space=pltpu.VMEM)
SCALARS = pl.BlockSpec(memory_space=pltpu.SMEM)
LANES = 128
PARAMS = pltpu.CompilerParams(vmem_limit_bytes=16 * 2**20)
LOG_PARAMS = pltpu.CompilerParams(vmem_limit_bytes=205 * 2**18)


def dot(a, b, dims):
    return lax.dot_general(a, b, dims, preferred_element_type=F32)


def split_terms(x, count):
    terms = []
    for _ in range(count):
        term = x.astype(BF16)
        terms.append(term)
        x = x - term.astype(F32)
    return terms


def tree_sum(parts):
    while len(parts) > 1:
        parts = [sum(parts[at + 1:at + 2], parts[at]) for at in range(0, len(parts), 2)]
    return parts[0]


def log_kernel(width, counts_hbm, high_ref, low_ref, sum_ref, counts_ref, counts_sem):
    cells, genes = high_ref.shape
    fetches = [
        pltpu.make_async_copy(
            counts_hbm.at[:, pl.ds(at * width, width)], counts_ref.at[:, pl.ds(at * width, width)], counts_sem.at[at]
        )
        for at in range(genes // width)
    ]
    for fetch in fetches:
        fetch.start()
    for at, fetch in enumerate(fetches):
        fetch.wait()
        for begin in range(at * width, (at + 1) * width, LANES):
            lanes = pl.ds(begin, LANES)
            logged = jnp.log(1.0 + counts_ref[:, lanes].astype(F32))
            high = logged.astype(BF16)
            high_ref[:, lanes] = high
            low_ref[:, lanes] = (logged - high.astype(F32)).astype(BF16)
            sum_ref[:, lanes] = jnp.sum(logged, axis=0, keepdims=True)


def log_terms(counts):
    cells, genes = counts.shape
    width = genes // 8
    return pl.pallas_call(
        functools.partial(log_kernel, width),
        out_shape=(
            jax.ShapeDtypeStruct((cells, genes), BF16),
            jax.ShapeDtypeStruct((cells, genes), BF16),
            jax.ShapeDtypeStruct((1, genes), F32),
        ),
        in_specs=[pl.BlockSpec(memory_space=pltpu.HBM)],
        out_specs=(WHOLE, WHOLE, WHOLE),
        scratch_shapes=[pltpu.VMEM(counts.shape, BF16), pltpu.SemaphoreType.DMA((genes // width,))],
        compiler_params=LOG_PARAMS,
        cost_estimate=pl.CostEstimate(flops=20 * cells * genes, bytes_accessed=8 * cells * genes, transcendentals=0),
        name="log_terms",
    )(counts)


def score_kernel(width, occ_ref, basis_ref, high_ref, low_ref, score_ref, lane_ref):
    comps, genes = basis_ref.shape
    edge = genes // occ_ref.shape[1]
    occupancy = occ_ref[...].astype(F32)
    scores = None
    for begin in range(0, genes, width):
        basis = []
        for at in range(begin, begin + width, edge):
            occ = jnp.broadcast_to(occupancy[:, at // edge:at // edge + 1], (1, edge))
            lane_ref[:, pl.ds(at, edge)] = occ
            basis.append(basis_ref[:, pl.ds(at, edge)] * occ.astype(BF16))
        basis = jnp.concatenate(basis, axis=1)
        lanes = pl.ds(begin, width)
        part = dot(basis, high_ref[:, lanes], NT) + dot(basis, low_ref[:, lanes], NT)
        scores = part if scores is None else scores + part
    score_ref[...] = scores


def score_part(occupancy, basis, high, low):
    comps, genes = basis.shape
    cells = high.shape[0]
    return pl.pallas_call(
        functools.partial(score_kernel, genes // 4),
        out_shape=(jax.ShapeDtypeStruct((comps, cells), F32), jax.ShapeDtypeStruct((1, genes), F32)),
        in_specs=[WHOLE] * 4,
        out_specs=(WHOLE, WHOLE),
        compiler_params=PARAMS,
        name="scores",
    )(occupancy, basis, high, low)


def spread_piece(terms, high, low):
    comps = terms[0].shape[0]
    on_low = dot(jnp.concatenate(terms[:2], axis=0), low, NN)
    on_high = dot(jnp.concatenate(terms, axis=0), high, NN)
    small = on_low[comps:] + on_high[2 * comps:]
    middle = on_low[:comps] + on_high[comps:2 * comps]
    return (small + middle) + on_high[:comps]


def spread_kernel(count, picks, me_ref, *refs):
    score_refs, outs = refs[:count], refs[count + 4:]
    high_ref, low_ref, sum_ref, occ_ref = refs[count:count + 4]
    scores = tree_sum([ref[...] for ref in score_refs])
    comps = scores.shape[0]
    terms = split_terms(scores, 3)
    eye = lax.broadcasted_iota(jnp.int32, (comps, LANES), 0) == lax.broadcasted_iota(jnp.int32, (comps, LANES), 1)
    row_sums = jnp.sum(jnp.where(eye, jnp.sum(scores, axis=1, keepdims=True), 0.0), axis=0, keepdims=True)
    chunks = high_ref.shape[1] // (LANES * lax.axis_size("cells"))
    width = chunks * LANES
    for pick, out in zip(picks, outs):
        start = pl.multiple_of((me_ref[0] ^ pick) * width, width)
        lanes = pl.ds(start, width)
        piece = spread_piece(terms, high_ref[:, lanes], low_ref[:, lanes]) * occ_ref[:, lanes]
        sums = sum_ref[:, lanes] * occ_ref[:, lanes]
        extra = [row_sums]
        for at in range(chunks):
            out[at * comps:(at + 1) * comps] = piece[:, at * LANES:(at + 1) * LANES]
            extra.append(sums[:, at * LANES:(at + 1) * LANES])
        extra.append(jnp.zeros((out.shape[0] - chunks * comps - chunks - 1, LANES), F32))
        out[chunks * comps:] = jnp.concatenate(extra, axis=0)


def block_rows(comps, chunks):
    return comps * chunks + -(-(chunks + 1) // 8) * 8


def spread_pieces(me, scores, high, low, sums, occ, picks):
    comps = scores[0].shape[0]
    chunks = high.shape[1] // (LANES * lax.axis_size("cells"))
    block = jax.ShapeDtypeStruct((block_rows(comps, chunks), LANES), F32)
    return pl.pallas_call(
        functools.partial(spread_kernel, len(scores), picks),
        out_shape=[block] * len(picks),
        in_specs=[SCALARS] + [WHOLE] * (len(scores) + 4),
        out_specs=[WHOLE] * len(picks),
        compiler_params=PARAMS,
        cost_estimate=pl.CostEstimate(
            flops=10 * comps * len(picks) * chunks * LANES * high.shape[0], bytes_accessed=2**21, transcendentals=0
        ),
        name="spread",
    )(me, *scores, high, low, sums, occ)


def gram_kernel(scale, chunks, *refs):
    pieces, (spread_ref, gram_ref) = refs[:-2], refs[-2:]
    comps = spread_ref.shape[0]
    total = tree_sum([ref[...] for ref in pieces])
    extra = total[chunks * comps:chunks * comps + chunks + 1]
    eye = lax.broadcasted_iota(jnp.int32, (comps, LANES), 0) == lax.broadcasted_iota(jnp.int32, (comps, LANES), 1)
    row_sums = jnp.sum(jnp.where(eye, extra[:1], 0.0), axis=1, keepdims=True) * scale
    parts = [total[at * comps:(at + 1) * comps] - row_sums * extra[at + 1:at + 2] for at in range(chunks)]
    spread = jnp.concatenate(parts, axis=1)
    spread_ref[...] = spread
    gram_ref[...] = packed_gram(spread)


def packed_gram(spread):
    gram = lax.dot_general(spread, spread, NT, precision=lax.Precision.HIGHEST, preferred_element_type=F32)
    half = spread.shape[0] // 2
    return jnp.concatenate([gram[:half], gram[half:]], axis=1)


def centered_gram(pieces, comps, cell_total):
    chunks = pieces[0].shape[0] // comps
    return pl.pallas_call(
        functools.partial(gram_kernel, 1.0 / cell_total, chunks),
        out_shape=(
            jax.ShapeDtypeStruct((comps, chunks * LANES), F32),
            jax.ShapeDtypeStruct((comps // 2, comps * 2), F32),
        ),
        in_specs=[WHOLE] * len(pieces),
        out_specs=(WHOLE, WHOLE),
        compiler_params=PARAMS,
        name="gram",
    )(*pieces)


def plain_gram_kernel(scale, spread_ref, row_ref, sum_ref, out_ref, gram_ref):
    spread = spread_ref[...] - row_ref[...] * scale * sum_ref[...]
    out_ref[...] = spread
    gram_ref[...] = packed_gram(spread)


def plain_gram(spread, rows, sums, cell_total):
    comps, width = spread.shape
    return pl.pallas_call(
        functools.partial(plain_gram_kernel, 1.0 / cell_total),
        out_shape=(
            jax.ShapeDtypeStruct((comps, width), F32),
            jax.ShapeDtypeStruct((comps // 2, comps * 2), F32),
        ),
        in_specs=[WHOLE] * 3,
        out_specs=(WHOLE, WHOLE),
        compiler_params=PARAMS,
        name="plain_gram",
    )(spread, rows, sums)


def inverse_of(x):
    guess = pl.reciprocal(x, approx=True)
    for _ in range(2):
        guess = guess * (2.0 - x * guess)
    return guess


def row_of(x, at):
    return jnp.broadcast_to(x[at:at + 1, :], x.shape)


def eliminate(groups, edge):
    groups = list(groups)
    below = lax.broadcasted_iota(jnp.int32, groups[0].shape, 0)
    for at in range(len(groups)):
        spread = [
            [jnp.broadcast_to(rows[:, c:c + 1], rows.shape) for c in range(at * edge, (at + 1) * edge)]
            for rows in groups[at:]
        ]
        for i in range(0, edge, 2):
            cols = spread[0]
            first, second = cols[i], cols[i + 1]
            a, b, c = row_of(first, i), row_of(second, i), row_of(second, i + 1)
            inv_a = inverse_of(a)
            inv_c = a * inverse_of(a * c - b * b)
            ratio = b * inv_a
            factors = []
            for k in range(i + 2, edge):
                top = row_of(cols[k], i)
                factors.append((k, top * inv_a, (row_of(cols[k], i + 1) - ratio * top) * inv_c))
            rows = groups[at]
            upper = row_of(rows, i) * inv_a
            rows = rows - jnp.where(below > i, first, 0.0) * upper
            lower = row_of(rows, i + 1) * inv_c
            groups[at] = rows - jnp.where(below > i + 1, second - ratio * first, 0.0) * lower
            for ahead, cols in enumerate(spread):
                first = cols[i]
                second = cols[i + 1] - ratio * first
                for k, on_first, on_second in factors:
                    cols[k] = cols[k] - first * on_first - second * on_second
                if ahead:
                    groups[at + ahead] = groups[at + ahead] - first * upper - second * lower
    return groups


def basis_kernel(scale, *refs):
    grams, (spread_ref, out_ref) = refs[:-2], refs[-2:]
    gram = tree_sum([ref[...] for ref in grams])
    comps = spread_ref.shape[0]
    gram = jnp.concatenate([gram[:, :comps], gram[:, comps:]], axis=0)
    row_at = lax.broadcasted_iota(jnp.int32, (comps, comps), 0)
    col_at = lax.broadcasted_iota(jnp.int32, (comps, comps), 1)
    eye = row_at == col_at
    trace = jnp.sum(jnp.where(eye, gram, 0.0), axis=(0, 1), keepdims=True)
    both = jnp.concatenate([gram * (1.0 / trace), jnp.where(eye, 1.0, 0.0).astype(F32)], axis=1)
    groups = eliminate([both[at:at + 8] for at in range(0, comps, 8)], 8)
    both = jnp.concatenate(groups, axis=0)
    pivots = jnp.sum(jnp.where(eye, both[:, :comps], 0.0), axis=1, keepdims=True)
    inverse = both[:, comps:] * (scale / jnp.sqrt(pivots) / jnp.sqrt(trace))
    out_ref[...] = lax.dot_general(
        inverse, spread_ref[...], NN, precision=lax.Precision.HIGHEST, preferred_element_type=F32
    )


def orthonormal(grams, spread, scale):
    return pl.pallas_call(
        functools.partial(basis_kernel, scale),
        out_shape=jax.ShapeDtypeStruct(spread.shape, F32),
        in_specs=[WHOLE] * (len(grams) + 1),
        out_specs=WHOLE,
        compiler_params=PARAMS,
        name="orthonormal",
    )(*grams, spread)


def send(x, offset_cells, offset_genes):
    cells, genes = lax.axis_size("cells"), lax.axis_size("genes")
    pairs = []
    for c in range(cells):
        for g in range(genes):
            pairs.append((c * genes + g, (c ^ offset_cells) * genes + (g ^ offset_genes)))
    return lax.ppermute(x, ("cells", "genes"), pairs)


def gene_terms(x):
    terms = [x, send(x, 0, 1)]
    for at in range(1, lax.axis_size("genes").bit_length() - 1):
        x = tree_sum(terms)
        terms = [x, send(x, 0, 1 << at | 1)]
    return terms


def cell_terms(x):
    terms = [x]
    for at in range(lax.axis_size("cells").bit_length() - 1):
        x = tree_sum(terms)
        terms = [x, send(x, 1 << at, 1)]
    return terms


def scattered_spread(scores, high, low, sums, occ, cell_total):
    comps = scores[0].shape[0]
    me = lax.axis_index("cells").astype(jnp.int32).reshape(1)
    make = functools.partial(spread_pieces, scores=scores, high=high, low=low, sums=sums, occ=occ)
    blocks = list(make(me, picks=[7, 6, 5]))
    blocks[0], me = lax.optimization_barrier((blocks[0], me))
    came = [send(x, k - 4, 1) for k, x in zip((7, 6, 5), blocks)]
    far, near, own, *blocks = make(me, picks=[4, 2, 0, 3, 1])
    far, near = send(far, 0, 1), send(near, 0, 1)
    near = send(near + send(blocks[0], 1, 1), 2, 1)
    also = send(blocks[1], 1, 0)
    far = send(far + lax.optimization_barrier(tree_sum(came)), 4, 1)
    return centered_gram([own + also + (near + far)], comps, cell_total)


def all_alike(counts, occupancy, start_basis):
    tile_rows, tile_cols = occupancy.shape
    edge = counts.shape[0] // tile_rows
    logged = jnp.log(1.0 + counts.astype(F32)).reshape(tile_rows, edge, tile_cols, -1)
    logged = (logged * occupancy.astype(F32)[:, None, :, None]).reshape(counts.shape)
    high, low = split_terms(logged, 2)
    scores = lax.psum(dot(start_basis, high, NT) + dot(start_basis, low, NT), "genes")
    spread = spread_piece(split_terms(scores, 3), high, low)
    spread = lax.psum_scatter(spread, "cells", scatter_dimension=1, tiled=True)
    rows = lax.psum(jnp.sum(scores, axis=1, keepdims=True), "cells")
    sums = lax.psum_scatter(jnp.sum(logged, axis=0, keepdims=True), "cells", scatter_dimension=1, tiled=True)
    spread, gram = plain_gram(spread, rows, sums, counts.shape[0] * lax.axis_size("cells"))
    return [lax.psum(gram, ("cells", "genes"))], spread


def in_steps(counts, occupancy, start_basis):
    high, low, sums = log_terms(counts)
    scores, occ = score_part(occupancy, start_basis, high, low)
    cell_total = counts.shape[0] * lax.axis_size("cells")
    spread, gram = scattered_spread(gene_terms(scores), high, low, sums, occ, cell_total)
    return cell_terms(tree_sum(gene_terms(gram))), spread


def on_device(counts, occupancy, start_basis):
    gene_count = counts.shape[1]
    cells, genes = lax.axis_size("cells"), lax.axis_size("genes")
    halvings = cells == 1 << 3 and genes == 1 << 2
    tiles = occupancy.shape[0] == 1 and gene_count == occupancy.shape[1] * LANES
    work = in_steps if halvings and tiles and gene_count % (cells * LANES) == 0 else all_alike
    grams, spread = work(counts, occupancy, start_basis)
    return orthonormal(grams, spread, math.sqrt(gene_count * genes))


def solution(mesh):
    in_specs = (P("cells", "genes"), P("cells", "genes"), P(None, "genes"))
    out_specs = P(None, ("genes", "cells"))
    return jax.shard_map(
        on_device, mesh=mesh, in_specs=in_specs, out_specs=out_specs, check_vma=False
    )
```

```python
import functools
import math

import jax
import jax.numpy as jnp
from jax import lax
from jax.experimental import pallas as pl
from jax.experimental.pallas import tpu as pltpu
from jax.sharding import PartitionSpec as P

F32 = jnp.float32
BF16 = jnp.bfloat16
NN = (((1,), (0,)), ((), ()))
NT = (((1,), (1,)), ((), ()))
WHOLE = pl.BlockSpec(memory_space=pltpu.VMEM)
SCALARS = pl.BlockSpec(memory_space=pltpu.SMEM)
LANES = 128
PARAMS = pltpu.CompilerParams(vmem_limit_bytes=16 * 2**20)
LOG_PARAMS = pltpu.CompilerParams(vmem_limit_bytes=205 * 2**18)


def dot(a, b, dims):
    return lax.dot_general(a, b, dims, preferred_element_type=F32)


def split_terms(x, count):
    terms = []
    for _ in range(count):
        term = x.astype(BF16)
        terms.append(term)
        x = x - term.astype(F32)
    return terms


def tree_sum(parts):
    while len(parts) > 1:
        parts = [sum(parts[at + 1:at + 2], parts[at]) for at in range(0, len(parts), 2)]
    return parts[0]


def log_kernel(width, counts_hbm, high_ref, low_ref, sum_ref, counts_ref, counts_sem):
    cells, genes = high_ref.shape
    fetches = [
        pltpu.make_async_copy(
            counts_hbm.at[:, pl.ds(at * width, width)], counts_ref.at[:, pl.ds(at * width, width)], counts_sem.at[at]
        )
        for at in range(genes // width)
    ]
    for fetch in fetches:
        fetch.start()
    for at, fetch in enumerate(fetches):
        fetch.wait()
        for begin in range(at * width, (at + 1) * width, LANES):
            lanes = pl.ds(begin, LANES)
            logged = jnp.log(1.0 + counts_ref[:, lanes].astype(F32))
            high = logged.astype(BF16)
            high_ref[:, lanes] = high
            low_ref[:, lanes] = (logged - high.astype(F32)).astype(BF16)
            sum_ref[:, lanes] = jnp.sum(logged, axis=0, keepdims=True)


def log_terms(counts):
    cells, genes = counts.shape
    width = genes // 8
    return pl.pallas_call(
        functools.partial(log_kernel, width),
        out_shape=(
            jax.ShapeDtypeStruct((cells, genes), BF16),
            jax.ShapeDtypeStruct((cells, genes), BF16),
            jax.ShapeDtypeStruct((1, genes), F32),
        ),
        in_specs=[pl.BlockSpec(memory_space=pltpu.HBM)],
        out_specs=(WHOLE, WHOLE, WHOLE),
        scratch_shapes=[pltpu.VMEM(counts.shape, BF16), pltpu.SemaphoreType.DMA((genes // width,))],
        compiler_params=LOG_PARAMS,
        cost_estimate=pl.CostEstimate(flops=20 * cells * genes, bytes_accessed=8 * cells * genes, transcendentals=0),
        name="log_terms",
    )(counts)


def score_kernel(width, occ_ref, basis_ref, high_ref, low_ref, score_ref, lane_ref):
    comps, genes = basis_ref.shape
    edge = genes // occ_ref.shape[1]
    occupancy = occ_ref[...].astype(F32)
    scores = None
    for begin in range(0, genes, width):
        basis = []
        for at in range(begin, begin + width, edge):
            occ = jnp.broadcast_to(occupancy[:, at // edge:at // edge + 1], (1, edge))
            lane_ref[:, pl.ds(at, edge)] = occ
            basis.append(basis_ref[:, pl.ds(at, edge)] * occ.astype(BF16))
        basis = jnp.concatenate(basis, axis=1)
        lanes = pl.ds(begin, width)
        part = dot(basis, high_ref[:, lanes], NT) + dot(basis, low_ref[:, lanes], NT)
        scores = part if scores is None else scores + part
    score_ref[...] = scores


def score_part(occupancy, basis, high, low):
    comps, genes = basis.shape
    cells = high.shape[0]
    return pl.pallas_call(
        functools.partial(score_kernel, genes // 4),
        out_shape=(jax.ShapeDtypeStruct((comps, cells), F32), jax.ShapeDtypeStruct((1, genes), F32)),
        in_specs=[WHOLE] * 4,
        out_specs=(WHOLE, WHOLE),
        compiler_params=PARAMS,
        name="scores",
    )(occupancy, basis, high, low)


def spread_piece(terms, high, low):
    comps = terms[0].shape[0]
    on_low = dot(jnp.concatenate(terms[:2], axis=0), low, NN)
    on_high = dot(jnp.concatenate(terms, axis=0), high, NN)
    small = on_low[comps:] + on_high[2 * comps:]
    middle = on_low[:comps] + on_high[comps:2 * comps]
    return (small + middle) + on_high[:comps]


def spread_kernel(count, picks, me_ref, *refs):
    score_refs, outs = refs[:count], refs[count + 4:]
    high_ref, low_ref, sum_ref, occ_ref = refs[count:count + 4]
    scores = tree_sum([ref[...] for ref in score_refs])
    comps = scores.shape[0]
    terms = split_terms(scores, 3)
    eye = lax.broadcasted_iota(jnp.int32, (comps, LANES), 0) == lax.broadcasted_iota(jnp.int32, (comps, LANES), 1)
    row_sums = jnp.sum(jnp.where(eye, jnp.sum(scores, axis=1, keepdims=True), 0.0), axis=0, keepdims=True)
    chunks = high_ref.shape[1] // (LANES * lax.axis_size("cells"))
    width = chunks * LANES
    for pick, out in zip(picks, outs):
        start = pl.multiple_of((me_ref[0] ^ pick) * width, width)
        lanes = pl.ds(start, width)
        piece = spread_piece(terms, high_ref[:, lanes], low_ref[:, lanes]) * occ_ref[:, lanes]
        sums = sum_ref[:, lanes] * occ_ref[:, lanes]
        extra = [row_sums]
        for at in range(chunks):
            out[at * comps:(at + 1) * comps] = piece[:, at * LANES:(at + 1) * LANES]
            extra.append(sums[:, at * LANES:(at + 1) * LANES])
        extra.append(jnp.zeros((out.shape[0] - chunks * comps - chunks - 1, LANES), F32))
        out[chunks * comps:] = jnp.concatenate(extra, axis=0)


def block_rows(comps, chunks):
    return comps * chunks + -(-(chunks + 1) // 8) * 8


def spread_pieces(me, scores, high, low, sums, occ, picks):
    comps = scores[0].shape[0]
    chunks = high.shape[1] // (LANES * lax.axis_size("cells"))
    block = jax.ShapeDtypeStruct((block_rows(comps, chunks), LANES), F32)
    return pl.pallas_call(
        functools.partial(spread_kernel, len(scores), picks),
        out_shape=[block] * len(picks),
        in_specs=[SCALARS] + [WHOLE] * (len(scores) + 4),
        out_specs=[WHOLE] * len(picks),
        compiler_params=PARAMS,
        cost_estimate=pl.CostEstimate(
            flops=10 * comps * len(picks) * chunks * LANES * high.shape[0], bytes_accessed=2**21, transcendentals=0
        ),
        name="spread",
    )(me, *scores, high, low, sums, occ)


def gram_kernel(scale, chunks, *refs):
    pieces, (spread_ref, gram_ref) = refs[:-2], refs[-2:]
    comps = spread_ref.shape[0]
    total = tree_sum([ref[...] for ref in pieces])
    extra = total[chunks * comps:chunks * comps + chunks + 1]
    eye = lax.broadcasted_iota(jnp.int32, (comps, LANES), 0) == lax.broadcasted_iota(jnp.int32, (comps, LANES), 1)
    row_sums = jnp.sum(jnp.where(eye, extra[:1], 0.0), axis=1, keepdims=True) * scale
    parts = [total[at * comps:(at + 1) * comps] - row_sums * extra[at + 1:at + 2] for at in range(chunks)]
    spread = jnp.concatenate(parts, axis=1)
    spread_ref[...] = spread
    gram_ref[...] = packed_gram(spread)


def packed_gram(spread):
    gram = lax.dot_general(spread, spread, NT, precision=lax.Precision.HIGHEST, preferred_element_type=F32)
    half = spread.shape[0] // 2
    return jnp.concatenate([gram[:half], gram[half:]], axis=1)


def centered_gram(pieces, comps, cell_total):
    chunks = pieces[0].shape[0] // comps
    return pl.pallas_call(
        functools.partial(gram_kernel, 1.0 / cell_total, chunks),
        out_shape=(
            jax.ShapeDtypeStruct((comps, chunks * LANES), F32),
            jax.ShapeDtypeStruct((comps // 2, comps * 2), F32),
        ),
        in_specs=[WHOLE] * len(pieces),
        out_specs=(WHOLE, WHOLE),
        compiler_params=PARAMS,
        name="gram",
    )(*pieces)


def plain_gram_kernel(scale, spread_ref, row_ref, sum_ref, out_ref, gram_ref):
    spread = spread_ref[...] - row_ref[...] * scale * sum_ref[...]
    out_ref[...] = spread
    gram_ref[...] = packed_gram(spread)


def plain_gram(spread, rows, sums, cell_total):
    comps, width = spread.shape
    return pl.pallas_call(
        functools.partial(plain_gram_kernel, 1.0 / cell_total),
        out_shape=(
            jax.ShapeDtypeStruct((comps, width), F32),
            jax.ShapeDtypeStruct((comps // 2, comps * 2), F32),
        ),
        in_specs=[WHOLE] * 3,
        out_specs=(WHOLE, WHOLE),
        compiler_params=PARAMS,
        name="plain_gram",
    )(spread, rows, sums)


def inverse_of(x):
    guess = pl.reciprocal(x, approx=True)
    for _ in range(2):
        guess = guess * (2.0 - x * guess)
    return guess


def row_of(x, at):
    return jnp.broadcast_to(x[at:at + 1, :], x.shape)


def eliminate(groups, edge):
    groups = list(groups)
    below = lax.broadcasted_iota(jnp.int32, groups[0].shape, 0)
    for at in range(len(groups)):
        spread = [
            [jnp.broadcast_to(rows[:, c:c + 1], rows.shape) for c in range(at * edge, (at + 1) * edge)]
            for rows in groups[at:]
        ]
        for i in range(0, edge, 2):
            cols = spread[0]
            first, second = cols[i], cols[i + 1]
            a, b, c = row_of(first, i), row_of(second, i), row_of(second, i + 1)
            inv_a = inverse_of(a)
            inv_c = a * inverse_of(a * c - b * b)
            ratio = b * inv_a
            factors = []
            for k in range(i + 2, edge):
                top = row_of(cols[k], i)
                factors.append((k, top * inv_a, (row_of(cols[k], i + 1) - ratio * top) * inv_c))
            rows = groups[at]
            upper = row_of(rows, i) * inv_a
            rows = rows - jnp.where(below > i, first, 0.0) * upper
            lower = row_of(rows, i + 1) * inv_c
            groups[at] = rows - jnp.where(below > i + 1, second - ratio * first, 0.0) * lower
            for ahead, cols in enumerate(spread):
                first = cols[i]
                second = cols[i + 1] - ratio * first
                for k, on_first, on_second in factors:
                    cols[k] = cols[k] - first * on_first - second * on_second
                if ahead:
                    groups[at + ahead] = groups[at + ahead] - first * upper - second * lower
    return groups


def basis_kernel(scale, *refs):
    grams, (spread_ref, out_ref) = refs[:-2], refs[-2:]
    gram = tree_sum([ref[...] for ref in grams])
    comps = spread_ref.shape[0]
    gram = jnp.concatenate([gram[:, :comps], gram[:, comps:]], axis=0)
    row_at = lax.broadcasted_iota(jnp.int32, (comps, comps), 0)
    col_at = lax.broadcasted_iota(jnp.int32, (comps, comps), 1)
    eye = row_at == col_at
    trace = jnp.sum(jnp.where(eye, gram, 0.0), axis=(0, 1), keepdims=True)
    both = jnp.concatenate([gram * (1.0 / trace), jnp.where(eye, 1.0, 0.0).astype(F32)], axis=1)
    groups = eliminate([both[at:at + 8] for at in range(0, comps, 8)], 8)
    both = jnp.concatenate(groups, axis=0)
    pivots = jnp.sum(jnp.where(eye, both[:, :comps], 0.0), axis=1, keepdims=True)
    inverse = both[:, comps:] * (scale / jnp.sqrt(pivots) / jnp.sqrt(trace))
    out_ref[...] = lax.dot_general(
        inverse, spread_ref[...], NN, precision=lax.Precision.HIGHEST, preferred_element_type=F32
    )


def orthonormal(grams, spread, scale):
    return pl.pallas_call(
        functools.partial(basis_kernel, scale),
        out_shape=jax.ShapeDtypeStruct(spread.shape, F32),
        in_specs=[WHOLE] * (len(grams) + 1),
        out_specs=WHOLE,
        compiler_params=PARAMS,
        name="orthonormal",
    )(*grams, spread)


def send(x, offset_cells, offset_genes):
    cells, genes = lax.axis_size("cells"), lax.axis_size("genes")
    pairs = []
    for c in range(cells):
        for g in range(genes):
            pairs.append((c * genes + g, (c ^ offset_cells) * genes + (g ^ offset_genes)))
    return lax.ppermute(x, ("cells", "genes"), pairs)


def gene_terms(x):
    terms = [x, send(x, 0, 1)]
    for at in range(1, lax.axis_size("genes").bit_length() - 1):
        x = tree_sum(terms)
        terms = [x, send(x, 0, 1 << at | 1)]
    return terms


def cell_terms(x):
    terms = [x]
    for at in range(lax.axis_size("cells").bit_length() - 1):
        x = tree_sum(terms)
        terms = [x, send(x, 1 << at, 1)]
    return terms


def scattered_spread(scores, high, low, sums, occ, cell_total):
    comps = scores[0].shape[0]
    me = lax.axis_index("cells").astype(jnp.int32).reshape(1)
    make = functools.partial(spread_pieces, scores=scores, high=high, low=low, sums=sums, occ=occ)
    blocks = list(make(me, picks=[7, 6, 5]))
    blocks[0], me = lax.optimization_barrier((blocks[0], me))
    came = [send(x, k - 4, 1) for k, x in zip((7, 6, 5), blocks)]
    far, near, own, *blocks = make(me, picks=[4, 2, 0, 3, 1])
    far, near = send(far, 0, 1), send(near, 0, 1)
    near = send(near + send(blocks[0], 1, 1), 2, 1)
    far = far + lax.optimization_barrier(tree_sum(came))
    far, last = lax.optimization_barrier((far, blocks[1]))
    far, also = send(far, 4, 1), send(last, 1, 0)
    return centered_gram([own + also + (near + far)], comps, cell_total)


def all_alike(counts, occupancy, start_basis):
    tile_rows, tile_cols = occupancy.shape
    edge = counts.shape[0] // tile_rows
    logged = jnp.log(1.0 + counts.astype(F32)).reshape(tile_rows, edge, tile_cols, -1)
    logged = (logged * occupancy.astype(F32)[:, None, :, None]).reshape(counts.shape)
    high, low = split_terms(logged, 2)
    scores = lax.psum(dot(start_basis, high, NT) + dot(start_basis, low, NT), "genes")
    spread = spread_piece(split_terms(scores, 3), high, low)
    spread = lax.psum_scatter(spread, "cells", scatter_dimension=1, tiled=True)
    rows = lax.psum(jnp.sum(scores, axis=1, keepdims=True), "cells")
    sums = lax.psum_scatter(jnp.sum(logged, axis=0, keepdims=True), "cells", scatter_dimension=1, tiled=True)
    spread, gram = plain_gram(spread, rows, sums, counts.shape[0] * lax.axis_size("cells"))
    return [lax.psum(gram, ("cells", "genes"))], spread


def in_steps(counts, occupancy, start_basis):
    high, low, sums = log_terms(counts)
    scores, occ = score_part(occupancy, start_basis, high, low)
    cell_total = counts.shape[0] * lax.axis_size("cells")
    spread, gram = scattered_spread(gene_terms(scores), high, low, sums, occ, cell_total)
    return cell_terms(tree_sum(gene_terms(gram))), spread


def on_device(counts, occupancy, start_basis):
    gene_count = counts.shape[1]
    cells, genes = lax.axis_size("cells"), lax.axis_size("genes")
    halvings = cells == 1 << 3 and genes == 1 << 2
    tiles = occupancy.shape[0] == 1 and gene_count == occupancy.shape[1] * LANES
    work = in_steps if halvings and tiles and gene_count % (cells * LANES) == 0 else all_alike
    grams, spread = work(counts, occupancy, start_basis)
    return orthonormal(grams, spread, math.sqrt(gene_count * genes))


def solution(mesh):
    in_specs = (P("cells", "genes"), P("cells", "genes"), P(None, "genes"))
    out_specs = P(None, ("genes", "cells"))
    return jax.shard_map(
        on_device, mesh=mesh, in_specs=in_specs, out_specs=out_specs, check_vma=False
    )
```

```python
import functools
import math

import jax
import jax.numpy as jnp
from jax import lax
from jax.experimental import pallas as pl
from jax.experimental.pallas import tpu as pltpu
from jax.sharding import PartitionSpec as P

F32 = jnp.float32
BF16 = jnp.bfloat16
NN = (((1,), (0,)), ((), ()))
NT = (((1,), (1,)), ((), ()))
WHOLE = pl.BlockSpec(memory_space=pltpu.VMEM)
SCALARS = pl.BlockSpec(memory_space=pltpu.SMEM)
LANES = 128
PARAMS = pltpu.CompilerParams(vmem_limit_bytes=16 * 2**20)
LOG_PARAMS = pltpu.CompilerParams(vmem_limit_bytes=205 * 2**18)


def dot(a, b, dims):
    return lax.dot_general(a, b, dims, preferred_element_type=F32)


def split_terms(x, count):
    terms = []
    for _ in range(count):
        term = x.astype(BF16)
        terms.append(term)
        x = x - term.astype(F32)
    return terms


def tree_sum(parts):
    while len(parts) > 1:
        parts = [sum(parts[at + 1:at + 2], parts[at]) for at in range(0, len(parts), 2)]
    return parts[0]


def log_kernel(width, counts_hbm, high_ref, low_ref, sum_ref, counts_ref, counts_sem):
    cells, genes = high_ref.shape
    fetches = [
        pltpu.make_async_copy(
            counts_hbm.at[:, pl.ds(at * width, width)], counts_ref.at[:, pl.ds(at * width, width)], counts_sem.at[at]
        )
        for at in range(genes // width)
    ]
    for fetch in fetches:
        fetch.start()
    for at, fetch in enumerate(fetches):
        fetch.wait()
        for begin in range(at * width, (at + 1) * width, LANES):
            lanes = pl.ds(begin, LANES)
            logged = jnp.log(1.0 + counts_ref[:, lanes].astype(F32))
            high = logged.astype(BF16)
            high_ref[:, lanes] = high
            low_ref[:, lanes] = (logged - high.astype(F32)).astype(BF16)
            sum_ref[:, lanes] = jnp.sum(logged, axis=0, keepdims=True)


def log_terms(counts):
    cells, genes = counts.shape
    width = genes // 8
    return pl.pallas_call(
        functools.partial(log_kernel, width),
        out_shape=(
            jax.ShapeDtypeStruct((cells, genes), BF16),
            jax.ShapeDtypeStruct((cells, genes), BF16),
            jax.ShapeDtypeStruct((1, genes), F32),
        ),
        in_specs=[pl.BlockSpec(memory_space=pltpu.HBM)],
        out_specs=(WHOLE, WHOLE, WHOLE),
        scratch_shapes=[pltpu.VMEM(counts.shape, BF16), pltpu.SemaphoreType.DMA((genes // width,))],
        compiler_params=LOG_PARAMS,
        cost_estimate=pl.CostEstimate(flops=20 * cells * genes, bytes_accessed=8 * cells * genes, transcendentals=0),
        name="log_terms",
    )(counts)


def score_kernel(width, occ_ref, basis_ref, high_ref, low_ref, score_ref, lane_ref):
    comps, genes = basis_ref.shape
    edge = genes // occ_ref.shape[1]
    occupancy = occ_ref[...].astype(F32)
    scores = None
    for begin in range(0, genes, width):
        basis = []
        for at in range(begin, begin + width, edge):
            occ = jnp.broadcast_to(occupancy[:, at // edge:at // edge + 1], (1, edge))
            lane_ref[:, pl.ds(at, edge)] = occ
            basis.append(basis_ref[:, pl.ds(at, edge)] * occ.astype(BF16))
        basis = jnp.concatenate(basis, axis=1)
        lanes = pl.ds(begin, width)
        part = dot(basis, high_ref[:, lanes], NT) + dot(basis, low_ref[:, lanes], NT)
        scores = part if scores is None else scores + part
    score_ref[...] = scores


def score_part(occupancy, basis, high, low):
    comps, genes = basis.shape
    cells = high.shape[0]
    return pl.pallas_call(
        functools.partial(score_kernel, genes // 4),
        out_shape=(jax.ShapeDtypeStruct((comps, cells), F32), jax.ShapeDtypeStruct((1, genes), F32)),
        in_specs=[WHOLE] * 4,
        out_specs=(WHOLE, WHOLE),
        compiler_params=PARAMS,
        name="scores",
    )(occupancy, basis, high, low)


def spread_piece(terms, high, low):
    comps = terms[0].shape[0]
    on_low = dot(jnp.concatenate(terms[:2], axis=0), low, NN)
    on_high = dot(jnp.concatenate(terms, axis=0), high, NN)
    small = on_low[comps:] + on_high[2 * comps:]
    middle = on_low[:comps] + on_high[comps:2 * comps]
    return (small + middle) + on_high[:comps]


def spread_kernel(count, picks, me_ref, *refs):
    score_refs, outs = refs[:count], refs[count + 4:]
    high_ref, low_ref, sum_ref, occ_ref = refs[count:count + 4]
    scores = tree_sum([ref[...] for ref in score_refs])
    comps = scores.shape[0]
    terms = split_terms(scores, 3)
    eye = lax.broadcasted_iota(jnp.int32, (comps, LANES), 0) == lax.broadcasted_iota(jnp.int32, (comps, LANES), 1)
    row_sums = jnp.sum(jnp.where(eye, jnp.sum(scores, axis=1, keepdims=True), 0.0), axis=0, keepdims=True)
    chunks = high_ref.shape[1] // (LANES * lax.axis_size("cells"))
    width = chunks * LANES
    blocks = [(pick, out, at) for group, out in zip(picks, outs) for at, pick in enumerate(group)]
    for pick, out, at_block in blocks:
        base = at_block * block_rows(comps, chunks)
        start = pl.multiple_of((me_ref[0] ^ pick) * width, width)
        lanes = pl.ds(start, width)
        piece = spread_piece(terms, high_ref[:, lanes], low_ref[:, lanes]) * occ_ref[:, lanes]
        sums = sum_ref[:, lanes] * occ_ref[:, lanes]
        extra = [row_sums]
        for at in range(chunks):
            out[base + at * comps:base + (at + 1) * comps] = piece[:, at * LANES:(at + 1) * LANES]
            extra.append(sums[:, at * LANES:(at + 1) * LANES])
        extra.append(jnp.zeros((block_rows(comps, chunks) - chunks * comps - chunks - 1, LANES), F32))
        out[base + chunks * comps:base + block_rows(comps, chunks)] = jnp.concatenate(extra, axis=0)


def block_rows(comps, chunks):
    return comps * chunks + -(-(chunks + 1) // 8) * 8


def spread_pieces(me, scores, high, low, sums, occ, picks):
    comps = scores[0].shape[0]
    chunks = high.shape[1] // (LANES * lax.axis_size("cells"))
    rows = block_rows(comps, chunks)
    pairs = sum(len(group) for group in picks)
    return pl.pallas_call(
        functools.partial(spread_kernel, len(scores), picks),
        out_shape=[jax.ShapeDtypeStruct((len(group) * rows, LANES), F32) for group in picks],
        in_specs=[SCALARS] + [WHOLE] * (len(scores) + 4),
        out_specs=[WHOLE] * len(picks),
        compiler_params=PARAMS,
        cost_estimate=pl.CostEstimate(
            flops=10 * comps * pairs * chunks * LANES * high.shape[0], bytes_accessed=2**21, transcendentals=0
        ),
        name="spread",
    )(me, *scores, high, low, sums, occ)


def gram_kernel(scale, chunks, *refs):
    pieces, (spread_ref, gram_ref) = refs[:-2], refs[-2:]
    comps = spread_ref.shape[0]
    total = tree_sum([ref[...] for ref in pieces])
    extra = total[chunks * comps:chunks * comps + chunks + 1]
    eye = lax.broadcasted_iota(jnp.int32, (comps, LANES), 0) == lax.broadcasted_iota(jnp.int32, (comps, LANES), 1)
    row_sums = jnp.sum(jnp.where(eye, extra[:1], 0.0), axis=1, keepdims=True) * scale
    parts = [total[at * comps:(at + 1) * comps] - row_sums * extra[at + 1:at + 2] for at in range(chunks)]
    spread = jnp.concatenate(parts, axis=1)
    spread_ref[...] = spread
    gram_ref[...] = packed_gram(spread)


def packed_gram(spread):
    gram = lax.dot_general(spread, spread, NT, precision=lax.Precision.HIGHEST, preferred_element_type=F32)
    half = spread.shape[0] // 2
    return jnp.concatenate([gram[:half], gram[half:]], axis=1)


def centered_gram(pieces, comps, cell_total):
    chunks = pieces[0].shape[0] // comps
    return pl.pallas_call(
        functools.partial(gram_kernel, 1.0 / cell_total, chunks),
        out_shape=(
            jax.ShapeDtypeStruct((comps, chunks * LANES), F32),
            jax.ShapeDtypeStruct((comps // 2, comps * 2), F32),
        ),
        in_specs=[WHOLE] * len(pieces),
        out_specs=(WHOLE, WHOLE),
        compiler_params=PARAMS,
        name="gram",
    )(*pieces)


def plain_gram_kernel(scale, spread_ref, row_ref, sum_ref, out_ref, gram_ref):
    spread = spread_ref[...] - row_ref[...] * scale * sum_ref[...]
    out_ref[...] = spread
    gram_ref[...] = packed_gram(spread)


def plain_gram(spread, rows, sums, cell_total):
    comps, width = spread.shape
    return pl.pallas_call(
        functools.partial(plain_gram_kernel, 1.0 / cell_total),
        out_shape=(
            jax.ShapeDtypeStruct((comps, width), F32),
            jax.ShapeDtypeStruct((comps // 2, comps * 2), F32),
        ),
        in_specs=[WHOLE] * 3,
        out_specs=(WHOLE, WHOLE),
        compiler_params=PARAMS,
        name="plain_gram",
    )(spread, rows, sums)


def row_of(x, at):
    return jnp.broadcast_to(x[at:at + 1, :], x.shape)


def eliminate(groups, edge):
    groups = list(groups)
    below = lax.broadcasted_iota(jnp.int32, groups[0].shape, 0)
    for at in range(len(groups)):
        spread = [
            [jnp.broadcast_to(rows[:, c:c + 1], rows.shape) for c in range(at * edge, (at + 1) * edge)]
            for rows in groups[at:]
        ]
        for i in range(0, edge, 2):
            cols = spread[0]
            first, second = cols[i], cols[i + 1]
            a, b, c = row_of(first, i), row_of(second, i), row_of(second, i + 1)
            inv_a = pl.reciprocal(a, approx=True)
            inv_c = a * pl.reciprocal(a * c - b * b, approx=True)
            ratio = b * inv_a
            factors = []
            for k in range(i + 2, edge):
                top = row_of(cols[k], i)
                factors.append((k, top * inv_a, (row_of(cols[k], i + 1) - ratio * top) * inv_c))
            rows = groups[at]
            upper = row_of(rows, i) * inv_a
            rows = rows - jnp.where(below > i, first, 0.0) * upper
            lower = row_of(rows, i + 1) * inv_c
            groups[at] = rows - jnp.where(below > i + 1, second - ratio * first, 0.0) * lower
            for ahead, cols in enumerate(spread):
                first = cols[i]
                second = cols[i + 1] - ratio * first
                for k, on_first, on_second in factors:
                    cols[k] = cols[k] - first * on_first - second * on_second
                if ahead:
                    groups[at + ahead] = groups[at + ahead] - first * upper - second * lower
    return groups


def basis_kernel(scale, *refs):
    grams, (spread_ref, out_ref) = refs[:-2], refs[-2:]
    gram = tree_sum([ref[...] for ref in grams])
    comps = spread_ref.shape[0]
    gram = jnp.concatenate([gram[:, :comps], gram[:, comps:]], axis=0)
    row_at = lax.broadcasted_iota(jnp.int32, (comps, comps), 0)
    col_at = lax.broadcasted_iota(jnp.int32, (comps, comps), 1)
    eye = row_at == col_at
    diagonal = jnp.where(eye, gram, 0.0)
    row_scale = lax.rsqrt(jnp.sum(diagonal, axis=1, keepdims=True))
    col_scale = lax.rsqrt(jnp.sum(diagonal, axis=0, keepdims=True))
    both = jnp.concatenate([gram * row_scale * col_scale, jnp.where(eye, col_scale, 0.0)], axis=1)
    groups = eliminate([both[at:at + 8] for at in range(0, comps, 8)], 8)
    both = jnp.concatenate(groups, axis=0)
    pivots = jnp.sum(jnp.where(eye, both[:, :comps], 0.0), axis=1, keepdims=True)
    inverse = both[:, comps:] * (scale * lax.rsqrt(pivots))
    out_ref[...] = lax.dot_general(
        inverse, spread_ref[...], NN, precision=lax.Precision.HIGHEST, preferred_element_type=F32
    )


def orthonormal(grams, spread, scale):
    return pl.pallas_call(
        functools.partial(basis_kernel, scale),
        out_shape=jax.ShapeDtypeStruct(spread.shape, F32),
        in_specs=[WHOLE] * (len(grams) + 1),
        out_specs=WHOLE,
        compiler_params=PARAMS,
        name="orthonormal",
    )(*grams, spread)


def send(x, offset_cells, offset_genes):
    cells, genes = lax.axis_size("cells"), lax.axis_size("genes")
    pairs = []
    for c in range(cells):
        for g in range(genes):
            pairs.append((c * genes + g, (c ^ offset_cells) * genes + (g ^ offset_genes)))
    return lax.ppermute(x, ("cells", "genes"), pairs)


def gene_terms(x):
    terms = [x, send(x, 0, 1)]
    for at in range(1, lax.axis_size("genes").bit_length() - 1):
        x = tree_sum(terms)
        terms = [x, send(x, 0, 1 << at | 1)]
    return terms


def cell_terms(x):
    terms = [x]
    for at in range(lax.axis_size("cells").bit_length() - 1):
        x = tree_sum(terms)
        terms = [x, send(x, 1 << at, 1)]
    return terms


def scattered_spread(scores, high, low, sums, occ, cell_total):
    comps = scores[0].shape[0]
    me = lax.axis_index("cells").astype(jnp.int32).reshape(1)
    make = functools.partial(spread_pieces, scores=scores, high=high, low=low, sums=sums, occ=occ)
    blocks = list(make(me, picks=[[7], [6], [5]]))
    blocks[0], me = lax.optimization_barrier((blocks[0], me))
    came = [send(x, k - 4, 1) for k, x in zip((7, 6, 5), blocks)]
    stay, own, *blocks = make(me, picks=[[4, 2], [0], [3], [1]])
    stay = send(stay, 0, 1)
    far, near = stay[:own.shape[0]], stay[own.shape[0]:]
    near = send(near + send(blocks[0], 1, 1), 2, 1)
    far = far + lax.optimization_barrier(tree_sum(came))
    far, last = lax.optimization_barrier((far, blocks[1]))
    far, also = send(far, 4, 1), send(last, 1, 0)
    return centered_gram([own + also + (near + far)], comps, cell_total)


def all_alike(counts, occupancy, start_basis):
    tile_rows, tile_cols = occupancy.shape
    edge = counts.shape[0] // tile_rows
    logged = jnp.log(1.0 + counts.astype(F32)).reshape(tile_rows, edge, tile_cols, -1)
    logged = (logged * occupancy.astype(F32)[:, None, :, None]).reshape(counts.shape)
    high, low = split_terms(logged, 2)
    scores = lax.psum(dot(start_basis, high, NT) + dot(start_basis, low, NT), "genes")
    spread = spread_piece(split_terms(scores, 3), high, low)
    spread = lax.psum_scatter(spread, "cells", scatter_dimension=1, tiled=True)
    rows = lax.psum(jnp.sum(scores, axis=1, keepdims=True), "cells")
    sums = lax.psum_scatter(jnp.sum(logged, axis=0, keepdims=True), "cells", scatter_dimension=1, tiled=True)
    spread, gram = plain_gram(spread, rows, sums, counts.shape[0] * lax.axis_size("cells"))
    return [lax.psum(gram, ("cells", "genes"))], spread


def in_steps(counts, occupancy, start_basis):
    high, low, sums = log_terms(counts)
    scores, occ = score_part(occupancy, start_basis, high, low)
    cell_total = counts.shape[0] * lax.axis_size("cells")
    spread, gram = scattered_spread(gene_terms(scores), high, low, sums, occ, cell_total)
    return cell_terms(tree_sum(gene_terms(gram))), spread


def on_device(counts, occupancy, start_basis):
    gene_count = counts.shape[1]
    cells, genes = lax.axis_size("cells"), lax.axis_size("genes")
    halvings = cells == 1 << 3 and genes == 1 << 2
    tiles = occupancy.shape[0] == 1 and gene_count == occupancy.shape[1] * LANES
    work = in_steps if halvings and tiles and gene_count % (cells * LANES) == 0 else all_alike
    grams, spread = work(counts, occupancy, start_basis)
    return orthonormal(grams, spread, math.sqrt(gene_count * genes))


def solution(mesh):
    in_specs = (P("cells", "genes"), P("cells", "genes"), P(None, "genes"))
    out_specs = P(None, ("genes", "cells"))
    return jax.shard_map(
        on_device, mesh=mesh, in_specs=in_specs, out_specs=out_specs, check_vma=False
    )
```

```python
import functools
import math

import jax
import jax.numpy as jnp
from jax import lax
from jax.experimental import pallas as pl
from jax.experimental.pallas import tpu as pltpu
from jax.sharding import PartitionSpec as P

F32 = jnp.float32
BF16 = jnp.bfloat16
NN = (((1,), (0,)), ((), ()))
NT = (((1,), (1,)), ((), ()))
WHOLE = pl.BlockSpec(memory_space=pltpu.VMEM)
SCALARS = pl.BlockSpec(memory_space=pltpu.SMEM)
LANES = 128
PARAMS = pltpu.CompilerParams(vmem_limit_bytes=16 * 2**20)
LOG_PARAMS = pltpu.CompilerParams(vmem_limit_bytes=205 * 2**18)


def dot(a, b, dims):
    return lax.dot_general(a, b, dims, preferred_element_type=F32)


def split_terms(x, count):
    terms = []
    for _ in range(count):
        term = x.astype(BF16)
        terms.append(term)
        x = x - term.astype(F32)
    return terms


def tree_sum(parts):
    while len(parts) > 1:
        parts = [sum(parts[at + 1:at + 2], parts[at]) for at in range(0, len(parts), 2)]
    return parts[0]


def log_kernel(width, counts_hbm, high_ref, low_ref, sum_ref, counts_ref, counts_sem):
    cells, genes = high_ref.shape
    fetches = [
        pltpu.make_async_copy(
            counts_hbm.at[:, pl.ds(at * width, width)], counts_ref.at[:, pl.ds(at * width, width)], counts_sem.at[at]
        )
        for at in range(genes // width)
    ]
    for fetch in fetches:
        fetch.start()
    for at, fetch in enumerate(fetches):
        fetch.wait()
        for begin in range(at * width, (at + 1) * width, LANES):
            lanes = pl.ds(begin, LANES)
            logged = jnp.log(1.0 + counts_ref[:, lanes].astype(F32))
            high = logged.astype(BF16)
            high_ref[:, lanes] = high
            low_ref[:, lanes] = (logged - high.astype(F32)).astype(BF16)
            sum_ref[:, lanes] = jnp.sum(logged, axis=0, keepdims=True)


def log_terms(counts):
    cells, genes = counts.shape
    width = genes // 8
    return pl.pallas_call(
        functools.partial(log_kernel, width),
        out_shape=(
            jax.ShapeDtypeStruct((cells, genes), BF16),
            jax.ShapeDtypeStruct((cells, genes), BF16),
            jax.ShapeDtypeStruct((1, genes), F32),
        ),
        in_specs=[pl.BlockSpec(memory_space=pltpu.HBM)],
        out_specs=(WHOLE, WHOLE, WHOLE),
        scratch_shapes=[pltpu.VMEM(counts.shape, BF16), pltpu.SemaphoreType.DMA((genes // width,))],
        compiler_params=LOG_PARAMS,
        cost_estimate=pl.CostEstimate(flops=20 * cells * genes, bytes_accessed=8 * cells * genes, transcendentals=0),
        name="log_terms",
    )(counts)


def score_kernel(width, occ_ref, basis_ref, high_ref, low_ref, score_ref, lane_ref):
    comps, genes = basis_ref.shape
    edge = genes // occ_ref.shape[1]
    occupancy = occ_ref[...].astype(F32)
    scores = None
    for begin in range(0, genes, width):
        basis = []
        for at in range(begin, begin + width, edge):
            occ = jnp.broadcast_to(occupancy[:, at // edge:at // edge + 1], (1, edge))
            lane_ref[:, pl.ds(at, edge)] = occ
            basis.append(basis_ref[:, pl.ds(at, edge)] * occ.astype(BF16))
        basis = jnp.concatenate(basis, axis=1)
        lanes = pl.ds(begin, width)
        part = dot(basis, high_ref[:, lanes], NT) + dot(basis, low_ref[:, lanes], NT)
        scores = part if scores is None else scores + part
    score_ref[...] = scores


def score_part(occupancy, basis, high, low):
    comps, genes = basis.shape
    cells = high.shape[0]
    return pl.pallas_call(
        functools.partial(score_kernel, genes // 4),
        out_shape=(jax.ShapeDtypeStruct((comps, cells), F32), jax.ShapeDtypeStruct((1, genes), F32)),
        in_specs=[WHOLE] * 4,
        out_specs=(WHOLE, WHOLE),
        compiler_params=PARAMS,
        name="scores",
    )(occupancy, basis, high, low)


def spread_piece(terms, high, low):
    comps = terms[0].shape[0]
    on_low = dot(jnp.concatenate(terms[:2], axis=0), low, NN)
    on_high = dot(jnp.concatenate(terms, axis=0), high, NN)
    small = on_low[comps:] + on_high[2 * comps:]
    middle = on_low[:comps] + on_high[comps:2 * comps]
    return (small + middle) + on_high[:comps]


def spread_kernel(count, picks, me_ref, *refs):
    score_refs, outs = refs[:count], refs[count + 4:]
    high_ref, low_ref, sum_ref, occ_ref = refs[count:count + 4]
    scores = tree_sum([ref[...] for ref in score_refs])
    comps = scores.shape[0]
    terms = split_terms(scores, 3)
    eye = lax.broadcasted_iota(jnp.int32, (comps, LANES), 0) == lax.broadcasted_iota(jnp.int32, (comps, LANES), 1)
    row_sums = jnp.sum(jnp.where(eye, jnp.sum(scores, axis=1, keepdims=True), 0.0), axis=0, keepdims=True)
    chunks = high_ref.shape[1] // (LANES * lax.axis_size("cells"))
    width = chunks * LANES
    blocks = [(pick, out, at) for group, out in zip(picks, outs) for at, pick in enumerate(group)]
    for pick, out, at_block in blocks:
        base = at_block * block_rows(comps, chunks)
        start = pl.multiple_of((me_ref[0] ^ pick) * width, width)
        lanes = pl.ds(start, width)
        piece = spread_piece(terms, high_ref[:, lanes], low_ref[:, lanes]) * occ_ref[:, lanes]
        sums = sum_ref[:, lanes] * occ_ref[:, lanes]
        extra = [row_sums]
        for at in range(chunks):
            out[base + at * comps:base + (at + 1) * comps] = piece[:, at * LANES:(at + 1) * LANES]
            extra.append(sums[:, at * LANES:(at + 1) * LANES])
        extra.append(jnp.zeros((block_rows(comps, chunks) - chunks * comps - chunks - 1, LANES), F32))
        out[base + chunks * comps:base + block_rows(comps, chunks)] = jnp.concatenate(extra, axis=0)


def block_rows(comps, chunks):
    return comps * chunks + -(-(chunks + 1) // 8) * 8


def spread_pieces(me, scores, high, low, sums, occ, picks):
    comps = scores[0].shape[0]
    chunks = high.shape[1] // (LANES * lax.axis_size("cells"))
    rows = block_rows(comps, chunks)
    pairs = sum(len(group) for group in picks)
    return pl.pallas_call(
        functools.partial(spread_kernel, len(scores), picks),
        out_shape=[jax.ShapeDtypeStruct((len(group) * rows, LANES), F32) for group in picks],
        in_specs=[SCALARS] + [WHOLE] * (len(scores) + 4),
        out_specs=[WHOLE] * len(picks),
        compiler_params=PARAMS,
        cost_estimate=pl.CostEstimate(
            flops=10 * comps * pairs * chunks * LANES * high.shape[0], bytes_accessed=2**21, transcendentals=0
        ),
        name="spread",
    )(me, *scores, high, low, sums, occ)


def gram_kernel(scale, chunks, *refs):
    pieces, (spread_ref, gram_ref) = refs[:-2], refs[-2:]
    comps = spread_ref.shape[0]
    total = tree_sum([ref[...] for ref in pieces])
    extra = total[chunks * comps:chunks * comps + chunks + 1]
    eye = lax.broadcasted_iota(jnp.int32, (comps, LANES), 0) == lax.broadcasted_iota(jnp.int32, (comps, LANES), 1)
    row_sums = jnp.sum(jnp.where(eye, extra[:1], 0.0), axis=1, keepdims=True) * scale
    parts = [total[at * comps:(at + 1) * comps] - row_sums * extra[at + 1:at + 2] for at in range(chunks)]
    spread = jnp.concatenate(parts, axis=1)
    spread_ref[...] = spread
    gram_ref[...] = packed_gram(spread)


def packed_gram(spread):
    gram = lax.dot_general(spread, spread, NT, precision=lax.Precision.HIGHEST, preferred_element_type=F32)
    half = spread.shape[0] // 2
    return jnp.concatenate([gram[:half], gram[half:]], axis=1)


def centered_gram(pieces, comps, cell_total):
    chunks = pieces[0].shape[0] // comps
    return pl.pallas_call(
        functools.partial(gram_kernel, 1.0 / cell_total, chunks),
        out_shape=(
            jax.ShapeDtypeStruct((comps, chunks * LANES), F32),
            jax.ShapeDtypeStruct((comps // 2, comps * 2), F32),
        ),
        in_specs=[WHOLE] * len(pieces),
        out_specs=(WHOLE, WHOLE),
        compiler_params=PARAMS,
        name="gram",
    )(*pieces)


def plain_gram_kernel(scale, spread_ref, row_ref, sum_ref, out_ref, gram_ref):
    spread = spread_ref[...] - row_ref[...] * scale * sum_ref[...]
    out_ref[...] = spread
    gram_ref[...] = packed_gram(spread)


def plain_gram(spread, rows, sums, cell_total):
    comps, width = spread.shape
    return pl.pallas_call(
        functools.partial(plain_gram_kernel, 1.0 / cell_total),
        out_shape=(
            jax.ShapeDtypeStruct((comps, width), F32),
            jax.ShapeDtypeStruct((comps // 2, comps * 2), F32),
        ),
        in_specs=[WHOLE] * 3,
        out_specs=(WHOLE, WHOLE),
        compiler_params=PARAMS,
        name="plain_gram",
    )(spread, rows, sums)


def row_of(x, at):
    return jnp.broadcast_to(x[at:at + 1, :], x.shape)


def eliminate(groups, edge):
    groups = list(groups)
    below = lax.broadcasted_iota(jnp.int32, groups[0].shape, 0)
    for at in range(len(groups)):
        spread = [
            [jnp.broadcast_to(rows[:, c:c + 1], rows.shape) for c in range(at * edge, (at + 1) * edge)]
            for rows in groups[at:]
        ]
        for i in range(0, edge, 2):
            cols = spread[0]
            first, second = cols[i], cols[i + 1]
            a, b, c = row_of(first, i), row_of(second, i), row_of(second, i + 1)
            inv_a = pl.reciprocal(a, approx=True)
            inv_c = a * pl.reciprocal(a * c - b * b, approx=True)
            ratio = b * inv_a
            factors = []
            for k in range(i + 2, edge):
                top = row_of(cols[k], i)
                factors.append((k, top * inv_a, (row_of(cols[k], i + 1) - ratio * top) * inv_c))
            rows = groups[at]
            upper = row_of(rows, i) * inv_a
            rows = rows - jnp.where(below > i, first, 0.0) * upper
            lower = row_of(rows, i + 1) * inv_c
            groups[at] = rows - jnp.where(below > i + 1, second - ratio * first, 0.0) * lower
            for ahead, cols in enumerate(spread):
                first = cols[i]
                second = cols[i + 1] - ratio * first
                for k, on_first, on_second in factors:
                    cols[k] = cols[k] - first * on_first - second * on_second
                if ahead:
                    groups[at + ahead] = groups[at + ahead] - first * upper - second * lower
    return groups


def basis_kernel(scale, *refs):
    grams, (spread_ref, out_ref) = refs[:-2], refs[-2:]
    gram = tree_sum([ref[...] for ref in grams])
    comps = spread_ref.shape[0]
    gram = jnp.concatenate([gram[:, :comps], gram[:, comps:]], axis=0)
    row_at = lax.broadcasted_iota(jnp.int32, (comps, comps), 0)
    col_at = lax.broadcasted_iota(jnp.int32, (comps, comps), 1)
    eye = row_at == col_at
    diagonal = jnp.where(eye, gram, 0.0)
    row_scale = lax.rsqrt(jnp.sum(diagonal, axis=1, keepdims=True))
    col_scale = lax.rsqrt(jnp.sum(diagonal, axis=0, keepdims=True))
    both = jnp.concatenate([gram * row_scale * col_scale, jnp.where(eye, col_scale, 0.0)], axis=1)
    groups = eliminate([both[at:at + 8] for at in range(0, comps, 8)], 8)
    both = jnp.concatenate(groups, axis=0)
    pivots = jnp.sum(jnp.where(eye, both[:, :comps], 0.0), axis=1, keepdims=True)
    inverse = both[:, comps:] * (scale * lax.rsqrt(pivots))
    out_ref[...] = lax.dot_general(
        inverse, spread_ref[...], NN, precision=lax.Precision.HIGHEST, preferred_element_type=F32
    )


def orthonormal(grams, spread, scale):
    return pl.pallas_call(
        functools.partial(basis_kernel, scale),
        out_shape=jax.ShapeDtypeStruct(spread.shape, F32),
        in_specs=[WHOLE] * (len(grams) + 1),
        out_specs=WHOLE,
        compiler_params=PARAMS,
        name="orthonormal",
    )(*grams, spread)


def send(x, offset_cells, offset_genes):
    cells, genes = lax.axis_size("cells"), lax.axis_size("genes")
    pairs = []
    for c in range(cells):
        for g in range(genes):
            pairs.append((c * genes + g, (c ^ offset_cells) * genes + (g ^ offset_genes)))
    return lax.ppermute(x, ("cells", "genes"), pairs)


def gene_terms(x):
    terms = [x, send(x, 0, 1)]
    for at in range(1, lax.axis_size("genes").bit_length() - 1):
        x = tree_sum(terms)
        terms = [x, send(x, 0, 1 << at | 1)]
    return terms


def cell_terms(x):
    terms = [x]
    for at in range(lax.axis_size("cells").bit_length() - 1):
        x = tree_sum(terms)
        terms = [x, send(x, 1 << at, 1)]
    return terms


def scattered_spread(scores, high, low, sums, occ, cell_total):
    comps = scores[0].shape[0]
    me = lax.axis_index("cells").astype(jnp.int32).reshape(1)
    make = functools.partial(spread_pieces, scores=scores, high=high, low=low, sums=sums, occ=occ)
    blocks = list(make(me, picks=[[7], [6], [5]]))
    blocks[0], me = lax.optimization_barrier((blocks[0], me))
    came = [send(x, k - 4, 1) for k, x in zip((7, 6, 5), blocks)]
    stay, own, *blocks = make(me, picks=[[4, 2], [0], [3], [1]])
    stay = send(stay, 0, 1)
    far, near = lax.optimization_barrier((stay[:own.shape[0]], stay[own.shape[0]:]))
    near = near + send(blocks[0], 1, 1)
    far = far + lax.optimization_barrier(tree_sum(came))
    near, last = lax.optimization_barrier((near, blocks[1]))
    far, near, also = send(far, 4, 1), send(near, 2, 1), send(last, 1, 0)
    return centered_gram([own + also + (near + far)], comps, cell_total)


def all_alike(counts, occupancy, start_basis):
    tile_rows, tile_cols = occupancy.shape
    edge = counts.shape[0] // tile_rows
    logged = jnp.log(1.0 + counts.astype(F32)).reshape(tile_rows, edge, tile_cols, -1)
    logged = (logged * occupancy.astype(F32)[:, None, :, None]).reshape(counts.shape)
    high, low = split_terms(logged, 2)
    scores = lax.psum(dot(start_basis, high, NT) + dot(start_basis, low, NT), "genes")
    spread = spread_piece(split_terms(scores, 3), high, low)
    spread = lax.psum_scatter(spread, "cells", scatter_dimension=1, tiled=True)
    rows = lax.psum(jnp.sum(scores, axis=1, keepdims=True), "cells")
    sums = lax.psum_scatter(jnp.sum(logged, axis=0, keepdims=True), "cells", scatter_dimension=1, tiled=True)
    spread, gram = plain_gram(spread, rows, sums, counts.shape[0] * lax.axis_size("cells"))
    return [lax.psum(gram, ("cells", "genes"))], spread


def in_steps(counts, occupancy, start_basis):
    high, low, sums = log_terms(counts)
    scores, occ = score_part(occupancy, start_basis, high, low)
    cell_total = counts.shape[0] * lax.axis_size("cells")
    spread, gram = scattered_spread(gene_terms(scores), high, low, sums, occ, cell_total)
    return cell_terms(tree_sum(gene_terms(gram))), spread


def on_device(counts, occupancy, start_basis):
    gene_count = counts.shape[1]
    cells, genes = lax.axis_size("cells"), lax.axis_size("genes")
    halvings = cells == 1 << 3 and genes == 1 << 2
    tiles = occupancy.shape[0] == 1 and gene_count == occupancy.shape[1] * LANES
    work = in_steps if halvings and tiles and gene_count % (cells * LANES) == 0 else all_alike
    grams, spread = work(counts, occupancy, start_basis)
    return orthonormal(grams, spread, math.sqrt(gene_count * genes))


def solution(mesh):
    in_specs = (P("cells", "genes"), P("cells", "genes"), P(None, "genes"))
    out_specs = P(None, ("genes", "cells"))
    return jax.shard_map(
        on_device, mesh=mesh, in_specs=in_specs, out_specs=out_specs, check_vma=False
    )
```

```python
import functools
import math

import jax
import jax.numpy as jnp
from jax import lax
from jax.experimental import pallas as pl
from jax.experimental.pallas import tpu as pltpu
from jax.sharding import PartitionSpec as P

F32 = jnp.float32
BF16 = jnp.bfloat16
NN = (((1,), (0,)), ((), ()))
NT = (((1,), (1,)), ((), ()))
WHOLE = pl.BlockSpec(memory_space=pltpu.VMEM)
SCALARS = pl.BlockSpec(memory_space=pltpu.SMEM)
LANES = 128
PARAMS = pltpu.CompilerParams(vmem_limit_bytes=16 * 2**20)
LOG_PARAMS = pltpu.CompilerParams(vmem_limit_bytes=205 * 2**18)


def dot(a, b, dims):
    return lax.dot_general(a, b, dims, preferred_element_type=F32)


def split_terms(x, count):
    terms = []
    for _ in range(count):
        term = x.astype(BF16)
        terms.append(term)
        x = x - term.astype(F32)
    return terms


def tree_sum(parts):
    while len(parts) > 1:
        parts = [sum(parts[at + 1:at + 2], parts[at]) for at in range(0, len(parts), 2)]
    return parts[0]


def log_kernel(width, counts_hbm, high_ref, low_ref, sum_ref, counts_ref, counts_sem):
    cells, genes = high_ref.shape
    fetches = [
        pltpu.make_async_copy(
            counts_hbm.at[:, pl.ds(at * width, width)], counts_ref.at[:, pl.ds(at * width, width)], counts_sem.at[at]
        )
        for at in range(genes // width)
    ]
    for fetch in fetches:
        fetch.start()
    for at, fetch in enumerate(fetches):
        fetch.wait()
        for begin in range(at * width, (at + 1) * width, LANES):
            lanes = pl.ds(begin, LANES)
            logged = jnp.log(1.0 + counts_ref[:, lanes].astype(F32))
            high = logged.astype(BF16)
            high_ref[:, lanes] = high
            low_ref[:, lanes] = (logged - high.astype(F32)).astype(BF16)
            sum_ref[:, lanes] = jnp.sum(logged, axis=0, keepdims=True)


def log_terms(counts):
    cells, genes = counts.shape
    width = genes // 8
    return pl.pallas_call(
        functools.partial(log_kernel, width),
        out_shape=(
            jax.ShapeDtypeStruct((cells, genes), BF16),
            jax.ShapeDtypeStruct((cells, genes), BF16),
            jax.ShapeDtypeStruct((1, genes), F32),
        ),
        in_specs=[pl.BlockSpec(memory_space=pltpu.HBM)],
        out_specs=(WHOLE, WHOLE, WHOLE),
        scratch_shapes=[pltpu.VMEM(counts.shape, BF16), pltpu.SemaphoreType.DMA((genes // width,))],
        compiler_params=LOG_PARAMS,
        cost_estimate=pl.CostEstimate(flops=20 * cells * genes, bytes_accessed=8 * cells * genes, transcendentals=0),
        name="log_terms",
    )(counts)


def score_kernel(width, occ_ref, basis_ref, high_ref, low_ref, score_ref, lane_ref):
    comps, genes = basis_ref.shape
    edge = genes // occ_ref.shape[1]
    occupancy = occ_ref[...].astype(F32)
    scores = None
    for begin in range(0, genes, width):
        basis = []
        for at in range(begin, begin + width, edge):
            occ = jnp.broadcast_to(occupancy[:, at // edge:at // edge + 1], (1, edge))
            lane_ref[:, pl.ds(at, edge)] = occ
            basis.append(basis_ref[:, pl.ds(at, edge)] * occ.astype(BF16))
        basis = jnp.concatenate(basis, axis=1)
        lanes = pl.ds(begin, width)
        part = dot(basis, high_ref[:, lanes], NT) + dot(basis, low_ref[:, lanes], NT)
        scores = part if scores is None else scores + part
    score_ref[...] = scores


def score_part(occupancy, basis, high, low):
    comps, genes = basis.shape
    cells = high.shape[0]
    return pl.pallas_call(
        functools.partial(score_kernel, genes // 4),
        out_shape=(jax.ShapeDtypeStruct((comps, cells), F32), jax.ShapeDtypeStruct((1, genes), F32)),
        in_specs=[WHOLE] * 4,
        out_specs=(WHOLE, WHOLE),
        compiler_params=PARAMS,
        name="scores",
    )(occupancy, basis, high, low)


def spread_piece(terms, high, low):
    comps = terms[0].shape[0]
    on_low = dot(jnp.concatenate(terms[:2], axis=0), low, NN)
    on_high = dot(jnp.concatenate(terms, axis=0), high, NN)
    small = on_low[comps:] + on_high[2 * comps:]
    middle = on_low[:comps] + on_high[comps:2 * comps]
    return (small + middle) + on_high[:comps]


def spread_kernel(count, picks, me_ref, *refs):
    score_refs, outs = refs[:count], refs[count + 4:]
    high_ref, low_ref, sum_ref, occ_ref = refs[count:count + 4]
    scores = tree_sum([ref[...] for ref in score_refs])
    comps = scores.shape[0]
    terms = split_terms(scores, 3)
    eye = lax.broadcasted_iota(jnp.int32, (comps, LANES), 0) == lax.broadcasted_iota(jnp.int32, (comps, LANES), 1)
    row_sums = jnp.sum(jnp.where(eye, jnp.sum(scores, axis=1, keepdims=True), 0.0), axis=0, keepdims=True)
    chunks = high_ref.shape[1] // (LANES * lax.axis_size("cells"))
    width = chunks * LANES
    for pick, out in zip(picks, outs):
        start = pl.multiple_of((me_ref[0] ^ pick) * width, width)
        lanes = pl.ds(start, width)
        piece = spread_piece(terms, high_ref[:, lanes], low_ref[:, lanes]) * occ_ref[:, lanes]
        sums = sum_ref[:, lanes] * occ_ref[:, lanes]
        extra = [row_sums]
        for at in range(chunks):
            out[at * comps:(at + 1) * comps] = piece[:, at * LANES:(at + 1) * LANES]
            extra.append(sums[:, at * LANES:(at + 1) * LANES])
        extra.append(jnp.zeros((out.shape[0] - chunks * comps - chunks - 1, LANES), F32))
        out[chunks * comps:] = jnp.concatenate(extra, axis=0)


def block_rows(comps, chunks):
    return comps * chunks + -(-(chunks + 1) // 8) * 8


def spread_pieces(me, scores, high, low, sums, occ, picks):
    comps = scores[0].shape[0]
    chunks = high.shape[1] // (LANES * lax.axis_size("cells"))
    block = jax.ShapeDtypeStruct((block_rows(comps, chunks), LANES), F32)
    return pl.pallas_call(
        functools.partial(spread_kernel, len(scores), picks),
        out_shape=[block] * len(picks),
        in_specs=[SCALARS] + [WHOLE] * (len(scores) + 4),
        out_specs=[WHOLE] * len(picks),
        compiler_params=PARAMS,
        cost_estimate=pl.CostEstimate(
            flops=10 * comps * len(picks) * chunks * LANES * high.shape[0], bytes_accessed=2**21, transcendentals=0
        ),
        name="spread",
    )(me, *scores, high, low, sums, occ)


def gram_kernel(scale, chunks, *refs):
    pieces, (spread_ref, gram_ref) = refs[:-2], refs[-2:]
    comps = spread_ref.shape[0]
    total = tree_sum([ref[...] for ref in pieces])
    extra = total[chunks * comps:chunks * comps + chunks + 1]
    eye = lax.broadcasted_iota(jnp.int32, (comps, LANES), 0) == lax.broadcasted_iota(jnp.int32, (comps, LANES), 1)
    row_sums = jnp.sum(jnp.where(eye, extra[:1], 0.0), axis=1, keepdims=True) * scale
    parts = [total[at * comps:(at + 1) * comps] - row_sums * extra[at + 1:at + 2] for at in range(chunks)]
    spread = jnp.concatenate(parts, axis=1)
    spread_ref[...] = spread
    gram_ref[...] = packed_gram(spread)


def packed_gram(spread):
    gram = lax.dot_general(spread, spread, NT, precision=lax.Precision.HIGHEST, preferred_element_type=F32)
    half = spread.shape[0] // 2
    return jnp.concatenate([gram[:half], gram[half:]], axis=1)


def centered_gram(pieces, comps, cell_total):
    chunks = pieces[0].shape[0] // comps
    return pl.pallas_call(
        functools.partial(gram_kernel, 1.0 / cell_total, chunks),
        out_shape=(
            jax.ShapeDtypeStruct((comps, chunks * LANES), F32),
            jax.ShapeDtypeStruct((comps // 2, comps * 2), F32),
        ),
        in_specs=[WHOLE] * len(pieces),
        out_specs=(WHOLE, WHOLE),
        compiler_params=PARAMS,
        name="gram",
    )(*pieces)


def plain_gram_kernel(scale, spread_ref, row_ref, sum_ref, out_ref, gram_ref):
    spread = spread_ref[...] - row_ref[...] * scale * sum_ref[...]
    out_ref[...] = spread
    gram_ref[...] = packed_gram(spread)


def plain_gram(spread, rows, sums, cell_total):
    comps, width = spread.shape
    return pl.pallas_call(
        functools.partial(plain_gram_kernel, 1.0 / cell_total),
        out_shape=(
            jax.ShapeDtypeStruct((comps, width), F32),
            jax.ShapeDtypeStruct((comps // 2, comps * 2), F32),
        ),
        in_specs=[WHOLE] * 3,
        out_specs=(WHOLE, WHOLE),
        compiler_params=PARAMS,
        name="plain_gram",
    )(spread, rows, sums)


def row_of(x, at):
    return jnp.broadcast_to(x[at:at + 1, :], x.shape)


def eliminate(groups, edge):
    groups = list(groups)
    below = lax.broadcasted_iota(jnp.int32, groups[0].shape, 0)
    for at in range(len(groups)):
        spread = [
            [jnp.broadcast_to(rows[:, c:c + 1], rows.shape) for c in range(at * edge, (at + 1) * edge)]
            for rows in groups[at:]
        ]
        for i in range(0, edge, 2):
            cols = spread[0]
            first, second = cols[i], cols[i + 1]
            a, b, c = row_of(first, i), row_of(second, i), row_of(second, i + 1)
            inv_a = pl.reciprocal(a, approx=True)
            inv_c = a * pl.reciprocal(a * c - b * b, approx=True)
            ratio = b * inv_a
            factors = []
            for k in range(i + 2, edge):
                top = row_of(cols[k], i)
                factors.append((k, top * inv_a, (row_of(cols[k], i + 1) - ratio * top) * inv_c))
            rows = groups[at]
            upper = row_of(rows, i) * inv_a
            rows = rows - jnp.where(below > i, first, 0.0) * upper
            lower = row_of(rows, i + 1) * inv_c
            groups[at] = rows - jnp.where(below > i + 1, second - ratio * first, 0.0) * lower
            for ahead, cols in enumerate(spread):
                first = cols[i]
                second = cols[i + 1] - ratio * first
                for k, on_first, on_second in factors:
                    cols[k] = cols[k] - first * on_first - second * on_second
                if ahead:
                    groups[at + ahead] = groups[at + ahead] - first * upper - second * lower
    return groups


def basis_kernel(scale, gram_ref, spread_ref, out_ref):
    gram = tree_sum([gram_ref[at] for at in range(gram_ref.shape[0])])
    comps = spread_ref.shape[0]
    gram = jnp.concatenate([gram[:, :comps], gram[:, comps:]], axis=0)
    row_at = lax.broadcasted_iota(jnp.int32, (comps, comps), 0)
    col_at = lax.broadcasted_iota(jnp.int32, (comps, comps), 1)
    eye = row_at == col_at
    diagonal = jnp.where(eye, gram, 0.0)
    row_scale = lax.rsqrt(jnp.sum(diagonal, axis=1, keepdims=True))
    col_scale = lax.rsqrt(jnp.sum(diagonal, axis=0, keepdims=True))
    both = jnp.concatenate([gram * row_scale * col_scale, jnp.where(eye, col_scale, 0.0)], axis=1)
    groups = eliminate([both[at:at + 8] for at in range(0, comps, 8)], 8)
    both = jnp.concatenate(groups, axis=0)
    pivots = jnp.sum(jnp.where(eye, both[:, :comps], 0.0), axis=1, keepdims=True)
    inverse = both[:, comps:] * (scale * lax.rsqrt(pivots))
    out_ref[...] = lax.dot_general(
        inverse, spread_ref[...], NN, precision=lax.Precision.HIGHEST, preferred_element_type=F32
    )


def orthonormal(grams, spread, scale):
    return pl.pallas_call(
        functools.partial(basis_kernel, scale),
        out_shape=jax.ShapeDtypeStruct(spread.shape, F32),
        in_specs=[WHOLE, WHOLE],
        out_specs=WHOLE,
        compiler_params=PARAMS,
        name="orthonormal",
    )(grams, spread)


def send(x, offset_cells, offset_genes):
    cells, genes = lax.axis_size("cells"), lax.axis_size("genes")
    pairs = []
    for c in range(cells):
        for g in range(genes):
            pairs.append((c * genes + g, (c ^ offset_cells) * genes + (g ^ offset_genes)))
    return lax.ppermute(x, ("cells", "genes"), pairs)


def gene_terms(x):
    terms = [x, send(x, 0, 1)]
    for at in range(1, lax.axis_size("genes").bit_length() - 1):
        x = tree_sum(terms)
        terms = [x, send(x, 0, 1 << at | 1)]
    return terms


def cell_terms(x):
    copies = jnp.broadcast_to(x, (lax.axis_size("cells"),) + x.shape)
    return lax.all_to_all(copies, "cells", 0, 0)


def scattered_spread(scores, high, low, sums, occ, cell_total):
    comps = scores[0].shape[0]
    me = lax.axis_index("cells").astype(jnp.int32).reshape(1)
    make = functools.partial(spread_pieces, scores=scores, high=high, low=low, sums=sums, occ=occ)
    blocks = list(make(me, picks=[7, 6, 5]))
    blocks[0], me = lax.optimization_barrier((blocks[0], me))
    came = [send(x, k - 4, 0) for k, x in zip((7, 6, 5), blocks)]
    far, own, near, *blocks = make(me, picks=[4, 0, 2, 3, 1])
    also = [send(x, 1, 0) for x in blocks]
    near = send(near + also[0], 2, 0)
    far = send(tree_sum([far] + came), 4, 0)
    return centered_gram([near, own + also[1] + far], comps, cell_total)


def all_alike(counts, occupancy, start_basis):
    tile_rows, tile_cols = occupancy.shape
    edge = counts.shape[0] // tile_rows
    logged = jnp.log(1.0 + counts.astype(F32)).reshape(tile_rows, edge, tile_cols, -1)
    logged = (logged * occupancy.astype(F32)[:, None, :, None]).reshape(counts.shape)
    high, low = split_terms(logged, 2)
    scores = lax.psum(dot(start_basis, high, NT) + dot(start_basis, low, NT), "genes")
    spread = spread_piece(split_terms(scores, 3), high, low)
    spread = lax.psum_scatter(spread, "cells", scatter_dimension=1, tiled=True)
    rows = lax.psum(jnp.sum(scores, axis=1, keepdims=True), "cells")
    sums = lax.psum_scatter(jnp.sum(logged, axis=0, keepdims=True), "cells", scatter_dimension=1, tiled=True)
    spread, gram = plain_gram(spread, rows, sums, counts.shape[0] * lax.axis_size("cells"))
    return lax.psum(gram, ("cells", "genes"))[None], spread


def in_steps(counts, occupancy, start_basis):
    high, low, sums = log_terms(counts)
    scores, occ = score_part(occupancy, start_basis, high, low)
    cell_total = counts.shape[0] * lax.axis_size("cells")
    spread, gram = scattered_spread(gene_terms(scores), high, low, sums, occ, cell_total)
    return cell_terms(tree_sum(gene_terms(gram))), spread


def on_device(counts, occupancy, start_basis):
    gene_count = counts.shape[1]
    cells, genes = lax.axis_size("cells"), lax.axis_size("genes")
    halvings = cells == 1 << 3 and genes == 1 << 2
    tiles = occupancy.shape[0] == 1 and gene_count == occupancy.shape[1] * LANES
    work = in_steps if halvings and tiles and gene_count % (cells * LANES) == 0 else all_alike
    grams, spread = work(counts, occupancy, start_basis)
    return orthonormal(grams, spread, math.sqrt(gene_count * genes))


def solution(mesh):
    in_specs = (P("cells", "genes"), P("cells", "genes"), P(None, "genes"))
    out_specs = P(None, ("genes", "cells"))
    return jax.shard_map(
        on_device, mesh=mesh, in_specs=in_specs, out_specs=out_specs, check_vma=False
    )
```

```python
import functools
import math

import jax
import jax.numpy as jnp
from jax import lax
from jax.experimental import pallas as pl
from jax.experimental.pallas import tpu as pltpu
from jax.sharding import PartitionSpec as P

F32 = jnp.float32
BF16 = jnp.bfloat16
NN = (((1,), (0,)), ((), ()))
NT = (((1,), (1,)), ((), ()))
WHOLE = pl.BlockSpec(memory_space=pltpu.VMEM)
SCALARS = pl.BlockSpec(memory_space=pltpu.SMEM)
LANES = 128
PARAMS = pltpu.CompilerParams(vmem_limit_bytes=16 * 2**20)
LOG_PARAMS = pltpu.CompilerParams(vmem_limit_bytes=205 * 2**18)


def dot(a, b, dims):
    return lax.dot_general(a, b, dims, preferred_element_type=F32)


def split_terms(x, count):
    terms = []
    for _ in range(count):
        term = x.astype(BF16)
        terms.append(term)
        x = x - term.astype(F32)
    return terms


def tree_sum(parts):
    while len(parts) > 1:
        parts = [sum(parts[at + 1:at + 2], parts[at]) for at in range(0, len(parts), 2)]
    return parts[0]


def log_kernel(width, counts_hbm, high_ref, low_ref, sum_ref, counts_ref, counts_sem):
    cells, genes = high_ref.shape
    fetches = [
        pltpu.make_async_copy(
            counts_hbm.at[:, pl.ds(at * width, width)], counts_ref.at[:, pl.ds(at * width, width)], counts_sem.at[at]
        )
        for at in range(genes // width)
    ]
    for fetch in fetches:
        fetch.start()
    for at, fetch in enumerate(fetches):
        fetch.wait()
        for begin in range(at * width, (at + 1) * width, LANES):
            lanes = pl.ds(begin, LANES)
            logged = jnp.log(1.0 + counts_ref[:, lanes].astype(F32))
            high = logged.astype(BF16)
            high_ref[:, lanes] = high
            low_ref[:, lanes] = (logged - high.astype(F32)).astype(BF16)
            sum_ref[:, lanes] = jnp.sum(logged, axis=0, keepdims=True)


def log_terms(counts):
    cells, genes = counts.shape
    width = genes // 8
    return pl.pallas_call(
        functools.partial(log_kernel, width),
        out_shape=(
            jax.ShapeDtypeStruct((cells, genes), BF16),
            jax.ShapeDtypeStruct((cells, genes), BF16),
            jax.ShapeDtypeStruct((1, genes), F32),
        ),
        in_specs=[pl.BlockSpec(memory_space=pltpu.HBM)],
        out_specs=(WHOLE, WHOLE, WHOLE),
        scratch_shapes=[pltpu.VMEM(counts.shape, BF16), pltpu.SemaphoreType.DMA((genes // width,))],
        compiler_params=LOG_PARAMS,
        cost_estimate=pl.CostEstimate(flops=20 * cells * genes, bytes_accessed=8 * cells * genes, transcendentals=0),
        name="log_terms",
    )(counts)


def score_kernel(width, occ_ref, basis_ref, high_ref, low_ref, score_ref, lane_ref):
    comps, genes = basis_ref.shape
    edge = genes // occ_ref.shape[1]
    occupancy = occ_ref[...].astype(F32)
    scores = None
    for begin in range(0, genes, width):
        basis = []
        for at in range(begin, begin + width, edge):
            occ = jnp.broadcast_to(occupancy[:, at // edge:at // edge + 1], (1, edge))
            lane_ref[:, pl.ds(at, edge)] = occ
            basis.append(basis_ref[:, pl.ds(at, edge)] * occ.astype(BF16))
        basis = jnp.concatenate(basis, axis=1)
        lanes = pl.ds(begin, width)
        part = dot(basis, high_ref[:, lanes], NT) + dot(basis, low_ref[:, lanes], NT)
        scores = part if scores is None else scores + part
    score_ref[...] = scores


def score_part(occupancy, basis, high, low):
    comps, genes = basis.shape
    cells = high.shape[0]
    return pl.pallas_call(
        functools.partial(score_kernel, genes // 4),
        out_shape=(jax.ShapeDtypeStruct((comps, cells), F32), jax.ShapeDtypeStruct((1, genes), F32)),
        in_specs=[WHOLE] * 4,
        out_specs=(WHOLE, WHOLE),
        compiler_params=PARAMS,
        name="scores",
    )(occupancy, basis, high, low)


def spread_piece(terms, high, low):
    comps = terms[0].shape[0]
    on_low = dot(jnp.concatenate(terms[:2], axis=0), low, NN)
    on_high = dot(jnp.concatenate(terms, axis=0), high, NN)
    small = on_low[comps:] + on_high[2 * comps:]
    middle = on_low[:comps] + on_high[comps:2 * comps]
    return (small + middle) + on_high[:comps]


def spread_kernel(count, picks, me_ref, *refs):
    score_refs, outs = refs[:count], refs[count + 4:]
    high_ref, low_ref, sum_ref, occ_ref = refs[count:count + 4]
    scores = tree_sum([ref[...] for ref in score_refs])
    comps = scores.shape[0]
    terms = split_terms(scores, 3)
    eye = lax.broadcasted_iota(jnp.int32, (comps, LANES), 0) == lax.broadcasted_iota(jnp.int32, (comps, LANES), 1)
    row_sums = jnp.sum(jnp.where(eye, jnp.sum(scores, axis=1, keepdims=True), 0.0), axis=0, keepdims=True)
    chunks = high_ref.shape[1] // (LANES * lax.axis_size("cells"))
    width = chunks * LANES
    for pick, out in zip(picks, outs):
        start = pl.multiple_of((me_ref[0] ^ pick) * width, width)
        lanes = pl.ds(start, width)
        piece = spread_piece(terms, high_ref[:, lanes], low_ref[:, lanes]) * occ_ref[:, lanes]
        sums = sum_ref[:, lanes] * occ_ref[:, lanes]
        extra = [row_sums]
        for at in range(chunks):
            out[at * comps:(at + 1) * comps] = piece[:, at * LANES:(at + 1) * LANES]
            extra.append(sums[:, at * LANES:(at + 1) * LANES])
        extra.append(jnp.zeros((out.shape[0] - chunks * comps - chunks - 1, LANES), F32))
        out[chunks * comps:] = jnp.concatenate(extra, axis=0)


def block_rows(comps, chunks):
    return comps * chunks + -(-(chunks + 1) // 8) * 8


def spread_pieces(me, scores, high, low, sums, occ, picks):
    comps = scores[0].shape[0]
    chunks = high.shape[1] // (LANES * lax.axis_size("cells"))
    block = jax.ShapeDtypeStruct((block_rows(comps, chunks), LANES), F32)
    return pl.pallas_call(
        functools.partial(spread_kernel, len(scores), picks),
        out_shape=[block] * len(picks),
        in_specs=[SCALARS] + [WHOLE] * (len(scores) + 4),
        out_specs=[WHOLE] * len(picks),
        compiler_params=PARAMS,
        cost_estimate=pl.CostEstimate(
            flops=10 * comps * len(picks) * chunks * LANES * high.shape[0], bytes_accessed=2**21, transcendentals=0
        ),
        name="spread",
    )(me, *scores, high, low, sums, occ)


def gram_kernel(scale, chunks, *refs):
    pieces, (spread_ref, gram_ref) = refs[:-2], refs[-2:]
    comps = spread_ref.shape[0]
    total = tree_sum([ref[...] for ref in pieces])
    extra = total[chunks * comps:chunks * comps + chunks + 1]
    eye = lax.broadcasted_iota(jnp.int32, (comps, LANES), 0) == lax.broadcasted_iota(jnp.int32, (comps, LANES), 1)
    row_sums = jnp.sum(jnp.where(eye, extra[:1], 0.0), axis=1, keepdims=True) * scale
    parts = [total[at * comps:(at + 1) * comps] - row_sums * extra[at + 1:at + 2] for at in range(chunks)]
    spread = jnp.concatenate(parts, axis=1)
    spread_ref[...] = spread
    gram_ref[...] = packed_gram(spread)


def packed_gram(spread):
    gram = lax.dot_general(spread, spread, NT, precision=lax.Precision.HIGHEST, preferred_element_type=F32)
    half = spread.shape[0] // 2
    return jnp.concatenate([gram[:half], gram[half:]], axis=1)


def centered_gram(pieces, comps, cell_total):
    chunks = pieces[0].shape[0] // comps
    return pl.pallas_call(
        functools.partial(gram_kernel, 1.0 / cell_total, chunks),
        out_shape=(
            jax.ShapeDtypeStruct((comps, chunks * LANES), F32),
            jax.ShapeDtypeStruct((comps // 2, comps * 2), F32),
        ),
        in_specs=[WHOLE] * len(pieces),
        out_specs=(WHOLE, WHOLE),
        compiler_params=PARAMS,
        name="gram",
    )(*pieces)


def plain_gram_kernel(scale, spread_ref, row_ref, sum_ref, out_ref, gram_ref):
    spread = spread_ref[...] - row_ref[...] * scale * sum_ref[...]
    out_ref[...] = spread
    gram_ref[...] = packed_gram(spread)


def plain_gram(spread, rows, sums, cell_total):
    comps, width = spread.shape
    return pl.pallas_call(
        functools.partial(plain_gram_kernel, 1.0 / cell_total),
        out_shape=(
            jax.ShapeDtypeStruct((comps, width), F32),
            jax.ShapeDtypeStruct((comps // 2, comps * 2), F32),
        ),
        in_specs=[WHOLE] * 3,
        out_specs=(WHOLE, WHOLE),
        compiler_params=PARAMS,
        name="plain_gram",
    )(spread, rows, sums)


def row_of(x, at):
    return jnp.broadcast_to(x[at:at + 1, :], x.shape)


def eliminate(groups, edge):
    groups = list(groups)
    below = lax.broadcasted_iota(jnp.int32, groups[0].shape, 0)
    for at in range(len(groups)):
        spread = [
            [jnp.broadcast_to(rows[:, c:c + 1], rows.shape) for c in range(at * edge, (at + 1) * edge)]
            for rows in groups[at:]
        ]
        for i in range(0, edge, 2):
            cols = spread[0]
            first, second = cols[i], cols[i + 1]
            a, b, c = row_of(first, i), row_of(second, i), row_of(second, i + 1)
            inv_a = pl.reciprocal(a, approx=True)
            inv_c = a * pl.reciprocal(a * c - b * b, approx=True)
            ratio = b * inv_a
            factors = []
            for k in range(i + 2, edge):
                top = row_of(cols[k], i)
                factors.append((k, top * inv_a, (row_of(cols[k], i + 1) - ratio * top) * inv_c))
            rows = groups[at]
            upper = row_of(rows, i) * inv_a
            rows = rows - jnp.where(below > i, first, 0.0) * upper
            lower = row_of(rows, i + 1) * inv_c
            groups[at] = rows - jnp.where(below > i + 1, second - ratio * first, 0.0) * lower
            for ahead, cols in enumerate(spread):
                first = cols[i]
                second = cols[i + 1] - ratio * first
                for k, on_first, on_second in factors:
                    cols[k] = cols[k] - first * on_first - second * on_second
                if ahead:
                    groups[at + ahead] = groups[at + ahead] - first * upper - second * lower
    return groups


def basis_kernel(scale, *refs):
    grams, (spread_ref, out_ref) = refs[:-2], refs[-2:]
    gram = tree_sum([ref[...] for ref in grams])
    comps = spread_ref.shape[0]
    gram = jnp.concatenate([gram[:, :comps], gram[:, comps:]], axis=0)
    row_at = lax.broadcasted_iota(jnp.int32, (comps, comps), 0)
    col_at = lax.broadcasted_iota(jnp.int32, (comps, comps), 1)
    eye = row_at == col_at
    diagonal = jnp.where(eye, gram, 0.0)
    row_scale = lax.rsqrt(jnp.sum(diagonal, axis=1, keepdims=True))
    col_scale = lax.rsqrt(jnp.sum(diagonal, axis=0, keepdims=True))
    both = jnp.concatenate([gram * row_scale * col_scale, jnp.where(eye, col_scale, 0.0)], axis=1)
    groups = eliminate([both[at:at + 8] for at in range(0, comps, 8)], 8)
    both = jnp.concatenate(groups, axis=0)
    pivots = jnp.sum(jnp.where(eye, both[:, :comps], 0.0), axis=1, keepdims=True)
    inverse = both[:, comps:] * (scale * lax.rsqrt(pivots))
    out_ref[...] = lax.dot_general(
        inverse, spread_ref[...], NN, precision=lax.Precision.HIGHEST, preferred_element_type=F32
    )


def orthonormal(grams, spread, scale):
    return pl.pallas_call(
        functools.partial(basis_kernel, scale),
        out_shape=jax.ShapeDtypeStruct(spread.shape, F32),
        in_specs=[WHOLE] * (len(grams) + 1),
        out_specs=WHOLE,
        compiler_params=PARAMS,
        name="orthonormal",
    )(*grams, spread)


def send(x, offset_cells, offset_genes):
    cells, genes = lax.axis_size("cells"), lax.axis_size("genes")
    pairs = []
    for c in range(cells):
        for g in range(genes):
            pairs.append((c * genes + g, (c ^ offset_cells) * genes + (g ^ offset_genes)))
    return lax.ppermute(x, ("cells", "genes"), pairs)


def gene_terms(x):
    terms = [x, send(x, 0, 1)]
    for at in range(1, lax.axis_size("genes").bit_length() - 1):
        x = tree_sum(terms)
        terms = [x, send(x, 0, 1 << at | 1)]
    return terms


def cell_terms(x):
    terms = [x]
    for at in range(lax.axis_size("cells").bit_length() - 1):
        x = tree_sum(terms)
        terms = [x, send(x, 1 << at, 1)]
    return terms


def scattered_spread(scores, high, low, sums, occ, cell_total):
    comps = scores[0].shape[0]
    me = lax.axis_index("cells").astype(jnp.int32).reshape(1)
    make = functools.partial(spread_pieces, scores=scores, high=high, low=low, sums=sums, occ=occ)
    blocks = list(make(me, picks=[7, 6, 5]))
    blocks[0], me = lax.optimization_barrier((blocks[0], me))
    came = [send(x, k - 4, 0) for k, x in zip((7, 6, 5), blocks)]
    far, own, near, *blocks = make(me, picks=[4, 0, 2, 3, 1])
    also = [send(x, 1, 0) for x in blocks]
    near = send(near + also[0], 2, 0)
    far = send(tree_sum([far] + came), 4, 0)
    return centered_gram([near, own + also[1] + far], comps, cell_total)


def all_alike(counts, occupancy, start_basis):
    tile_rows, tile_cols = occupancy.shape
    edge = counts.shape[0] // tile_rows
    logged = jnp.log(1.0 + counts.astype(F32)).reshape(tile_rows, edge, tile_cols, -1)
    logged = (logged * occupancy.astype(F32)[:, None, :, None]).reshape(counts.shape)
    high, low = split_terms(logged, 2)
    scores = lax.psum(dot(start_basis, high, NT) + dot(start_basis, low, NT), "genes")
    spread = spread_piece(split_terms(scores, 3), high, low)
    spread = lax.psum_scatter(spread, "cells", scatter_dimension=1, tiled=True)
    rows = lax.psum(jnp.sum(scores, axis=1, keepdims=True), "cells")
    sums = lax.psum_scatter(jnp.sum(logged, axis=0, keepdims=True), "cells", scatter_dimension=1, tiled=True)
    spread, gram = plain_gram(spread, rows, sums, counts.shape[0] * lax.axis_size("cells"))
    return [lax.psum(gram, ("cells", "genes"))], spread


def in_steps(counts, occupancy, start_basis):
    high, low, sums = log_terms(counts)
    scores, occ = score_part(occupancy, start_basis, high, low)
    cell_total = counts.shape[0] * lax.axis_size("cells")
    spread, gram = scattered_spread(gene_terms(scores), high, low, sums, occ, cell_total)
    return cell_terms(tree_sum(gene_terms(gram))), spread


def on_device(counts, occupancy, start_basis):
    gene_count = counts.shape[1]
    cells, genes = lax.axis_size("cells"), lax.axis_size("genes")
    halvings = cells == 1 << 3 and genes == 1 << 2
    tiles = occupancy.shape[0] == 1 and gene_count == occupancy.shape[1] * LANES
    work = in_steps if halvings and tiles and gene_count % (cells * LANES) == 0 else all_alike
    grams, spread = work(counts, occupancy, start_basis)
    return orthonormal(grams, spread, math.sqrt(gene_count * genes))


def solution(mesh):
    in_specs = (P("cells", "genes"), P("cells", "genes"), P(None, "genes"))
    out_specs = P(None, ("genes", "cells"))
    return jax.shard_map(
        on_device, mesh=mesh, in_specs=in_specs, out_specs=out_specs, check_vma=False
    )
```

```python
import functools
import math

import jax
import jax.numpy as jnp
from jax import lax
from jax.experimental import pallas as pl
from jax.experimental.pallas import tpu as pltpu
from jax.sharding import PartitionSpec as P

F32 = jnp.float32
BF16 = jnp.bfloat16
NN = (((1,), (0,)), ((), ()))
NT = (((1,), (1,)), ((), ()))
WHOLE = pl.BlockSpec(memory_space=pltpu.VMEM)
SCALARS = pl.BlockSpec(memory_space=pltpu.SMEM)
LANES = 128
PARAMS = pltpu.CompilerParams(vmem_limit_bytes=16 * 2**20)
LOG_PARAMS = pltpu.CompilerParams(vmem_limit_bytes=205 * 2**18)


def dot(a, b, dims):
    return lax.dot_general(a, b, dims, preferred_element_type=F32)


def split_terms(x, count):
    terms = []
    for _ in range(count):
        term = x.astype(BF16)
        terms.append(term)
        x = x - term.astype(F32)
    return terms


def tree_sum(parts):
    while len(parts) > 1:
        parts = [sum(parts[at + 1:at + 2], parts[at]) for at in range(0, len(parts), 2)]
    return parts[0]


def log_kernel(width, counts_hbm, high_ref, low_ref, sum_ref, counts_ref, counts_sem):
    cells, genes = high_ref.shape
    fetches = [
        pltpu.make_async_copy(
            counts_hbm.at[:, pl.ds(at * width, width)], counts_ref.at[:, pl.ds(at * width, width)], counts_sem.at[at]
        )
        for at in range(genes // width)
    ]
    for fetch in fetches:
        fetch.start()
    for at, fetch in enumerate(fetches):
        fetch.wait()
        for begin in range(at * width, (at + 1) * width, LANES):
            lanes = pl.ds(begin, LANES)
            logged = jnp.log(1.0 + counts_ref[:, lanes].astype(F32))
            high = logged.astype(BF16)
            high_ref[:, lanes] = high
            low_ref[:, lanes] = (logged - high.astype(F32)).astype(BF16)
            sum_ref[:, lanes] = jnp.sum(logged, axis=0, keepdims=True)


def log_terms(counts):
    cells, genes = counts.shape
    width = genes // 8
    return pl.pallas_call(
        functools.partial(log_kernel, width),
        out_shape=(
            jax.ShapeDtypeStruct((cells, genes), BF16),
            jax.ShapeDtypeStruct((cells, genes), BF16),
            jax.ShapeDtypeStruct((1, genes), F32),
        ),
        in_specs=[pl.BlockSpec(memory_space=pltpu.HBM)],
        out_specs=(WHOLE, WHOLE, WHOLE),
        scratch_shapes=[pltpu.VMEM(counts.shape, BF16), pltpu.SemaphoreType.DMA((genes // width,))],
        compiler_params=LOG_PARAMS,
        cost_estimate=pl.CostEstimate(flops=20 * cells * genes, bytes_accessed=8 * cells * genes, transcendentals=0),
        name="log_terms",
    )(counts)


def score_kernel(width, occ_ref, basis_ref, high_ref, low_ref, score_ref, lane_ref):
    comps, genes = basis_ref.shape
    edge = genes // occ_ref.shape[1]
    occupancy = occ_ref[...].astype(F32)
    scores = None
    for begin in range(0, genes, width):
        basis = []
        for at in range(begin, begin + width, edge):
            occ = jnp.broadcast_to(occupancy[:, at // edge:at // edge + 1], (1, edge))
            lane_ref[:, pl.ds(at, edge)] = occ
            basis.append(basis_ref[:, pl.ds(at, edge)] * occ.astype(BF16))
        basis = jnp.concatenate(basis, axis=1)
        lanes = pl.ds(begin, width)
        part = dot(basis, high_ref[:, lanes], NT) + dot(basis, low_ref[:, lanes], NT)
        scores = part if scores is None else scores + part
    score_ref[...] = scores


def score_part(occupancy, basis, high, low):
    comps, genes = basis.shape
    cells = high.shape[0]
    return pl.pallas_call(
        functools.partial(score_kernel, genes // 4),
        out_shape=(jax.ShapeDtypeStruct((comps, cells), F32), jax.ShapeDtypeStruct((1, genes), F32)),
        in_specs=[WHOLE] * 4,
        out_specs=(WHOLE, WHOLE),
        compiler_params=PARAMS,
        name="scores",
    )(occupancy, basis, high, low)


def spread_piece(terms, high, low):
    comps = terms[0].shape[0]
    on_low = dot(jnp.concatenate(terms[:2], axis=0), low, NN)
    on_high = dot(jnp.concatenate(terms, axis=0), high, NN)
    small = on_low[comps:] + on_high[2 * comps:]
    middle = on_low[:comps] + on_high[comps:2 * comps]
    return (small + middle) + on_high[:comps]


def spread_kernel(count, picks, me_ref, *refs):
    score_refs, outs = refs[:count], refs[count + 4:]
    high_ref, low_ref, sum_ref, occ_ref = refs[count:count + 4]
    scores = tree_sum([ref[...] for ref in score_refs])
    comps = scores.shape[0]
    terms = split_terms(scores, 3)
    eye = lax.broadcasted_iota(jnp.int32, (comps, LANES), 0) == lax.broadcasted_iota(jnp.int32, (comps, LANES), 1)
    row_sums = jnp.sum(jnp.where(eye, jnp.sum(scores, axis=1, keepdims=True), 0.0), axis=0, keepdims=True)
    chunks = high_ref.shape[1] // (LANES * lax.axis_size("cells"))
    width = chunks * LANES
    for pick, out in zip(picks, outs):
        start = pl.multiple_of((me_ref[0] ^ pick) * width, width)
        lanes = pl.ds(start, width)
        piece = spread_piece(terms, high_ref[:, lanes], low_ref[:, lanes]) * occ_ref[:, lanes]
        sums = sum_ref[:, lanes] * occ_ref[:, lanes]
        extra = [row_sums]
        for at in range(chunks):
            out[at * comps:(at + 1) * comps] = piece[:, at * LANES:(at + 1) * LANES]
            extra.append(sums[:, at * LANES:(at + 1) * LANES])
        extra.append(jnp.zeros((out.shape[0] - chunks * comps - chunks - 1, LANES), F32))
        out[chunks * comps:] = jnp.concatenate(extra, axis=0)


def block_rows(comps, chunks):
    return comps * chunks + -(-(chunks + 1) // 8) * 8


def spread_pieces(me, scores, high, low, sums, occ, picks):
    comps = scores[0].shape[0]
    chunks = high.shape[1] // (LANES * lax.axis_size("cells"))
    block = jax.ShapeDtypeStruct((block_rows(comps, chunks), LANES), F32)
    return pl.pallas_call(
        functools.partial(spread_kernel, len(scores), picks),
        out_shape=[block] * len(picks),
        in_specs=[SCALARS] + [WHOLE] * (len(scores) + 4),
        out_specs=[WHOLE] * len(picks),
        compiler_params=PARAMS,
        cost_estimate=pl.CostEstimate(
            flops=10 * comps * len(picks) * chunks * LANES * high.shape[0], bytes_accessed=2**21, transcendentals=0
        ),
        name="spread",
    )(me, *scores, high, low, sums, occ)


def gram_kernel(scale, chunks, *refs):
    pieces, (spread_ref, gram_ref) = refs[:-2], refs[-2:]
    comps = spread_ref.shape[0]
    total = tree_sum([ref[...] for ref in pieces])
    extra = total[chunks * comps:chunks * comps + chunks + 1]
    eye = lax.broadcasted_iota(jnp.int32, (comps, LANES), 0) == lax.broadcasted_iota(jnp.int32, (comps, LANES), 1)
    row_sums = jnp.sum(jnp.where(eye, extra[:1], 0.0), axis=1, keepdims=True) * scale
    parts = [total[at * comps:(at + 1) * comps] - row_sums * extra[at + 1:at + 2] for at in range(chunks)]
    spread = jnp.concatenate(parts, axis=1)
    spread_ref[...] = spread
    gram_ref[...] = packed_gram(spread)


def packed_gram(spread):
    gram = lax.dot_general(spread, spread, NT, precision=lax.Precision.HIGHEST, preferred_element_type=F32)
    half = spread.shape[0] // 2
    return jnp.concatenate([gram[:half], gram[half:]], axis=1)


def centered_gram(pieces, comps, cell_total):
    chunks = pieces[0].shape[0] // comps
    return pl.pallas_call(
        functools.partial(gram_kernel, 1.0 / cell_total, chunks),
        out_shape=(
            jax.ShapeDtypeStruct((comps, chunks * LANES), F32),
            jax.ShapeDtypeStruct((comps // 2, comps * 2), F32),
        ),
        in_specs=[WHOLE] * len(pieces),
        out_specs=(WHOLE, WHOLE),
        compiler_params=PARAMS,
        name="gram",
    )(*pieces)


def plain_gram_kernel(scale, spread_ref, row_ref, sum_ref, out_ref, gram_ref):
    spread = spread_ref[...] - row_ref[...] * scale * sum_ref[...]
    out_ref[...] = spread
    gram_ref[...] = packed_gram(spread)


def plain_gram(spread, rows, sums, cell_total):
    comps, width = spread.shape
    return pl.pallas_call(
        functools.partial(plain_gram_kernel, 1.0 / cell_total),
        out_shape=(
            jax.ShapeDtypeStruct((comps, width), F32),
            jax.ShapeDtypeStruct((comps // 2, comps * 2), F32),
        ),
        in_specs=[WHOLE] * 3,
        out_specs=(WHOLE, WHOLE),
        compiler_params=PARAMS,
        name="plain_gram",
    )(spread, rows, sums)


def row_of(x, at):
    return jnp.broadcast_to(x[at:at + 1, :], x.shape)


def eliminate(groups, edge):
    groups = list(groups)
    below = lax.broadcasted_iota(jnp.int32, groups[0].shape, 0)
    for at in range(len(groups)):
        spread = [
            [jnp.broadcast_to(rows[:, c:c + 1], rows.shape) for c in range(at * edge, (at + 1) * edge)]
            for rows in groups[at:]
        ]
        for i in range(0, edge, 2):
            cols = spread[0]
            first, second = cols[i], cols[i + 1]
            a, b, c = row_of(first, i), row_of(second, i), row_of(second, i + 1)
            inv_a = pl.reciprocal(a, approx=True)
            inv_c = a * pl.reciprocal(a * c - b * b, approx=True)
            ratio = b * inv_a
            factors = []
            for k in range(i + 2, edge):
                top = row_of(cols[k], i)
                factors.append((k, top * inv_a, (row_of(cols[k], i + 1) - ratio * top) * inv_c))
            rows = groups[at]
            upper = row_of(rows, i) * inv_a
            rows = rows - jnp.where(below > i, first, 0.0) * upper
            lower = row_of(rows, i + 1) * inv_c
            groups[at] = rows - jnp.where(below > i + 1, second - ratio * first, 0.0) * lower
            for ahead, cols in enumerate(spread):
                first = cols[i]
                second = cols[i + 1] - ratio * first
                for k, on_first, on_second in factors:
                    cols[k] = cols[k] - first * on_first - second * on_second
                if ahead:
                    groups[at + ahead] = groups[at + ahead] - first * upper - second * lower
    return groups


def basis_kernel(scale, *refs):
    grams, (spread_ref, out_ref) = refs[:-2], refs[-2:]
    gram = tree_sum([ref[...] for ref in grams])
    comps = spread_ref.shape[0]
    gram = jnp.concatenate([gram[:, :comps], gram[:, comps:]], axis=0)
    row_at = lax.broadcasted_iota(jnp.int32, (comps, comps), 0)
    col_at = lax.broadcasted_iota(jnp.int32, (comps, comps), 1)
    eye = row_at == col_at
    diagonal = jnp.where(eye, gram, 0.0)
    row_scale = lax.rsqrt(jnp.sum(diagonal, axis=1, keepdims=True))
    col_scale = lax.rsqrt(jnp.sum(diagonal, axis=0, keepdims=True))
    both = jnp.concatenate([gram * row_scale * col_scale, jnp.where(eye, col_scale, 0.0)], axis=1)
    groups = eliminate([both[at:at + 8] for at in range(0, comps, 8)], 8)
    both = jnp.concatenate(groups, axis=0)
    pivots = jnp.sum(jnp.where(eye, both[:, :comps], 0.0), axis=1, keepdims=True)
    inverse = both[:, comps:] * (scale * lax.rsqrt(pivots))
    out_ref[...] = lax.dot_general(
        inverse, spread_ref[...], NN, precision=lax.Precision.HIGHEST, preferred_element_type=F32
    )


def orthonormal(grams, spread, scale):
    return pl.pallas_call(
        functools.partial(basis_kernel, scale),
        out_shape=jax.ShapeDtypeStruct(spread.shape, F32),
        in_specs=[WHOLE] * (len(grams) + 1),
        out_specs=WHOLE,
        compiler_params=PARAMS,
        name="orthonormal",
    )(*grams, spread)


def send(x, offset_cells, offset_genes):
    cells, genes = lax.axis_size("cells"), lax.axis_size("genes")
    pairs = []
    for c in range(cells):
        for g in range(genes):
            pairs.append((c * genes + g, (c ^ offset_cells) * genes + (g ^ offset_genes)))
    return lax.ppermute(x, ("cells", "genes"), pairs)


def gene_terms(x):
    terms = [x, send(x, 0, 1)]
    for at in range(1, lax.axis_size("genes").bit_length() - 1):
        x = tree_sum(terms)
        terms = [x, send(x, 0, 1 << at | 1)]
    return terms


def cell_terms(x):
    terms = [x]
    for at in range(lax.axis_size("cells").bit_length() - 1):
        x = tree_sum(terms)
        terms = [x, send(x, 1 << at, 1)]
    return terms


def scattered_spread(scores, high, low, sums, occ, cell_total):
    comps = scores[0].shape[0]
    me = lax.axis_index("cells").astype(jnp.int32).reshape(1)
    make = functools.partial(spread_pieces, scores=scores, high=high, low=low, sums=sums, occ=occ)
    first = list(make(me, picks=[6, 5, 7]))
    first[0], me = lax.optimization_barrier((first[0], me))
    came = [send(x, k - 4, 0) for k, x in zip((6, 5), first)]
    straight = [send(first[2], 7, 0)]
    far, own, *second = make(me, picks=[4, 0, 3, 2, 1])
    came[0], second[0] = lax.optimization_barrier((came[0], second[0]))
    far = tree_sum([far] + came)
    far, second[1], second[2] = lax.optimization_barrier((far, second[1], second[2]))
    straight += [send(x, k, 0) for k, x in zip((3, 2, 1), second)]
    return centered_gram([own, send(far, 4, 0)] + straight, comps, cell_total)


def all_alike(counts, occupancy, start_basis):
    tile_rows, tile_cols = occupancy.shape
    edge = counts.shape[0] // tile_rows
    logged = jnp.log(1.0 + counts.astype(F32)).reshape(tile_rows, edge, tile_cols, -1)
    logged = (logged * occupancy.astype(F32)[:, None, :, None]).reshape(counts.shape)
    high, low = split_terms(logged, 2)
    scores = lax.psum(dot(start_basis, high, NT) + dot(start_basis, low, NT), "genes")
    spread = spread_piece(split_terms(scores, 3), high, low)
    spread = lax.psum_scatter(spread, "cells", scatter_dimension=1, tiled=True)
    rows = lax.psum(jnp.sum(scores, axis=1, keepdims=True), "cells")
    sums = lax.psum_scatter(jnp.sum(logged, axis=0, keepdims=True), "cells", scatter_dimension=1, tiled=True)
    spread, gram = plain_gram(spread, rows, sums, counts.shape[0] * lax.axis_size("cells"))
    return [lax.psum(gram, ("cells", "genes"))], spread


def in_steps(counts, occupancy, start_basis):
    high, low, sums = log_terms(counts)
    scores, occ = score_part(occupancy, start_basis, high, low)
    cell_total = counts.shape[0] * lax.axis_size("cells")
    spread, gram = scattered_spread(gene_terms(scores), high, low, sums, occ, cell_total)
    return cell_terms(tree_sum(gene_terms(gram))), spread


def on_device(counts, occupancy, start_basis):
    gene_count = counts.shape[1]
    cells, genes = lax.axis_size("cells"), lax.axis_size("genes")
    halvings = cells == 1 << 3 and genes == 1 << 2
    tiles = occupancy.shape[0] == 1 and gene_count == occupancy.shape[1] * LANES
    work = in_steps if halvings and tiles and gene_count % (cells * LANES) == 0 else all_alike
    grams, spread = work(counts, occupancy, start_basis)
    return orthonormal(grams, spread, math.sqrt(gene_count * genes))


def solution(mesh):
    in_specs = (P("cells", "genes"), P("cells", "genes"), P(None, "genes"))
    out_specs = P(None, ("genes", "cells"))
    return jax.shard_map(
        on_device, mesh=mesh, in_specs=in_specs, out_specs=out_specs, check_vma=False
    )
```

```python
import functools
import math

import jax
import jax.numpy as jnp
from jax import lax
from jax.experimental import pallas as pl
from jax.experimental.pallas import tpu as pltpu
from jax.sharding import PartitionSpec as P

F32 = jnp.float32
BF16 = jnp.bfloat16
NN = (((1,), (0,)), ((), ()))
NT = (((1,), (1,)), ((), ()))
WHOLE = pl.BlockSpec(memory_space=pltpu.VMEM)
SCALARS = pl.BlockSpec(memory_space=pltpu.SMEM)
LANES = 128
PARAMS = pltpu.CompilerParams(vmem_limit_bytes=16 * 2**20)
LOG_PARAMS = pltpu.CompilerParams(vmem_limit_bytes=205 * 2**18)


def dot(a, b, dims):
    return lax.dot_general(a, b, dims, preferred_element_type=F32)


def split_terms(x, count):
    terms = []
    for _ in range(count):
        term = x.astype(BF16)
        terms.append(term)
        x = x - term.astype(F32)
    return terms


def tree_sum(parts):
    while len(parts) > 1:
        parts = [sum(parts[at + 1:at + 2], parts[at]) for at in range(0, len(parts), 2)]
    return parts[0]


def log_kernel(width, counts_hbm, high_ref, low_ref, sum_ref, counts_ref, counts_sem):
    cells, genes = high_ref.shape
    fetches = [
        pltpu.make_async_copy(
            counts_hbm.at[:, pl.ds(at * width, width)], counts_ref.at[:, pl.ds(at * width, width)], counts_sem.at[at]
        )
        for at in range(genes // width)
    ]
    for fetch in fetches:
        fetch.start()
    for at, fetch in enumerate(fetches):
        fetch.wait()
        for begin in range(at * width, (at + 1) * width, LANES):
            lanes = pl.ds(begin, LANES)
            logged = jnp.log(1.0 + counts_ref[:, lanes].astype(F32))
            high = logged.astype(BF16)
            high_ref[:, lanes] = high
            low_ref[:, lanes] = (logged - high.astype(F32)).astype(BF16)
            sum_ref[:, lanes] = jnp.sum(logged, axis=0, keepdims=True)


def log_terms(counts):
    cells, genes = counts.shape
    width = genes // 8
    return pl.pallas_call(
        functools.partial(log_kernel, width),
        out_shape=(
            jax.ShapeDtypeStruct((cells, genes), BF16),
            jax.ShapeDtypeStruct((cells, genes), BF16),
            jax.ShapeDtypeStruct((1, genes), F32),
        ),
        in_specs=[pl.BlockSpec(memory_space=pltpu.HBM)],
        out_specs=(WHOLE, WHOLE, WHOLE),
        scratch_shapes=[pltpu.VMEM(counts.shape, BF16), pltpu.SemaphoreType.DMA((genes // width,))],
        compiler_params=LOG_PARAMS,
        cost_estimate=pl.CostEstimate(flops=20 * cells * genes, bytes_accessed=8 * cells * genes, transcendentals=0),
        name="log_terms",
    )(counts)


def score_kernel(width, occ_ref, basis_ref, high_ref, low_ref, score_ref, lane_ref):
    comps, genes = basis_ref.shape
    edge = genes // occ_ref.shape[1]
    occupancy = occ_ref[...].astype(F32)
    scores = None
    for begin in range(0, genes, width):
        basis = []
        for at in range(begin, begin + width, edge):
            occ = jnp.broadcast_to(occupancy[:, at // edge:at // edge + 1], (1, edge))
            lane_ref[:, pl.ds(at, edge)] = occ
            basis.append(basis_ref[:, pl.ds(at, edge)] * occ.astype(BF16))
        basis = jnp.concatenate(basis, axis=1)
        lanes = pl.ds(begin, width)
        part = dot(basis, high_ref[:, lanes], NT) + dot(basis, low_ref[:, lanes], NT)
        scores = part if scores is None else scores + part
    score_ref[...] = scores


def score_part(occupancy, basis, high, low):
    comps, genes = basis.shape
    cells = high.shape[0]
    return pl.pallas_call(
        functools.partial(score_kernel, genes // 4),
        out_shape=(jax.ShapeDtypeStruct((comps, cells), F32), jax.ShapeDtypeStruct((1, genes), F32)),
        in_specs=[WHOLE] * 4,
        out_specs=(WHOLE, WHOLE),
        compiler_params=PARAMS,
        name="scores",
    )(occupancy, basis, high, low)


def spread_piece(terms, high, low):
    comps = terms[0].shape[0]
    on_low = dot(jnp.concatenate(terms[:2], axis=0), low, NN)
    on_high = dot(jnp.concatenate(terms, axis=0), high, NN)
    small = on_low[comps:] + on_high[2 * comps:]
    middle = on_low[:comps] + on_high[comps:2 * comps]
    return (small + middle) + on_high[:comps]


def spread_kernel(count, picks, me_ref, *refs):
    score_refs, outs = refs[:count], refs[count + 4:]
    high_ref, low_ref, sum_ref, occ_ref = refs[count:count + 4]
    scores = tree_sum([ref[...] for ref in score_refs])
    comps = scores.shape[0]
    terms = split_terms(scores, 3)
    eye = lax.broadcasted_iota(jnp.int32, (comps, LANES), 0) == lax.broadcasted_iota(jnp.int32, (comps, LANES), 1)
    row_sums = jnp.sum(jnp.where(eye, jnp.sum(scores, axis=1, keepdims=True), 0.0), axis=0, keepdims=True)
    chunks = high_ref.shape[1] // (LANES * lax.axis_size("cells"))
    width = chunks * LANES
    for pick, out in zip(picks, outs):
        start = pl.multiple_of((me_ref[0] ^ pick) * width, width)
        lanes = pl.ds(start, width)
        piece = spread_piece(terms, high_ref[:, lanes], low_ref[:, lanes]) * occ_ref[:, lanes]
        sums = sum_ref[:, lanes] * occ_ref[:, lanes]
        extra = [row_sums]
        for at in range(chunks):
            out[at * comps:(at + 1) * comps] = piece[:, at * LANES:(at + 1) * LANES]
            extra.append(sums[:, at * LANES:(at + 1) * LANES])
        extra.append(jnp.zeros((out.shape[0] - chunks * comps - chunks - 1, LANES), F32))
        out[chunks * comps:] = jnp.concatenate(extra, axis=0)


def block_rows(comps, chunks):
    return comps * chunks + -(-(chunks + 1) // 8) * 8


def spread_pieces(me, scores, high, low, sums, occ, picks):
    comps = scores[0].shape[0]
    chunks = high.shape[1] // (LANES * lax.axis_size("cells"))
    block = jax.ShapeDtypeStruct((block_rows(comps, chunks), LANES), F32)
    return pl.pallas_call(
        functools.partial(spread_kernel, len(scores), picks),
        out_shape=[block] * len(picks),
        in_specs=[SCALARS] + [WHOLE] * (len(scores) + 4),
        out_specs=[WHOLE] * len(picks),
        compiler_params=PARAMS,
        cost_estimate=pl.CostEstimate(
            flops=10 * comps * len(picks) * chunks * LANES * high.shape[0], bytes_accessed=2**21, transcendentals=0
        ),
        name="spread",
    )(me, *scores, high, low, sums, occ)


def gram_kernel(scale, chunks, *refs):
    pieces, (spread_ref, gram_ref) = refs[:-2], refs[-2:]
    comps = spread_ref.shape[0]
    total = tree_sum([ref[...] for ref in pieces])
    extra = total[chunks * comps:chunks * comps + chunks + 1]
    eye = lax.broadcasted_iota(jnp.int32, (comps, LANES), 0) == lax.broadcasted_iota(jnp.int32, (comps, LANES), 1)
    row_sums = jnp.sum(jnp.where(eye, extra[:1], 0.0), axis=1, keepdims=True) * scale
    parts = [total[at * comps:(at + 1) * comps] - row_sums * extra[at + 1:at + 2] for at in range(chunks)]
    spread = jnp.concatenate(parts, axis=1)
    spread_ref[...] = spread
    gram_ref[...] = packed_gram(spread)


def packed_gram(spread):
    gram = lax.dot_general(spread, spread, NT, precision=lax.Precision.HIGHEST, preferred_element_type=F32)
    half = spread.shape[0] // 2
    return jnp.concatenate([gram[:half], gram[half:]], axis=1)


def centered_gram(pieces, comps, cell_total):
    chunks = pieces[0].shape[0] // comps
    return pl.pallas_call(
        functools.partial(gram_kernel, 1.0 / cell_total, chunks),
        out_shape=(
            jax.ShapeDtypeStruct((comps, chunks * LANES), F32),
            jax.ShapeDtypeStruct((comps // 2, comps * 2), F32),
        ),
        in_specs=[WHOLE] * len(pieces),
        out_specs=(WHOLE, WHOLE),
        compiler_params=PARAMS,
        name="gram",
    )(*pieces)


def plain_gram_kernel(scale, spread_ref, row_ref, sum_ref, out_ref, gram_ref):
    spread = spread_ref[...] - row_ref[...] * scale * sum_ref[...]
    out_ref[...] = spread
    gram_ref[...] = packed_gram(spread)


def plain_gram(spread, rows, sums, cell_total):
    comps, width = spread.shape
    return pl.pallas_call(
        functools.partial(plain_gram_kernel, 1.0 / cell_total),
        out_shape=(
            jax.ShapeDtypeStruct((comps, width), F32),
            jax.ShapeDtypeStruct((comps // 2, comps * 2), F32),
        ),
        in_specs=[WHOLE] * 3,
        out_specs=(WHOLE, WHOLE),
        compiler_params=PARAMS,
        name="plain_gram",
    )(spread, rows, sums)


def row_of(x, at):
    return jnp.broadcast_to(x[at:at + 1, :], x.shape)


def eliminate(groups, edge):
    groups = list(groups)
    below = lax.broadcasted_iota(jnp.int32, groups[0].shape, 0)
    for at in range(len(groups)):
        spread = [
            [jnp.broadcast_to(rows[:, c:c + 1], rows.shape) for c in range(at * edge, (at + 1) * edge)]
            for rows in groups[at:]
        ]
        for i in range(0, edge, 2):
            cols = spread[0]
            first, second = cols[i], cols[i + 1]
            a, b, c = row_of(first, i), row_of(second, i), row_of(second, i + 1)
            inv_a = pl.reciprocal(a, approx=True)
            inv_c = a * pl.reciprocal(a * c - b * b, approx=True)
            ratio = b * inv_a
            factors = []
            for k in range(i + 2, edge):
                top = row_of(cols[k], i)
                factors.append((k, top * inv_a, (row_of(cols[k], i + 1) - ratio * top) * inv_c))
            rows = groups[at]
            upper = row_of(rows, i) * inv_a
            rows = rows - jnp.where(below > i, first, 0.0) * upper
            lower = row_of(rows, i + 1) * inv_c
            groups[at] = rows - jnp.where(below > i + 1, second - ratio * first, 0.0) * lower
            for ahead, cols in enumerate(spread):
                first = cols[i]
                second = cols[i + 1] - ratio * first
                for k, on_first, on_second in factors:
                    cols[k] = cols[k] - first * on_first - second * on_second
                if ahead:
                    groups[at + ahead] = groups[at + ahead] - first * upper - second * lower
    return groups


def basis_kernel(scale, *refs):
    grams, (spread_ref, out_ref) = refs[:-2], refs[-2:]
    gram = tree_sum([ref[...] for ref in grams])
    comps = spread_ref.shape[0]
    gram = jnp.concatenate([gram[:, :comps], gram[:, comps:]], axis=0)
    row_at = lax.broadcasted_iota(jnp.int32, (comps, comps), 0)
    col_at = lax.broadcasted_iota(jnp.int32, (comps, comps), 1)
    eye = row_at == col_at
    diagonal = jnp.where(eye, gram, 0.0)
    row_scale = lax.rsqrt(jnp.sum(diagonal, axis=1, keepdims=True))
    col_scale = lax.rsqrt(jnp.sum(diagonal, axis=0, keepdims=True))
    both = jnp.concatenate([gram * row_scale * col_scale, jnp.where(eye, col_scale, 0.0)], axis=1)
    groups = eliminate([both[at:at + 8] for at in range(0, comps, 8)], 8)
    both = jnp.concatenate(groups, axis=0)
    pivots = jnp.sum(jnp.where(eye, both[:, :comps], 0.0), axis=1, keepdims=True)
    inverse = both[:, comps:] * (scale * lax.rsqrt(pivots))
    out_ref[...] = lax.dot_general(
        inverse, spread_ref[...], NN, precision=lax.Precision.HIGHEST, preferred_element_type=F32
    )


def orthonormal(grams, spread, scale):
    return pl.pallas_call(
        functools.partial(basis_kernel, scale),
        out_shape=jax.ShapeDtypeStruct(spread.shape, F32),
        in_specs=[WHOLE] * (len(grams) + 1),
        out_specs=WHOLE,
        compiler_params=PARAMS,
        name="orthonormal",
    )(*grams, spread)


def send(x, offset_cells, offset_genes):
    cells, genes = lax.axis_size("cells"), lax.axis_size("genes")
    pairs = []
    for c in range(cells):
        for g in range(genes):
            pairs.append((c * genes + g, (c ^ offset_cells) * genes + (g ^ offset_genes)))
    return lax.ppermute(x, ("cells", "genes"), pairs)


def gene_terms(x):
    terms = [x, send(x, 0, 1)]
    for at in range(1, lax.axis_size("genes").bit_length() - 1):
        x = tree_sum(terms)
        terms = [x, send(x, 0, 1 << at | 1)]
    return terms


def cell_terms(x):
    terms = [x]
    for at in range(lax.axis_size("cells").bit_length() - 1):
        x = tree_sum(terms)
        terms = [x, send(x, 1 << at, 1)]
    return terms


def scattered_spread(scores, high, low, sums, occ, cell_total):
    comps = scores[0].shape[0]
    me = lax.axis_index("cells").astype(jnp.int32).reshape(1)
    make = functools.partial(spread_pieces, scores=scores, high=high, low=low, sums=sums, occ=occ)
    first = list(make(me, picks=[6, 5, 7]))
    first[0], me = lax.optimization_barrier((first[0], me))
    came = [send(x, k - 4, 0) for k, x in zip((6, 5), first)]
    across = send(first[2], 7, 0)
    far, own, near, *second = make(me, picks=[4, 0, 2, 3, 1])
    came[0], second[0] = lax.optimization_barrier((came[0], second[0]))
    far = tree_sum([far] + came)
    far, second[1] = lax.optimization_barrier((far, second[1]))
    near = near + send(second[0], 1, 0)
    far, near, also = send(far, 4, 0), send(near, 2, 0), send(second[1], 1, 0)
    return centered_gram([own, far, across, also, near], comps, cell_total)


def all_alike(counts, occupancy, start_basis):
    tile_rows, tile_cols = occupancy.shape
    edge = counts.shape[0] // tile_rows
    logged = jnp.log(1.0 + counts.astype(F32)).reshape(tile_rows, edge, tile_cols, -1)
    logged = (logged * occupancy.astype(F32)[:, None, :, None]).reshape(counts.shape)
    high, low = split_terms(logged, 2)
    scores = lax.psum(dot(start_basis, high, NT) + dot(start_basis, low, NT), "genes")
    spread = spread_piece(split_terms(scores, 3), high, low)
    spread = lax.psum_scatter(spread, "cells", scatter_dimension=1, tiled=True)
    rows = lax.psum(jnp.sum(scores, axis=1, keepdims=True), "cells")
    sums = lax.psum_scatter(jnp.sum(logged, axis=0, keepdims=True), "cells", scatter_dimension=1, tiled=True)
    spread, gram = plain_gram(spread, rows, sums, counts.shape[0] * lax.axis_size("cells"))
    return [lax.psum(gram, ("cells", "genes"))], spread


def in_steps(counts, occupancy, start_basis):
    high, low, sums = log_terms(counts)
    scores, occ = score_part(occupancy, start_basis, high, low)
    cell_total = counts.shape[0] * lax.axis_size("cells")
    spread, gram = scattered_spread(gene_terms(scores), high, low, sums, occ, cell_total)
    return cell_terms(tree_sum(gene_terms(gram))), spread


def on_device(counts, occupancy, start_basis):
    gene_count = counts.shape[1]
    cells, genes = lax.axis_size("cells"), lax.axis_size("genes")
    halvings = cells == 1 << 3 and genes == 1 << 2
    tiles = occupancy.shape[0] == 1 and gene_count == occupancy.shape[1] * LANES
    work = in_steps if halvings and tiles and gene_count % (cells * LANES) == 0 else all_alike
    grams, spread = work(counts, occupancy, start_basis)
    return orthonormal(grams, spread, math.sqrt(gene_count * genes))


def solution(mesh):
    in_specs = (P("cells", "genes"), P("cells", "genes"), P(None, "genes"))
    out_specs = P(None, ("genes", "cells"))
    return jax.shard_map(
        on_device, mesh=mesh, in_specs=in_specs, out_specs=out_specs, check_vma=False
    )
```

```python
import functools
import math

import jax
import jax.numpy as jnp
from jax import lax
from jax.experimental import pallas as pl
from jax.experimental.pallas import tpu as pltpu
from jax.sharding import PartitionSpec as P

F32 = jnp.float32
BF16 = jnp.bfloat16
NN = (((1,), (0,)), ((), ()))
NT = (((1,), (1,)), ((), ()))
WHOLE = pl.BlockSpec(memory_space=pltpu.VMEM)
SCALARS = pl.BlockSpec(memory_space=pltpu.SMEM)
LANES = 128
PARAMS = pltpu.CompilerParams(vmem_limit_bytes=16 * 2**20)
LOG_PARAMS = pltpu.CompilerParams(vmem_limit_bytes=205 * 2**18)


def dot(a, b, dims):
    return lax.dot_general(a, b, dims, preferred_element_type=F32)


def split_terms(x, count):
    terms = []
    for _ in range(count):
        term = x.astype(BF16)
        terms.append(term)
        x = x - term.astype(F32)
    return terms


def tree_sum(parts):
    while len(parts) > 1:
        parts = [sum(parts[at + 1:at + 2], parts[at]) for at in range(0, len(parts), 2)]
    return parts[0]


def log_kernel(width, counts_hbm, high_ref, low_ref, sum_ref, counts_ref, counts_sem):
    cells, genes = high_ref.shape
    fetches = [
        pltpu.make_async_copy(
            counts_hbm.at[:, pl.ds(at * width, width)], counts_ref.at[:, pl.ds(at * width, width)], counts_sem.at[at]
        )
        for at in range(genes // width)
    ]
    for fetch in fetches:
        fetch.start()
    for at, fetch in enumerate(fetches):
        fetch.wait()
        for begin in range(at * width, (at + 1) * width, LANES):
            lanes = pl.ds(begin, LANES)
            logged = jnp.log(1.0 + counts_ref[:, lanes].astype(F32))
            high = logged.astype(BF16)
            high_ref[:, lanes] = high
            low_ref[:, lanes] = (logged - high.astype(F32)).astype(BF16)
            sum_ref[:, lanes] = jnp.sum(logged, axis=0, keepdims=True)


def log_terms(counts):
    cells, genes = counts.shape
    width = genes // 8
    return pl.pallas_call(
        functools.partial(log_kernel, width),
        out_shape=(
            jax.ShapeDtypeStruct((cells, genes), BF16),
            jax.ShapeDtypeStruct((cells, genes), BF16),
            jax.ShapeDtypeStruct((1, genes), F32),
        ),
        in_specs=[pl.BlockSpec(memory_space=pltpu.HBM)],
        out_specs=(WHOLE, WHOLE, WHOLE),
        scratch_shapes=[pltpu.VMEM(counts.shape, BF16), pltpu.SemaphoreType.DMA((genes // width,))],
        compiler_params=LOG_PARAMS,
        cost_estimate=pl.CostEstimate(flops=20 * cells * genes, bytes_accessed=8 * cells * genes, transcendentals=0),
        name="log_terms",
    )(counts)


def score_kernel(width, occ_ref, basis_ref, high_ref, low_ref, score_ref, lane_ref):
    comps, genes = basis_ref.shape
    edge = genes // occ_ref.shape[1]
    occupancy = occ_ref[...].astype(F32)
    scores = None
    for begin in range(0, genes, width):
        basis = []
        for at in range(begin, begin + width, edge):
            occ = jnp.broadcast_to(occupancy[:, at // edge:at // edge + 1], (1, edge))
            lane_ref[:, pl.ds(at, edge)] = occ
            basis.append(basis_ref[:, pl.ds(at, edge)] * occ.astype(BF16))
        basis = jnp.concatenate(basis, axis=1)
        lanes = pl.ds(begin, width)
        part = dot(basis, high_ref[:, lanes], NT) + dot(basis, low_ref[:, lanes], NT)
        scores = part if scores is None else scores + part
    score_ref[...] = scores


def score_part(occupancy, basis, high, low):
    comps, genes = basis.shape
    cells = high.shape[0]
    return pl.pallas_call(
        functools.partial(score_kernel, genes // 4),
        out_shape=(jax.ShapeDtypeStruct((comps, cells), F32), jax.ShapeDtypeStruct((1, genes), F32)),
        in_specs=[WHOLE] * 4,
        out_specs=(WHOLE, WHOLE),
        compiler_params=PARAMS,
        name="scores",
    )(occupancy, basis, high, low)


def spread_piece(terms, high, low):
    comps = terms[0].shape[0]
    on_low = dot(jnp.concatenate(terms[:2], axis=0), low, NN)
    on_high = dot(jnp.concatenate(terms, axis=0), high, NN)
    small = on_low[comps:] + on_high[2 * comps:]
    middle = on_low[:comps] + on_high[comps:2 * comps]
    return on_high[:comps], small + middle


def spread_kernel(count, picks, me_ref, *refs):
    score_refs, outs = refs[:count], refs[count + 4:]
    high_ref, low_ref, sum_ref, occ_ref = refs[count:count + 4]
    scores = tree_sum([ref[...] for ref in score_refs])
    comps = scores.shape[0]
    terms = split_terms(scores, 3)
    eye = lax.broadcasted_iota(jnp.int32, (comps, LANES), 0) == lax.broadcasted_iota(jnp.int32, (comps, LANES), 1)
    row_sums = jnp.sum(jnp.where(eye, jnp.sum(scores, axis=1, keepdims=True), 0.0), axis=0, keepdims=True)
    chunks = high_ref.shape[1] // (LANES * lax.axis_size("cells"))
    width = chunks * LANES
    for at_pick, (pick, out) in enumerate(zip(picks, outs)):
        start = pl.multiple_of((me_ref[0] ^ pick) * width, width)
        lanes = pl.ds(start, width)
        main, rest = spread_piece(terms, high_ref[:, lanes], low_ref[:, lanes])
        twice, again = picks.count(pick) == 2, pick in picks[:at_pick]
        piece = (rest if again else main if twice else main + rest) * occ_ref[:, lanes]
        sums = sum_ref[:, lanes] * occ_ref[:, lanes]
        extra = [row_sums]
        for at in range(chunks):
            out[at * comps:(at + 1) * comps] = piece[:, at * LANES:(at + 1) * LANES]
            extra.append(sums[:, at * LANES:(at + 1) * LANES])
        extra.append(jnp.zeros((out.shape[0] - chunks * comps - chunks - 1, LANES), F32))
        out[chunks * comps:] = jnp.concatenate(extra, axis=0) * (0.0 if again else 1.0)


def block_rows(comps, chunks):
    return comps * chunks + -(-(chunks + 1) // 8) * 8


def spread_pieces(me, scores, high, low, sums, occ, picks):
    comps = scores[0].shape[0]
    chunks = high.shape[1] // (LANES * lax.axis_size("cells"))
    block = jax.ShapeDtypeStruct((block_rows(comps, chunks), LANES), F32)
    return pl.pallas_call(
        functools.partial(spread_kernel, len(scores), picks),
        out_shape=[block] * len(picks),
        in_specs=[SCALARS] + [WHOLE] * (len(scores) + 4),
        out_specs=[WHOLE] * len(picks),
        compiler_params=PARAMS,
        cost_estimate=pl.CostEstimate(
            flops=10 * comps * len(picks) * chunks * LANES * high.shape[0], bytes_accessed=2**21, transcendentals=0
        ),
        name="spread",
    )(me, *scores, high, low, sums, occ)


def gram_kernel(scale, chunks, *refs):
    pieces, (spread_ref, gram_ref) = refs[:-2], refs[-2:]
    comps = spread_ref.shape[0]
    total = tree_sum([ref[...] for ref in pieces])
    extra = total[chunks * comps:chunks * comps + chunks + 1]
    eye = lax.broadcasted_iota(jnp.int32, (comps, LANES), 0) == lax.broadcasted_iota(jnp.int32, (comps, LANES), 1)
    row_sums = jnp.sum(jnp.where(eye, extra[:1], 0.0), axis=1, keepdims=True) * scale
    parts = [total[at * comps:(at + 1) * comps] - row_sums * extra[at + 1:at + 2] for at in range(chunks)]
    spread = jnp.concatenate(parts, axis=1)
    spread_ref[...] = spread
    gram_ref[...] = packed_gram(spread)


def packed_gram(spread):
    gram = lax.dot_general(spread, spread, NT, precision=lax.Precision.HIGHEST, preferred_element_type=F32)
    half = spread.shape[0] // 2
    return jnp.concatenate([gram[:half], gram[half:]], axis=1)


def centered_gram(pieces, comps, cell_total):
    chunks = pieces[0].shape[0] // comps
    return pl.pallas_call(
        functools.partial(gram_kernel, 1.0 / cell_total, chunks),
        out_shape=(
            jax.ShapeDtypeStruct((comps, chunks * LANES), F32),
            jax.ShapeDtypeStruct((comps // 2, comps * 2), F32),
        ),
        in_specs=[WHOLE] * len(pieces),
        out_specs=(WHOLE, WHOLE),
        compiler_params=PARAMS,
        name="gram",
    )(*pieces)


def plain_gram_kernel(scale, spread_ref, row_ref, sum_ref, out_ref, gram_ref):
    spread = spread_ref[...] - row_ref[...] * scale * sum_ref[...]
    out_ref[...] = spread
    gram_ref[...] = packed_gram(spread)


def plain_gram(spread, rows, sums, cell_total):
    comps, width = spread.shape
    return pl.pallas_call(
        functools.partial(plain_gram_kernel, 1.0 / cell_total),
        out_shape=(
            jax.ShapeDtypeStruct((comps, width), F32),
            jax.ShapeDtypeStruct((comps // 2, comps * 2), F32),
        ),
        in_specs=[WHOLE] * 3,
        out_specs=(WHOLE, WHOLE),
        compiler_params=PARAMS,
        name="plain_gram",
    )(spread, rows, sums)


def row_of(x, at):
    return jnp.broadcast_to(x[at:at + 1, :], x.shape)


def eliminate(groups, edge):
    groups = list(groups)
    below = lax.broadcasted_iota(jnp.int32, groups[0].shape, 0)
    for at in range(len(groups)):
        spread = [
            [jnp.broadcast_to(rows[:, c:c + 1], rows.shape) for c in range(at * edge, (at + 1) * edge)]
            for rows in groups[at:]
        ]
        for i in range(0, edge, 2):
            cols = spread[0]
            first, second = cols[i], cols[i + 1]
            a, b, c = row_of(first, i), row_of(second, i), row_of(second, i + 1)
            inv_a = pl.reciprocal(a, approx=True)
            inv_c = a * pl.reciprocal(a * c - b * b, approx=True)
            ratio = b * inv_a
            factors = []
            for k in range(i + 2, edge):
                top = row_of(cols[k], i)
                factors.append((k, top * inv_a, (row_of(cols[k], i + 1) - ratio * top) * inv_c))
            rows = groups[at]
            upper = row_of(rows, i) * inv_a
            rows = rows - jnp.where(below > i, first, 0.0) * upper
            lower = row_of(rows, i + 1) * inv_c
            groups[at] = rows - jnp.where(below > i + 1, second - ratio * first, 0.0) * lower
            for ahead, cols in enumerate(spread):
                first = cols[i]
                second = cols[i + 1] - ratio * first
                for k, on_first, on_second in factors:
                    cols[k] = cols[k] - first * on_first - second * on_second
                if ahead:
                    groups[at + ahead] = groups[at + ahead] - first * upper - second * lower
    return groups


def basis_kernel(scale, *refs):
    grams, (spread_ref, out_ref) = refs[:-2], refs[-2:]
    gram = tree_sum([ref[...] for ref in grams])
    comps = spread_ref.shape[0]
    gram = jnp.concatenate([gram[:, :comps], gram[:, comps:]], axis=0)
    row_at = lax.broadcasted_iota(jnp.int32, (comps, comps), 0)
    col_at = lax.broadcasted_iota(jnp.int32, (comps, comps), 1)
    eye = row_at == col_at
    diagonal = jnp.where(eye, gram, 0.0)
    row_scale = lax.rsqrt(jnp.sum(diagonal, axis=1, keepdims=True))
    col_scale = lax.rsqrt(jnp.sum(diagonal, axis=0, keepdims=True))
    both = jnp.concatenate([gram * row_scale * col_scale, jnp.where(eye, col_scale, 0.0)], axis=1)
    groups = eliminate([both[at:at + 8] for at in range(0, comps, 8)], 8)
    both = jnp.concatenate(groups, axis=0)
    pivots = jnp.sum(jnp.where(eye, both[:, :comps], 0.0), axis=1, keepdims=True)
    inverse = both[:, comps:] * (scale * lax.rsqrt(pivots))
    out_ref[...] = lax.dot_general(
        inverse, spread_ref[...], NN, precision=lax.Precision.HIGHEST, preferred_element_type=F32
    )


def orthonormal(grams, spread, scale):
    return pl.pallas_call(
        functools.partial(basis_kernel, scale),
        out_shape=jax.ShapeDtypeStruct(spread.shape, F32),
        in_specs=[WHOLE] * (len(grams) + 1),
        out_specs=WHOLE,
        compiler_params=PARAMS,
        name="orthonormal",
    )(*grams, spread)


def send(x, offset_cells, offset_genes):
    cells, genes = lax.axis_size("cells"), lax.axis_size("genes")
    pairs = []
    for c in range(cells):
        for g in range(genes):
            pairs.append((c * genes + g, (c ^ offset_cells) * genes + (g ^ offset_genes)))
    return lax.ppermute(x, ("cells", "genes"), pairs)


def gene_terms(x):
    terms = [x, send(x, 0, 1)]
    for at in range(1, lax.axis_size("genes").bit_length() - 1):
        x = tree_sum(terms)
        terms = [x, send(x, 0, 1 << at | 1)]
    return terms


def cell_terms(x):
    terms = [x]
    for at in range(lax.axis_size("cells").bit_length() - 1):
        x = tree_sum(terms)
        terms = [x, send(x, 1 << at, 1)]
    return terms


def scattered_spread(scores, high, low, sums, occ, cell_total):
    comps = scores[0].shape[0]
    me = lax.axis_index("cells").astype(jnp.int32).reshape(1)
    make = functools.partial(spread_pieces, scores=scores, high=high, low=low, sums=sums, occ=occ)
    first = list(make(me, picks=[6, 5, 7]))
    first[0], me = lax.optimization_barrier((first[0], me))
    came = [send(x, k - 4, 0) for k, x in zip((6, 5), first)]
    across = send(first[2], 7, 0)
    far, own, rest, near, *second = make(me, picks=[4, 0, 0, 2, 3, 1])
    far = far + lax.optimization_barrier(tree_sum(came))
    far, second[1] = lax.optimization_barrier((far, second[1]))
    own = own + lax.optimization_barrier(across + rest)
    near, own = lax.optimization_barrier((near + send(second[0], 1, 0), own))
    far, near, also = send(far, 4, 0), send(near, 2, 0), send(second[1], 1, 0)
    return centered_gram([far + own, also, near], comps, cell_total)


def all_alike(counts, occupancy, start_basis):
    tile_rows, tile_cols = occupancy.shape
    edge = counts.shape[0] // tile_rows
    logged = jnp.log(1.0 + counts.astype(F32)).reshape(tile_rows, edge, tile_cols, -1)
    logged = (logged * occupancy.astype(F32)[:, None, :, None]).reshape(counts.shape)
    high, low = split_terms(logged, 2)
    scores = lax.psum(dot(start_basis, high, NT) + dot(start_basis, low, NT), "genes")
    spread = sum(spread_piece(split_terms(scores, 3), high, low))
    spread = lax.psum_scatter(spread, "cells", scatter_dimension=1, tiled=True)
    rows = lax.psum(jnp.sum(scores, axis=1, keepdims=True), "cells")
    sums = lax.psum_scatter(jnp.sum(logged, axis=0, keepdims=True), "cells", scatter_dimension=1, tiled=True)
    spread, gram = plain_gram(spread, rows, sums, counts.shape[0] * lax.axis_size("cells"))
    return [lax.psum(gram, ("cells", "genes"))], spread


def in_steps(counts, occupancy, start_basis):
    high, low, sums = log_terms(counts)
    scores, occ = score_part(occupancy, start_basis, high, low)
    cell_total = counts.shape[0] * lax.axis_size("cells")
    spread, gram = scattered_spread(gene_terms(scores), high, low, sums, occ, cell_total)
    return cell_terms(tree_sum(gene_terms(gram))), spread


def on_device(counts, occupancy, start_basis):
    gene_count = counts.shape[1]
    cells, genes = lax.axis_size("cells"), lax.axis_size("genes")
    halvings = cells == 1 << 3 and genes == 1 << 2
    tiles = occupancy.shape[0] == 1 and gene_count == occupancy.shape[1] * LANES
    work = in_steps if halvings and tiles and gene_count % (cells * LANES) == 0 else all_alike
    grams, spread = work(counts, occupancy, start_basis)
    return orthonormal(grams, spread, math.sqrt(gene_count * genes))


def solution(mesh):
    in_specs = (P("cells", "genes"), P("cells", "genes"), P(None, "genes"))
    out_specs = P(None, ("genes", "cells"))
    return jax.shard_map(
        on_device, mesh=mesh, in_specs=in_specs, out_specs=out_specs, check_vma=False
    )
```

```python
import functools
import math

import jax
import jax.numpy as jnp
from jax import lax
from jax.experimental import pallas as pl
from jax.experimental.pallas import tpu as pltpu
from jax.sharding import PartitionSpec as P

F32 = jnp.float32
BF16 = jnp.bfloat16
NN = (((1,), (0,)), ((), ()))
NT = (((1,), (1,)), ((), ()))
WHOLE = pl.BlockSpec(memory_space=pltpu.VMEM)
SCALARS = pl.BlockSpec(memory_space=pltpu.SMEM)
LANES = 128
PARAMS = pltpu.CompilerParams(vmem_limit_bytes=16 * 2**20)
LOG_PARAMS = pltpu.CompilerParams(vmem_limit_bytes=205 * 2**18)


def dot(a, b, dims):
    return lax.dot_general(a, b, dims, preferred_element_type=F32)


def split_terms(x, count):
    terms = []
    for _ in range(count):
        term = x.astype(BF16)
        terms.append(term)
        x = x - term.astype(F32)
    return terms


def tree_sum(parts):
    while len(parts) > 1:
        parts = [sum(parts[at + 1:at + 2], parts[at]) for at in range(0, len(parts), 2)]
    return parts[0]


def log_kernel(width, counts_hbm, high_ref, low_ref, sum_ref, counts_ref, counts_sem):
    cells, genes = high_ref.shape
    fetches = [
        pltpu.make_async_copy(
            counts_hbm.at[:, pl.ds(at * width, width)], counts_ref.at[:, pl.ds(at * width, width)], counts_sem.at[at]
        )
        for at in range(genes // width)
    ]
    for fetch in fetches:
        fetch.start()
    for at, fetch in enumerate(fetches):
        fetch.wait()
        for begin in range(at * width, (at + 1) * width, LANES):
            lanes = pl.ds(begin, LANES)
            logged = jnp.log(1.0 + counts_ref[:, lanes].astype(F32))
            high = logged.astype(BF16)
            high_ref[:, lanes] = high
            low_ref[:, lanes] = (logged - high.astype(F32)).astype(BF16)
            sum_ref[:, lanes] = jnp.sum(logged, axis=0, keepdims=True)


def log_terms(counts):
    cells, genes = counts.shape
    width = genes // 8
    return pl.pallas_call(
        functools.partial(log_kernel, width),
        out_shape=(
            jax.ShapeDtypeStruct((cells, genes), BF16),
            jax.ShapeDtypeStruct((cells, genes), BF16),
            jax.ShapeDtypeStruct((1, genes), F32),
        ),
        in_specs=[pl.BlockSpec(memory_space=pltpu.HBM)],
        out_specs=(WHOLE, WHOLE, WHOLE),
        scratch_shapes=[pltpu.VMEM(counts.shape, BF16), pltpu.SemaphoreType.DMA((genes // width,))],
        compiler_params=LOG_PARAMS,
        cost_estimate=pl.CostEstimate(flops=20 * cells * genes, bytes_accessed=8 * cells * genes, transcendentals=0),
        name="log_terms",
    )(counts)


def score_kernel(width, occ_ref, basis_ref, high_ref, low_ref, score_ref, lane_ref):
    comps, genes = basis_ref.shape
    edge = genes // occ_ref.shape[1]
    occupancy = occ_ref[...].astype(F32)
    scores = None
    for begin in range(0, genes, width):
        basis = []
        for at in range(begin, begin + width, edge):
            occ = jnp.broadcast_to(occupancy[:, at // edge:at // edge + 1], (1, edge))
            lane_ref[:, pl.ds(at, edge)] = occ
            basis.append(basis_ref[:, pl.ds(at, edge)] * occ.astype(BF16))
        basis = jnp.concatenate(basis, axis=1)
        lanes = pl.ds(begin, width)
        part = dot(basis, high_ref[:, lanes], NT) + dot(basis, low_ref[:, lanes], NT)
        scores = part if scores is None else scores + part
    score_ref[...] = scores


def score_part(occupancy, basis, high, low):
    comps, genes = basis.shape
    cells = high.shape[0]
    return pl.pallas_call(
        functools.partial(score_kernel, genes // 4),
        out_shape=(jax.ShapeDtypeStruct((comps, cells), F32), jax.ShapeDtypeStruct((1, genes), F32)),
        in_specs=[WHOLE] * 4,
        out_specs=(WHOLE, WHOLE),
        compiler_params=PARAMS,
        name="scores",
    )(occupancy, basis, high, low)


def spread_piece(terms, high, low):
    comps = terms[0].shape[0]
    on_low = dot(jnp.concatenate(terms[:2], axis=0), low, NN)
    on_high = dot(jnp.concatenate(terms, axis=0), high, NN)
    small = on_low[comps:] + on_high[2 * comps:]
    middle = on_low[:comps] + on_high[comps:2 * comps]
    return (small + middle) + on_high[:comps]


def spread_kernel(count, picks, me_ref, *refs):
    score_refs, outs = refs[:count], refs[count + 4:]
    high_ref, low_ref, sum_ref, occ_ref = refs[count:count + 4]
    scores = tree_sum([ref[...] for ref in score_refs])
    comps = scores.shape[0]
    terms = split_terms(scores, 3)
    eye = lax.broadcasted_iota(jnp.int32, (comps, LANES), 0) == lax.broadcasted_iota(jnp.int32, (comps, LANES), 1)
    row_sums = jnp.sum(jnp.where(eye, jnp.sum(scores, axis=1, keepdims=True), 0.0), axis=0, keepdims=True)
    chunks = high_ref.shape[1] // (LANES * lax.axis_size("cells"))
    width = chunks * LANES
    for pick, out in zip(picks, outs):
        start = pl.multiple_of((me_ref[0] ^ pick) * width, width)
        lanes = pl.ds(start, width)
        piece = spread_piece(terms, high_ref[:, lanes], low_ref[:, lanes]) * occ_ref[:, lanes]
        sums = sum_ref[:, lanes] * occ_ref[:, lanes]
        extra = [row_sums]
        for at in range(chunks):
            out[at * comps:(at + 1) * comps] = piece[:, at * LANES:(at + 1) * LANES]
            extra.append(sums[:, at * LANES:(at + 1) * LANES])
        extra.append(jnp.zeros((out.shape[0] - chunks * comps - chunks - 1, LANES), F32))
        out[chunks * comps:] = jnp.concatenate(extra, axis=0)


def block_rows(comps, chunks):
    return comps * chunks + -(-(chunks + 1) // 8) * 8


def spread_pieces(me, scores, high, low, sums, occ, picks):
    comps = scores[0].shape[0]
    chunks = high.shape[1] // (LANES * lax.axis_size("cells"))
    block = jax.ShapeDtypeStruct((block_rows(comps, chunks), LANES), F32)
    return pl.pallas_call(
        functools.partial(spread_kernel, len(scores), picks),
        out_shape=[block] * len(picks),
        in_specs=[SCALARS] + [WHOLE] * (len(scores) + 4),
        out_specs=[WHOLE] * len(picks),
        compiler_params=PARAMS,
        cost_estimate=pl.CostEstimate(
            flops=10 * comps * len(picks) * chunks * LANES * high.shape[0], bytes_accessed=2**21, transcendentals=0
        ),
        name="spread",
    )(me, *scores, high, low, sums, occ)


def gram_kernel(scale, chunks, *refs):
    pieces, (spread_ref, gram_ref) = refs[:-2], refs[-2:]
    comps = spread_ref.shape[0]
    total = tree_sum([ref[...] for ref in pieces])
    extra = total[chunks * comps:chunks * comps + chunks + 1]
    eye = lax.broadcasted_iota(jnp.int32, (comps, LANES), 0) == lax.broadcasted_iota(jnp.int32, (comps, LANES), 1)
    row_sums = jnp.sum(jnp.where(eye, extra[:1], 0.0), axis=1, keepdims=True) * scale
    parts = [total[at * comps:(at + 1) * comps] - row_sums * extra[at + 1:at + 2] for at in range(chunks)]
    spread = jnp.concatenate(parts, axis=1)
    spread_ref[...] = spread
    gram_ref[...] = packed_gram(spread)


def packed_gram(spread):
    gram = lax.dot_general(spread, spread, NT, precision=lax.Precision.HIGHEST, preferred_element_type=F32)
    half = spread.shape[0] // 2
    return jnp.concatenate([gram[:half], gram[half:]], axis=1)


def centered_gram(pieces, comps, cell_total):
    chunks = pieces[0].shape[0] // comps
    return pl.pallas_call(
        functools.partial(gram_kernel, 1.0 / cell_total, chunks),
        out_shape=(
            jax.ShapeDtypeStruct((comps, chunks * LANES), F32),
            jax.ShapeDtypeStruct((comps // 2, comps * 2), F32),
        ),
        in_specs=[WHOLE] * len(pieces),
        out_specs=(WHOLE, WHOLE),
        compiler_params=PARAMS,
        name="gram",
    )(*pieces)


def plain_gram_kernel(scale, spread_ref, row_ref, sum_ref, out_ref, gram_ref):
    spread = spread_ref[...] - row_ref[...] * scale * sum_ref[...]
    out_ref[...] = spread
    gram_ref[...] = packed_gram(spread)


def plain_gram(spread, rows, sums, cell_total):
    comps, width = spread.shape
    return pl.pallas_call(
        functools.partial(plain_gram_kernel, 1.0 / cell_total),
        out_shape=(
            jax.ShapeDtypeStruct((comps, width), F32),
            jax.ShapeDtypeStruct((comps // 2, comps * 2), F32),
        ),
        in_specs=[WHOLE] * 3,
        out_specs=(WHOLE, WHOLE),
        compiler_params=PARAMS,
        name="plain_gram",
    )(spread, rows, sums)


def row_of(x, at):
    return jnp.broadcast_to(x[at:at + 1, :], x.shape)


def spread_column(rows, at):
    return jnp.broadcast_to(rows[:, at:at + 1], rows.shape)


def eliminate(groups, begin):
    groups = list(groups)
    edge = groups[0].shape[0]
    below = lax.broadcasted_iota(jnp.int32, groups[0].shape, 0)
    columns = [{c: spread_column(rows, begin + c) for c in range(edge)} for rows in groups]
    for at in range(len(groups)):
        scale = jnp.zeros_like(groups[0])
        later = (at + 1) * edge
        for i in range(at * edge, later, 2):
            if i == later - 4 and at + 1 < len(groups):
                for rows, cols in zip(groups[at:], columns[at:]):
                    cols.update({c: spread_column(rows, begin + c) for c in range(later, later + edge)})
            row = i - at * edge
            cols = columns[at]
            first, second = cols[i], cols[i + 1]
            a, b, c = row_of(first, row), row_of(second, row), row_of(second, row + 1)
            det = a * c - b * b
            inv_a = pl.reciprocal(a, approx=True)
            inv_c = a * pl.reciprocal(det, approx=True)
            ratio = b * inv_a
            scale = jnp.where(below == row, lax.rsqrt(a), jnp.where(below == row + 1, lax.rsqrt(det * inv_a), scale))
            factors = []
            for k in cols:
                if k > i + 1:
                    top = row_of(cols[k], row)
                    factors.append((k, top * inv_a, (row_of(cols[k], row + 1) - ratio * top) * inv_c))
            rows = groups[at]
            upper = row_of(rows, row) * inv_a
            rows = rows - jnp.where(below > row, first, 0.0) * upper
            lower = row_of(rows, row + 1) * inv_c
            groups[at] = rows - jnp.where(below > row + 1, second - ratio * first, 0.0) * lower
            for ahead in range(at, len(groups)):
                cols = columns[ahead]
                first = cols[i]
                second = cols[i + 1] - ratio * first
                for k, on_first, on_second in factors:
                    cols[k] = cols[k] - first * on_first - second * on_second
                if ahead > at:
                    groups[ahead] = groups[ahead] - first * upper - second * lower
                del cols[i], cols[i + 1]
        groups[at] = groups[at] * scale
    return groups


def scale_kernel(gram_ref, times_ref, plus_ref):
    gram = gram_ref[...]
    half, comps = gram.shape[0], gram.shape[1] // 2
    gram = jnp.concatenate([gram[:, :comps], gram[:, comps:]], axis=0)
    eye = lax.broadcasted_iota(jnp.int32, gram.shape, 0) == lax.broadcasted_iota(jnp.int32, gram.shape, 1)
    diagonal = jnp.where(eye, gram, 0.0)
    row_scale = lax.rsqrt(jnp.sum(diagonal, axis=1, keepdims=True))
    col_scale = lax.rsqrt(jnp.sum(diagonal, axis=0, keepdims=True))
    zeros = jnp.zeros_like(gram)
    times_ref[...] = jnp.concatenate([zeros, row_scale * col_scale], axis=1)
    plus_ref[...] = jnp.concatenate([jnp.where(eye, col_scale, 0.0), zeros], axis=1)


def scales(gram):
    half, lanes = gram.shape
    return pl.pallas_call(
        scale_kernel,
        out_shape=[jax.ShapeDtypeStruct((2 * half, lanes), F32)] * 2,
        in_specs=[WHOLE],
        out_specs=[WHOLE, WHOLE],
        compiler_params=PARAMS,
        name="scales",
    )(gram)


def basis_kernel(scale, *refs):
    grams, (times_ref, plus_ref, spread_ref, out_ref) = refs[:-4], refs[-4:]
    gram = tree_sum([ref[...] for ref in grams])
    comps = spread_ref.shape[0]
    gram = jnp.concatenate([pltpu.roll(gram, comps, 1), gram], axis=0)
    both = gram * times_ref[...] + plus_ref[...]
    groups = eliminate([both[at:at + 8] for at in range(0, comps, 8)], comps)
    inverse = jnp.concatenate(groups, axis=0)[:, :comps] * scale
    out_ref[...] = lax.dot_general(
        inverse, spread_ref[...], NN, precision=lax.Precision.HIGHEST, preferred_element_type=F32
    )


def orthonormal(grams, spread, scale):
    return pl.pallas_call(
        functools.partial(basis_kernel, scale),
        out_shape=jax.ShapeDtypeStruct(spread.shape, F32),
        in_specs=[WHOLE] * (len(grams) + 3),
        out_specs=WHOLE,
        compiler_params=PARAMS,
        name="orthonormal",
    )(*grams, *scales(grams[0]), spread)


def send(x, offset_cells, offset_genes):
    cells, genes = lax.axis_size("cells"), lax.axis_size("genes")
    pairs = []
    for c in range(cells):
        for g in range(genes):
            pairs.append((c * genes + g, (c ^ offset_cells) * genes + (g ^ offset_genes)))
    return lax.ppermute(x, ("cells", "genes"), pairs)


def gene_terms(x):
    terms = [x, send(x, 0, 1)]
    for at in range(1, lax.axis_size("genes").bit_length() - 1):
        x = tree_sum(terms)
        terms = [x, send(x, 0, 1 << at | 1)]
    return terms


def cell_terms(x):
    terms = [x]
    for at in range(lax.axis_size("cells").bit_length() - 1):
        x = tree_sum(terms)
        terms = [x, send(x, 1 << at, 1)]
    return terms


def scattered_spread(scores, high, low, sums, occ, cell_total):
    comps = scores[0].shape[0]
    me = lax.axis_index("cells").astype(jnp.int32).reshape(1)
    make = functools.partial(spread_pieces, scores=scores, high=high, low=low, sums=sums, occ=occ)
    first = list(make(me, picks=[6, 5, 7]))
    first[0], me = lax.optimization_barrier((first[0], me))
    came = [send(x, k - 4, 0) for k, x in zip((6, 5), first)]
    straight = [send(first[2], 7, 0)]
    far, own, *second = make(me, picks=[4, 0, 3, 2, 1])
    came[0], second[0] = lax.optimization_barrier((came[0], second[0]))
    far = tree_sum([far] + came)
    far, second[1], second[2] = lax.optimization_barrier((far, second[1], second[2]))
    straight += [send(x, k, 0) for k, x in zip((3, 2, 1), second)]
    return centered_gram([own, send(far, 4, 0)] + straight, comps, cell_total)


def all_alike(counts, occupancy, start_basis):
    tile_rows, tile_cols = occupancy.shape
    edge = counts.shape[0] // tile_rows
    logged = jnp.log(1.0 + counts.astype(F32)).reshape(tile_rows, edge, tile_cols, -1)
    logged = (logged * occupancy.astype(F32)[:, None, :, None]).reshape(counts.shape)
    high, low = split_terms(logged, 2)
    scores = lax.psum(dot(start_basis, high, NT) + dot(start_basis, low, NT), "genes")
    spread = spread_piece(split_terms(scores, 3), high, low)
    spread = lax.psum_scatter(spread, "cells", scatter_dimension=1, tiled=True)
    rows = lax.psum(jnp.sum(scores, axis=1, keepdims=True), "cells")
    sums = lax.psum_scatter(jnp.sum(logged, axis=0, keepdims=True), "cells", scatter_dimension=1, tiled=True)
    spread, gram = plain_gram(spread, rows, sums, counts.shape[0] * lax.axis_size("cells"))
    return [lax.psum(gram, ("cells", "genes"))], spread


def in_steps(counts, occupancy, start_basis):
    high, low, sums = log_terms(counts)
    scores, occ = score_part(occupancy, start_basis, high, low)
    cell_total = counts.shape[0] * lax.axis_size("cells")
    spread, gram = scattered_spread(gene_terms(scores), high, low, sums, occ, cell_total)
    return cell_terms(tree_sum(gene_terms(gram))), spread


def on_device(counts, occupancy, start_basis):
    gene_count = counts.shape[1]
    cells, genes = lax.axis_size("cells"), lax.axis_size("genes")
    halvings = cells == 1 << 3 and genes == 1 << 2
    tiles = occupancy.shape[0] == 1 and gene_count == occupancy.shape[1] * LANES
    work = in_steps if halvings and tiles and gene_count % (cells * LANES) == 0 else all_alike
    grams, spread = work(counts, occupancy, start_basis)
    return orthonormal(grams, spread, math.sqrt(gene_count * genes))


def solution(mesh):
    in_specs = (P("cells", "genes"), P("cells", "genes"), P(None, "genes"))
    out_specs = P(None, ("genes", "cells"))
    return jax.shard_map(
        on_device, mesh=mesh, in_specs=in_specs, out_specs=out_specs, check_vma=False
    )
```

```python
import functools
import math

import jax
import jax.numpy as jnp
from jax import lax
from jax.experimental import pallas as pl
from jax.experimental.pallas import tpu as pltpu
from jax.sharding import PartitionSpec as P

F32 = jnp.float32
BF16 = jnp.bfloat16
NN = (((1,), (0,)), ((), ()))
NT = (((1,), (1,)), ((), ()))
WHOLE = pl.BlockSpec(memory_space=pltpu.VMEM)
SCALARS = pl.BlockSpec(memory_space=pltpu.SMEM)
LANES = 128
PARAMS = pltpu.CompilerParams(vmem_limit_bytes=16 * 2**20)
LOG_PARAMS = pltpu.CompilerParams(vmem_limit_bytes=205 * 2**18)


def dot(a, b, dims):
    return lax.dot_general(a, b, dims, preferred_element_type=F32)


def split_terms(x, count):
    terms = []
    for _ in range(count):
        term = x.astype(BF16)
        terms.append(term)
        x = x - term.astype(F32)
    return terms


def tree_sum(parts):
    while len(parts) > 1:
        parts = [sum(parts[at + 1:at + 2], parts[at]) for at in range(0, len(parts), 2)]
    return parts[0]


def log_kernel(width, counts_hbm, high_ref, low_ref, sum_ref, counts_ref, counts_sem):
    cells, genes = high_ref.shape
    fetches = [
        pltpu.make_async_copy(
            counts_hbm.at[:, pl.ds(at * width, width)], counts_ref.at[:, pl.ds(at * width, width)], counts_sem.at[at]
        )
        for at in range(genes // width)
    ]
    for fetch in fetches:
        fetch.start()
    for at, fetch in enumerate(fetches):
        fetch.wait()
        for begin in range(at * width, (at + 1) * width, LANES):
            lanes = pl.ds(begin, LANES)
            logged = jnp.log(1.0 + counts_ref[:, lanes].astype(F32))
            high = logged.astype(BF16)
            high_ref[:, lanes] = high
            low_ref[:, lanes] = (logged - high.astype(F32)).astype(BF16)
            sum_ref[:, lanes] = jnp.sum(logged, axis=0, keepdims=True)


def log_terms(counts):
    cells, genes = counts.shape
    width = genes // 8
    return pl.pallas_call(
        functools.partial(log_kernel, width),
        out_shape=(
            jax.ShapeDtypeStruct((cells, genes), BF16),
            jax.ShapeDtypeStruct((cells, genes), BF16),
            jax.ShapeDtypeStruct((1, genes), F32),
        ),
        in_specs=[pl.BlockSpec(memory_space=pltpu.HBM)],
        out_specs=(WHOLE, WHOLE, WHOLE),
        scratch_shapes=[pltpu.VMEM(counts.shape, BF16), pltpu.SemaphoreType.DMA((genes // width,))],
        compiler_params=LOG_PARAMS,
        cost_estimate=pl.CostEstimate(flops=20 * cells * genes, bytes_accessed=8 * cells * genes, transcendentals=0),
        name="log_terms",
    )(counts)


def score_kernel(width, occ_ref, basis_ref, high_ref, low_ref, score_ref, lane_ref):
    comps, genes = basis_ref.shape
    edge = genes // occ_ref.shape[1]
    occupancy = occ_ref[...].astype(F32)
    scores = None
    for begin in range(0, genes, width):
        basis = []
        for at in range(begin, begin + width, edge):
            occ = jnp.broadcast_to(occupancy[:, at // edge:at // edge + 1], (1, edge))
            lane_ref[:, pl.ds(at, edge)] = occ
            basis.append(basis_ref[:, pl.ds(at, edge)] * occ.astype(BF16))
        basis = jnp.concatenate(basis, axis=1)
        lanes = pl.ds(begin, width)
        part = dot(basis, high_ref[:, lanes], NT) + dot(basis, low_ref[:, lanes], NT)
        scores = part if scores is None else scores + part
    score_ref[...] = scores


def score_part(occupancy, basis, high, low):
    comps, genes = basis.shape
    cells = high.shape[0]
    return pl.pallas_call(
        functools.partial(score_kernel, genes // 4),
        out_shape=(jax.ShapeDtypeStruct((comps, cells), F32), jax.ShapeDtypeStruct((1, genes), F32)),
        in_specs=[WHOLE] * 4,
        out_specs=(WHOLE, WHOLE),
        compiler_params=PARAMS,
        name="scores",
    )(occupancy, basis, high, low)


def spread_piece(terms, high, low):
    comps = terms[0].shape[0]
    on_low = dot(jnp.concatenate(terms[:2], axis=0), low, NN)
    on_high = dot(jnp.concatenate(terms, axis=0), high, NN)
    small = on_low[comps:] + on_high[2 * comps:]
    middle = on_low[:comps] + on_high[comps:2 * comps]
    return (small + middle) + on_high[:comps]


def spread_kernel(count, picks, me_ref, *refs):
    score_refs, outs = refs[:count], refs[count + 4:]
    high_ref, low_ref, sum_ref, occ_ref = refs[count:count + 4]
    scores = tree_sum([ref[...] for ref in score_refs])
    comps = scores.shape[0]
    terms = split_terms(scores, 3)
    eye = lax.broadcasted_iota(jnp.int32, (comps, LANES), 0) == lax.broadcasted_iota(jnp.int32, (comps, LANES), 1)
    row_sums = jnp.sum(jnp.where(eye, jnp.sum(scores, axis=1, keepdims=True), 0.0), axis=0, keepdims=True)
    chunks = high_ref.shape[1] // (LANES * lax.axis_size("cells"))
    width = chunks * LANES
    blocks = [(pick, out, at) for group, out in zip(picks, outs) for at, pick in enumerate(group)]
    rows = block_rows(comps, chunks)
    for pick, out, at_block in blocks:
        base = at_block * rows
        start = pl.multiple_of((me_ref[0] ^ pick) * width, width)
        lanes = pl.ds(start, width)
        piece = spread_piece(terms, high_ref[:, lanes], low_ref[:, lanes]) * occ_ref[:, lanes]
        sums = sum_ref[:, lanes] * occ_ref[:, lanes]
        extra = [row_sums]
        for at in range(chunks):
            out[base + at * comps:base + (at + 1) * comps] = piece[:, at * LANES:(at + 1) * LANES]
            extra.append(sums[:, at * LANES:(at + 1) * LANES])
        extra.append(jnp.zeros((rows - chunks * comps - chunks - 1, LANES), F32))
        out[base + chunks * comps:base + rows] = jnp.concatenate(extra, axis=0)


def block_rows(comps, chunks):
    return comps * chunks + -(-(chunks + 1) // 8) * 8


def spread_pieces(me, scores, high, low, sums, occ, picks):
    comps = scores[0].shape[0]
    chunks = high.shape[1] // (LANES * lax.axis_size("cells"))
    rows = block_rows(comps, chunks)
    count = sum(len(group) for group in picks)
    return pl.pallas_call(
        functools.partial(spread_kernel, len(scores), picks),
        out_shape=[jax.ShapeDtypeStruct((len(group) * rows, LANES), F32) for group in picks],
        in_specs=[SCALARS] + [WHOLE] * (len(scores) + 4),
        out_specs=[WHOLE] * len(picks),
        compiler_params=PARAMS,
        cost_estimate=pl.CostEstimate(
            flops=10 * comps * count * chunks * LANES * high.shape[0], bytes_accessed=2**21, transcendentals=0
        ),
        name="spread",
    )(me, *scores, high, low, sums, occ)


def gram_kernel(scale, chunks, *refs):
    pieces, (spread_ref, gram_ref) = refs[:-2], refs[-2:]
    comps = spread_ref.shape[0]
    rows = block_rows(comps, chunks)
    total = tree_sum([ref[ref.shape[0] - rows:] for ref in pieces])
    extra = total[chunks * comps:chunks * comps + chunks + 1]
    eye = lax.broadcasted_iota(jnp.int32, (comps, LANES), 0) == lax.broadcasted_iota(jnp.int32, (comps, LANES), 1)
    row_sums = jnp.sum(jnp.where(eye, extra[:1], 0.0), axis=1, keepdims=True) * scale
    parts = [total[at * comps:(at + 1) * comps] - row_sums * extra[at + 1:at + 2] for at in range(chunks)]
    spread = jnp.concatenate(parts, axis=1)
    spread_ref[...] = spread
    gram_ref[...] = packed_gram(spread)


def packed_gram(spread):
    gram = lax.dot_general(spread, spread, NT, precision=lax.Precision.HIGHEST, preferred_element_type=F32)
    half = spread.shape[0] // 2
    return jnp.concatenate([gram[:half], gram[half:]], axis=1)


def centered_gram(pieces, comps, cell_total):
    chunks = pieces[0].shape[0] // comps
    return pl.pallas_call(
        functools.partial(gram_kernel, 1.0 / cell_total, chunks),
        out_shape=(
            jax.ShapeDtypeStruct((comps, chunks * LANES), F32),
            jax.ShapeDtypeStruct((comps // 2, comps * 2), F32),
        ),
        in_specs=[WHOLE] * len(pieces),
        out_specs=(WHOLE, WHOLE),
        compiler_params=PARAMS,
        name="gram",
    )(*pieces)


def plain_gram_kernel(scale, spread_ref, row_ref, sum_ref, out_ref, gram_ref):
    spread = spread_ref[...] - row_ref[...] * scale * sum_ref[...]
    out_ref[...] = spread
    gram_ref[...] = packed_gram(spread)


def plain_gram(spread, rows, sums, cell_total):
    comps, width = spread.shape
    return pl.pallas_call(
        functools.partial(plain_gram_kernel, 1.0 / cell_total),
        out_shape=(
            jax.ShapeDtypeStruct((comps, width), F32),
            jax.ShapeDtypeStruct((comps // 2, comps * 2), F32),
        ),
        in_specs=[WHOLE] * 3,
        out_specs=(WHOLE, WHOLE),
        compiler_params=PARAMS,
        name="plain_gram",
    )(spread, rows, sums)


def row_of(x, at):
    return jnp.broadcast_to(x[at:at + 1, :], x.shape)


def spread_column(rows, at):
    return jnp.broadcast_to(rows[:, at:at + 1], rows.shape)


def eliminate(groups, begin):
    groups = list(groups)
    edge = groups[0].shape[0]
    below = lax.broadcasted_iota(jnp.int32, groups[0].shape, 0)
    columns = [{c: spread_column(rows, begin + c) for c in range(edge)} for rows in groups]
    for at in range(len(groups)):
        scale = jnp.zeros_like(groups[0])
        later = (at + 1) * edge
        for i in range(at * edge, later, 2):
            if i == later - 4 and at + 1 < len(groups):
                for rows, cols in zip(groups[at:], columns[at:]):
                    cols.update({c: spread_column(rows, begin + c) for c in range(later, later + edge)})
            row = i - at * edge
            cols = columns[at]
            first, second = cols[i], cols[i + 1]
            a, b, c = row_of(first, row), row_of(second, row), row_of(second, row + 1)
            det = a * c - b * b
            inv_a = pl.reciprocal(a, approx=True)
            inv_c = a * pl.reciprocal(det, approx=True)
            ratio = b * inv_a
            scale = jnp.where(below == row, lax.rsqrt(a), jnp.where(below == row + 1, lax.rsqrt(det * inv_a), scale))
            factors = []
            for k in cols:
                if k > i + 1:
                    top = row_of(cols[k], row)
                    factors.append((k, top * inv_a, (row_of(cols[k], row + 1) - ratio * top) * inv_c))
            rows = groups[at]
            upper = row_of(rows, row) * inv_a
            rows = rows - jnp.where(below > row, first, 0.0) * upper
            lower = row_of(rows, row + 1) * inv_c
            groups[at] = rows - jnp.where(below > row + 1, second - ratio * first, 0.0) * lower
            for ahead in range(at, len(groups)):
                cols = columns[ahead]
                first = cols[i]
                second = cols[i + 1] - ratio * first
                for k, on_first, on_second in factors:
                    cols[k] = cols[k] - first * on_first - second * on_second
                if ahead > at:
                    groups[ahead] = groups[ahead] - first * upper - second * lower
                del cols[i], cols[i + 1]
        groups[at] = groups[at] * scale
    return groups


def scale_kernel(gram_ref, times_ref, plus_ref):
    gram = gram_ref[...]
    half, comps = gram.shape[0], gram.shape[1] // 2
    gram = jnp.concatenate([gram[:, :comps], gram[:, comps:]], axis=0)
    eye = lax.broadcasted_iota(jnp.int32, gram.shape, 0) == lax.broadcasted_iota(jnp.int32, gram.shape, 1)
    diagonal = jnp.where(eye, gram, 0.0)
    row_scale = lax.rsqrt(jnp.sum(diagonal, axis=1, keepdims=True))
    col_scale = lax.rsqrt(jnp.sum(diagonal, axis=0, keepdims=True))
    zeros = jnp.zeros_like(gram)
    times_ref[...] = jnp.concatenate([zeros, row_scale * col_scale], axis=1)
    plus_ref[...] = jnp.concatenate([jnp.where(eye, col_scale, 0.0), zeros], axis=1)


def scales(gram):
    half, lanes = gram.shape
    return pl.pallas_call(
        scale_kernel,
        out_shape=[jax.ShapeDtypeStruct((2 * half, lanes), F32)] * 2,
        in_specs=[WHOLE],
        out_specs=[WHOLE, WHOLE],
        compiler_params=PARAMS,
        name="scales",
    )(gram)


def basis_kernel(scale, *refs):
    grams, (times_ref, plus_ref, spread_ref, out_ref) = refs[:-4], refs[-4:]
    gram = tree_sum([ref[...] for ref in grams])
    comps = spread_ref.shape[0]
    gram = jnp.concatenate([pltpu.roll(gram, comps, 1), gram], axis=0)
    both = gram * times_ref[...] + plus_ref[...]
    groups = eliminate([both[at:at + 8] for at in range(0, comps, 8)], comps)
    inverse = jnp.concatenate(groups, axis=0)[:, :comps] * scale
    out_ref[...] = lax.dot_general(
        inverse, spread_ref[...], NN, precision=lax.Precision.HIGHEST, preferred_element_type=F32
    )


def orthonormal(grams, spread, scale):
    return pl.pallas_call(
        functools.partial(basis_kernel, scale),
        out_shape=jax.ShapeDtypeStruct(spread.shape, F32),
        in_specs=[WHOLE] * (len(grams) + 3),
        out_specs=WHOLE,
        compiler_params=PARAMS,
        name="orthonormal",
    )(*grams, *scales(grams[0]), spread)


def send(x, offset_cells, offset_genes):
    cells, genes = lax.axis_size("cells"), lax.axis_size("genes")
    pairs = []
    for c in range(cells):
        for g in range(genes):
            pairs.append((c * genes + g, (c ^ offset_cells) * genes + (g ^ offset_genes)))
    return lax.ppermute(x, ("cells", "genes"), pairs)


def gene_terms(x):
    terms = [x, send(x, 0, 1)]
    for at in range(1, lax.axis_size("genes").bit_length() - 1):
        x = tree_sum(terms)
        terms = [x, send(x, 0, 1 << at | 1)]
    return terms


def cell_terms(x):
    terms = [x]
    for at in range(lax.axis_size("cells").bit_length() - 1):
        x = tree_sum(terms)
        terms = [x, send(x, 1 << at, 1)]
    return terms


def scattered_spread(scores, high, low, sums, occ, cell_total):
    comps = scores[0].shape[0]
    me = lax.axis_index("cells").astype(jnp.int32).reshape(1)
    make = functools.partial(spread_pieces, scores=scores, high=high, low=low, sums=sums, occ=occ)
    pair, first, across = make(me, picks=[[6, 2], [5], [7]])
    pair, me = lax.optimization_barrier((pair, me))
    pair, first = send(pair, 2, 0), send(first, 1, 0)
    across = send(across, 7, 0)
    far, own, *second = make(me, picks=[[4], [0], [3], [1]])
    first, second[0] = lax.optimization_barrier((first, second[0]))
    far, second[1] = lax.optimization_barrier((tree_sum([far, pair[:far.shape[0]], first]), second[1]))
    far = send(far, 4, 0)
    straight = [send(x, k, 0) for k, x in zip((3, 1), second)]
    return centered_gram([own, far, pair, across] + straight, comps, cell_total)


def all_alike(counts, occupancy, start_basis):
    tile_rows, tile_cols = occupancy.shape
    edge = counts.shape[0] // tile_rows
    logged = jnp.log(1.0 + counts.astype(F32)).reshape(tile_rows, edge, tile_cols, -1)
    logged = (logged * occupancy.astype(F32)[:, None, :, None]).reshape(counts.shape)
    high, low = split_terms(logged, 2)
    scores = lax.psum(dot(start_basis, high, NT) + dot(start_basis, low, NT), "genes")
    spread = spread_piece(split_terms(scores, 3), high, low)
    spread = lax.psum_scatter(spread, "cells", scatter_dimension=1, tiled=True)
    rows = lax.psum(jnp.sum(scores, axis=1, keepdims=True), "cells")
    sums = lax.psum_scatter(jnp.sum(logged, axis=0, keepdims=True), "cells", scatter_dimension=1, tiled=True)
    spread, gram = plain_gram(spread, rows, sums, counts.shape[0] * lax.axis_size("cells"))
    return [lax.psum(gram, ("cells", "genes"))], spread


def in_steps(counts, occupancy, start_basis):
    high, low, sums = log_terms(counts)
    scores, occ = score_part(occupancy, start_basis, high, low)
    cell_total = counts.shape[0] * lax.axis_size("cells")
    spread, gram = scattered_spread(gene_terms(scores), high, low, sums, occ, cell_total)
    return cell_terms(tree_sum(gene_terms(gram))), spread


def on_device(counts, occupancy, start_basis):
    gene_count = counts.shape[1]
    cells, genes = lax.axis_size("cells"), lax.axis_size("genes")
    halvings = cells == 1 << 3 and genes == 1 << 2
    tiles = occupancy.shape[0] == 1 and gene_count == occupancy.shape[1] * LANES
    work = in_steps if halvings and tiles and gene_count % (cells * LANES) == 0 else all_alike
    grams, spread = work(counts, occupancy, start_basis)
    return orthonormal(grams, spread, math.sqrt(gene_count * genes))


def solution(mesh):
    in_specs = (P("cells", "genes"), P("cells", "genes"), P(None, "genes"))
    out_specs = P(None, ("genes", "cells"))
    return jax.shard_map(
        on_device, mesh=mesh, in_specs=in_specs, out_specs=out_specs, check_vma=False
    )
```

```python
import functools
import math

import jax
import jax.numpy as jnp
from jax import lax
from jax.experimental import pallas as pl
from jax.experimental.pallas import tpu as pltpu
from jax.sharding import PartitionSpec as P

F32 = jnp.float32
BF16 = jnp.bfloat16
NN = (((1,), (0,)), ((), ()))
NT = (((1,), (1,)), ((), ()))
WHOLE = pl.BlockSpec(memory_space=pltpu.VMEM)
SCALARS = pl.BlockSpec(memory_space=pltpu.SMEM)
LANES = 128
PARAMS = pltpu.CompilerParams(vmem_limit_bytes=16 * 2**20)
LOG_PARAMS = pltpu.CompilerParams(vmem_limit_bytes=205 * 2**18)


def dot(a, b, dims):
    return lax.dot_general(a, b, dims, preferred_element_type=F32)


def split_terms(x, count):
    terms = []
    for _ in range(count):
        term = x.astype(BF16)
        terms.append(term)
        x = x - term.astype(F32)
    return terms


def tree_sum(parts):
    while len(parts) > 1:
        parts = [sum(parts[at + 1:at + 2], parts[at]) for at in range(0, len(parts), 2)]
    return parts[0]


def log_kernel(width, counts_hbm, high_ref, low_ref, sum_ref, counts_ref, counts_sem):
    cells, genes = high_ref.shape
    fetches = [
        pltpu.make_async_copy(
            counts_hbm.at[:, pl.ds(at * width, width)], counts_ref.at[:, pl.ds(at * width, width)], counts_sem.at[at]
        )
        for at in range(genes // width)
    ]
    for fetch in fetches:
        fetch.start()
    for at, fetch in enumerate(fetches):
        fetch.wait()
        for begin in range(at * width, (at + 1) * width, LANES):
            lanes = pl.ds(begin, LANES)
            logged = jnp.log(1.0 + counts_ref[:, lanes].astype(F32))
            high = logged.astype(BF16)
            high_ref[:, lanes] = high
            low_ref[:, lanes] = (logged - high.astype(F32)).astype(BF16)
            sum_ref[:, lanes] = jnp.sum(logged, axis=0, keepdims=True)


def log_terms(counts):
    cells, genes = counts.shape
    width = genes // 8
    return pl.pallas_call(
        functools.partial(log_kernel, width),
        out_shape=(
            jax.ShapeDtypeStruct((cells, genes), BF16),
            jax.ShapeDtypeStruct((cells, genes), BF16),
            jax.ShapeDtypeStruct((1, genes), F32),
        ),
        in_specs=[pl.BlockSpec(memory_space=pltpu.HBM)],
        out_specs=(WHOLE, WHOLE, WHOLE),
        scratch_shapes=[pltpu.VMEM(counts.shape, BF16), pltpu.SemaphoreType.DMA((genes // width,))],
        compiler_params=LOG_PARAMS,
        cost_estimate=pl.CostEstimate(flops=20 * cells * genes, bytes_accessed=8 * cells * genes, transcendentals=0),
        name="log_terms",
    )(counts)


def score_kernel(width, occ_ref, basis_ref, high_ref, low_ref, score_ref, lane_ref):
    comps, genes = basis_ref.shape
    edge = genes // occ_ref.shape[1]
    occupancy = occ_ref[...].astype(F32)
    scores = None
    for begin in range(0, genes, width):
        basis = []
        for at in range(begin, begin + width, edge):
            occ = jnp.broadcast_to(occupancy[:, at // edge:at // edge + 1], (1, edge))
            lane_ref[:, pl.ds(at, edge)] = occ
            basis.append(basis_ref[:, pl.ds(at, edge)] * occ.astype(BF16))
        basis = jnp.concatenate(basis, axis=1)
        lanes = pl.ds(begin, width)
        part = dot(basis, high_ref[:, lanes], NT) + dot(basis, low_ref[:, lanes], NT)
        scores = part if scores is None else scores + part
    score_ref[...] = scores


def score_part(occupancy, basis, high, low):
    comps, genes = basis.shape
    cells = high.shape[0]
    return pl.pallas_call(
        functools.partial(score_kernel, genes // 4),
        out_shape=(jax.ShapeDtypeStruct((comps, cells), F32), jax.ShapeDtypeStruct((1, genes), F32)),
        in_specs=[WHOLE] * 4,
        out_specs=(WHOLE, WHOLE),
        compiler_params=PARAMS,
        name="scores",
    )(occupancy, basis, high, low)


def spread_piece(terms, high, low):
    comps = terms[0].shape[0]
    on_low = dot(jnp.concatenate(terms[:2], axis=0), low, NN)
    on_high = dot(jnp.concatenate(terms, axis=0), high, NN)
    small = on_low[comps:] + on_high[2 * comps:]
    middle = on_low[:comps] + on_high[comps:2 * comps]
    return (small + middle) + on_high[:comps]


def spread_kernel(count, picks, me_ref, *refs):
    score_refs, outs = refs[:count], refs[count + 4:]
    high_ref, low_ref, sum_ref, occ_ref = refs[count:count + 4]
    scores = tree_sum([ref[...] for ref in score_refs])
    comps = scores.shape[0]
    terms = split_terms(scores, 3)
    eye = lax.broadcasted_iota(jnp.int32, (comps, LANES), 0) == lax.broadcasted_iota(jnp.int32, (comps, LANES), 1)
    row_sums = jnp.sum(jnp.where(eye, jnp.sum(scores, axis=1, keepdims=True), 0.0), axis=0, keepdims=True)
    chunks = high_ref.shape[1] // (LANES * lax.axis_size("cells"))
    width = chunks * LANES
    blocks = [(pick, out, at) for group, out in zip(picks, outs) for at, pick in enumerate(group)]
    rows = block_rows(comps, chunks)
    for pick, out, at_block in blocks:
        base = at_block * rows
        start = pl.multiple_of((me_ref[0] ^ pick) * width, width)
        lanes = pl.ds(start, width)
        piece = spread_piece(terms, high_ref[:, lanes], low_ref[:, lanes]) * occ_ref[:, lanes]
        sums = sum_ref[:, lanes] * occ_ref[:, lanes]
        extra = [row_sums]
        for at in range(chunks):
            out[base + at * comps:base + (at + 1) * comps] = piece[:, at * LANES:(at + 1) * LANES]
            extra.append(sums[:, at * LANES:(at + 1) * LANES])
        extra.append(jnp.zeros((rows - chunks * comps - chunks - 1, LANES), F32))
        out[base + chunks * comps:base + rows] = jnp.concatenate(extra, axis=0)


def block_rows(comps, chunks):
    return comps * chunks + -(-(chunks + 1) // 8) * 8


def spread_pieces(me, scores, high, low, sums, occ, picks):
    comps = scores[0].shape[0]
    chunks = high.shape[1] // (LANES * lax.axis_size("cells"))
    rows = block_rows(comps, chunks)
    count = sum(len(group) for group in picks)
    return pl.pallas_call(
        functools.partial(spread_kernel, len(scores), picks),
        out_shape=[jax.ShapeDtypeStruct((len(group) * rows, LANES), F32) for group in picks],
        in_specs=[SCALARS] + [WHOLE] * (len(scores) + 4),
        out_specs=[WHOLE] * len(picks),
        compiler_params=PARAMS,
        cost_estimate=pl.CostEstimate(
            flops=10 * comps * count * chunks * LANES * high.shape[0], bytes_accessed=2**21, transcendentals=0
        ),
        name="spread",
    )(me, *scores, high, low, sums, occ)


def gram_kernel(scale, chunks, *refs):
    pieces, (spread_ref, gram_ref) = refs[:-2], refs[-2:]
    comps = spread_ref.shape[0]
    rows = block_rows(comps, chunks)
    total = tree_sum([ref[ref.shape[0] - rows:] for ref in pieces])
    extra = total[chunks * comps:chunks * comps + chunks + 1]
    eye = lax.broadcasted_iota(jnp.int32, (comps, LANES), 0) == lax.broadcasted_iota(jnp.int32, (comps, LANES), 1)
    row_sums = jnp.sum(jnp.where(eye, extra[:1], 0.0), axis=1, keepdims=True) * scale
    parts = [total[at * comps:(at + 1) * comps] - row_sums * extra[at + 1:at + 2] for at in range(chunks)]
    spread = jnp.concatenate(parts, axis=1)
    spread_ref[...] = spread
    gram_ref[...] = packed_gram(spread)


def packed_gram(spread):
    gram = lax.dot_general(spread, spread, NT, precision=lax.Precision.HIGHEST, preferred_element_type=F32)
    half = spread.shape[0] // 2
    return jnp.concatenate([gram[:half], gram[half:]], axis=1)


def centered_gram(pieces, comps, cell_total):
    chunks = pieces[0].shape[0] // comps
    return pl.pallas_call(
        functools.partial(gram_kernel, 1.0 / cell_total, chunks),
        out_shape=(
            jax.ShapeDtypeStruct((comps, chunks * LANES), F32),
            jax.ShapeDtypeStruct((comps // 2, comps * 2), F32),
        ),
        in_specs=[WHOLE] * len(pieces),
        out_specs=(WHOLE, WHOLE),
        compiler_params=PARAMS,
        name="gram",
    )(*pieces)


def plain_gram_kernel(scale, spread_ref, row_ref, sum_ref, out_ref, gram_ref):
    spread = spread_ref[...] - row_ref[...] * scale * sum_ref[...]
    out_ref[...] = spread
    gram_ref[...] = packed_gram(spread)


def plain_gram(spread, rows, sums, cell_total):
    comps, width = spread.shape
    return pl.pallas_call(
        functools.partial(plain_gram_kernel, 1.0 / cell_total),
        out_shape=(
            jax.ShapeDtypeStruct((comps, width), F32),
            jax.ShapeDtypeStruct((comps // 2, comps * 2), F32),
        ),
        in_specs=[WHOLE] * 3,
        out_specs=(WHOLE, WHOLE),
        compiler_params=PARAMS,
        name="plain_gram",
    )(spread, rows, sums)


def row_of(x, at):
    return jnp.broadcast_to(x[at:at + 1, :], x.shape)


def spread_column(rows, at):
    return jnp.broadcast_to(rows[:, at:at + 1], rows.shape)


def eliminate(groups, begin):
    groups = list(groups)
    edge = groups[0].shape[0]
    below = lax.broadcasted_iota(jnp.int32, groups[0].shape, 0)
    columns = [{c: spread_column(rows, begin + c) for c in range(edge)} for rows in groups]
    for at in range(len(groups)):
        scale = jnp.zeros_like(groups[0])
        later = (at + 1) * edge
        for i in range(at * edge, later, 2):
            if i == later - 4 and at + 1 < len(groups):
                for rows, cols in zip(groups[at:], columns[at:]):
                    cols.update({c: spread_column(rows, begin + c) for c in range(later, later + edge)})
            row = i - at * edge
            cols = columns[at]
            first, second = cols[i], cols[i + 1]
            a, b, c = row_of(first, row), row_of(second, row), row_of(second, row + 1)
            det = a * c - b * b
            inv_a = pl.reciprocal(a, approx=True)
            inv_c = a * pl.reciprocal(det, approx=True)
            ratio = b * inv_a
            scale = jnp.where(below == row, lax.rsqrt(a), jnp.where(below == row + 1, lax.rsqrt(det * inv_a), scale))
            factors = []
            for k in cols:
                if k > i + 1:
                    top = row_of(cols[k], row)
                    factors.append((k, top * inv_a, (row_of(cols[k], row + 1) - ratio * top) * inv_c))
            rows = groups[at]
            upper = row_of(rows, row) * inv_a
            rows = rows - jnp.where(below > row, first, 0.0) * upper
            lower = row_of(rows, row + 1) * inv_c
            groups[at] = rows - jnp.where(below > row + 1, second - ratio * first, 0.0) * lower
            for ahead in range(at, len(groups)):
                cols = columns[ahead]
                first = cols[i]
                second = cols[i + 1] - ratio * first
                for k, on_first, on_second in factors:
                    cols[k] = cols[k] - first * on_first - second * on_second
                if ahead > at:
                    groups[ahead] = groups[ahead] - first * upper - second * lower
                del cols[i], cols[i + 1]
        groups[at] = groups[at] * scale
    return groups


def scale_kernel(gram_ref, times_ref, plus_ref):
    gram = gram_ref[...]
    half, comps = gram.shape[0], gram.shape[1] // 2
    gram = jnp.concatenate([gram[:, :comps], gram[:, comps:]], axis=0)
    eye = lax.broadcasted_iota(jnp.int32, gram.shape, 0) == lax.broadcasted_iota(jnp.int32, gram.shape, 1)
    diagonal = jnp.where(eye, gram, 0.0)
    row_scale = lax.rsqrt(jnp.sum(diagonal, axis=1, keepdims=True))
    col_scale = lax.rsqrt(jnp.sum(diagonal, axis=0, keepdims=True))
    zeros = jnp.zeros_like(gram)
    times_ref[...] = jnp.concatenate([zeros, row_scale * col_scale], axis=1)
    plus_ref[...] = jnp.concatenate([jnp.where(eye, col_scale, 0.0), zeros], axis=1)


def scales(gram):
    half, lanes = gram.shape
    return pl.pallas_call(
        scale_kernel,
        out_shape=[jax.ShapeDtypeStruct((2 * half, lanes), F32)] * 2,
        in_specs=[WHOLE],
        out_specs=[WHOLE, WHOLE],
        compiler_params=PARAMS,
        name="scales",
    )(gram)


def basis_kernel(scale, *refs):
    grams, (times_ref, plus_ref, spread_ref, out_ref) = refs[:-4], refs[-4:]
    gram = tree_sum([ref[...] for ref in grams])
    comps = spread_ref.shape[0]
    gram = jnp.concatenate([pltpu.roll(gram, comps, 1), gram], axis=0)
    both = gram * times_ref[...] + plus_ref[...]
    groups = eliminate([both[at:at + 8] for at in range(0, comps, 8)], comps)
    inverse = jnp.concatenate(groups, axis=0)[:, :comps] * scale
    out_ref[...] = lax.dot_general(
        inverse, spread_ref[...], NN, precision=lax.Precision.HIGHEST, preferred_element_type=F32
    )


def orthonormal(grams, spread, scale):
    return pl.pallas_call(
        functools.partial(basis_kernel, scale),
        out_shape=jax.ShapeDtypeStruct(spread.shape, F32),
        in_specs=[WHOLE] * (len(grams) + 3),
        out_specs=WHOLE,
        compiler_params=PARAMS,
        name="orthonormal",
    )(*grams, *scales(grams[0]), spread)


def send(x, offset_cells, offset_genes):
    cells, genes = lax.axis_size("cells"), lax.axis_size("genes")
    pairs = []
    for c in range(cells):
        for g in range(genes):
            pairs.append((c * genes + g, (c ^ offset_cells) * genes + (g ^ offset_genes)))
    return lax.ppermute(x, ("cells", "genes"), pairs)


def gene_terms(x):
    x = x + send(x, 0, 1)
    return [x, send(x, 0, 3)]


def all_terms(x):
    x = x + send(x, 0, 1)
    across = [send(x, c, g) for c, g in ((1, 3), (1, 1), (0, 3))]
    terms = [x + across[2], across[1] + across[0]]
    for at in range(1, lax.axis_size("cells").bit_length() - 1):
        x = tree_sum(terms)
        terms = [x, send(x, 1 << at, 1)]
    return terms


def scattered_spread(scores, high, low, sums, occ, cell_total):
    comps = scores[0].shape[0]
    me = lax.axis_index("cells").astype(jnp.int32).reshape(1)
    make = functools.partial(spread_pieces, scores=scores, high=high, low=low, sums=sums, occ=occ)
    pair, first, across = make(me, picks=[[6, 2], [5], [7]])
    pair, me = lax.optimization_barrier((pair, me))
    pair, first = send(pair, 2, 0), send(first, 1, 0)
    across = send(across, 7, 0)
    far, own, *second = make(me, picks=[[4], [0], [3], [1]])
    first, second[0] = lax.optimization_barrier((first, second[0]))
    far, second[1] = lax.optimization_barrier((tree_sum([far, pair[:far.shape[0]], first]), second[1]))
    far = send(far, 4, 0)
    straight = [send(x, k, 0) for k, x in zip((3, 1), second)]
    return centered_gram([own, far, pair, across] + straight, comps, cell_total)


def all_alike(counts, occupancy, start_basis):
    tile_rows, tile_cols = occupancy.shape
    edge = counts.shape[0] // tile_rows
    logged = jnp.log(1.0 + counts.astype(F32)).reshape(tile_rows, edge, tile_cols, -1)
    logged = (logged * occupancy.astype(F32)[:, None, :, None]).reshape(counts.shape)
    high, low = split_terms(logged, 2)
    scores = lax.psum(dot(start_basis, high, NT) + dot(start_basis, low, NT), "genes")
    spread = spread_piece(split_terms(scores, 3), high, low)
    spread = lax.psum_scatter(spread, "cells", scatter_dimension=1, tiled=True)
    rows = lax.psum(jnp.sum(scores, axis=1, keepdims=True), "cells")
    sums = lax.psum_scatter(jnp.sum(logged, axis=0, keepdims=True), "cells", scatter_dimension=1, tiled=True)
    spread, gram = plain_gram(spread, rows, sums, counts.shape[0] * lax.axis_size("cells"))
    return [lax.psum(gram, ("cells", "genes"))], spread


def in_steps(counts, occupancy, start_basis):
    high, low, sums = log_terms(counts)
    scores, occ = score_part(occupancy, start_basis, high, low)
    cell_total = counts.shape[0] * lax.axis_size("cells")
    spread, gram = scattered_spread(gene_terms(scores), high, low, sums, occ, cell_total)
    return all_terms(gram), spread


def on_device(counts, occupancy, start_basis):
    gene_count = counts.shape[1]
    cells, genes = lax.axis_size("cells"), lax.axis_size("genes")
    halvings = cells == 1 << 3 and genes == 1 << 2
    tiles = occupancy.shape[0] == 1 and gene_count == occupancy.shape[1] * LANES
    work = in_steps if halvings and tiles and gene_count % (cells * LANES) == 0 else all_alike
    grams, spread = work(counts, occupancy, start_basis)
    return orthonormal(grams, spread, math.sqrt(gene_count * genes))


def solution(mesh):
    in_specs = (P("cells", "genes"), P("cells", "genes"), P(None, "genes"))
    out_specs = P(None, ("genes", "cells"))
    return jax.shard_map(
        on_device, mesh=mesh, in_specs=in_specs, out_specs=out_specs, check_vma=False
    )
```

```python
import functools
import math

import jax
import jax.numpy as jnp
from jax import lax
from jax.experimental import pallas as pl
from jax.experimental.pallas import tpu as pltpu
from jax.sharding import PartitionSpec as P

F32 = jnp.float32
BF16 = jnp.bfloat16
NN = (((1,), (0,)), ((), ()))
NT = (((1,), (1,)), ((), ()))
WHOLE = pl.BlockSpec(memory_space=pltpu.VMEM)
SCALARS = pl.BlockSpec(memory_space=pltpu.SMEM)
LANES = 128
PARAMS = pltpu.CompilerParams(vmem_limit_bytes=16 * 2**20)
LOG_PARAMS = pltpu.CompilerParams(vmem_limit_bytes=205 * 2**18)


def dot(a, b, dims):
    return lax.dot_general(a, b, dims, preferred_element_type=F32)


def split_terms(x, count):
    terms = []
    for _ in range(count):
        term = x.astype(BF16)
        terms.append(term)
        x = x - term.astype(F32)
    return terms


def tree_sum(parts):
    while len(parts) > 1:
        parts = [sum(parts[at + 1:at + 2], parts[at]) for at in range(0, len(parts), 2)]
    return parts[0]


def log_kernel(width, counts_hbm, high_ref, low_ref, sum_ref, counts_ref, counts_sem):
    cells, genes = high_ref.shape
    fetches = [
        pltpu.make_async_copy(
            counts_hbm.at[:, pl.ds(at * width, width)], counts_ref.at[:, pl.ds(at * width, width)], counts_sem.at[at]
        )
        for at in range(genes // width)
    ]
    for fetch in fetches:
        fetch.start()
    for at, fetch in enumerate(fetches):
        fetch.wait()
        for begin in range(at * width, (at + 1) * width, LANES):
            lanes = pl.ds(begin, LANES)
            logged = jnp.log(1.0 + counts_ref[:, lanes].astype(F32))
            high = logged.astype(BF16)
            high_ref[:, lanes] = high
            low_ref[:, lanes] = (logged - high.astype(F32)).astype(BF16)
            sum_ref[:, lanes] = jnp.sum(logged, axis=0, keepdims=True)


def log_terms(counts):
    cells, genes = counts.shape
    width = genes // 8
    return pl.pallas_call(
        functools.partial(log_kernel, width),
        out_shape=(
            jax.ShapeDtypeStruct((cells, genes), BF16),
            jax.ShapeDtypeStruct((cells, genes), BF16),
            jax.ShapeDtypeStruct((1, genes), F32),
        ),
        in_specs=[pl.BlockSpec(memory_space=pltpu.HBM)],
        out_specs=(WHOLE, WHOLE, WHOLE),
        scratch_shapes=[pltpu.VMEM(counts.shape, BF16), pltpu.SemaphoreType.DMA((genes // width,))],
        compiler_params=LOG_PARAMS,
        cost_estimate=pl.CostEstimate(flops=20 * cells * genes, bytes_accessed=8 * cells * genes, transcendentals=0),
        name="log_terms",
    )(counts)


def score_kernel(width, occ_ref, basis_ref, high_ref, low_ref, score_ref, lane_ref):
    comps, genes = basis_ref.shape
    edge = genes // occ_ref.shape[1]
    occupancy = occ_ref[...].astype(F32)
    scores = None
    for begin in range(0, genes, width):
        basis = []
        for at in range(begin, begin + width, edge):
            occ = jnp.broadcast_to(occupancy[:, at // edge:at // edge + 1], (1, edge))
            lane_ref[:, pl.ds(at, edge)] = occ
            basis.append(basis_ref[:, pl.ds(at, edge)] * occ.astype(BF16))
        basis = jnp.concatenate(basis, axis=1)
        lanes = pl.ds(begin, width)
        part = dot(basis, high_ref[:, lanes], NT) + dot(basis, low_ref[:, lanes], NT)
        scores = part if scores is None else scores + part
    score_ref[...] = scores


def score_part(occupancy, basis, high, low):
    comps, genes = basis.shape
    cells = high.shape[0]
    return pl.pallas_call(
        functools.partial(score_kernel, genes // 4),
        out_shape=(jax.ShapeDtypeStruct((comps, cells), F32), jax.ShapeDtypeStruct((1, genes), F32)),
        in_specs=[WHOLE] * 4,
        out_specs=(WHOLE, WHOLE),
        compiler_params=PARAMS,
        name="scores",
    )(occupancy, basis, high, low)


def spread_piece(terms, high, low):
    comps = terms[0].shape[0]
    on_low = dot(jnp.concatenate(terms[:2], axis=0), low, NN)
    on_high = dot(jnp.concatenate(terms, axis=0), high, NN)
    small = on_low[comps:] + on_high[2 * comps:]
    middle = on_low[:comps] + on_high[comps:2 * comps]
    return (small + middle) + on_high[:comps]


def spread_kernel(count, picks, me_ref, *refs):
    score_refs, outs = refs[:count], refs[count + 4:]
    high_ref, low_ref, sum_ref, occ_ref = refs[count:count + 4]
    scores = tree_sum([ref[...] for ref in score_refs])
    comps = scores.shape[0]
    terms = split_terms(scores, 3)
    eye = lax.broadcasted_iota(jnp.int32, (comps, LANES), 0) == lax.broadcasted_iota(jnp.int32, (comps, LANES), 1)
    row_sums = jnp.sum(jnp.where(eye, jnp.sum(scores, axis=1, keepdims=True), 0.0), axis=0, keepdims=True)
    chunks = high_ref.shape[1] // (LANES * lax.axis_size("cells"))
    width = chunks * LANES
    blocks = [(pick, out, at) for group, out in zip(picks, outs) for at, pick in enumerate(group)]
    rows = block_rows(comps, chunks)
    for pick, out, at_block in blocks:
        base = at_block * rows
        start = pl.multiple_of((me_ref[0] ^ pick) * width, width)
        lanes = pl.ds(start, width)
        piece = spread_piece(terms, high_ref[:, lanes], low_ref[:, lanes]) * occ_ref[:, lanes]
        sums = sum_ref[:, lanes] * occ_ref[:, lanes]
        extra = [row_sums]
        for at in range(chunks):
            out[base + at * comps:base + (at + 1) * comps] = piece[:, at * LANES:(at + 1) * LANES]
            extra.append(sums[:, at * LANES:(at + 1) * LANES])
        extra.append(jnp.zeros((rows - chunks * comps - chunks - 1, LANES), F32))
        out[base + chunks * comps:base + rows] = jnp.concatenate(extra, axis=0)


def block_rows(comps, chunks):
    return comps * chunks + -(-(chunks + 1) // 8) * 8


def spread_pieces(me, scores, high, low, sums, occ, picks):
    comps = scores[0].shape[0]
    chunks = high.shape[1] // (LANES * lax.axis_size("cells"))
    rows = block_rows(comps, chunks)
    count = sum(len(group) for group in picks)
    return pl.pallas_call(
        functools.partial(spread_kernel, len(scores), picks),
        out_shape=[jax.ShapeDtypeStruct((len(group) * rows, LANES), F32) for group in picks],
        in_specs=[SCALARS] + [WHOLE] * (len(scores) + 4),
        out_specs=[WHOLE] * len(picks),
        compiler_params=PARAMS,
        cost_estimate=pl.CostEstimate(
            flops=10 * comps * count * chunks * LANES * high.shape[0], bytes_accessed=2**21, transcendentals=0
        ),
        name="spread",
    )(me, *scores, high, low, sums, occ)


def gram_kernel(scale, chunks, *refs):
    pieces, (spread_ref, gram_ref) = refs[:-2], refs[-2:]
    comps = spread_ref.shape[0]
    rows = block_rows(comps, chunks)
    total = tree_sum([ref[ref.shape[0] - rows:] for ref in pieces])
    extra = total[chunks * comps:chunks * comps + chunks + 1]
    eye = lax.broadcasted_iota(jnp.int32, (comps, LANES), 0) == lax.broadcasted_iota(jnp.int32, (comps, LANES), 1)
    row_sums = jnp.sum(jnp.where(eye, extra[:1], 0.0), axis=1, keepdims=True) * scale
    parts = [total[at * comps:(at + 1) * comps] - row_sums * extra[at + 1:at + 2] for at in range(chunks)]
    spread = jnp.concatenate(parts, axis=1)
    spread_ref[...] = spread
    gram_ref[...] = packed_gram(spread)


def packed_gram(spread):
    gram = lax.dot_general(spread, spread, NT, precision=lax.Precision.HIGHEST, preferred_element_type=F32)
    half = spread.shape[0] // 2
    return jnp.concatenate([gram[:half], gram[half:]], axis=1)


def centered_gram(pieces, comps, cell_total):
    chunks = pieces[0].shape[0] // comps
    return pl.pallas_call(
        functools.partial(gram_kernel, 1.0 / cell_total, chunks),
        out_shape=(
            jax.ShapeDtypeStruct((comps, chunks * LANES), F32),
            jax.ShapeDtypeStruct((comps // 2, comps * 2), F32),
        ),
        in_specs=[WHOLE] * len(pieces),
        out_specs=(WHOLE, WHOLE),
        compiler_params=PARAMS,
        name="gram",
    )(*pieces)


def plain_gram_kernel(scale, spread_ref, row_ref, sum_ref, out_ref, gram_ref):
    spread = spread_ref[...] - row_ref[...] * scale * sum_ref[...]
    out_ref[...] = spread
    gram_ref[...] = packed_gram(spread)


def plain_gram(spread, rows, sums, cell_total):
    comps, width = spread.shape
    return pl.pallas_call(
        functools.partial(plain_gram_kernel, 1.0 / cell_total),
        out_shape=(
            jax.ShapeDtypeStruct((comps, width), F32),
            jax.ShapeDtypeStruct((comps // 2, comps * 2), F32),
        ),
        in_specs=[WHOLE] * 3,
        out_specs=(WHOLE, WHOLE),
        compiler_params=PARAMS,
        name="plain_gram",
    )(spread, rows, sums)


def row_of(x, at):
    return jnp.broadcast_to(x[at:at + 1, :], x.shape)


def spread_column(rows, at):
    return jnp.broadcast_to(rows[:, at:at + 1], rows.shape)


def eliminate(groups, begin):
    groups = list(groups)
    edge = groups[0].shape[0]
    below = lax.broadcasted_iota(jnp.int32, groups[0].shape, 0)
    columns = [{c: spread_column(rows, begin + c) for c in range(edge)} for rows in groups]
    for at in range(len(groups)):
        scale = jnp.zeros_like(groups[0])
        later = (at + 1) * edge
        for i in range(at * edge, later, 2):
            if i == later - 4 and at + 1 < len(groups):
                for rows, cols in zip(groups[at:], columns[at:]):
                    cols.update({c: spread_column(rows, begin + c) for c in range(later, later + edge)})
            row = i - at * edge
            cols = columns[at]
            first, second = cols[i], cols[i + 1]
            a, b, c = row_of(first, row), row_of(second, row), row_of(second, row + 1)
            det = a * c - b * b
            inv_a = pl.reciprocal(a, approx=True)
            inv_c = a * pl.reciprocal(det, approx=True)
            ratio = b * inv_a
            scale = jnp.where(below == row, lax.rsqrt(a), jnp.where(below == row + 1, lax.rsqrt(det * inv_a), scale))
            factors = []
            for k in cols:
                if k > i + 1:
                    top = row_of(cols[k], row)
                    factors.append((k, top * inv_a, (row_of(cols[k], row + 1) - ratio * top) * inv_c))
            rows = groups[at]
            upper = row_of(rows, row) * inv_a
            rows = rows - jnp.where(below > row, first, 0.0) * upper
            lower = row_of(rows, row + 1) * inv_c
            groups[at] = rows - jnp.where(below > row + 1, second - ratio * first, 0.0) * lower
            for ahead in range(at, len(groups)):
                cols = columns[ahead]
                first = cols[i]
                second = cols[i + 1] - ratio * first
                for k, on_first, on_second in factors:
                    cols[k] = cols[k] - first * on_first - second * on_second
                if ahead > at:
                    groups[ahead] = groups[ahead] - first * upper - second * lower
                del cols[i], cols[i + 1]
        groups[at] = groups[at] * scale
    return groups


def scale_kernel(gram_ref, times_ref, plus_ref):
    gram = gram_ref[...]
    half, comps = gram.shape[0], gram.shape[1] // 2
    gram = jnp.concatenate([gram[:, :comps], gram[:, comps:]], axis=0)
    eye = lax.broadcasted_iota(jnp.int32, gram.shape, 0) == lax.broadcasted_iota(jnp.int32, gram.shape, 1)
    diagonal = jnp.where(eye, gram, 0.0)
    row_scale = lax.rsqrt(jnp.sum(diagonal, axis=1, keepdims=True))
    col_scale = lax.rsqrt(jnp.sum(diagonal, axis=0, keepdims=True))
    zeros = jnp.zeros_like(gram)
    times_ref[...] = jnp.concatenate([zeros, row_scale * col_scale], axis=1)
    plus_ref[...] = jnp.concatenate([jnp.where(eye, col_scale, 0.0), zeros], axis=1)


def scales(gram):
    half, lanes = gram.shape
    return pl.pallas_call(
        scale_kernel,
        out_shape=[jax.ShapeDtypeStruct((2 * half, lanes), F32)] * 2,
        in_specs=[WHOLE],
        out_specs=[WHOLE, WHOLE],
        compiler_params=PARAMS,
        name="scales",
    )(gram)


def basis_kernel(scale, *refs):
    grams, (times_ref, plus_ref, spread_ref, out_ref) = refs[:-4], refs[-4:]
    gram = tree_sum([ref[...] for ref in grams])
    comps = spread_ref.shape[0]
    gram = jnp.concatenate([pltpu.roll(gram, comps, 1), gram], axis=0)
    both = gram * times_ref[...] + plus_ref[...]
    groups = eliminate([both[at:at + 8] for at in range(0, comps, 8)], comps)
    inverse = jnp.concatenate(groups, axis=0)[:, :comps] * scale
    out_ref[...] = lax.dot_general(
        inverse, spread_ref[...], NN, precision=lax.Precision.HIGHEST, preferred_element_type=F32
    )


def orthonormal(grams, spread, scale):
    return pl.pallas_call(
        functools.partial(basis_kernel, scale),
        out_shape=jax.ShapeDtypeStruct(spread.shape, F32),
        in_specs=[WHOLE] * (len(grams) + 3),
        out_specs=WHOLE,
        compiler_params=PARAMS,
        name="orthonormal",
    )(*grams, *scales(grams[0]), spread)


def send(x, offset_cells, offset_genes):
    cells, genes = lax.axis_size("cells"), lax.axis_size("genes")
    pairs = []
    for c in range(cells):
        for g in range(genes):
            pairs.append((c * genes + g, (c ^ offset_cells) * genes + (g ^ offset_genes)))
    return lax.ppermute(x, ("cells", "genes"), pairs)


def gene_terms(x):
    x = x + send(x, 0, 1)
    return [x, send(x, 0, 3)]


def all_terms(x):
    x = x + send(x, 0, 1)
    across = [send(x, c, g) for c, g in ((1, 3), (1, 1), (0, 3))]
    terms = [x + across[2], across[1] + across[0]]
    for at in range(1, lax.axis_size("cells").bit_length() - 1):
        x = tree_sum(terms)
        terms = [x, send(x, 1 << at, 1)]
    return terms


def scattered_spread(scores, high, low, sums, occ, cell_total):
    comps = scores[0].shape[0]
    me = lax.axis_index("cells").astype(jnp.int32).reshape(1)
    make = functools.partial(spread_pieces, scores=scores, high=high, low=low, sums=sums, occ=occ)
    pair, first, across = make(me, picks=[[6, 2], [5], [7]])
    pair, me = lax.optimization_barrier((pair, me))
    pair, first = send(pair, 2, 0), send(first, 1, 0)
    across = send(across, 7, 0)
    far, own, *second = make(me, picks=[[4], [0], [3], [1]])
    far, second = lax.optimization_barrier((tree_sum([far, pair[:far.shape[0]], first]), second))
    far = send(far, 4, 0)
    straight = [send(x, k, 0) for k, x in zip((3, 1), second)]
    return centered_gram([own, far, pair, across] + straight, comps, cell_total)


def all_alike(counts, occupancy, start_basis):
    tile_rows, tile_cols = occupancy.shape
    edge = counts.shape[0] // tile_rows
    logged = jnp.log(1.0 + counts.astype(F32)).reshape(tile_rows, edge, tile_cols, -1)
    logged = (logged * occupancy.astype(F32)[:, None, :, None]).reshape(counts.shape)
    high, low = split_terms(logged, 2)
    scores = lax.psum(dot(start_basis, high, NT) + dot(start_basis, low, NT), "genes")
    spread = spread_piece(split_terms(scores, 3), high, low)
    spread = lax.psum_scatter(spread, "cells", scatter_dimension=1, tiled=True)
    rows = lax.psum(jnp.sum(scores, axis=1, keepdims=True), "cells")
    sums = lax.psum_scatter(jnp.sum(logged, axis=0, keepdims=True), "cells", scatter_dimension=1, tiled=True)
    spread, gram = plain_gram(spread, rows, sums, counts.shape[0] * lax.axis_size("cells"))
    return [lax.psum(gram, ("cells", "genes"))], spread


def in_steps(counts, occupancy, start_basis):
    high, low, sums = log_terms(counts)
    scores, occ = score_part(occupancy, start_basis, high, low)
    cell_total = counts.shape[0] * lax.axis_size("cells")
    spread, gram = scattered_spread(gene_terms(scores), high, low, sums, occ, cell_total)
    return all_terms(gram), spread


def on_device(counts, occupancy, start_basis):
    gene_count = counts.shape[1]
    cells, genes = lax.axis_size("cells"), lax.axis_size("genes")
    halvings = cells == 1 << 3 and genes == 1 << 2
    tiles = occupancy.shape[0] == 1 and gene_count == occupancy.shape[1] * LANES
    work = in_steps if halvings and tiles and gene_count % (cells * LANES) == 0 else all_alike
    grams, spread = work(counts, occupancy, start_basis)
    return orthonormal(grams, spread, math.sqrt(gene_count * genes))


def solution(mesh):
    in_specs = (P("cells", "genes"), P("cells", "genes"), P(None, "genes"))
    out_specs = P(None, ("genes", "cells"))
    return jax.shard_map(
        on_device, mesh=mesh, in_specs=in_specs, out_specs=out_specs, check_vma=False
    )
```

```python
import functools
import math

import jax
import jax.numpy as jnp
from jax import lax
from jax.experimental import pallas as pl
from jax.experimental.pallas import tpu as pltpu
from jax.sharding import PartitionSpec as P

F32 = jnp.float32
BF16 = jnp.bfloat16
NN = (((1,), (0,)), ((), ()))
NT = (((1,), (1,)), ((), ()))
WHOLE = pl.BlockSpec(memory_space=pltpu.VMEM)
SCALARS = pl.BlockSpec(memory_space=pltpu.SMEM)
LANES = 128
PARAMS = pltpu.CompilerParams(vmem_limit_bytes=16 * 2**20)
LOG_PARAMS = pltpu.CompilerParams(vmem_limit_bytes=205 * 2**18)


def dot(a, b, dims):
    return lax.dot_general(a, b, dims, preferred_element_type=F32)


def split_terms(x, count):
    terms = []
    for _ in range(count):
        term = x.astype(BF16)
        terms.append(term)
        x = x - term.astype(F32)
    return terms


def tree_sum(parts):
    while len(parts) > 1:
        parts = [sum(parts[at + 1:at + 2], parts[at]) for at in range(0, len(parts), 2)]
    return parts[0]


def log_kernel(width, counts_hbm, high_ref, low_ref, sum_ref, counts_ref, counts_sem):
    cells, genes = high_ref.shape
    fetches = [
        pltpu.make_async_copy(
            counts_hbm.at[:, pl.ds(at * width, width)], counts_ref.at[:, pl.ds(at * width, width)], counts_sem.at[at]
        )
        for at in range(genes // width)
    ]
    for fetch in fetches:
        fetch.start()
    for at, fetch in enumerate(fetches):
        fetch.wait()
        for begin in range(at * width, (at + 1) * width, LANES):
            lanes = pl.ds(begin, LANES)
            logged = jnp.log(1.0 + counts_ref[:, lanes].astype(F32))
            high = logged.astype(BF16)
            high_ref[:, lanes] = high
            low_ref[:, lanes] = (logged - high.astype(F32)).astype(BF16)
            sum_ref[:, lanes] = jnp.sum(logged, axis=0, keepdims=True)


def log_terms(counts):
    cells, genes = counts.shape
    width = genes // 8
    return pl.pallas_call(
        functools.partial(log_kernel, width),
        out_shape=(
            jax.ShapeDtypeStruct((cells, genes), BF16),
            jax.ShapeDtypeStruct((cells, genes), BF16),
            jax.ShapeDtypeStruct((1, genes), F32),
        ),
        in_specs=[pl.BlockSpec(memory_space=pltpu.HBM)],
        out_specs=(WHOLE, WHOLE, WHOLE),
        scratch_shapes=[pltpu.VMEM(counts.shape, BF16), pltpu.SemaphoreType.DMA((genes // width,))],
        compiler_params=LOG_PARAMS,
        cost_estimate=pl.CostEstimate(flops=20 * cells * genes, bytes_accessed=8 * cells * genes, transcendentals=0),
        name="log_terms",
    )(counts)


def score_kernel(width, occ_ref, basis_ref, high_ref, low_ref, score_ref, lane_ref):
    comps, genes = basis_ref.shape
    edge = genes // occ_ref.shape[1]
    occupancy = occ_ref[...].astype(F32)
    scores = None
    for begin in range(0, genes, width):
        basis = []
        for at in range(begin, begin + width, edge):
            occ = jnp.broadcast_to(occupancy[:, at // edge:at // edge + 1], (1, edge))
            lane_ref[:, pl.ds(at, edge)] = occ
            basis.append(basis_ref[:, pl.ds(at, edge)] * occ.astype(BF16))
        basis = jnp.concatenate(basis, axis=1)
        lanes = pl.ds(begin, width)
        part = dot(basis, high_ref[:, lanes], NT) + dot(basis, low_ref[:, lanes], NT)
        scores = part if scores is None else scores + part
    score_ref[...] = scores


def score_part(occupancy, basis, high, low):
    comps, genes = basis.shape
    cells = high.shape[0]
    return pl.pallas_call(
        functools.partial(score_kernel, genes // 4),
        out_shape=(jax.ShapeDtypeStruct((comps, cells), F32), jax.ShapeDtypeStruct((1, genes), F32)),
        in_specs=[WHOLE] * 4,
        out_specs=(WHOLE, WHOLE),
        compiler_params=PARAMS,
        name="scores",
    )(occupancy, basis, high, low)


def spread_piece(terms, high, low):
    comps = terms[0].shape[0]
    on_low = dot(jnp.concatenate(terms[:2], axis=0), low, NN)
    on_high = dot(jnp.concatenate(terms, axis=0), high, NN)
    small = on_low[comps:] + on_high[2 * comps:]
    middle = on_low[:comps] + on_high[comps:2 * comps]
    return (small + middle) + on_high[:comps]


def spread_kernel(count, picks, me_ref, *refs):
    score_refs, outs = refs[:count], refs[count + 4:]
    high_ref, low_ref, sum_ref, occ_ref = refs[count:count + 4]
    scores = tree_sum([ref[...] for ref in score_refs])
    comps = scores.shape[0]
    terms = split_terms(scores, 3)
    eye = lax.broadcasted_iota(jnp.int32, (comps, LANES), 0) == lax.broadcasted_iota(jnp.int32, (comps, LANES), 1)
    row_sums = jnp.sum(jnp.where(eye, jnp.sum(scores, axis=1, keepdims=True), 0.0), axis=0, keepdims=True)
    chunks = high_ref.shape[1] // (LANES * lax.axis_size("cells"))
    width = chunks * LANES
    blocks = [(pick, out, at) for group, out in zip(picks, outs) for at, pick in enumerate(group)]
    rows = block_rows(comps, chunks)
    for pick, out, at_block in blocks:
        base = at_block * rows
        start = pl.multiple_of((me_ref[0] ^ pick) * width, width)
        lanes = pl.ds(start, width)
        piece = spread_piece(terms, high_ref[:, lanes], low_ref[:, lanes]) * occ_ref[:, lanes]
        sums = sum_ref[:, lanes] * occ_ref[:, lanes]
        extra = [row_sums]
        for at in range(chunks):
            out[base + at * comps:base + (at + 1) * comps] = piece[:, at * LANES:(at + 1) * LANES]
            extra.append(sums[:, at * LANES:(at + 1) * LANES])
        extra.append(jnp.zeros((rows - chunks * comps - chunks - 1, LANES), F32))
        out[base + chunks * comps:base + rows] = jnp.concatenate(extra, axis=0)


def block_rows(comps, chunks):
    return comps * chunks + -(-(chunks + 1) // 8) * 8


def spread_pieces(me, scores, high, low, sums, occ, picks):
    comps = scores[0].shape[0]
    chunks = high.shape[1] // (LANES * lax.axis_size("cells"))
    rows = block_rows(comps, chunks)
    count = sum(len(group) for group in picks)
    return pl.pallas_call(
        functools.partial(spread_kernel, len(scores), picks),
        out_shape=[jax.ShapeDtypeStruct((len(group) * rows, LANES), F32) for group in picks],
        in_specs=[SCALARS] + [WHOLE] * (len(scores) + 4),
        out_specs=[WHOLE] * len(picks),
        compiler_params=PARAMS,
        cost_estimate=pl.CostEstimate(
            flops=10 * comps * count * chunks * LANES * high.shape[0], bytes_accessed=2**21, transcendentals=0
        ),
        name="spread",
    )(me, *scores, high, low, sums, occ)


def gram_kernel(scale, chunks, *refs):
    pieces, (spread_ref, gram_ref) = refs[:-2], refs[-2:]
    comps = spread_ref.shape[0]
    rows = block_rows(comps, chunks)
    total = tree_sum([ref[ref.shape[0] - rows:] for ref in pieces])
    extra = total[chunks * comps:chunks * comps + chunks + 1]
    eye = lax.broadcasted_iota(jnp.int32, (comps, LANES), 0) == lax.broadcasted_iota(jnp.int32, (comps, LANES), 1)
    row_sums = jnp.sum(jnp.where(eye, extra[:1], 0.0), axis=1, keepdims=True) * scale
    parts = [total[at * comps:(at + 1) * comps] - row_sums * extra[at + 1:at + 2] for at in range(chunks)]
    spread = jnp.concatenate(parts, axis=1)
    spread_ref[...] = spread
    gram_ref[...] = packed_gram(spread)


def packed_gram(spread):
    gram = lax.dot_general(spread, spread, NT, precision=lax.Precision.HIGHEST, preferred_element_type=F32)
    half = spread.shape[0] // 2
    return jnp.concatenate([gram[:half], gram[half:]], axis=1)


def centered_gram(pieces, comps, cell_total):
    chunks = pieces[0].shape[0] // comps
    return pl.pallas_call(
        functools.partial(gram_kernel, 1.0 / cell_total, chunks),
        out_shape=(
            jax.ShapeDtypeStruct((comps, chunks * LANES), F32),
            jax.ShapeDtypeStruct((comps // 2, comps * 2), F32),
        ),
        in_specs=[WHOLE] * len(pieces),
        out_specs=(WHOLE, WHOLE),
        compiler_params=PARAMS,
        name="gram",
    )(*pieces)


def plain_gram_kernel(scale, spread_ref, row_ref, sum_ref, out_ref, gram_ref):
    spread = spread_ref[...] - row_ref[...] * scale * sum_ref[...]
    out_ref[...] = spread
    gram_ref[...] = packed_gram(spread)


def plain_gram(spread, rows, sums, cell_total):
    comps, width = spread.shape
    return pl.pallas_call(
        functools.partial(plain_gram_kernel, 1.0 / cell_total),
        out_shape=(
            jax.ShapeDtypeStruct((comps, width), F32),
            jax.ShapeDtypeStruct((comps // 2, comps * 2), F32),
        ),
        in_specs=[WHOLE] * 3,
        out_specs=(WHOLE, WHOLE),
        compiler_params=PARAMS,
        name="plain_gram",
    )(spread, rows, sums)


def row_of(x, at):
    return jnp.broadcast_to(x[at:at + 1, :], x.shape)


def spread_column(rows, at):
    return jnp.broadcast_to(rows[:, at:at + 1], rows.shape)


def eliminate(groups, begin):
    groups = list(groups)
    edge = groups[0].shape[0]
    below = lax.broadcasted_iota(jnp.int32, groups[0].shape, 0)
    columns = [{c: spread_column(rows, begin + c) for c in range(edge)} for rows in groups]
    for at in range(len(groups)):
        scale = jnp.zeros_like(groups[0])
        later = (at + 1) * edge
        for i in range(at * edge, later, 2):
            if i == later - 4 and at + 1 < len(groups):
                for rows, cols in zip(groups[at:], columns[at:]):
                    cols.update({c: spread_column(rows, begin + c) for c in range(later, later + edge)})
            row = i - at * edge
            cols = columns[at]
            first, second = cols[i], cols[i + 1]
            a, b, c = row_of(first, row), row_of(second, row), row_of(second, row + 1)
            det = a * c - b * b
            inv_a = pl.reciprocal(a, approx=True)
            inv_c = a * pl.reciprocal(det, approx=True)
            ratio = b * inv_a
            scale = jnp.where(below == row, lax.rsqrt(a), jnp.where(below == row + 1, lax.rsqrt(det * inv_a), scale))
            factors = []
            for k in cols:
                if k > i + 1:
                    top = row_of(cols[k], row)
                    factors.append((k, top * inv_a, (row_of(cols[k], row + 1) - ratio * top) * inv_c))
            rows = groups[at]
            upper = row_of(rows, row) * inv_a
            rows = rows - jnp.where(below > row, first, 0.0) * upper
            lower = row_of(rows, row + 1) * inv_c
            groups[at] = rows - jnp.where(below > row + 1, second - ratio * first, 0.0) * lower
            for ahead in range(at, len(groups)):
                cols = columns[ahead]
                first = cols[i]
                second = cols[i + 1] - ratio * first
                for k, on_first, on_second in factors:
                    cols[k] = cols[k] - first * on_first - second * on_second
                if ahead > at:
                    groups[ahead] = groups[ahead] - first * upper - second * lower
                del cols[i], cols[i + 1]
        groups[at] = groups[at] * scale
    return groups


def scale_kernel(gram_ref, times_ref, plus_ref):
    gram = gram_ref[...]
    half, comps = gram.shape[0], gram.shape[1] // 2
    gram = jnp.concatenate([gram[:, :comps], gram[:, comps:]], axis=0)
    eye = lax.broadcasted_iota(jnp.int32, gram.shape, 0) == lax.broadcasted_iota(jnp.int32, gram.shape, 1)
    diagonal = jnp.where(eye, gram, 0.0)
    row_scale = lax.rsqrt(jnp.sum(diagonal, axis=1, keepdims=True))
    col_scale = lax.rsqrt(jnp.sum(diagonal, axis=0, keepdims=True))
    zeros = jnp.zeros_like(gram)
    times_ref[...] = jnp.concatenate([zeros, row_scale * col_scale], axis=1)
    plus_ref[...] = jnp.concatenate([jnp.where(eye, col_scale, 0.0), zeros], axis=1)


def scales(gram):
    half, lanes = gram.shape
    return pl.pallas_call(
        scale_kernel,
        out_shape=[jax.ShapeDtypeStruct((2 * half, lanes), F32)] * 2,
        in_specs=[WHOLE],
        out_specs=[WHOLE, WHOLE],
        compiler_params=PARAMS,
        name="scales",
    )(gram)


def basis_kernel(scale, *refs):
    grams, (times_ref, plus_ref, spread_ref, out_ref) = refs[:-4], refs[-4:]
    gram = tree_sum([ref[...] for ref in grams])
    comps = spread_ref.shape[0]
    gram = jnp.concatenate([pltpu.roll(gram, comps, 1), gram], axis=0)
    both = gram * times_ref[...] + plus_ref[...]
    groups = eliminate([both[at:at + 8] for at in range(0, comps, 8)], comps)
    inverse = jnp.concatenate(groups, axis=0)[:, :comps] * scale
    out_ref[...] = lax.dot_general(
        inverse, spread_ref[...], NN, precision=lax.Precision.HIGHEST, preferred_element_type=F32
    )


def orthonormal(grams, spread, scale):
    return pl.pallas_call(
        functools.partial(basis_kernel, scale),
        out_shape=jax.ShapeDtypeStruct(spread.shape, F32),
        in_specs=[WHOLE] * (len(grams) + 3),
        out_specs=WHOLE,
        compiler_params=PARAMS,
        name="orthonormal",
    )(*grams, *scales(grams[0]), spread)


def send(x, offset_cells, offset_genes):
    cells, genes = lax.axis_size("cells"), lax.axis_size("genes")
    pairs = []
    for c in range(cells):
        for g in range(genes):
            pairs.append((c * genes + g, (c ^ offset_cells) * genes + (g ^ offset_genes)))
    return lax.ppermute(x, ("cells", "genes"), pairs)


def gene_terms(x):
    x = x + send(x, 0, 1)
    return [x, send(x, 0, 3)]


def all_terms(x):
    x = x + send(x, 0, 1)
    across = [send(x, c, g) for c, g in ((1, 3), (1, 1), (0, 3))]
    terms = [x + across[2], across[1] + across[0]]
    for at in range(1, lax.axis_size("cells").bit_length() - 1):
        x = tree_sum(terms)
        terms = [x, send(x, 1 << at, 1)]
    return terms


def scattered_spread(scores, high, low, sums, occ, cell_total):
    comps = scores[0].shape[0]
    me = lax.axis_index("cells").astype(jnp.int32).reshape(1)
    make = functools.partial(spread_pieces, scores=scores, high=high, low=low, sums=sums, occ=occ)
    first, second, across = make(me, picks=[[5], [6], [7]])
    first, me = lax.optimization_barrier((first, me))
    first, second = send(first, 1, 0), send(second, 2, 0)
    straight = [send(across, 7, 0)]
    far, own, *others = make(me, picks=[[4], [0], [3], [2], [1]])
    first, others[0] = lax.optimization_barrier((first, others[0]))
    far = lax.optimization_barrier(far + first) + second
    far, others[1], others[2] = lax.optimization_barrier((far, others[1], others[2]))
    straight += [send(x, k, 0) for k, x in zip((3, 2, 1), others)]
    return centered_gram([own, send(far, 4, 0)] + straight, comps, cell_total)


def all_alike(counts, occupancy, start_basis):
    tile_rows, tile_cols = occupancy.shape
    edge = counts.shape[0] // tile_rows
    logged = jnp.log(1.0 + counts.astype(F32)).reshape(tile_rows, edge, tile_cols, -1)
    logged = (logged * occupancy.astype(F32)[:, None, :, None]).reshape(counts.shape)
    high, low = split_terms(logged, 2)
    scores = lax.psum(dot(start_basis, high, NT) + dot(start_basis, low, NT), "genes")
    spread = spread_piece(split_terms(scores, 3), high, low)
    spread = lax.psum_scatter(spread, "cells", scatter_dimension=1, tiled=True)
    rows = lax.psum(jnp.sum(scores, axis=1, keepdims=True), "cells")
    sums = lax.psum_scatter(jnp.sum(logged, axis=0, keepdims=True), "cells", scatter_dimension=1, tiled=True)
    spread, gram = plain_gram(spread, rows, sums, counts.shape[0] * lax.axis_size("cells"))
    return [lax.psum(gram, ("cells", "genes"))], spread


def in_steps(counts, occupancy, start_basis):
    high, low, sums = log_terms(counts)
    scores, occ = score_part(occupancy, start_basis, high, low)
    cell_total = counts.shape[0] * lax.axis_size("cells")
    spread, gram = scattered_spread(gene_terms(scores), high, low, sums, occ, cell_total)
    return all_terms(gram), spread


def on_device(counts, occupancy, start_basis):
    gene_count = counts.shape[1]
    cells, genes = lax.axis_size("cells"), lax.axis_size("genes")
    halvings = cells == 1 << 3 and genes == 1 << 2
    tiles = occupancy.shape[0] == 1 and gene_count == occupancy.shape[1] * LANES
    work = in_steps if halvings and tiles and gene_count % (cells * LANES) == 0 else all_alike
    grams, spread = work(counts, occupancy, start_basis)
    return orthonormal(grams, spread, math.sqrt(gene_count * genes))


def solution(mesh):
    in_specs = (P("cells", "genes"), P("cells", "genes"), P(None, "genes"))
    out_specs = P(None, ("genes", "cells"))
    return jax.shard_map(
        on_device, mesh=mesh, in_specs=in_specs, out_specs=out_specs, check_vma=False
    )
```

```python
import functools
import math

import jax
import jax.numpy as jnp
from jax import lax
from jax.experimental import pallas as pl
from jax.experimental.pallas import tpu as pltpu
from jax.sharding import PartitionSpec as P

F32 = jnp.float32
BF16 = jnp.bfloat16
NN = (((1,), (0,)), ((), ()))
NT = (((1,), (1,)), ((), ()))
WHOLE = pl.BlockSpec(memory_space=pltpu.VMEM)
SCALARS = pl.BlockSpec(memory_space=pltpu.SMEM)
LANES = 128
PARAMS = pltpu.CompilerParams(vmem_limit_bytes=16 * 2**20)
LOG_PARAMS = pltpu.CompilerParams(vmem_limit_bytes=205 * 2**18)


def dot(a, b, dims):
    return lax.dot_general(a, b, dims, preferred_element_type=F32)


def split_terms(x, count):
    terms = []
    for _ in range(count):
        term = x.astype(BF16)
        terms.append(term)
        x = x - term.astype(F32)
    return terms


def tree_sum(parts):
    while len(parts) > 1:
        parts = [sum(parts[at + 1:at + 2], parts[at]) for at in range(0, len(parts), 2)]
    return parts[0]


def log_kernel(width, counts_hbm, high_ref, low_ref, sum_ref, counts_ref, counts_sem):
    cells, genes = high_ref.shape
    fetches = [
        pltpu.make_async_copy(
            counts_hbm.at[:, pl.ds(at * width, width)], counts_ref.at[:, pl.ds(at * width, width)], counts_sem.at[at]
        )
        for at in range(genes // width)
    ]
    for fetch in fetches:
        fetch.start()
    for at, fetch in enumerate(fetches):
        fetch.wait()
        for begin in range(at * width, (at + 1) * width, LANES):
            lanes = pl.ds(begin, LANES)
            logged = jnp.log(1.0 + counts_ref[:, lanes].astype(F32))
            high = logged.astype(BF16)
            high_ref[:, lanes] = high
            low_ref[:, lanes] = (logged - high.astype(F32)).astype(BF16)
            sum_ref[:, lanes] = jnp.sum(logged, axis=0, keepdims=True)


def log_terms(counts):
    cells, genes = counts.shape
    width = genes // 8
    return pl.pallas_call(
        functools.partial(log_kernel, width),
        out_shape=(
            jax.ShapeDtypeStruct((cells, genes), BF16),
            jax.ShapeDtypeStruct((cells, genes), BF16),
            jax.ShapeDtypeStruct((1, genes), F32),
        ),
        in_specs=[pl.BlockSpec(memory_space=pltpu.HBM)],
        out_specs=(WHOLE, WHOLE, WHOLE),
        scratch_shapes=[pltpu.VMEM(counts.shape, BF16), pltpu.SemaphoreType.DMA((genes // width,))],
        compiler_params=LOG_PARAMS,
        cost_estimate=pl.CostEstimate(flops=20 * cells * genes, bytes_accessed=8 * cells * genes, transcendentals=0),
        name="log_terms",
    )(counts)


def score_kernel(width, occ_ref, basis_ref, high_ref, low_ref, score_ref, lane_ref):
    comps, genes = basis_ref.shape
    edge = genes // occ_ref.shape[1]
    occupancy = occ_ref[...].astype(F32)
    scores = None
    for begin in range(0, genes, width):
        basis = []
        for at in range(begin, begin + width, edge):
            occ = jnp.broadcast_to(occupancy[:, at // edge:at // edge + 1], (1, edge))
            lane_ref[:, pl.ds(at, edge)] = occ
            basis.append(basis_ref[:, pl.ds(at, edge)] * occ.astype(BF16))
        basis = jnp.concatenate(basis, axis=1)
        lanes = pl.ds(begin, width)
        part = dot(basis, high_ref[:, lanes], NT) + dot(basis, low_ref[:, lanes], NT)
        scores = part if scores is None else scores + part
    score_ref[...] = scores


def score_part(occupancy, basis, high, low):
    comps, genes = basis.shape
    cells = high.shape[0]
    return pl.pallas_call(
        functools.partial(score_kernel, genes // 4),
        out_shape=(jax.ShapeDtypeStruct((comps, cells), F32), jax.ShapeDtypeStruct((1, genes), F32)),
        in_specs=[WHOLE] * 4,
        out_specs=(WHOLE, WHOLE),
        compiler_params=PARAMS,
        name="scores",
    )(occupancy, basis, high, low)


def spread_piece(terms, high, low):
    comps = terms[0].shape[0]
    on_low = dot(jnp.concatenate(terms[:2], axis=0), low, NN)
    on_high = dot(jnp.concatenate(terms, axis=0), high, NN)
    small = on_low[comps:] + on_high[2 * comps:]
    middle = on_low[:comps] + on_high[comps:2 * comps]
    return (small + middle) + on_high[:comps]


def spread_kernel(count, picks, me_ref, *refs):
    score_refs, outs = refs[:count], refs[count + 4:]
    high_ref, low_ref, sum_ref, occ_ref = refs[count:count + 4]
    scores = tree_sum([ref[...] for ref in score_refs])
    comps = scores.shape[0]
    terms = split_terms(scores, 3)
    eye = lax.broadcasted_iota(jnp.int32, (comps, LANES), 0) == lax.broadcasted_iota(jnp.int32, (comps, LANES), 1)
    row_sums = jnp.sum(jnp.where(eye, jnp.sum(scores, axis=1, keepdims=True), 0.0), axis=0, keepdims=True)
    chunks = high_ref.shape[1] // (LANES * lax.axis_size("cells"))
    width = chunks * LANES
    blocks = [(pick, out, at) for group, out in zip(picks, outs) for at, pick in enumerate(group)]
    rows = block_rows(comps, chunks)
    for pick, out, at_block in blocks:
        base = at_block * rows
        start = pl.multiple_of((me_ref[0] ^ pick) * width, width)
        lanes = pl.ds(start, width)
        piece = spread_piece(terms, high_ref[:, lanes], low_ref[:, lanes]) * occ_ref[:, lanes]
        sums = sum_ref[:, lanes] * occ_ref[:, lanes]
        extra = [row_sums]
        for at in range(chunks):
            out[base + at * comps:base + (at + 1) * comps] = piece[:, at * LANES:(at + 1) * LANES]
            extra.append(sums[:, at * LANES:(at + 1) * LANES])
        extra.append(jnp.zeros((rows - chunks * comps - chunks - 1, LANES), F32))
        out[base + chunks * comps:base + rows] = jnp.concatenate(extra, axis=0)


def block_rows(comps, chunks):
    return comps * chunks + -(-(chunks + 1) // 8) * 8


def spread_pieces(me, scores, high, low, sums, occ, picks):
    comps = scores[0].shape[0]
    chunks = high.shape[1] // (LANES * lax.axis_size("cells"))
    rows = block_rows(comps, chunks)
    count = sum(len(group) for group in picks)
    return pl.pallas_call(
        functools.partial(spread_kernel, len(scores), picks),
        out_shape=[jax.ShapeDtypeStruct((len(group) * rows, LANES), F32) for group in picks],
        in_specs=[SCALARS] + [WHOLE] * (len(scores) + 4),
        out_specs=[WHOLE] * len(picks),
        compiler_params=PARAMS,
        cost_estimate=pl.CostEstimate(
            flops=10 * comps * count * chunks * LANES * high.shape[0], bytes_accessed=2**21, transcendentals=0
        ),
        name="spread",
    )(me, *scores, high, low, sums, occ)


def gram_kernel(scale, chunks, *refs):
    pieces, (spread_ref, gram_ref) = refs[:-2], refs[-2:]
    comps = spread_ref.shape[0]
    rows = block_rows(comps, chunks)
    total = tree_sum([ref[ref.shape[0] - rows:] for ref in pieces])
    extra = total[chunks * comps:chunks * comps + chunks + 1]
    eye = lax.broadcasted_iota(jnp.int32, (comps, LANES), 0) == lax.broadcasted_iota(jnp.int32, (comps, LANES), 1)
    row_sums = jnp.sum(jnp.where(eye, extra[:1], 0.0), axis=1, keepdims=True) * scale
    parts = [total[at * comps:(at + 1) * comps] - row_sums * extra[at + 1:at + 2] for at in range(chunks)]
    spread = jnp.concatenate(parts, axis=1)
    spread_ref[...] = spread
    gram_ref[...] = packed_gram(spread)


def packed_gram(spread):
    gram = lax.dot_general(spread, spread, NT, precision=lax.Precision.HIGHEST, preferred_element_type=F32)
    half = spread.shape[0] // 2
    return jnp.concatenate([gram[:half], gram[half:]], axis=1)


def centered_gram(pieces, comps, cell_total):
    chunks = pieces[0].shape[0] // comps
    return pl.pallas_call(
        functools.partial(gram_kernel, 1.0 / cell_total, chunks),
        out_shape=(
            jax.ShapeDtypeStruct((comps, chunks * LANES), F32),
            jax.ShapeDtypeStruct((comps // 2, comps * 2), F32),
        ),
        in_specs=[WHOLE] * len(pieces),
        out_specs=(WHOLE, WHOLE),
        compiler_params=PARAMS,
        name="gram",
    )(*pieces)


def plain_gram_kernel(scale, spread_ref, row_ref, sum_ref, out_ref, gram_ref):
    spread = spread_ref[...] - row_ref[...] * scale * sum_ref[...]
    out_ref[...] = spread
    gram_ref[...] = packed_gram(spread)


def plain_gram(spread, rows, sums, cell_total):
    comps, width = spread.shape
    return pl.pallas_call(
        functools.partial(plain_gram_kernel, 1.0 / cell_total),
        out_shape=(
            jax.ShapeDtypeStruct((comps, width), F32),
            jax.ShapeDtypeStruct((comps // 2, comps * 2), F32),
        ),
        in_specs=[WHOLE] * 3,
        out_specs=(WHOLE, WHOLE),
        compiler_params=PARAMS,
        name="plain_gram",
    )(spread, rows, sums)


def row_of(x, at):
    return jnp.broadcast_to(x[at:at + 1, :], x.shape)


def spread_column(rows, at):
    return jnp.broadcast_to(rows[:, at:at + 1], rows.shape)


def eliminate(groups, begin):
    groups = list(groups)
    edge = groups[0].shape[0]
    below = lax.broadcasted_iota(jnp.int32, groups[0].shape, 0)
    columns = [{c: spread_column(rows, begin + c) for c in range(edge)} for rows in groups]
    for at in range(len(groups)):
        scale = jnp.zeros_like(groups[0])
        later = (at + 1) * edge
        for i in range(at * edge, later, 2):
            if i == later - 4 and at + 1 < len(groups):
                for rows, cols in zip(groups[at:], columns[at:]):
                    cols.update({c: spread_column(rows, begin + c) for c in range(later, later + edge)})
            row = i - at * edge
            cols = columns[at]
            first, second = cols[i], cols[i + 1]
            a, b, c = row_of(first, row), row_of(second, row), row_of(second, row + 1)
            det = a * c - b * b
            inv_a = pl.reciprocal(a, approx=True)
            inv_c = a * pl.reciprocal(det, approx=True)
            ratio = b * inv_a
            scale = jnp.where(below == row, lax.rsqrt(a), jnp.where(below == row + 1, lax.rsqrt(det * inv_a), scale))
            factors = []
            for k in cols:
                if k > i + 1:
                    top = row_of(cols[k], row)
                    factors.append((k, top * inv_a, (row_of(cols[k], row + 1) - ratio * top) * inv_c))
            rows = groups[at]
            upper = row_of(rows, row) * inv_a
            rows = rows - jnp.where(below > row, first, 0.0) * upper
            lower = row_of(rows, row + 1) * inv_c
            groups[at] = rows - jnp.where(below > row + 1, second - ratio * first, 0.0) * lower
            for ahead in range(at, len(groups)):
                cols = columns[ahead]
                first = cols[i]
                second = cols[i + 1] - ratio * first
                for k, on_first, on_second in factors:
                    cols[k] = cols[k] - first * on_first - second * on_second
                if ahead > at:
                    groups[ahead] = groups[ahead] - first * upper - second * lower
                del cols[i], cols[i + 1]
        groups[at] = groups[at] * scale
    return groups


def scale_kernel(gram_ref, times_ref, plus_ref):
    gram = gram_ref[...]
    half, comps = gram.shape[0], gram.shape[1] // 2
    gram = jnp.concatenate([gram[:, :comps], gram[:, comps:]], axis=0)
    eye = lax.broadcasted_iota(jnp.int32, gram.shape, 0) == lax.broadcasted_iota(jnp.int32, gram.shape, 1)
    diagonal = jnp.where(eye, gram, 0.0)
    row_scale = lax.rsqrt(jnp.sum(diagonal, axis=1, keepdims=True))
    col_scale = lax.rsqrt(jnp.sum(diagonal, axis=0, keepdims=True))
    zeros = jnp.zeros_like(gram)
    times_ref[...] = jnp.concatenate([zeros, row_scale * col_scale], axis=1)
    plus_ref[...] = jnp.concatenate([jnp.where(eye, col_scale, 0.0), zeros], axis=1)


def scales(gram):
    half, lanes = gram.shape
    return pl.pallas_call(
        scale_kernel,
        out_shape=[jax.ShapeDtypeStruct((2 * half, lanes), F32)] * 2,
        in_specs=[WHOLE],
        out_specs=[WHOLE, WHOLE],
        compiler_params=PARAMS,
        name="scales",
    )(gram)


def basis_kernel(scale, *refs):
    grams, (times_ref, plus_ref, spread_ref, out_ref) = refs[:-4], refs[-4:]
    gram = tree_sum([ref[...] for ref in grams])
    comps = spread_ref.shape[0]
    gram = jnp.concatenate([pltpu.roll(gram, comps, 1), gram], axis=0)
    both = gram * times_ref[...] + plus_ref[...]
    groups = eliminate([both[at:at + 8] for at in range(0, comps, 8)], comps)
    inverse = jnp.concatenate(groups, axis=0)[:, :comps] * scale
    out_ref[...] = lax.dot_general(
        inverse, spread_ref[...], NN, precision=lax.Precision.HIGHEST, preferred_element_type=F32
    )


def orthonormal(grams, spread, scale):
    return pl.pallas_call(
        functools.partial(basis_kernel, scale),
        out_shape=jax.ShapeDtypeStruct(spread.shape, F32),
        in_specs=[WHOLE] * (len(grams) + 3),
        out_specs=WHOLE,
        compiler_params=PARAMS,
        name="orthonormal",
    )(*grams, *scales(grams[0]), spread)


def send(x, offset_cells, offset_genes):
    cells, genes = lax.axis_size("cells"), lax.axis_size("genes")
    pairs = []
    for c in range(cells):
        for g in range(genes):
            pairs.append((c * genes + g, (c ^ offset_cells) * genes + (g ^ offset_genes)))
    return lax.ppermute(x, ("cells", "genes"), pairs)


def gene_terms(x):
    x = x + send(x, 0, 1)
    return [x, send(x, 0, 3)]


def all_terms(x):
    x = x + send(x, 0, 1)
    across = [send(x, c, g) for c, g in ((1, 3), (1, 1), (0, 3))]
    terms = [x + across[2], across[1] + across[0]]
    for at in range(1, lax.axis_size("cells").bit_length() - 1):
        x = tree_sum(terms)
        terms = [x, send(x, 1 << at, 1)]
    return terms


def scattered_spread(scores, high, low, sums, occ, cell_total):
    comps = scores[0].shape[0]
    me = lax.axis_index("cells").astype(jnp.int32).reshape(1)
    make = functools.partial(spread_pieces, scores=scores, high=high, low=low, sums=sums, occ=occ)
    first, second, near, across = make(me, picks=[[5], [6], [2], [7]])
    first, me = lax.optimization_barrier((first, me))
    first, second = send(first, 1, 0), send(second, 2, 0)
    straight = [send(near, 2, 0), send(across, 7, 0)]
    far, own, *others = make(me, picks=[[4], [0], [3], [1]])
    far = lax.optimization_barrier(far + first) + second
    far, others = lax.optimization_barrier((far, others))
    straight += [send(x, k, 0) for k, x in zip((3, 1), others)]
    return centered_gram([own, send(far, 4, 0)] + straight, comps, cell_total)


def all_alike(counts, occupancy, start_basis):
    tile_rows, tile_cols = occupancy.shape
    edge = counts.shape[0] // tile_rows
    logged = jnp.log(1.0 + counts.astype(F32)).reshape(tile_rows, edge, tile_cols, -1)
    logged = (logged * occupancy.astype(F32)[:, None, :, None]).reshape(counts.shape)
    high, low = split_terms(logged, 2)
    scores = lax.psum(dot(start_basis, high, NT) + dot(start_basis, low, NT), "genes")
    spread = spread_piece(split_terms(scores, 3), high, low)
    spread = lax.psum_scatter(spread, "cells", scatter_dimension=1, tiled=True)
    rows = lax.psum(jnp.sum(scores, axis=1, keepdims=True), "cells")
    sums = lax.psum_scatter(jnp.sum(logged, axis=0, keepdims=True), "cells", scatter_dimension=1, tiled=True)
    spread, gram = plain_gram(spread, rows, sums, counts.shape[0] * lax.axis_size("cells"))
    return [lax.psum(gram, ("cells", "genes"))], spread


def in_steps(counts, occupancy, start_basis):
    high, low, sums = log_terms(counts)
    scores, occ = score_part(occupancy, start_basis, high, low)
    cell_total = counts.shape[0] * lax.axis_size("cells")
    spread, gram = scattered_spread(gene_terms(scores), high, low, sums, occ, cell_total)
    return all_terms(gram), spread


def on_device(counts, occupancy, start_basis):
    gene_count = counts.shape[1]
    cells, genes = lax.axis_size("cells"), lax.axis_size("genes")
    halvings = cells == 1 << 3 and genes == 1 << 2
    tiles = occupancy.shape[0] == 1 and gene_count == occupancy.shape[1] * LANES
    work = in_steps if halvings and tiles and gene_count % (cells * LANES) == 0 else all_alike
    grams, spread = work(counts, occupancy, start_basis)
    return orthonormal(grams, spread, math.sqrt(gene_count * genes))


def solution(mesh):
    in_specs = (P("cells", "genes"), P("cells", "genes"), P(None, "genes"))
    out_specs = P(None, ("genes", "cells"))
    return jax.shard_map(
        on_device, mesh=mesh, in_specs=in_specs, out_specs=out_specs, check_vma=False
    )
```

```python
import functools
import math

import jax
import jax.numpy as jnp
from jax import lax
from jax.experimental import pallas as pl
from jax.experimental.pallas import tpu as pltpu
from jax.sharding import PartitionSpec as P

F32 = jnp.float32
BF16 = jnp.bfloat16
NN = (((1,), (0,)), ((), ()))
NT = (((1,), (1,)), ((), ()))
WHOLE = pl.BlockSpec(memory_space=pltpu.VMEM)
SCALARS = pl.BlockSpec(memory_space=pltpu.SMEM)
LANES = 128
PARAMS = pltpu.CompilerParams(vmem_limit_bytes=16 * 2**20)
LOG_PARAMS = pltpu.CompilerParams(vmem_limit_bytes=205 * 2**18)


def dot(a, b, dims):
    return lax.dot_general(a, b, dims, preferred_element_type=F32)


def split_terms(x, count):
    terms = []
    for _ in range(count):
        term = x.astype(BF16)
        terms.append(term)
        x = x - term.astype(F32)
    return terms


def tree_sum(parts):
    while len(parts) > 1:
        parts = [sum(parts[at + 1:at + 2], parts[at]) for at in range(0, len(parts), 2)]
    return parts[0]


def log_kernel(width, counts_hbm, high_ref, low_ref, sum_ref, counts_ref, counts_sem):
    cells, genes = high_ref.shape
    fetches = [
        pltpu.make_async_copy(
            counts_hbm.at[:, pl.ds(at * width, width)], counts_ref.at[:, pl.ds(at * width, width)], counts_sem.at[at]
        )
        for at in range(genes // width)
    ]
    for fetch in fetches:
        fetch.start()
    for at, fetch in enumerate(fetches):
        fetch.wait()
        for begin in range(at * width, (at + 1) * width, LANES):
            lanes = pl.ds(begin, LANES)
            logged = jnp.log(1.0 + counts_ref[:, lanes].astype(F32))
            high = logged.astype(BF16)
            high_ref[:, lanes] = high
            low_ref[:, lanes] = (logged - high.astype(F32)).astype(BF16)
            sum_ref[:, lanes] = jnp.sum(logged, axis=0, keepdims=True)


def log_terms(counts):
    cells, genes = counts.shape
    width = genes // 8
    return pl.pallas_call(
        functools.partial(log_kernel, width),
        out_shape=(
            jax.ShapeDtypeStruct((cells, genes), BF16),
            jax.ShapeDtypeStruct((cells, genes), BF16),
            jax.ShapeDtypeStruct((1, genes), F32),
        ),
        in_specs=[pl.BlockSpec(memory_space=pltpu.HBM)],
        out_specs=(WHOLE, WHOLE, WHOLE),
        scratch_shapes=[pltpu.VMEM(counts.shape, BF16), pltpu.SemaphoreType.DMA((genes // width,))],
        compiler_params=LOG_PARAMS,
        cost_estimate=pl.CostEstimate(flops=20 * cells * genes, bytes_accessed=8 * cells * genes, transcendentals=0),
        name="log_terms",
    )(counts)


def score_kernel(width, occ_ref, basis_ref, high_ref, low_ref, score_ref, lane_ref):
    comps, genes = basis_ref.shape
    edge = genes // occ_ref.shape[1]
    occupancy = occ_ref[...].astype(F32)
    scores = None
    for begin in range(0, genes, width):
        basis = []
        for at in range(begin, begin + width, edge):
            occ = jnp.broadcast_to(occupancy[:, at // edge:at // edge + 1], (1, edge))
            lane_ref[:, pl.ds(at, edge)] = occ
            basis.append(basis_ref[:, pl.ds(at, edge)] * occ.astype(BF16))
        basis = jnp.concatenate(basis, axis=1)
        lanes = pl.ds(begin, width)
        part = dot(basis, jnp.concatenate([high_ref[:, lanes], low_ref[:, lanes]], axis=0), NT)
        scores = part if scores is None else scores + part
    cells = score_ref.shape[1]
    score_ref[...] = scores[:, :cells] + scores[:, cells:]


def score_part(occupancy, basis, high, low):
    comps, genes = basis.shape
    cells = high.shape[0]
    return pl.pallas_call(
        functools.partial(score_kernel, genes // 4),
        out_shape=(jax.ShapeDtypeStruct((comps, cells), F32), jax.ShapeDtypeStruct((1, genes), F32)),
        in_specs=[WHOLE] * 4,
        out_specs=(WHOLE, WHOLE),
        compiler_params=PARAMS,
        name="scores",
    )(occupancy, basis, high, low)


def term_product(left, right, dims):
    rows = left[0].shape[0]
    left = jnp.concatenate([jnp.concatenate([term] * len(right), axis=1) for term in left], axis=0)
    out = dot(left, jnp.concatenate(right, axis=dims[0][1][0]), dims)
    parts = [out[at:at + rows] for at in range(0, out.shape[0], rows)]
    return functools.reduce(jnp.add, parts[::-1])


def spread_piece(terms, high, low):
    return term_product(terms, [high, low], NN)


def spread_kernel(count, picks, me_ref, *refs):
    score_refs, outs = refs[:count], refs[count + 4:]
    high_ref, low_ref, sum_ref, occ_ref = refs[count:count + 4]
    scores = tree_sum([ref[...] for ref in score_refs])
    comps = scores.shape[0]
    terms = split_terms(scores, 3)
    eye = lax.broadcasted_iota(jnp.int32, (comps, LANES), 0) == lax.broadcasted_iota(jnp.int32, (comps, LANES), 1)
    row_sums = jnp.sum(jnp.where(eye, jnp.sum(scores, axis=1, keepdims=True), 0.0), axis=0, keepdims=True)
    chunks = high_ref.shape[1] // (LANES * lax.axis_size("cells"))
    width = chunks * LANES
    blocks = [(pick, out, at) for group, out in zip(picks, outs) for at, pick in enumerate(group)]
    rows = block_rows(comps, chunks)
    for pick, out, at_block in blocks:
        base = at_block * rows
        start = pl.multiple_of((me_ref[0] ^ pick) * width, width)
        lanes = pl.ds(start, width)
        piece = spread_piece(terms, high_ref[:, lanes], low_ref[:, lanes]) * occ_ref[:, lanes]
        sums = sum_ref[:, lanes] * occ_ref[:, lanes]
        extra = [row_sums]
        for at in range(chunks):
            out[base + at * comps:base + (at + 1) * comps] = piece[:, at * LANES:(at + 1) * LANES]
            extra.append(sums[:, at * LANES:(at + 1) * LANES])
        extra.append(jnp.zeros((rows - chunks * comps - chunks - 1, LANES), F32))
        out[base + chunks * comps:base + rows] = jnp.concatenate(extra, axis=0)


def block_rows(comps, chunks):
    return comps * chunks + -(-(chunks + 1) // 8) * 8


def spread_pieces(me, scores, high, low, sums, occ, picks):
    comps = scores[0].shape[0]
    chunks = high.shape[1] // (LANES * lax.axis_size("cells"))
    rows = block_rows(comps, chunks)
    count = sum(len(group) for group in picks)
    return pl.pallas_call(
        functools.partial(spread_kernel, len(scores), picks),
        out_shape=[jax.ShapeDtypeStruct((len(group) * rows, LANES), F32) for group in picks],
        in_specs=[SCALARS] + [WHOLE] * (len(scores) + 4),
        out_specs=[WHOLE] * len(picks),
        compiler_params=PARAMS,
        cost_estimate=pl.CostEstimate(
            flops=10 * comps * count * chunks * LANES * high.shape[0], bytes_accessed=2**21, transcendentals=0
        ),
        name="spread",
    )(me, *scores, high, low, sums, occ)


def gram_kernel(scale, chunks, *refs):
    pieces, (spread_ref, gram_ref) = refs[:-2], refs[-2:]
    comps = spread_ref.shape[0]
    rows = block_rows(comps, chunks)
    total = tree_sum([ref[ref.shape[0] - rows:] for ref in pieces])
    extra = total[chunks * comps:chunks * comps + chunks + 1]
    eye = lax.broadcasted_iota(jnp.int32, (comps, LANES), 0) == lax.broadcasted_iota(jnp.int32, (comps, LANES), 1)
    row_sums = jnp.sum(jnp.where(eye, extra[:1], 0.0), axis=1, keepdims=True) * scale
    parts = [total[at * comps:(at + 1) * comps] - row_sums * extra[at + 1:at + 2] for at in range(chunks)]
    spread = jnp.concatenate(parts, axis=1)
    spread_ref[...] = spread
    gram_ref[...] = packed_gram(spread)


def packed_gram(spread):
    terms = split_terms(spread, 3)
    gram = term_product(terms, terms, NT)
    half = spread.shape[0] // 2
    return jnp.concatenate([gram[:half], gram[half:]], axis=1)


def centered_gram(pieces, comps, cell_total):
    chunks = pieces[0].shape[0] // comps
    return pl.pallas_call(
        functools.partial(gram_kernel, 1.0 / cell_total, chunks),
        out_shape=(
            jax.ShapeDtypeStruct((comps, chunks * LANES), F32),
            jax.ShapeDtypeStruct((comps // 2, comps * 2), F32),
        ),
        in_specs=[WHOLE] * len(pieces),
        out_specs=(WHOLE, WHOLE),
        compiler_params=PARAMS,
        name="gram",
    )(*pieces)


def plain_gram_kernel(scale, spread_ref, row_ref, sum_ref, out_ref, gram_ref):
    spread = spread_ref[...] - row_ref[...] * scale * sum_ref[...]
    out_ref[...] = spread
    gram_ref[...] = packed_gram(spread)


def plain_gram(spread, rows, sums, cell_total):
    comps, width = spread.shape
    return pl.pallas_call(
        functools.partial(plain_gram_kernel, 1.0 / cell_total),
        out_shape=(
            jax.ShapeDtypeStruct((comps, width), F32),
            jax.ShapeDtypeStruct((comps // 2, comps * 2), F32),
        ),
        in_specs=[WHOLE] * 3,
        out_specs=(WHOLE, WHOLE),
        compiler_params=PARAMS,
        name="plain_gram",
    )(spread, rows, sums)


def row_of(x, at):
    return jnp.broadcast_to(x[at:at + 1, :], x.shape)


def spread_column(rows, at):
    return jnp.broadcast_to(rows[:, at:at + 1], rows.shape)


def eliminate(groups, begin):
    groups = list(groups)
    edge = groups[0].shape[0]
    below = lax.broadcasted_iota(jnp.int32, groups[0].shape, 0)
    columns = [{c: spread_column(rows, begin + c) for c in range(edge)} for rows in groups]
    for at in range(len(groups)):
        scale = jnp.zeros_like(groups[0])
        later = (at + 1) * edge
        for i in range(at * edge, later, 2):
            if i == later - 4 and at + 1 < len(groups):
                for rows, cols in zip(groups[at:], columns[at:]):
                    cols.update({c: spread_column(rows, begin + c) for c in range(later, later + edge)})
            row = i - at * edge
            cols = columns[at]
            first, second = cols[i], cols[i + 1]
            a, b, c = row_of(first, row), row_of(second, row), row_of(second, row + 1)
            det = a * c - b * b
            inv_a = pl.reciprocal(a, approx=True)
            inv_c = a * pl.reciprocal(det, approx=True)
            ratio = b * inv_a
            scale = jnp.where(below == row, lax.rsqrt(a), jnp.where(below == row + 1, lax.rsqrt(det * inv_a), scale))
            factors = []
            for k in cols:
                if k > i + 1:
                    top = row_of(cols[k], row)
                    factors.append((k, top * inv_a, (row_of(cols[k], row + 1) - ratio * top) * inv_c))
            rows = groups[at]
            upper = row_of(rows, row) * inv_a
            rows = rows - jnp.where(below > row, first, 0.0) * upper
            lower = row_of(rows, row + 1) * inv_c
            groups[at] = rows - jnp.where(below > row + 1, second - ratio * first, 0.0) * lower
            for ahead in range(at, len(groups)):
                cols = columns[ahead]
                first = cols[i]
                second = cols[i + 1] - ratio * first
                for k, on_first, on_second in factors:
                    cols[k] = cols[k] - first * on_first - second * on_second
                if ahead > at:
                    groups[ahead] = groups[ahead] - first * upper - second * lower
                del cols[i], cols[i + 1]
        groups[at] = groups[at] * scale
    return groups


def scale_kernel(gram_ref, times_ref, plus_ref):
    gram = gram_ref[...]
    half, comps = gram.shape[0], gram.shape[1] // 2
    gram = jnp.concatenate([gram[:, :comps], gram[:, comps:]], axis=0)
    eye = lax.broadcasted_iota(jnp.int32, gram.shape, 0) == lax.broadcasted_iota(jnp.int32, gram.shape, 1)
    diagonal = jnp.where(eye, gram, 0.0)
    row_scale = lax.rsqrt(jnp.sum(diagonal, axis=1, keepdims=True))
    col_scale = lax.rsqrt(jnp.sum(diagonal, axis=0, keepdims=True))
    zeros = jnp.zeros_like(gram)
    times_ref[...] = jnp.concatenate([zeros, row_scale * col_scale], axis=1)
    plus_ref[...] = jnp.concatenate([jnp.where(eye, col_scale, 0.0), zeros], axis=1)


def scales(gram):
    half, lanes = gram.shape
    return pl.pallas_call(
        scale_kernel,
        out_shape=[jax.ShapeDtypeStruct((2 * half, lanes), F32)] * 2,
        in_specs=[WHOLE],
        out_specs=[WHOLE, WHOLE],
        compiler_params=PARAMS,
        name="scales",
    )(gram)


def basis_kernel(scale, *refs):
    grams, (times_ref, plus_ref, spread_ref, out_ref) = refs[:-4], refs[-4:]
    gram = tree_sum([ref[...] for ref in grams])
    comps = spread_ref.shape[0]
    gram = jnp.concatenate([pltpu.roll(gram, comps, 1), gram], axis=0)
    both = gram * times_ref[...] + plus_ref[...]
    groups = eliminate([both[at:at + 8] for at in range(0, comps, 8)], comps)
    inverse = jnp.concatenate(groups, axis=0)[:, :comps] * scale
    out_ref[...] = term_product(split_terms(inverse, 3), split_terms(spread_ref[...], 3), NN)


def orthonormal(grams, spread, scale):
    return pl.pallas_call(
        functools.partial(basis_kernel, scale),
        out_shape=jax.ShapeDtypeStruct(spread.shape, F32),
        in_specs=[WHOLE] * (len(grams) + 3),
        out_specs=WHOLE,
        compiler_params=PARAMS,
        name="orthonormal",
    )(*grams, *scales(grams[0]), spread)


def send(x, offset_cells, offset_genes):
    cells, genes = lax.axis_size("cells"), lax.axis_size("genes")
    pairs = []
    for c in range(cells):
        for g in range(genes):
            pairs.append((c * genes + g, (c ^ offset_cells) * genes + (g ^ offset_genes)))
    return lax.ppermute(x, ("cells", "genes"), pairs)


def gene_terms(x):
    x = x + send(x, 0, 1)
    return [x, send(x, 0, 3)]


def all_terms(x):
    x = x + send(x, 0, 1)
    across = [send(x, c, g) for c, g in ((1, 3), (1, 1), (0, 3))]
    terms = [x + across[2], across[1] + across[0]]
    for at in range(1, lax.axis_size("cells").bit_length() - 1):
        x = tree_sum(terms)
        terms = [x, send(x, 1 << at, 1)]
    return terms


def scattered_spread(scores, high, low, sums, occ, cell_total):
    comps = scores[0].shape[0]
    me = lax.axis_index("cells").astype(jnp.int32).reshape(1)
    make = functools.partial(spread_pieces, scores=scores, high=high, low=low, sums=sums, occ=occ)
    pair, first, across = make(me, picks=[[6, 2], [5], [7]])
    pair, me = lax.optimization_barrier((pair, me))
    pair, first = send(pair, 2, 0), send(first, 1, 0)
    across = send(across, 7, 0)
    far, own, *second = make(me, picks=[[4], [0], [3], [1]])
    first, second[0] = lax.optimization_barrier((first, second[0]))
    far, second[1] = lax.optimization_barrier((tree_sum([far, pair[:far.shape[0]], first]), second[1]))
    far = send(far, 4, 0)
    straight = [send(x, k, 0) for k, x in zip((3, 1), second)]
    return centered_gram([own, far, pair, across] + straight, comps, cell_total)


def all_alike(counts, occupancy, start_basis):
    tile_rows, tile_cols = occupancy.shape
    edge = counts.shape[0] // tile_rows
    logged = jnp.log(1.0 + counts.astype(F32)).reshape(tile_rows, edge, tile_cols, -1)
    logged = (logged * occupancy.astype(F32)[:, None, :, None]).reshape(counts.shape)
    high, low = split_terms(logged, 2)
    scores = lax.psum(dot(start_basis, high, NT) + dot(start_basis, low, NT), "genes")
    spread = spread_piece(split_terms(scores, 3), high, low)
    spread = lax.psum_scatter(spread, "cells", scatter_dimension=1, tiled=True)
    rows = lax.psum(jnp.sum(scores, axis=1, keepdims=True), "cells")
    sums = lax.psum_scatter(jnp.sum(logged, axis=0, keepdims=True), "cells", scatter_dimension=1, tiled=True)
    spread, gram = plain_gram(spread, rows, sums, counts.shape[0] * lax.axis_size("cells"))
    return [lax.psum(gram, ("cells", "genes"))], spread


def in_steps(counts, occupancy, start_basis):
    high, low, sums = log_terms(counts)
    scores, occ = score_part(occupancy, start_basis, high, low)
    cell_total = counts.shape[0] * lax.axis_size("cells")
    spread, gram = scattered_spread(gene_terms(scores), high, low, sums, occ, cell_total)
    return all_terms(gram), spread


def on_device(counts, occupancy, start_basis):
    gene_count = counts.shape[1]
    cells, genes = lax.axis_size("cells"), lax.axis_size("genes")
    halvings = cells == 1 << 3 and genes == 1 << 2
    tiles = occupancy.shape[0] == 1 and gene_count == occupancy.shape[1] * LANES
    work = in_steps if halvings and tiles and gene_count % (cells * LANES) == 0 else all_alike
    grams, spread = work(counts, occupancy, start_basis)
    return orthonormal(grams, spread, math.sqrt(gene_count * genes))


def solution(mesh):
    in_specs = (P("cells", "genes"), P("cells", "genes"), P(None, "genes"))
    out_specs = P(None, ("genes", "cells"))
    return jax.shard_map(
        on_device, mesh=mesh, in_specs=in_specs, out_specs=out_specs, check_vma=False
    )
```

```python
import functools
import math

import jax
import jax.numpy as jnp
from jax import lax
from jax.experimental import pallas as pl
from jax.experimental.pallas import tpu as pltpu
from jax.sharding import PartitionSpec as P

F32 = jnp.float32
BF16 = jnp.bfloat16
NN = (((1,), (0,)), ((), ()))
NT = (((1,), (1,)), ((), ()))
WHOLE = pl.BlockSpec(memory_space=pltpu.VMEM)
SCALARS = pl.BlockSpec(memory_space=pltpu.SMEM)
LANES = 128
PARAMS = pltpu.CompilerParams(vmem_limit_bytes=16 * 2**20)
LOG_PARAMS = pltpu.CompilerParams(vmem_limit_bytes=205 * 2**18)


def dot(a, b, dims):
    return lax.dot_general(a, b, dims, preferred_element_type=F32)


def split_terms(x, count):
    terms = []
    for _ in range(count):
        term = x.astype(BF16)
        terms.append(term)
        x = x - term.astype(F32)
    return terms


def tree_sum(parts):
    while len(parts) > 1:
        parts = [sum(parts[at + 1:at + 2], parts[at]) for at in range(0, len(parts), 2)]
    return parts[0]


def log_kernel(width, counts_hbm, high_ref, low_ref, sum_ref, counts_ref, counts_sem):
    cells, genes = high_ref.shape
    fetches = [
        pltpu.make_async_copy(
            counts_hbm.at[:, pl.ds(at * width, width)], counts_ref.at[:, pl.ds(at * width, width)], counts_sem.at[at]
        )
        for at in range(genes // width)
    ]
    for fetch in fetches:
        fetch.start()
    for at, fetch in enumerate(fetches):
        fetch.wait()
        for begin in range(at * width, (at + 1) * width, LANES):
            lanes = pl.ds(begin, LANES)
            logged = jnp.log(1.0 + counts_ref[:, lanes].astype(F32))
            high = logged.astype(BF16)
            high_ref[:, lanes] = high
            low_ref[:, lanes] = (logged - high.astype(F32)).astype(BF16)
            sum_ref[:, lanes] = jnp.sum(logged, axis=0, keepdims=True)


def log_terms(counts):
    cells, genes = counts.shape
    width = genes // 8
    return pl.pallas_call(
        functools.partial(log_kernel, width),
        out_shape=(
            jax.ShapeDtypeStruct((cells, genes), BF16),
            jax.ShapeDtypeStruct((cells, genes), BF16),
            jax.ShapeDtypeStruct((1, genes), F32),
        ),
        in_specs=[pl.BlockSpec(memory_space=pltpu.HBM)],
        out_specs=(WHOLE, WHOLE, WHOLE),
        scratch_shapes=[pltpu.VMEM(counts.shape, BF16), pltpu.SemaphoreType.DMA((genes // width,))],
        compiler_params=LOG_PARAMS,
        cost_estimate=pl.CostEstimate(flops=20 * cells * genes, bytes_accessed=8 * cells * genes, transcendentals=0),
        name="log_terms",
    )(counts)


def score_kernel(width, occ_ref, basis_ref, high_ref, low_ref, score_ref, lane_ref):
    comps, genes = basis_ref.shape
    edge = genes // occ_ref.shape[1]
    occupancy = occ_ref[...].astype(F32)
    scores = None
    for begin in range(0, genes, width):
        basis = []
        for at in range(begin, begin + width, edge):
            occ = jnp.broadcast_to(occupancy[:, at // edge:at // edge + 1], (1, edge))
            lane_ref[:, pl.ds(at, edge)] = occ
            basis.append(basis_ref[:, pl.ds(at, edge)] * occ.astype(BF16))
        basis = jnp.concatenate(basis, axis=1)
        lanes = pl.ds(begin, width)
        part = dot(basis, jnp.concatenate([high_ref[:, lanes], low_ref[:, lanes]], axis=0), NT)
        scores = part if scores is None else scores + part
    cells = score_ref.shape[1]
    score_ref[...] = scores[:, :cells] + scores[:, cells:]


def score_part(occupancy, basis, high, low):
    comps, genes = basis.shape
    cells = high.shape[0]
    return pl.pallas_call(
        functools.partial(score_kernel, genes // 4),
        out_shape=(jax.ShapeDtypeStruct((comps, cells), F32), jax.ShapeDtypeStruct((1, genes), F32)),
        in_specs=[WHOLE] * 4,
        out_specs=(WHOLE, WHOLE),
        compiler_params=PARAMS,
        name="scores",
    )(occupancy, basis, high, low)


def term_product(left, right, dims):
    rows = left[0].shape[0]
    left = jnp.concatenate([jnp.concatenate([term] * len(right), axis=1) for term in left], axis=0)
    out = dot(left, jnp.concatenate(right, axis=dims[0][1][0]), dims)
    parts = [out[at:at + rows] for at in range(0, out.shape[0], rows)]
    return functools.reduce(jnp.add, parts[::-1])


def spread_piece(terms, high, low):
    return term_product(terms, [high, low], NN)


def spread_kernel(count, picks, me_ref, *refs):
    score_refs, outs = refs[:count], refs[count + 4:]
    high_ref, low_ref, sum_ref, occ_ref = refs[count:count + 4]
    scores = tree_sum([ref[...] for ref in score_refs])
    comps = scores.shape[0]
    terms = split_terms(scores, 3)
    eye = lax.broadcasted_iota(jnp.int32, (comps, LANES), 0) == lax.broadcasted_iota(jnp.int32, (comps, LANES), 1)
    row_sums = jnp.sum(jnp.where(eye, jnp.sum(scores, axis=1, keepdims=True), 0.0), axis=0, keepdims=True)
    chunks = high_ref.shape[1] // (LANES * lax.axis_size("cells"))
    width = chunks * LANES
    blocks = [(pick, out, at) for group, out in zip(picks, outs) for at, pick in enumerate(group)]
    rows = block_rows(comps, chunks)
    for pick, out, at_block in blocks:
        base = at_block * rows
        start = pl.multiple_of((me_ref[0] ^ pick) * width, width)
        lanes = pl.ds(start, width)
        piece = spread_piece(terms, high_ref[:, lanes], low_ref[:, lanes]) * occ_ref[:, lanes]
        sums = sum_ref[:, lanes] * occ_ref[:, lanes]
        extra = [row_sums]
        for at in range(chunks):
            out[base + at * comps:base + (at + 1) * comps] = piece[:, at * LANES:(at + 1) * LANES]
            extra.append(sums[:, at * LANES:(at + 1) * LANES])
        extra.append(jnp.zeros((rows - chunks * comps - chunks - 1, LANES), F32))
        out[base + chunks * comps:base + rows] = jnp.concatenate(extra, axis=0)


def block_rows(comps, chunks):
    return comps * chunks + -(-(chunks + 1) // 8) * 8


def spread_pieces(me, scores, high, low, sums, occ, picks):
    comps = scores[0].shape[0]
    chunks = high.shape[1] // (LANES * lax.axis_size("cells"))
    rows = block_rows(comps, chunks)
    count = sum(len(group) for group in picks)
    return pl.pallas_call(
        functools.partial(spread_kernel, len(scores), picks),
        out_shape=[jax.ShapeDtypeStruct((len(group) * rows, LANES), F32) for group in picks],
        in_specs=[SCALARS] + [WHOLE] * (len(scores) + 4),
        out_specs=[WHOLE] * len(picks),
        compiler_params=PARAMS,
        cost_estimate=pl.CostEstimate(
            flops=10 * comps * count * chunks * LANES * high.shape[0], bytes_accessed=2**21, transcendentals=0
        ),
        name="spread",
    )(me, *scores, high, low, sums, occ)


def gram_kernel(scale, chunks, *refs):
    pieces, (spread_ref, gram_ref) = refs[:-2], refs[-2:]
    comps = spread_ref.shape[0]
    rows = block_rows(comps, chunks)
    total = tree_sum([ref[ref.shape[0] - rows:] for ref in pieces])
    extra = total[chunks * comps:chunks * comps + chunks + 1]
    eye = lax.broadcasted_iota(jnp.int32, (comps, LANES), 0) == lax.broadcasted_iota(jnp.int32, (comps, LANES), 1)
    row_sums = jnp.sum(jnp.where(eye, extra[:1], 0.0), axis=1, keepdims=True) * scale
    parts = [total[at * comps:(at + 1) * comps] - row_sums * extra[at + 1:at + 2] for at in range(chunks)]
    spread = jnp.concatenate(parts, axis=1)
    spread_ref[...] = spread
    gram_ref[...] = packed_gram(spread)


def packed_gram(spread):
    terms = split_terms(spread, 3)
    gram = term_product(terms, terms, NT)
    half = spread.shape[0] // 2
    return jnp.concatenate([gram[:half], gram[half:]], axis=1)


def centered_gram(pieces, comps, cell_total):
    chunks = pieces[0].shape[0] // comps
    return pl.pallas_call(
        functools.partial(gram_kernel, 1.0 / cell_total, chunks),
        out_shape=(
            jax.ShapeDtypeStruct((comps, chunks * LANES), F32),
            jax.ShapeDtypeStruct((comps // 2, comps * 2), F32),
        ),
        in_specs=[WHOLE] * len(pieces),
        out_specs=(WHOLE, WHOLE),
        compiler_params=PARAMS,
        name="gram",
    )(*pieces)


def plain_gram_kernel(scale, spread_ref, row_ref, sum_ref, out_ref, gram_ref):
    spread = spread_ref[...] - row_ref[...] * scale * sum_ref[...]
    out_ref[...] = spread
    gram_ref[...] = packed_gram(spread)


def plain_gram(spread, rows, sums, cell_total):
    comps, width = spread.shape
    return pl.pallas_call(
        functools.partial(plain_gram_kernel, 1.0 / cell_total),
        out_shape=(
            jax.ShapeDtypeStruct((comps, width), F32),
            jax.ShapeDtypeStruct((comps // 2, comps * 2), F32),
        ),
        in_specs=[WHOLE] * 3,
        out_specs=(WHOLE, WHOLE),
        compiler_params=PARAMS,
        name="plain_gram",
    )(spread, rows, sums)


def row_of(x, at):
    return jnp.broadcast_to(x[at:at + 1, :], x.shape)


def spread_column(rows, at):
    return jnp.broadcast_to(rows[:, at:at + 1], rows.shape)


def eliminate(groups, begin):
    groups = list(groups)
    edge = groups[0].shape[0]
    below = lax.broadcasted_iota(jnp.int32, groups[0].shape, 0)
    columns = [{c: spread_column(rows, begin + c) for c in range(edge)} for rows in groups]
    for at in range(len(groups)):
        scale = jnp.zeros_like(groups[0])
        later = (at + 1) * edge
        for i in range(at * edge, later, 2):
            if i == later - 4 and at + 1 < len(groups):
                for rows, cols in zip(groups[at:], columns[at:]):
                    cols.update({c: spread_column(rows, begin + c) for c in range(later, later + edge)})
            row = i - at * edge
            cols = columns[at]
            first, second = cols[i], cols[i + 1]
            a, b, c = row_of(first, row), row_of(second, row), row_of(second, row + 1)
            det = a * c - b * b
            inv_a = pl.reciprocal(a, approx=True)
            inv_c = a * pl.reciprocal(det, approx=True)
            ratio = b * inv_a
            scale = jnp.where(below == row, lax.rsqrt(a), jnp.where(below == row + 1, lax.rsqrt(det * inv_a), scale))
            factors = []
            for k in cols:
                if k > i + 1:
                    top = row_of(cols[k], row)
                    factors.append((k, top * inv_a, (row_of(cols[k], row + 1) - ratio * top) * inv_c))
            rows = groups[at]
            upper = row_of(rows, row) * inv_a
            rows = rows - jnp.where(below > row, first, 0.0) * upper
            lower = row_of(rows, row + 1) * inv_c
            groups[at] = rows - jnp.where(below > row + 1, second - ratio * first, 0.0) * lower
            for ahead in range(at, len(groups)):
                cols = columns[ahead]
                first = cols[i]
                second = cols[i + 1] - ratio * first
                for k, on_first, on_second in factors:
                    cols[k] = cols[k] - first * on_first - second * on_second
                if ahead > at:
                    groups[ahead] = groups[ahead] - first * upper - second * lower
                del cols[i], cols[i + 1]
        groups[at] = groups[at] * scale
    return groups


def scale_kernel(gram_ref, times_ref, plus_ref):
    gram = gram_ref[...]
    half, comps = gram.shape[0], gram.shape[1] // 2
    gram = jnp.concatenate([gram[:, :comps], gram[:, comps:]], axis=0)
    eye = lax.broadcasted_iota(jnp.int32, gram.shape, 0) == lax.broadcasted_iota(jnp.int32, gram.shape, 1)
    diagonal = jnp.where(eye, gram, 0.0)
    row_scale = lax.rsqrt(jnp.sum(diagonal, axis=1, keepdims=True))
    col_scale = lax.rsqrt(jnp.sum(diagonal, axis=0, keepdims=True))
    zeros = jnp.zeros_like(gram)
    times_ref[...] = jnp.concatenate([zeros, row_scale * col_scale], axis=1)
    plus_ref[...] = jnp.concatenate([jnp.where(eye, col_scale, 0.0), zeros], axis=1)


def scales(gram):
    half, lanes = gram.shape
    return pl.pallas_call(
        scale_kernel,
        out_shape=[jax.ShapeDtypeStruct((2 * half, lanes), F32)] * 2,
        in_specs=[WHOLE],
        out_specs=[WHOLE, WHOLE],
        compiler_params=PARAMS,
        name="scales",
    )(gram)


def basis_kernel(scale, *refs):
    grams, (times_ref, plus_ref, spread_ref, out_ref) = refs[:-4], refs[-4:]
    gram = tree_sum([ref[...] for ref in grams])
    comps = spread_ref.shape[0]
    gram = jnp.concatenate([pltpu.roll(gram, comps, 1), gram], axis=0)
    both = gram * times_ref[...] + plus_ref[...]
    groups = eliminate([both[at:at + 8] for at in range(0, comps, 8)], comps)
    inverse = jnp.concatenate(groups, axis=0)[:, :comps] * scale
    out_ref[...] = term_product(split_terms(inverse, 3), split_terms(spread_ref[...], 3), NN)


def orthonormal(grams, spread, scale):
    return pl.pallas_call(
        functools.partial(basis_kernel, scale),
        out_shape=jax.ShapeDtypeStruct(spread.shape, F32),
        in_specs=[WHOLE] * (len(grams) + 3),
        out_specs=WHOLE,
        compiler_params=PARAMS,
        name="orthonormal",
    )(*grams, *scales(grams[0]), spread)


def send(x, offset_cells, offset_genes):
    cells, genes = lax.axis_size("cells"), lax.axis_size("genes")
    pairs = []
    for c in range(cells):
        for g in range(genes):
            pairs.append((c * genes + g, (c ^ offset_cells) * genes + (g ^ offset_genes)))
    return lax.ppermute(x, ("cells", "genes"), pairs)


def gene_terms(x):
    x = x + send(x, 0, 1)
    return [x, send(x, 0, 3)]


def all_terms(x):
    x = x + send(x, 0, 1)
    across = [send(x, c, g) for c, g in ((1, 3), (1, 1), (0, 3))]
    x = (x + across[2]) + (across[1] + across[0])
    across = [send(x, c, 1) for c in (6, 4, 2)]
    return [x, across[2], across[1], across[0]]


def scattered_spread(scores, high, low, sums, occ, cell_total):
    comps = scores[0].shape[0]
    me = lax.axis_index("cells").astype(jnp.int32).reshape(1)
    make = functools.partial(spread_pieces, scores=scores, high=high, low=low, sums=sums, occ=occ)
    pair, first, across = make(me, picks=[[6, 2], [5], [7]])
    pair, me = lax.optimization_barrier((pair, me))
    pair, first = send(pair, 2, 0), send(first, 1, 0)
    across = send(across, 7, 0)
    far, own, *second = make(me, picks=[[4], [0], [3], [1]])
    first, second[0] = lax.optimization_barrier((first, second[0]))
    far, second[1] = lax.optimization_barrier((tree_sum([far, pair[:far.shape[0]], first]), second[1]))
    far = send(far, 4, 0)
    straight = [send(x, k, 0) for k, x in zip((3, 1), second)]
    return centered_gram([own, far, pair, across] + straight, comps, cell_total)


def all_alike(counts, occupancy, start_basis):
    tile_rows, tile_cols = occupancy.shape
    edge = counts.shape[0] // tile_rows
    logged = jnp.log(1.0 + counts.astype(F32)).reshape(tile_rows, edge, tile_cols, -1)
    logged = (logged * occupancy.astype(F32)[:, None, :, None]).reshape(counts.shape)
    high, low = split_terms(logged, 2)
    scores = lax.psum(dot(start_basis, high, NT) + dot(start_basis, low, NT), "genes")
    spread = spread_piece(split_terms(scores, 3), high, low)
    spread = lax.psum_scatter(spread, "cells", scatter_dimension=1, tiled=True)
    rows = lax.psum(jnp.sum(scores, axis=1, keepdims=True), "cells")
    sums = lax.psum_scatter(jnp.sum(logged, axis=0, keepdims=True), "cells", scatter_dimension=1, tiled=True)
    spread, gram = plain_gram(spread, rows, sums, counts.shape[0] * lax.axis_size("cells"))
    return [lax.psum(gram, ("cells", "genes"))], spread


def in_steps(counts, occupancy, start_basis):
    high, low, sums = log_terms(counts)
    scores, occ = score_part(occupancy, start_basis, high, low)
    cell_total = counts.shape[0] * lax.axis_size("cells")
    spread, gram = scattered_spread(gene_terms(scores), high, low, sums, occ, cell_total)
    return all_terms(gram), spread


def on_device(counts, occupancy, start_basis):
    gene_count = counts.shape[1]
    cells, genes = lax.axis_size("cells"), lax.axis_size("genes")
    halvings = cells == 1 << 3 and genes == 1 << 2
    tiles = occupancy.shape[0] == 1 and gene_count == occupancy.shape[1] * LANES
    work = in_steps if halvings and tiles and gene_count % (cells * LANES) == 0 else all_alike
    grams, spread = work(counts, occupancy, start_basis)
    return orthonormal(grams, spread, math.sqrt(gene_count * genes))


def solution(mesh):
    in_specs = (P("cells", "genes"), P("cells", "genes"), P(None, "genes"))
    out_specs = P(None, ("genes", "cells"))
    return jax.shard_map(
        on_device, mesh=mesh, in_specs=in_specs, out_specs=out_specs, check_vma=False
    )
```

```python
import functools
import math

import jax
import jax.numpy as jnp
from jax import lax
from jax.experimental import pallas as pl
from jax.experimental.pallas import tpu as pltpu
from jax.sharding import PartitionSpec as P

F32 = jnp.float32
BF16 = jnp.bfloat16
NN = (((1,), (0,)), ((), ()))
NT = (((1,), (1,)), ((), ()))
WHOLE = pl.BlockSpec(memory_space=pltpu.VMEM)
SCALARS = pl.BlockSpec(memory_space=pltpu.SMEM)
LANES = 128
PARAMS = pltpu.CompilerParams(vmem_limit_bytes=16 * 2**20)
LOG_PARAMS = pltpu.CompilerParams(vmem_limit_bytes=205 * 2**18)


def dot(a, b, dims):
    return lax.dot_general(a, b, dims, preferred_element_type=F32)


def split_terms(x, count):
    terms = []
    for _ in range(count):
        term = x.astype(BF16)
        terms.append(term)
        x = x - term.astype(F32)
    return terms


def tree_sum(parts):
    while len(parts) > 1:
        parts = [sum(parts[at + 1:at + 2], parts[at]) for at in range(0, len(parts), 2)]
    return parts[0]


def log_kernel(width, counts_hbm, high_ref, low_ref, counts_ref, counts_sem):
    cells, genes = high_ref.shape
    fetches = [
        pltpu.make_async_copy(
            counts_hbm.at[:, pl.ds(at * width, width)], counts_ref.at[:, pl.ds(at * width, width)], counts_sem.at[at]
        )
        for at in range(genes // width)
    ]
    for fetch in fetches:
        fetch.start()
    for at, fetch in enumerate(fetches):
        fetch.wait()
        for begin in range(at * width, (at + 1) * width, LANES):
            lanes = pl.ds(begin, LANES)
            logged = jnp.log(1.0 + counts_ref[:, lanes].astype(F32))
            high = logged.astype(BF16)
            high_ref[:, lanes] = high
            low_ref[:, lanes] = (logged - high.astype(F32)).astype(BF16)


def log_terms(counts):
    cells, genes = counts.shape
    width = genes // 8
    return pl.pallas_call(
        functools.partial(log_kernel, width),
        out_shape=(
            jax.ShapeDtypeStruct((cells, genes), BF16),
            jax.ShapeDtypeStruct((cells, genes), BF16),
        ),
        in_specs=[pl.BlockSpec(memory_space=pltpu.HBM)],
        out_specs=(WHOLE, WHOLE),
        scratch_shapes=[pltpu.VMEM(counts.shape, BF16), pltpu.SemaphoreType.DMA((genes // width,))],
        compiler_params=LOG_PARAMS,
        cost_estimate=pl.CostEstimate(flops=20 * cells * genes, bytes_accessed=8 * cells * genes, transcendentals=0),
        name="log_terms",
    )(counts)


def score_kernel(width, occ_ref, basis_ref, high_ref, low_ref, score_ref, lane_ref):
    comps, genes = basis_ref.shape
    edge = genes // occ_ref.shape[1]
    occupancy = occ_ref[...].astype(F32)
    scores = None
    for begin in range(0, genes, width):
        basis = []
        for at in range(begin, begin + width, edge):
            occ = jnp.broadcast_to(occupancy[:, at // edge:at // edge + 1], (1, edge))
            lane_ref[:, pl.ds(at, edge)] = occ
            basis.append(basis_ref[:, pl.ds(at, edge)] * occ.astype(BF16))
        basis = jnp.concatenate(basis, axis=1)
        lanes = pl.ds(begin, width)
        part = dot(basis, jnp.concatenate([high_ref[:, lanes], low_ref[:, lanes]], axis=0), NT)
        scores = part if scores is None else scores + part
    cells = score_ref.shape[1]
    score_ref[...] = scores[:, :cells] + scores[:, cells:]


def score_part(occupancy, basis, high, low):
    comps, genes = basis.shape
    cells = high.shape[0]
    return pl.pallas_call(
        functools.partial(score_kernel, genes // 4),
        out_shape=(jax.ShapeDtypeStruct((comps, cells), F32), jax.ShapeDtypeStruct((1, genes), F32)),
        in_specs=[WHOLE] * 4,
        out_specs=(WHOLE, WHOLE),
        compiler_params=PARAMS,
        name="scores",
    )(occupancy, basis, high, low)


def term_product(left, right, dims):
    rows = left[0].shape[0]
    left = jnp.concatenate([jnp.concatenate([term] * len(right), axis=1) for term in left], axis=0)
    out = dot(left, jnp.concatenate(right, axis=dims[0][1][0]), dims)
    parts = [out[at:at + rows] for at in range(0, out.shape[0], rows)]
    return functools.reduce(jnp.add, parts[::-1])


def spread_kernel(count, picks, me_ref, *refs):
    score_refs, outs = refs[:count], refs[count + 3:]
    high_ref, low_ref, occ_ref = refs[count:count + 3]
    scores = tree_sum([ref[...] for ref in score_refs])
    comps = scores.shape[0]
    terms = split_terms(scores, 2)
    scores = terms[0].astype(F32) + terms[1].astype(F32)
    terms = terms + [jnp.ones_like(scores, BF16)[:8]]
    eye = lax.broadcasted_iota(jnp.int32, (comps, LANES), 0) == lax.broadcasted_iota(jnp.int32, (comps, LANES), 1)
    row_sums = jnp.sum(jnp.where(eye, jnp.sum(scores, axis=1, keepdims=True), 0.0), axis=0, keepdims=True)
    chunks = high_ref.shape[1] // (LANES * lax.axis_size("cells"))
    width = chunks * LANES
    blocks = [(pick, out, at) for group, out in zip(picks, outs) for at, pick in enumerate(group)]
    rows = block_rows(comps, chunks)
    for pick, out, at_block in blocks:
        base = at_block * rows
        start = pl.multiple_of((me_ref[0] ^ pick) * width, width)
        lanes = pl.ds(start, width)
        left = jnp.concatenate([jnp.concatenate([term, term], axis=1) for term in terms], axis=0)
        out_all = dot(left, jnp.concatenate([high_ref[:, lanes], low_ref[:, lanes]], axis=0), NN) * occ_ref[:, lanes]
        piece = out_all[comps:2 * comps] + out_all[:comps]
        sums = out_all[2 * comps:2 * comps + 1]
        extra = [row_sums]
        for at in range(chunks):
            out[base + at * comps:base + (at + 1) * comps] = piece[:, at * LANES:(at + 1) * LANES]
            extra.append(sums[:, at * LANES:(at + 1) * LANES])
        extra.append(jnp.zeros((rows - chunks * comps - chunks - 1, LANES), F32))
        out[base + chunks * comps:base + rows] = jnp.concatenate(extra, axis=0)


def block_rows(comps, chunks):
    return comps * chunks + -(-(chunks + 1) // 8) * 8


def spread_pieces(me, scores, high, low, occ, picks):
    comps = scores[0].shape[0]
    chunks = high.shape[1] // (LANES * lax.axis_size("cells"))
    rows = block_rows(comps, chunks)
    count = sum(len(group) for group in picks)
    return pl.pallas_call(
        functools.partial(spread_kernel, len(scores), picks),
        out_shape=[jax.ShapeDtypeStruct((len(group) * rows, LANES), F32) for group in picks],
        in_specs=[SCALARS] + [WHOLE] * (len(scores) + 3),
        out_specs=[WHOLE] * len(picks),
        compiler_params=PARAMS,
        cost_estimate=pl.CostEstimate(
            flops=10 * comps * count * chunks * LANES * high.shape[0], bytes_accessed=2**21, transcendentals=0
        ),
        name="spread",
    )(me, *scores, high, low, occ)


def gram_kernel(scale, chunks, *refs):
    pieces, (spread_ref, gram_ref) = refs[:-2], refs[-2:]
    comps = spread_ref.shape[0]
    rows = block_rows(comps, chunks)
    total = tree_sum([ref[ref.shape[0] - rows:] for ref in pieces])
    extra = total[chunks * comps:chunks * comps + chunks + 1]
    eye = lax.broadcasted_iota(jnp.int32, (comps, LANES), 0) == lax.broadcasted_iota(jnp.int32, (comps, LANES), 1)
    row_sums = jnp.sum(jnp.where(eye, extra[:1], 0.0), axis=1, keepdims=True) * scale
    parts = [total[at * comps:(at + 1) * comps] - row_sums * extra[at + 1:at + 2] for at in range(chunks)]
    spread = jnp.concatenate(parts, axis=1)
    spread_ref[...] = spread
    gram_ref[...] = packed_gram(spread)


def packed_gram(spread):
    terms = split_terms(spread, 3)
    gram = term_product(terms, terms, NT)
    half = spread.shape[0] // 2
    return jnp.concatenate([gram[:half], gram[half:]], axis=1)


def centered_gram(pieces, comps, cell_total):
    chunks = pieces[0].shape[0] // comps
    return pl.pallas_call(
        functools.partial(gram_kernel, 1.0 / cell_total, chunks),
        out_shape=(
            jax.ShapeDtypeStruct((comps, chunks * LANES), F32),
            jax.ShapeDtypeStruct((comps // 2, comps * 2), F32),
        ),
        in_specs=[WHOLE] * len(pieces),
        out_specs=(WHOLE, WHOLE),
        compiler_params=PARAMS,
        name="gram",
    )(*pieces)


def plain_gram_kernel(scale, spread_ref, row_ref, sum_ref, out_ref, gram_ref):
    spread = spread_ref[...] - row_ref[...] * scale * sum_ref[...]
    out_ref[...] = spread
    gram_ref[...] = packed_gram(spread)


def plain_gram(spread, rows, sums, cell_total):
    comps, width = spread.shape
    return pl.pallas_call(
        functools.partial(plain_gram_kernel, 1.0 / cell_total),
        out_shape=(
            jax.ShapeDtypeStruct((comps, width), F32),
            jax.ShapeDtypeStruct((comps // 2, comps * 2), F32),
        ),
        in_specs=[WHOLE] * 3,
        out_specs=(WHOLE, WHOLE),
        compiler_params=PARAMS,
        name="plain_gram",
    )(spread, rows, sums)


def row_of(x, at):
    return jnp.broadcast_to(x[at:at + 1, :], x.shape)


def spread_column(rows, at):
    return jnp.broadcast_to(rows[:, at:at + 1], rows.shape)


def eliminate(groups, begin):
    groups = list(groups)
    edge = groups[0].shape[0]
    below = lax.broadcasted_iota(jnp.int32, groups[0].shape, 0)
    columns = [{c: spread_column(rows, begin + c) for c in range(edge)} for rows in groups]
    for at in range(len(groups)):
        scale = jnp.zeros_like(groups[0])
        later = (at + 1) * edge
        for i in range(at * edge, later, 2):
            if i == later - 4 and at + 1 < len(groups):
                for rows, cols in zip(groups[at:], columns[at:]):
                    cols.update({c: spread_column(rows, begin + c) for c in range(later, later + edge)})
            row = i - at * edge
            cols = columns[at]
            first, second = cols[i], cols[i + 1]
            a, b, c = row_of(first, row), row_of(second, row), row_of(second, row + 1)
            det = a * c - b * b
            inv_a = pl.reciprocal(a, approx=True)
            inv_c = a * pl.reciprocal(det, approx=True)
            ratio = b * inv_a
            scale = jnp.where(below == row, lax.rsqrt(a), jnp.where(below == row + 1, lax.rsqrt(det * inv_a), scale))
            factors = []
            for k in cols:
                if k > i + 1:
                    top = row_of(cols[k], row)
                    factors.append((k, top * inv_a, (row_of(cols[k], row + 1) - ratio * top) * inv_c))
            rows = groups[at]
            upper = row_of(rows, row) * inv_a
            rows = rows - jnp.where(below > row, first, 0.0) * upper
            lower = row_of(rows, row + 1) * inv_c
            groups[at] = rows - jnp.where(below > row + 1, second - ratio * first, 0.0) * lower
            for ahead in range(at, len(groups)):
                cols = columns[ahead]
                first = cols[i]
                second = cols[i + 1] - ratio * first
                for k, on_first, on_second in factors:
                    cols[k] = cols[k] - first * on_first - second * on_second
                if ahead > at:
                    groups[ahead] = groups[ahead] - first * upper - second * lower
                del cols[i], cols[i + 1]
        groups[at] = groups[at] * scale
    return groups


def scale_kernel(gram_ref, times_ref, plus_ref):
    gram = gram_ref[...]
    half, comps = gram.shape[0], gram.shape[1] // 2
    gram = jnp.concatenate([gram[:, :comps], gram[:, comps:]], axis=0)
    eye = lax.broadcasted_iota(jnp.int32, gram.shape, 0) == lax.broadcasted_iota(jnp.int32, gram.shape, 1)
    diagonal = jnp.where(eye, gram, 0.0)
    row_scale = lax.rsqrt(jnp.sum(diagonal, axis=1, keepdims=True))
    col_scale = lax.rsqrt(jnp.sum(diagonal, axis=0, keepdims=True))
    zeros = jnp.zeros_like(gram)
    times_ref[...] = jnp.concatenate([zeros, row_scale * col_scale], axis=1)
    plus_ref[...] = jnp.concatenate([jnp.where(eye, col_scale, 0.0), zeros], axis=1)


def scales(gram):
    half, lanes = gram.shape
    return pl.pallas_call(
        scale_kernel,
        out_shape=[jax.ShapeDtypeStruct((2 * half, lanes), F32)] * 2,
        in_specs=[WHOLE],
        out_specs=[WHOLE, WHOLE],
        compiler_params=PARAMS,
        name="scales",
    )(gram)


def basis_kernel(scale, *refs):
    grams, (times_ref, plus_ref, spread_ref, out_ref) = refs[:-4], refs[-4:]
    gram = tree_sum([ref[...] for ref in grams])
    comps = spread_ref.shape[0]
    gram = jnp.concatenate([pltpu.roll(gram, comps, 1), gram], axis=0)
    both = gram * times_ref[...] + plus_ref[...]
    groups = eliminate([both[at:at + 8] for at in range(0, comps, 8)], comps)
    inverse = jnp.concatenate(groups, axis=0)[:, :comps] * scale
    out_ref[...] = term_product(split_terms(inverse, 3), split_terms(spread_ref[...], 3), NN)


def orthonormal(grams, spread, scale):
    return pl.pallas_call(
        functools.partial(basis_kernel, scale),
        out_shape=jax.ShapeDtypeStruct(spread.shape, F32),
        in_specs=[WHOLE] * (len(grams) + 3),
        out_specs=WHOLE,
        compiler_params=PARAMS,
        name="orthonormal",
    )(*grams, *scales(grams[0]), spread)


def send(x, offset_cells, offset_genes):
    cells, genes = lax.axis_size("cells"), lax.axis_size("genes")
    pairs = []
    for c in range(cells):
        for g in range(genes):
            pairs.append((c * genes + g, (c ^ offset_cells) * genes + (g ^ offset_genes)))
    return lax.ppermute(x, ("cells", "genes"), pairs)


def gene_terms(x):
    x = x + send(x, 0, 1)
    return [x, send(x, 0, 3)]


def all_terms(x):
    x = x + send(x, 0, 1)
    across = [send(x, c, g) for c, g in ((1, 3), (1, 1), (0, 3))]
    x = (x + across[2]) + (across[1] + across[0])
    across = [send(x, c, 1) for c in (6, 4, 2)]
    return [x, across[2], across[1], across[0]]


def scattered_spread(scores, high, low, occ, cell_total):
    comps = scores[0].shape[0]
    me = lax.axis_index("cells").astype(jnp.int32).reshape(1)
    make = functools.partial(spread_pieces, scores=scores, high=high, low=low, occ=occ)
    pair, first, across = make(me, picks=[[6, 2], [5], [7]])
    pair, me = lax.optimization_barrier((pair, me))
    pair, first = send(pair, 2, 0), send(first, 1, 0)
    across = send(across, 7, 0)
    far, own, *second = make(me, picks=[[4], [0], [3], [1]])
    first, second[0] = lax.optimization_barrier((first, second[0]))
    far, second[1] = lax.optimization_barrier((tree_sum([far, pair[:far.shape[0]], first]), second[1]))
    far = send(far, 4, 0)
    straight = [send(x, k, 0) for k, x in zip((3, 1), second)]
    return centered_gram([own, far, pair, across] + straight, comps, cell_total)


def all_alike(counts, occupancy, start_basis):
    tile_rows, tile_cols = occupancy.shape
    edge = counts.shape[0] // tile_rows
    logged = jnp.log(1.0 + counts.astype(F32)).reshape(tile_rows, edge, tile_cols, -1)
    logged = (logged * occupancy.astype(F32)[:, None, :, None]).reshape(counts.shape)
    high, low = split_terms(logged, 2)
    scores = lax.psum(dot(start_basis, high, NT) + dot(start_basis, low, NT), "genes")
    spread = term_product(split_terms(scores, 2), [high, low], NN)
    spread = lax.psum_scatter(spread, "cells", scatter_dimension=1, tiled=True)
    rows = lax.psum(jnp.sum(scores, axis=1, keepdims=True), "cells")
    sums = lax.psum_scatter(jnp.sum(logged, axis=0, keepdims=True), "cells", scatter_dimension=1, tiled=True)
    spread, gram = plain_gram(spread, rows, sums, counts.shape[0] * lax.axis_size("cells"))
    return [lax.psum(gram, ("cells", "genes"))], spread


def in_steps(counts, occupancy, start_basis):
    high, low = log_terms(counts)
    scores, occ = score_part(occupancy, start_basis, high, low)
    cell_total = counts.shape[0] * lax.axis_size("cells")
    spread, gram = scattered_spread(gene_terms(scores), high, low, occ, cell_total)
    return all_terms(gram), spread


def on_device(counts, occupancy, start_basis):
    gene_count = counts.shape[1]
    cells, genes = lax.axis_size("cells"), lax.axis_size("genes")
    halvings = cells == 1 << 3 and genes == 1 << 2
    tiles = occupancy.shape[0] == 1 and gene_count == occupancy.shape[1] * LANES
    work = in_steps if halvings and tiles and gene_count % (cells * LANES) == 0 else all_alike
    grams, spread = work(counts, occupancy, start_basis)
    return orthonormal(grams, spread, math.sqrt(gene_count * genes))


def solution(mesh):
    in_specs = (P("cells", "genes"), P("cells", "genes"), P(None, "genes"))
    out_specs = P(None, ("genes", "cells"))
    return jax.shard_map(
        on_device, mesh=mesh, in_specs=in_specs, out_specs=out_specs, check_vma=False
    )
```

```python
import functools
import math

import jax
import jax.numpy as jnp
from jax import lax
from jax.experimental import pallas as pl
from jax.experimental.pallas import tpu as pltpu
from jax.sharding import PartitionSpec as P

F32 = jnp.float32
BF16 = jnp.bfloat16
NN = (((1,), (0,)), ((), ()))
NT = (((1,), (1,)), ((), ()))
WHOLE = pl.BlockSpec(memory_space=pltpu.VMEM)
SCALARS = pl.BlockSpec(memory_space=pltpu.SMEM)
LANES = 128
PARAMS = pltpu.CompilerParams(vmem_limit_bytes=16 * 2**20)
LOG_PARAMS = pltpu.CompilerParams(vmem_limit_bytes=205 * 2**18)


def dot(a, b, dims):
    return lax.dot_general(a, b, dims, preferred_element_type=F32)


def split_terms(x, count):
    terms = []
    for _ in range(count):
        term = x.astype(BF16)
        terms.append(term)
        x = x - term.astype(F32)
    return terms


def tree_sum(parts):
    while len(parts) > 1:
        parts = [sum(parts[at + 1:at + 2], parts[at]) for at in range(0, len(parts), 2)]
    return parts[0]


def log_kernel(width, counts_hbm, high_ref, low_ref, counts_ref, counts_sem):
    cells, genes = high_ref.shape
    fetches = [
        pltpu.make_async_copy(
            counts_hbm.at[:, pl.ds(at * width, width)], counts_ref.at[:, pl.ds(at * width, width)], counts_sem.at[at]
        )
        for at in range(genes // width)
    ]
    for fetch in fetches:
        fetch.start()
    for at, fetch in enumerate(fetches):
        fetch.wait()
        for begin in range(at * width, (at + 1) * width, LANES):
            lanes = pl.ds(begin, LANES)
            logged = jnp.log(1.0 + counts_ref[:, lanes].astype(F32))
            high = logged.astype(BF16)
            high_ref[:, lanes] = high
            low_ref[:, lanes] = (logged - high.astype(F32)).astype(BF16)


def log_terms(counts):
    cells, genes = counts.shape
    width = genes // 8
    return pl.pallas_call(
        functools.partial(log_kernel, width),
        out_shape=(
            jax.ShapeDtypeStruct((cells, genes), BF16),
            jax.ShapeDtypeStruct((cells, genes), BF16),
        ),
        in_specs=[pl.BlockSpec(memory_space=pltpu.HBM)],
        out_specs=(WHOLE, WHOLE),
        scratch_shapes=[pltpu.VMEM(counts.shape, BF16), pltpu.SemaphoreType.DMA((genes // width,))],
        compiler_params=LOG_PARAMS,
        cost_estimate=pl.CostEstimate(flops=20 * cells * genes, bytes_accessed=8 * cells * genes, transcendentals=0),
        name="log_terms",
    )(counts)


def score_kernel(width, occ_ref, basis_ref, high_ref, low_ref, score_ref, lane_ref):
    comps, genes = basis_ref.shape
    edge = genes // occ_ref.shape[1]
    occupancy = occ_ref[...].astype(F32)
    scores = None
    for begin in range(0, genes, width):
        basis = []
        for at in range(begin, begin + width, edge):
            occ = jnp.broadcast_to(occupancy[:, at // edge:at // edge + 1], (1, edge))
            lane_ref[:, pl.ds(at, edge)] = occ
            basis.append(basis_ref[:, pl.ds(at, edge)] * occ.astype(BF16))
        basis = jnp.concatenate(basis, axis=1)
        lanes = pl.ds(begin, width)
        part = dot(basis, jnp.concatenate([high_ref[:, lanes], low_ref[:, lanes]], axis=0), NT)
        scores = part if scores is None else scores + part
    cells = score_ref.shape[1]
    score_ref[...] = scores[:, :cells] + scores[:, cells:]


def score_part(occupancy, basis, high, low):
    comps, genes = basis.shape
    cells = high.shape[0]
    return pl.pallas_call(
        functools.partial(score_kernel, genes // 4),
        out_shape=(jax.ShapeDtypeStruct((comps, cells), F32), jax.ShapeDtypeStruct((1, genes), F32)),
        in_specs=[WHOLE] * 4,
        out_specs=(WHOLE, WHOLE),
        compiler_params=PARAMS,
        name="scores",
    )(occupancy, basis, high, low)


def term_product(left, right, dims):
    rows = left[0].shape[0]
    left = jnp.concatenate([jnp.concatenate([term] * len(right), axis=1) for term in left], axis=0)
    out = dot(left, jnp.concatenate(right, axis=dims[0][1][0]), dims)
    parts = [out[at:at + rows] for at in range(0, out.shape[0], rows)]
    return functools.reduce(jnp.add, parts[::-1])


def spread_kernel(count, picks, me_ref, *refs):
    score_refs, outs = refs[:count], refs[count + 3:]
    high_ref, low_ref, occ_ref = refs[count:count + 3]
    scores = tree_sum([ref[...] for ref in score_refs])
    comps = scores.shape[0]
    terms = split_terms(scores, 2)
    scores = terms[0].astype(F32) + terms[1].astype(F32)
    terms = terms + [jnp.ones_like(scores, BF16)[:8]]
    eye = lax.broadcasted_iota(jnp.int32, (comps, LANES), 0) == lax.broadcasted_iota(jnp.int32, (comps, LANES), 1)
    row_sums = jnp.sum(jnp.where(eye, jnp.sum(scores, axis=1, keepdims=True), 0.0), axis=0, keepdims=True)
    chunks = high_ref.shape[1] // (LANES * lax.axis_size("cells"))
    width = chunks * LANES
    blocks = [(pick, out, at) for group, out in zip(picks, outs) for at, pick in enumerate(group)]
    rows = block_rows(comps, chunks)
    for pick, out, at_block in blocks:
        base = at_block * rows
        start = pl.multiple_of((me_ref[0] ^ pick) * width, width)
        lanes = pl.ds(start, width)
        left = jnp.concatenate([jnp.concatenate([term, term], axis=1) for term in terms], axis=0)
        out_all = dot(left, jnp.concatenate([high_ref[:, lanes], low_ref[:, lanes]], axis=0), NN) * occ_ref[:, lanes]
        piece = out_all[comps:2 * comps] + out_all[:comps]
        sums = out_all[2 * comps:2 * comps + 1]
        extra = [row_sums]
        for at in range(chunks):
            out[base + at * comps:base + (at + 1) * comps] = piece[:, at * LANES:(at + 1) * LANES]
            extra.append(sums[:, at * LANES:(at + 1) * LANES])
        extra.append(jnp.zeros((rows - chunks * comps - chunks - 1, LANES), F32))
        out[base + chunks * comps:base + rows] = jnp.concatenate(extra, axis=0)


def block_rows(comps, chunks):
    return comps * chunks + -(-(chunks + 1) // 8) * 8


def spread_pieces(me, scores, high, low, occ, picks):
    comps = scores[0].shape[0]
    chunks = high.shape[1] // (LANES * lax.axis_size("cells"))
    rows = block_rows(comps, chunks)
    count = sum(len(group) for group in picks)
    return pl.pallas_call(
        functools.partial(spread_kernel, len(scores), picks),
        out_shape=[jax.ShapeDtypeStruct((len(group) * rows, LANES), F32) for group in picks],
        in_specs=[SCALARS] + [WHOLE] * (len(scores) + 3),
        out_specs=[WHOLE] * len(picks),
        compiler_params=PARAMS,
        cost_estimate=pl.CostEstimate(
            flops=10 * comps * count * chunks * LANES * high.shape[0], bytes_accessed=2**21, transcendentals=0
        ),
        name="spread",
    )(me, *scores, high, low, occ)


def gram_kernel(scale, chunks, *refs):
    pieces, (spread_ref, gram_ref) = refs[:-2], refs[-2:]
    comps = spread_ref.shape[0]
    rows = block_rows(comps, chunks)
    total = tree_sum([ref[ref.shape[0] - rows:] for ref in pieces])
    extra = total[chunks * comps:chunks * comps + chunks + 1]
    eye = lax.broadcasted_iota(jnp.int32, (comps, LANES), 0) == lax.broadcasted_iota(jnp.int32, (comps, LANES), 1)
    row_sums = jnp.sum(jnp.where(eye, extra[:1], 0.0), axis=1, keepdims=True) * scale
    parts = [total[at * comps:(at + 1) * comps] - row_sums * extra[at + 1:at + 2] for at in range(chunks)]
    spread = jnp.concatenate(parts, axis=1)
    spread_ref[...] = spread
    gram_ref[...] = packed_gram(spread)


def packed_gram(spread):
    terms = split_terms(spread, 3)
    gram = term_product(terms, terms, NT)
    half = spread.shape[0] // 2
    return jnp.concatenate([gram[:half], gram[half:]], axis=1)


def centered_gram(pieces, comps, cell_total):
    chunks = pieces[0].shape[0] // comps
    return pl.pallas_call(
        functools.partial(gram_kernel, 1.0 / cell_total, chunks),
        out_shape=(
            jax.ShapeDtypeStruct((comps, chunks * LANES), F32),
            jax.ShapeDtypeStruct((comps // 2, comps * 2), F32),
        ),
        in_specs=[WHOLE] * len(pieces),
        out_specs=(WHOLE, WHOLE),
        compiler_params=PARAMS,
        name="gram",
    )(*pieces)


def plain_gram_kernel(scale, spread_ref, row_ref, sum_ref, out_ref, gram_ref):
    spread = spread_ref[...] - row_ref[...] * scale * sum_ref[...]
    out_ref[...] = spread
    gram_ref[...] = packed_gram(spread)


def plain_gram(spread, rows, sums, cell_total):
    comps, width = spread.shape
    return pl.pallas_call(
        functools.partial(plain_gram_kernel, 1.0 / cell_total),
        out_shape=(
            jax.ShapeDtypeStruct((comps, width), F32),
            jax.ShapeDtypeStruct((comps // 2, comps * 2), F32),
        ),
        in_specs=[WHOLE] * 3,
        out_specs=(WHOLE, WHOLE),
        compiler_params=PARAMS,
        name="plain_gram",
    )(spread, rows, sums)


def row_of(x, at):
    return jnp.broadcast_to(x[at:at + 1, :], x.shape)


def spread_column(rows, at):
    return jnp.broadcast_to(rows[:, at:at + 1], rows.shape)


def eliminate(groups, begin):
    groups = list(groups)
    edge = groups[0].shape[0]
    below = lax.broadcasted_iota(jnp.int32, groups[0].shape, 0)
    columns = [{c: spread_column(rows, begin + c) for c in range(edge)} for rows in groups]
    for at in range(len(groups)):
        scale = jnp.zeros_like(groups[0])
        later = (at + 1) * edge
        for i in range(at * edge, later, 2):
            if i == later - 4 and at + 1 < len(groups):
                for rows, cols in zip(groups[at:], columns[at:]):
                    cols.update({c: spread_column(rows, begin + c) for c in range(later, later + edge)})
            row = i - at * edge
            cols = columns[at]
            first, second = cols[i], cols[i + 1]
            a, b, c = row_of(first, row), row_of(second, row), row_of(second, row + 1)
            det = a * c - b * b
            inv_a = pl.reciprocal(a, approx=True)
            inv_c = a * pl.reciprocal(det, approx=True)
            ratio = b * inv_a
            scale = jnp.where(below == row, lax.rsqrt(a), jnp.where(below == row + 1, lax.rsqrt(det * inv_a), scale))
            factors = []
            for k in cols:
                if k > i + 1:
                    top = row_of(cols[k], row)
                    factors.append((k, top * inv_a, (row_of(cols[k], row + 1) - ratio * top) * inv_c))
            rows = groups[at]
            upper = row_of(rows, row) * inv_a
            rows = rows - jnp.where(below > row, first, 0.0) * upper
            lower = row_of(rows, row + 1) * inv_c
            groups[at] = rows - jnp.where(below > row + 1, second - ratio * first, 0.0) * lower
            for ahead in range(at, len(groups)):
                cols = columns[ahead]
                first = cols[i]
                second = cols[i + 1] - ratio * first
                for k, on_first, on_second in factors:
                    cols[k] = cols[k] - first * on_first - second * on_second
                if ahead > at:
                    groups[ahead] = groups[ahead] - first * upper - second * lower
                del cols[i], cols[i + 1]
        groups[at] = groups[at] * scale
    return groups


def scale_kernel(gram_ref, times_ref, plus_ref):
    gram = gram_ref[...]
    half, comps = gram.shape[0], gram.shape[1] // 2
    gram = jnp.concatenate([gram[:, :comps], gram[:, comps:]], axis=0)
    eye = lax.broadcasted_iota(jnp.int32, gram.shape, 0) == lax.broadcasted_iota(jnp.int32, gram.shape, 1)
    diagonal = jnp.where(eye, gram, 0.0)
    row_scale = lax.rsqrt(jnp.sum(diagonal, axis=1, keepdims=True))
    col_scale = lax.rsqrt(jnp.sum(diagonal, axis=0, keepdims=True))
    zeros = jnp.zeros_like(gram)
    times_ref[...] = jnp.concatenate([zeros, row_scale * col_scale], axis=1)
    plus_ref[...] = jnp.concatenate([jnp.where(eye, col_scale, 0.0), zeros], axis=1)


def scales(gram):
    half, lanes = gram.shape
    return pl.pallas_call(
        scale_kernel,
        out_shape=[jax.ShapeDtypeStruct((2 * half, lanes), F32)] * 2,
        in_specs=[WHOLE],
        out_specs=[WHOLE, WHOLE],
        compiler_params=PARAMS,
        name="scales",
    )(gram)


def basis_kernel(scale, *refs):
    grams, (times_ref, plus_ref, spread_ref, out_ref) = refs[:-4], refs[-4:]
    gram = tree_sum([ref[...] for ref in grams])
    comps = spread_ref.shape[0]
    gram = jnp.concatenate([pltpu.roll(gram, comps, 1), gram], axis=0)
    both = gram * times_ref[...] + plus_ref[...]
    groups = eliminate([both[at:at + 8] for at in range(0, comps, 8)], comps)
    inverse = jnp.concatenate(groups, axis=0)[:, :comps] * scale
    out_ref[...] = term_product(split_terms(inverse, 3), split_terms(spread_ref[...], 3), NN)


def orthonormal(grams, spread, scale):
    return pl.pallas_call(
        functools.partial(basis_kernel, scale),
        out_shape=jax.ShapeDtypeStruct(spread.shape, F32),
        in_specs=[WHOLE] * (len(grams) + 3),
        out_specs=WHOLE,
        compiler_params=PARAMS,
        name="orthonormal",
    )(*grams, *scales(grams[0]), spread)


def send(x, offset_cells, offset_genes):
    cells, genes = lax.axis_size("cells"), lax.axis_size("genes")
    pairs = []
    for c in range(cells):
        for g in range(genes):
            pairs.append((c * genes + g, (c ^ offset_cells) * genes + (g ^ offset_genes)))
    return lax.ppermute(x, ("cells", "genes"), pairs)


def gene_terms(x):
    x = x + send(x, 0, 1)
    return [x, send(x, 0, 3)]


def all_terms(x):
    x = x + send(x, 0, 1)
    across = [send(x, c, g) for c, g in ((1, 3), (1, 1), (0, 3))]
    x = (x + across[2]) + (across[1] + across[0])
    far, both, near = [send(x, c, 1) for c in (4, 6, 2)]
    return [x, near, far, both]


def scattered_spread(scores, high, low, occ, cell_total):
    comps = scores[0].shape[0]
    me = lax.axis_index("cells").astype(jnp.int32).reshape(1)
    make = functools.partial(spread_pieces, scores=scores, high=high, low=low, occ=occ)
    pair, first, across = make(me, picks=[[6, 2], [5], [7]])
    pair, me = lax.optimization_barrier((pair, me))
    pair, first = send(pair, 2, 0), send(first, 1, 0)
    across = send(across, 7, 0)
    far, own, *second = make(me, picks=[[4], [0], [3], [1]])
    first, second[0] = lax.optimization_barrier((first, second[0]))
    far, second[1] = lax.optimization_barrier((tree_sum([far, pair[:far.shape[0]], first]), second[1]))
    far = send(far, 4, 0)
    straight = [send(x, k, 0) for k, x in zip((3, 1), second)]
    return centered_gram([own, far, pair, across] + straight, comps, cell_total)


def all_alike(counts, occupancy, start_basis):
    tile_rows, tile_cols = occupancy.shape
    edge = counts.shape[0] // tile_rows
    logged = jnp.log(1.0 + counts.astype(F32)).reshape(tile_rows, edge, tile_cols, -1)
    logged = (logged * occupancy.astype(F32)[:, None, :, None]).reshape(counts.shape)
    high, low = split_terms(logged, 2)
    scores = lax.psum(dot(start_basis, high, NT) + dot(start_basis, low, NT), "genes")
    spread = term_product(split_terms(scores, 2), [high, low], NN)
    spread = lax.psum_scatter(spread, "cells", scatter_dimension=1, tiled=True)
    rows = lax.psum(jnp.sum(scores, axis=1, keepdims=True), "cells")
    sums = lax.psum_scatter(jnp.sum(logged, axis=0, keepdims=True), "cells", scatter_dimension=1, tiled=True)
    spread, gram = plain_gram(spread, rows, sums, counts.shape[0] * lax.axis_size("cells"))
    return [lax.psum(gram, ("cells", "genes"))], spread


def in_steps(counts, occupancy, start_basis):
    high, low = log_terms(counts)
    scores, occ = score_part(occupancy, start_basis, high, low)
    cell_total = counts.shape[0] * lax.axis_size("cells")
    spread, gram = scattered_spread(gene_terms(scores), high, low, occ, cell_total)
    return all_terms(gram), spread


def on_device(counts, occupancy, start_basis):
    gene_count = counts.shape[1]
    cells, genes = lax.axis_size("cells"), lax.axis_size("genes")
    halvings = cells == 1 << 3 and genes == 1 << 2
    tiles = occupancy.shape[0] == 1 and gene_count == occupancy.shape[1] * LANES
    work = in_steps if halvings and tiles and gene_count % (cells * LANES) == 0 else all_alike
    grams, spread = work(counts, occupancy, start_basis)
    return orthonormal(grams, spread, math.sqrt(gene_count * genes))


def solution(mesh):
    in_specs = (P("cells", "genes"), P("cells", "genes"), P(None, "genes"))
    out_specs = P(None, ("genes", "cells"))
    return jax.shard_map(
        on_device, mesh=mesh, in_specs=in_specs, out_specs=out_specs, check_vma=False
    )
```

```python
import functools
import math

import jax
import jax.numpy as jnp
from jax import lax
from jax.experimental import pallas as pl
from jax.experimental.pallas import tpu as pltpu
from jax.sharding import PartitionSpec as P

F32 = jnp.float32
BF16 = jnp.bfloat16
NN = (((1,), (0,)), ((), ()))
NT = (((1,), (1,)), ((), ()))
WHOLE = pl.BlockSpec(memory_space=pltpu.VMEM)
SCALARS = pl.BlockSpec(memory_space=pltpu.SMEM)
LANES = 128
PARAMS = pltpu.CompilerParams(vmem_limit_bytes=16 * 2**20)
LOG_PARAMS = pltpu.CompilerParams(vmem_limit_bytes=205 * 2**18)


def dot(a, b, dims):
    return lax.dot_general(a, b, dims, preferred_element_type=F32)


def split_terms(x, count):
    terms = []
    for _ in range(count):
        term = x.astype(BF16)
        terms.append(term)
        x = x - term.astype(F32)
    return terms


def tree_sum(parts):
    while len(parts) > 1:
        parts = [sum(parts[at + 1:at + 2], parts[at]) for at in range(0, len(parts), 2)]
    return parts[0]


def log_kernel(width, counts_hbm, high_ref, low_ref, counts_ref, counts_sem):
    cells, genes = high_ref.shape
    fetches = [
        pltpu.make_async_copy(
            counts_hbm.at[:, pl.ds(at * width, width)], counts_ref.at[:, pl.ds(at * width, width)], counts_sem.at[at]
        )
        for at in range(genes // width)
    ]
    for fetch in fetches:
        fetch.start()
    for at, fetch in enumerate(fetches):
        fetch.wait()
        for begin in range(at * width, (at + 1) * width, LANES):
            lanes = pl.ds(begin, LANES)
            logged = jnp.log(1.0 + counts_ref[:, lanes].astype(F32))
            high = logged.astype(BF16)
            high_ref[:, lanes] = high
            low_ref[:, lanes] = (logged - high.astype(F32)).astype(BF16)


def log_terms(counts):
    cells, genes = counts.shape
    width = genes // 8
    return pl.pallas_call(
        functools.partial(log_kernel, width),
        out_shape=(
            jax.ShapeDtypeStruct((cells, genes), BF16),
            jax.ShapeDtypeStruct((cells, genes), BF16),
        ),
        in_specs=[pl.BlockSpec(memory_space=pltpu.HBM)],
        out_specs=(WHOLE, WHOLE),
        scratch_shapes=[pltpu.VMEM(counts.shape, BF16), pltpu.SemaphoreType.DMA((genes // width,))],
        compiler_params=LOG_PARAMS,
        cost_estimate=pl.CostEstimate(flops=20 * cells * genes, bytes_accessed=8 * cells * genes, transcendentals=0),
        name="log_terms",
    )(counts)


def score_kernel(width, occ_ref, basis_ref, high_ref, low_ref, score_ref, lane_ref):
    comps, genes = basis_ref.shape
    edge = genes // occ_ref.shape[1]
    occupancy = occ_ref[...].astype(F32)
    scores = None
    for begin in range(0, genes, width):
        basis = []
        for at in range(begin, begin + width, edge):
            occ = jnp.broadcast_to(occupancy[:, at // edge:at // edge + 1], (1, edge))
            lane_ref[:, pl.ds(at, edge)] = occ
            basis.append(basis_ref[:, pl.ds(at, edge)] * occ.astype(BF16))
        basis = jnp.concatenate(basis, axis=1)
        lanes = pl.ds(begin, width)
        part = dot(basis, jnp.concatenate([high_ref[:, lanes], low_ref[:, lanes]], axis=0), NT)
        scores = part if scores is None else scores + part
    cells = score_ref.shape[1]
    score_ref[...] = scores[:, :cells] + scores[:, cells:]


def score_part(occupancy, basis, high, low):
    comps, genes = basis.shape
    cells = high.shape[0]
    return pl.pallas_call(
        functools.partial(score_kernel, genes // 4),
        out_shape=(jax.ShapeDtypeStruct((comps, cells), F32), jax.ShapeDtypeStruct((1, genes), F32)),
        in_specs=[WHOLE] * 4,
        out_specs=(WHOLE, WHOLE),
        compiler_params=PARAMS,
        name="scores",
    )(occupancy, basis, high, low)


def term_product(left, right, dims):
    rows = left[0].shape[0]
    left = jnp.concatenate([jnp.concatenate([term] * len(right), axis=1) for term in left], axis=0)
    out = dot(left, jnp.concatenate(right, axis=dims[0][1][0]), dims)
    parts = [out[at:at + rows] for at in range(0, out.shape[0], rows)]
    return functools.reduce(jnp.add, parts[::-1])


def spread_kernel(count, picks, me_ref, *refs):
    score_refs, outs = refs[:count], refs[count + 3:]
    high_ref, low_ref, occ_ref = refs[count:count + 3]
    scores = tree_sum([ref[...] for ref in score_refs])
    comps = scores.shape[0]
    terms = split_terms(scores, 2)
    scores = terms[0].astype(F32) + terms[1].astype(F32)
    terms = terms + [jnp.ones_like(scores, BF16)[:8]]
    eye = lax.broadcasted_iota(jnp.int32, (comps, LANES), 0) == lax.broadcasted_iota(jnp.int32, (comps, LANES), 1)
    row_sums = jnp.sum(jnp.where(eye, jnp.sum(scores, axis=1, keepdims=True), 0.0), axis=0, keepdims=True)
    chunks = high_ref.shape[1] // (LANES * lax.axis_size("cells"))
    width = chunks * LANES
    blocks = [(pick, out, at) for group, out in zip(picks, outs) for at, pick in enumerate(group)]
    rows = block_rows(comps, chunks)
    for pick, out, at_block in blocks:
        base = at_block * rows
        start = pl.multiple_of((me_ref[0] ^ pick) * width, width)
        lanes = pl.ds(start, width)
        left = jnp.concatenate([jnp.concatenate([term, term], axis=1) for term in terms], axis=0)
        out_all = dot(left, jnp.concatenate([high_ref[:, lanes], low_ref[:, lanes]], axis=0), NN) * occ_ref[:, lanes]
        piece = out_all[comps:2 * comps] + out_all[:comps]
        sums = out_all[2 * comps:2 * comps + 1]
        extra = [row_sums]
        for at in range(chunks):
            out[base + at * comps:base + (at + 1) * comps] = piece[:, at * LANES:(at + 1) * LANES]
            extra.append(sums[:, at * LANES:(at + 1) * LANES])
        extra.append(jnp.zeros((rows - chunks * comps - chunks - 1, LANES), F32))
        out[base + chunks * comps:base + rows] = jnp.concatenate(extra, axis=0)


def block_rows(comps, chunks):
    return comps * chunks + -(-(chunks + 1) // 8) * 8


def spread_pieces(me, scores, high, low, occ, picks):
    comps = scores[0].shape[0]
    chunks = high.shape[1] // (LANES * lax.axis_size("cells"))
    rows = block_rows(comps, chunks)
    count = sum(len(group) for group in picks)
    return pl.pallas_call(
        functools.partial(spread_kernel, len(scores), picks),
        out_shape=[jax.ShapeDtypeStruct((len(group) * rows, LANES), F32) for group in picks],
        in_specs=[SCALARS] + [WHOLE] * (len(scores) + 3),
        out_specs=[WHOLE] * len(picks),
        compiler_params=PARAMS,
        cost_estimate=pl.CostEstimate(
            flops=10 * comps * count * chunks * LANES * high.shape[0], bytes_accessed=2**21, transcendentals=0
        ),
        name="spread",
    )(me, *scores, high, low, occ)


def gram_kernel(scale, chunks, *refs):
    pieces, (spread_ref, gram_ref) = refs[:-2], refs[-2:]
    comps = spread_ref.shape[0]
    rows = block_rows(comps, chunks)
    total = tree_sum([ref[ref.shape[0] - rows:] for ref in pieces])
    extra = total[chunks * comps:chunks * comps + chunks + 1]
    eye = lax.broadcasted_iota(jnp.int32, (comps, LANES), 0) == lax.broadcasted_iota(jnp.int32, (comps, LANES), 1)
    row_sums = jnp.sum(jnp.where(eye, extra[:1], 0.0), axis=1, keepdims=True) * scale
    parts = [total[at * comps:(at + 1) * comps] - row_sums * extra[at + 1:at + 2] for at in range(chunks)]
    spread = jnp.concatenate(parts, axis=1)
    spread_ref[...] = spread
    gram_ref[...] = packed_gram(spread)


def packed_gram(spread):
    terms = split_terms(spread, 3)
    gram = term_product(terms, terms, NT)
    half = spread.shape[0] // 2
    return jnp.concatenate([gram[:half], gram[half:]], axis=1)


def centered_gram(pieces, comps, cell_total):
    chunks = pieces[0].shape[0] // comps
    return pl.pallas_call(
        functools.partial(gram_kernel, 1.0 / cell_total, chunks),
        out_shape=(
            jax.ShapeDtypeStruct((comps, chunks * LANES), F32),
            jax.ShapeDtypeStruct((comps // 2, comps * 2), F32),
        ),
        in_specs=[WHOLE] * len(pieces),
        out_specs=(WHOLE, WHOLE),
        compiler_params=PARAMS,
        name="gram",
    )(*pieces)


def plain_gram_kernel(scale, spread_ref, row_ref, sum_ref, out_ref, gram_ref):
    spread = spread_ref[...] - row_ref[...] * scale * sum_ref[...]
    out_ref[...] = spread
    gram_ref[...] = packed_gram(spread)


def plain_gram(spread, rows, sums, cell_total):
    comps, width = spread.shape
    return pl.pallas_call(
        functools.partial(plain_gram_kernel, 1.0 / cell_total),
        out_shape=(
            jax.ShapeDtypeStruct((comps, width), F32),
            jax.ShapeDtypeStruct((comps // 2, comps * 2), F32),
        ),
        in_specs=[WHOLE] * 3,
        out_specs=(WHOLE, WHOLE),
        compiler_params=PARAMS,
        name="plain_gram",
    )(spread, rows, sums)


def row_of(x, at):
    return jnp.broadcast_to(x[at:at + 1, :], x.shape)


def spread_column(rows, at):
    return jnp.broadcast_to(rows[:, at:at + 1], rows.shape)


def eliminate(groups, begin):
    groups = list(groups)
    edge = groups[0].shape[0]
    below = lax.broadcasted_iota(jnp.int32, groups[0].shape, 0)
    columns = [{c: spread_column(rows, begin + c) for c in range(edge)} for rows in groups]
    for at in range(len(groups)):
        scale = jnp.zeros_like(groups[0])
        later = (at + 1) * edge
        for i in range(at * edge, later, 2):
            if i == later - 4 and at + 1 < len(groups):
                for rows, cols in zip(groups[at:], columns[at:]):
                    cols.update({c: spread_column(rows, begin + c) for c in range(later, later + edge)})
            row = i - at * edge
            cols = columns[at]
            first, second = cols[i], cols[i + 1]
            a, b, c = row_of(first, row), row_of(second, row), row_of(second, row + 1)
            det = a * c - b * b
            inv_a = pl.reciprocal(a, approx=True)
            inv_c = a * pl.reciprocal(det, approx=True)
            ratio = b * inv_a
            scale = jnp.where(below == row, lax.rsqrt(a), jnp.where(below == row + 1, lax.rsqrt(det * inv_a), scale))
            factors = []
            for k in cols:
                if k > i + 1:
                    top = row_of(cols[k], row)
                    factors.append((k, top * inv_a, (row_of(cols[k], row + 1) - ratio * top) * inv_c))
            rows = groups[at]
            upper = row_of(rows, row) * inv_a
            rows = rows - jnp.where(below > row, first, 0.0) * upper
            lower = row_of(rows, row + 1) * inv_c
            groups[at] = rows - jnp.where(below > row + 1, second - ratio * first, 0.0) * lower
            for ahead in range(at, len(groups)):
                cols = columns[ahead]
                first = cols[i]
                second = cols[i + 1] - ratio * first
                for k, on_first, on_second in factors:
                    cols[k] = cols[k] - first * on_first - second * on_second
                if ahead > at:
                    groups[ahead] = groups[ahead] - first * upper - second * lower
                del cols[i], cols[i + 1]
        groups[at] = groups[at] * scale
    return groups


def scale_kernel(gram_ref, times_ref, plus_ref):
    gram = gram_ref[...]
    half, comps = gram.shape[0], gram.shape[1] // 2
    gram = jnp.concatenate([gram[:, :comps], gram[:, comps:]], axis=0)
    eye = lax.broadcasted_iota(jnp.int32, gram.shape, 0) == lax.broadcasted_iota(jnp.int32, gram.shape, 1)
    diagonal = jnp.where(eye, gram, 0.0)
    row_scale = lax.rsqrt(jnp.sum(diagonal, axis=1, keepdims=True))
    col_scale = lax.rsqrt(jnp.sum(diagonal, axis=0, keepdims=True))
    zeros = jnp.zeros_like(gram)
    times_ref[...] = jnp.concatenate([zeros, row_scale * col_scale], axis=1)
    plus_ref[...] = jnp.concatenate([jnp.where(eye, col_scale, 0.0), zeros], axis=1)


def scales(gram):
    half, lanes = gram.shape
    return pl.pallas_call(
        scale_kernel,
        out_shape=[jax.ShapeDtypeStruct((2 * half, lanes), F32)] * 2,
        in_specs=[WHOLE],
        out_specs=[WHOLE, WHOLE],
        compiler_params=PARAMS,
        name="scales",
    )(gram)


def basis_kernel(scale, *refs):
    grams, (times_ref, plus_ref, spread_ref, out_ref) = refs[:-4], refs[-4:]
    gram = tree_sum([ref[...] for ref in grams])
    comps = spread_ref.shape[0]
    gram = jnp.concatenate([pltpu.roll(gram, comps, 1), gram], axis=0)
    both = gram * times_ref[...] + plus_ref[...]
    groups = eliminate([both[at:at + 8] for at in range(0, comps, 8)], comps)
    inverse = jnp.concatenate(groups, axis=0)[:, :comps] * scale
    out_ref[...] = term_product(split_terms(inverse, 3), split_terms(spread_ref[...], 3), NN)


def orthonormal(grams, spread, scale):
    return pl.pallas_call(
        functools.partial(basis_kernel, scale),
        out_shape=jax.ShapeDtypeStruct(spread.shape, F32),
        in_specs=[WHOLE] * (len(grams) + 3),
        out_specs=WHOLE,
        compiler_params=PARAMS,
        name="orthonormal",
    )(*grams, *scales(grams[0]), spread)


def send(x, offset_cells, offset_genes):
    cells, genes = lax.axis_size("cells"), lax.axis_size("genes")
    pairs = []
    for c in range(cells):
        for g in range(genes):
            pairs.append((c * genes + g, (c ^ offset_cells) * genes + (g ^ offset_genes)))
    return lax.ppermute(x, ("cells", "genes"), pairs)


def gene_terms(x):
    x = x + send(x, 0, 1)
    return [x, send(x, 0, 3)]


def all_terms(x):
    x = x + send(x, 0, 1)
    across = [send(x, c, g) for c, g in ((1, 3), (1, 1), (0, 3))]
    x = (x + across[2]) + (across[1] + across[0])
    far, both, near = [send(x, c, 1) for c in (4, 6, 2)]
    return [x, near, both, far]


def scattered_spread(scores, high, low, occ, cell_total):
    comps = scores[0].shape[0]
    me = lax.axis_index("cells").astype(jnp.int32).reshape(1)
    make = functools.partial(spread_pieces, scores=scores, high=high, low=low, occ=occ)
    pair, first, across = make(me, picks=[[6, 2], [5], [7]])
    pair, me = lax.optimization_barrier((pair, me))
    pair, first = send(pair, 2, 0), send(first, 1, 0)
    across = send(across, 7, 0)
    far, own, *second = make(me, picks=[[4], [0], [3], [1]])
    first, second[0] = lax.optimization_barrier((first, second[0]))
    far, second[1] = lax.optimization_barrier((tree_sum([far, pair[:far.shape[0]], first]), second[1]))
    far = send(far, 4, 0)
    straight = [send(x, k, 0) for k, x in zip((3, 1), second)]
    return centered_gram([own, far, pair, across] + straight, comps, cell_total)


def all_alike(counts, occupancy, start_basis):
    tile_rows, tile_cols = occupancy.shape
    edge = counts.shape[0] // tile_rows
    logged = jnp.log(1.0 + counts.astype(F32)).reshape(tile_rows, edge, tile_cols, -1)
    logged = (logged * occupancy.astype(F32)[:, None, :, None]).reshape(counts.shape)
    high, low = split_terms(logged, 2)
    scores = lax.psum(dot(start_basis, high, NT) + dot(start_basis, low, NT), "genes")
    spread = term_product(split_terms(scores, 2), [high, low], NN)
    spread = lax.psum_scatter(spread, "cells", scatter_dimension=1, tiled=True)
    rows = lax.psum(jnp.sum(scores, axis=1, keepdims=True), "cells")
    sums = lax.psum_scatter(jnp.sum(logged, axis=0, keepdims=True), "cells", scatter_dimension=1, tiled=True)
    spread, gram = plain_gram(spread, rows, sums, counts.shape[0] * lax.axis_size("cells"))
    return [lax.psum(gram, ("cells", "genes"))], spread


def in_steps(counts, occupancy, start_basis):
    high, low = log_terms(counts)
    scores, occ = score_part(occupancy, start_basis, high, low)
    cell_total = counts.shape[0] * lax.axis_size("cells")
    spread, gram = scattered_spread(gene_terms(scores), high, low, occ, cell_total)
    return all_terms(gram), spread


def on_device(counts, occupancy, start_basis):
    gene_count = counts.shape[1]
    cells, genes = lax.axis_size("cells"), lax.axis_size("genes")
    halvings = cells == 1 << 3 and genes == 1 << 2
    tiles = occupancy.shape[0] == 1 and gene_count == occupancy.shape[1] * LANES
    work = in_steps if halvings and tiles and gene_count % (cells * LANES) == 0 else all_alike
    grams, spread = work(counts, occupancy, start_basis)
    return orthonormal(grams, spread, math.sqrt(gene_count * genes))


def solution(mesh):
    in_specs = (P("cells", "genes"), P("cells", "genes"), P(None, "genes"))
    out_specs = P(None, ("genes", "cells"))
    return jax.shard_map(
        on_device, mesh=mesh, in_specs=in_specs, out_specs=out_specs, check_vma=False
    )
```

```python
import functools
import math

import jax
import jax.numpy as jnp
from jax import lax
from jax.experimental import pallas as pl
from jax.experimental.pallas import tpu as pltpu
from jax.sharding import PartitionSpec as P

F32 = jnp.float32
BF16 = jnp.bfloat16
NN = (((1,), (0,)), ((), ()))
NT = (((1,), (1,)), ((), ()))
WHOLE = pl.BlockSpec(memory_space=pltpu.VMEM)
SCALARS = pl.BlockSpec(memory_space=pltpu.SMEM)
LANES = 128
PARAMS = pltpu.CompilerParams(vmem_limit_bytes=16 * 2**20)
LOG_PARAMS = pltpu.CompilerParams(vmem_limit_bytes=205 * 2**18)


def dot(a, b, dims):
    return lax.dot_general(a, b, dims, preferred_element_type=F32)


def split_terms(x, count):
    terms = []
    for _ in range(count):
        term = x.astype(BF16)
        terms.append(term)
        x = x - term.astype(F32)
    return terms


def tree_sum(parts):
    while len(parts) > 1:
        parts = [sum(parts[at + 1:at + 2], parts[at]) for at in range(0, len(parts), 2)]
    return parts[0]


def log_kernel(width, counts_hbm, high_ref, low_ref, counts_ref, counts_sem):
    cells, genes = high_ref.shape
    fetches = [
        pltpu.make_async_copy(
            counts_hbm.at[:, pl.ds(at * width, width)], counts_ref.at[:, pl.ds(at * width, width)], counts_sem.at[at]
        )
        for at in range(genes // width)
    ]
    for fetch in fetches:
        fetch.start()
    for at, fetch in enumerate(fetches):
        fetch.wait()
        for begin in range(at * width, (at + 1) * width, LANES):
            lanes = pl.ds(begin, LANES)
            logged = jnp.log(1.0 + counts_ref[:, lanes].astype(F32))
            high = logged.astype(BF16)
            high_ref[:, lanes] = high
            low_ref[:, lanes] = (logged - high.astype(F32)).astype(BF16)


def log_terms(counts):
    cells, genes = counts.shape
    width = genes // 8
    return pl.pallas_call(
        functools.partial(log_kernel, width),
        out_shape=(
            jax.ShapeDtypeStruct((cells, genes), BF16),
            jax.ShapeDtypeStruct((cells, genes), BF16),
        ),
        in_specs=[pl.BlockSpec(memory_space=pltpu.HBM)],
        out_specs=(WHOLE, WHOLE),
        scratch_shapes=[pltpu.VMEM(counts.shape, BF16), pltpu.SemaphoreType.DMA((genes // width,))],
        compiler_params=LOG_PARAMS,
        cost_estimate=pl.CostEstimate(flops=20 * cells * genes, bytes_accessed=8 * cells * genes, transcendentals=0),
        name="log_terms",
    )(counts)


def score_kernel(width, occ_ref, basis_ref, high_ref, low_ref, score_ref, lane_ref):
    comps, genes = basis_ref.shape
    edge = genes // occ_ref.shape[1]
    occupancy = occ_ref[...].astype(F32)
    scores = None
    for begin in range(0, genes, width):
        basis = []
        for at in range(begin, begin + width, edge):
            occ = jnp.broadcast_to(occupancy[:, at // edge:at // edge + 1], (1, edge))
            lane_ref[:, pl.ds(at, edge)] = occ
            basis.append(basis_ref[:, pl.ds(at, edge)] * occ.astype(BF16))
        basis = jnp.concatenate(basis, axis=1)
        lanes = pl.ds(begin, width)
        part = dot(basis, jnp.concatenate([high_ref[:, lanes], low_ref[:, lanes]], axis=0), NT)
        scores = part if scores is None else scores + part
    cells = score_ref.shape[1]
    score_ref[...] = scores[:, :cells] + scores[:, cells:]


def score_part(occupancy, basis, high, low):
    comps, genes = basis.shape
    cells = high.shape[0]
    return pl.pallas_call(
        functools.partial(score_kernel, genes // 4),
        out_shape=(jax.ShapeDtypeStruct((comps, cells), F32), jax.ShapeDtypeStruct((1, genes), F32)),
        in_specs=[WHOLE] * 4,
        out_specs=(WHOLE, WHOLE),
        compiler_params=PARAMS,
        name="scores",
    )(occupancy, basis, high, low)


def term_product(left, right, dims):
    rows = left[0].shape[0]
    left = jnp.concatenate([jnp.concatenate([term] * len(right), axis=1) for term in left], axis=0)
    out = dot(left, jnp.concatenate(right, axis=dims[0][1][0]), dims)
    parts = [out[at:at + rows] for at in range(0, out.shape[0], rows)]
    return functools.reduce(jnp.add, parts[::-1])


def spread_kernel(count, picks, me_ref, *refs):
    score_refs, outs = refs[:count], refs[count + 3:]
    high_ref, low_ref, occ_ref = refs[count:count + 3]
    scores = tree_sum([ref[...] for ref in score_refs])
    comps = scores.shape[0]
    terms = split_terms(scores, 2)
    scores = terms[0].astype(F32) + terms[1].astype(F32)
    terms = terms + [jnp.ones_like(scores, BF16)[:8]]
    eye = lax.broadcasted_iota(jnp.int32, (comps, LANES), 0) == lax.broadcasted_iota(jnp.int32, (comps, LANES), 1)
    row_sums = jnp.sum(jnp.where(eye, jnp.sum(scores, axis=1, keepdims=True), 0.0), axis=0, keepdims=True)
    chunks = high_ref.shape[1] // (LANES * lax.axis_size("cells"))
    width = chunks * LANES
    blocks = [(pick, out, at) for group, out in zip(picks, outs) for at, pick in enumerate(group)]
    rows = block_rows(comps, chunks)
    for pick, out, at_block in blocks:
        base = at_block * rows
        start = pl.multiple_of((me_ref[0] ^ pick) * width, width)
        lanes = pl.ds(start, width)
        left = jnp.concatenate([jnp.concatenate([term, term], axis=1) for term in terms], axis=0)
        out_all = dot(left, jnp.concatenate([high_ref[:, lanes], low_ref[:, lanes]], axis=0), NN) * occ_ref[:, lanes]
        piece = out_all[comps:2 * comps] + out_all[:comps]
        sums = out_all[2 * comps:2 * comps + 1]
        extra = [row_sums]
        for at in range(chunks):
            out[base + at * comps:base + (at + 1) * comps] = piece[:, at * LANES:(at + 1) * LANES]
            extra.append(sums[:, at * LANES:(at + 1) * LANES])
        extra.append(jnp.zeros((rows - chunks * comps - chunks - 1, LANES), F32))
        out[base + chunks * comps:base + rows] = jnp.concatenate(extra, axis=0)


def block_rows(comps, chunks):
    return comps * chunks + -(-(chunks + 1) // 8) * 8


def spread_pieces(me, scores, high, low, occ, picks):
    comps = scores[0].shape[0]
    chunks = high.shape[1] // (LANES * lax.axis_size("cells"))
    rows = block_rows(comps, chunks)
    count = sum(len(group) for group in picks)
    return pl.pallas_call(
        functools.partial(spread_kernel, len(scores), picks),
        out_shape=[jax.ShapeDtypeStruct((len(group) * rows, LANES), F32) for group in picks],
        in_specs=[SCALARS] + [WHOLE] * (len(scores) + 3),
        out_specs=[WHOLE] * len(picks),
        compiler_params=PARAMS,
        cost_estimate=pl.CostEstimate(
            flops=10 * comps * count * chunks * LANES * high.shape[0], bytes_accessed=2**21, transcendentals=0
        ),
        name="spread",
    )(me, *scores, high, low, occ)


def gram_kernel(scale, chunks, *refs):
    pieces, (spread_ref, gram_ref) = refs[:-2], refs[-2:]
    comps = spread_ref.shape[0]
    rows = block_rows(comps, chunks)
    total = tree_sum([ref[ref.shape[0] - rows:] for ref in pieces])
    extra = total[chunks * comps:chunks * comps + chunks + 1]
    eye = lax.broadcasted_iota(jnp.int32, (comps, LANES), 0) == lax.broadcasted_iota(jnp.int32, (comps, LANES), 1)
    row_sums = jnp.sum(jnp.where(eye, extra[:1], 0.0), axis=1, keepdims=True) * scale
    parts = [total[at * comps:(at + 1) * comps] - row_sums * extra[at + 1:at + 2] for at in range(chunks)]
    spread = jnp.concatenate(parts, axis=1)
    spread_ref[...] = spread
    gram_ref[...] = packed_gram(spread)


def packed_gram(spread):
    terms = split_terms(spread, 3)
    gram = term_product(terms, terms, NT)
    half = spread.shape[0] // 2
    return jnp.concatenate([gram[:half], gram[half:]], axis=1)


def centered_gram(pieces, comps, cell_total):
    chunks = pieces[0].shape[0] // comps
    return pl.pallas_call(
        functools.partial(gram_kernel, 1.0 / cell_total, chunks),
        out_shape=(
            jax.ShapeDtypeStruct((comps, chunks * LANES), F32),
            jax.ShapeDtypeStruct((comps // 2, comps * 2), F32),
        ),
        in_specs=[WHOLE] * len(pieces),
        out_specs=(WHOLE, WHOLE),
        compiler_params=PARAMS,
        name="gram",
    )(*pieces)


def plain_gram_kernel(scale, spread_ref, row_ref, sum_ref, out_ref, gram_ref):
    spread = spread_ref[...] - row_ref[...] * scale * sum_ref[...]
    out_ref[...] = spread
    gram_ref[...] = packed_gram(spread)


def plain_gram(spread, rows, sums, cell_total):
    comps, width = spread.shape
    return pl.pallas_call(
        functools.partial(plain_gram_kernel, 1.0 / cell_total),
        out_shape=(
            jax.ShapeDtypeStruct((comps, width), F32),
            jax.ShapeDtypeStruct((comps // 2, comps * 2), F32),
        ),
        in_specs=[WHOLE] * 3,
        out_specs=(WHOLE, WHOLE),
        compiler_params=PARAMS,
        name="plain_gram",
    )(spread, rows, sums)


def row_of(x, at):
    return jnp.broadcast_to(x[at:at + 1, :], x.shape)


def spread_column(rows, at):
    return jnp.broadcast_to(rows[:, at:at + 1], rows.shape)


def eliminate(groups, begin):
    groups = list(groups)
    edge = groups[0].shape[0]
    below = lax.broadcasted_iota(jnp.int32, groups[0].shape, 0)
    columns = [{c: spread_column(rows, begin + c) for c in range(edge)} for rows in groups]
    for at in range(len(groups)):
        scale = jnp.zeros_like(groups[0])
        later = (at + 1) * edge
        for i in range(at * edge, later, 2):
            if i == later - 4 and at + 1 < len(groups):
                for rows, cols in zip(groups[at:], columns[at:]):
                    cols.update({c: spread_column(rows, begin + c) for c in range(later, later + edge)})
            row = i - at * edge
            cols = columns[at]
            first, second = cols[i], cols[i + 1]
            a, b, c = row_of(first, row), row_of(second, row), row_of(second, row + 1)
            det = a * c - b * b
            inv_a = pl.reciprocal(a, approx=True)
            inv_c = a * pl.reciprocal(det, approx=True)
            ratio = b * inv_a
            scale = jnp.where(below == row, lax.rsqrt(a), jnp.where(below == row + 1, lax.rsqrt(det * inv_a), scale))
            factors = []
            for k in cols:
                if k > i + 1:
                    top = row_of(cols[k], row)
                    factors.append((k, top * inv_a, (row_of(cols[k], row + 1) - ratio * top) * inv_c))
            rows = groups[at]
            upper = row_of(rows, row) * inv_a
            rows = rows - jnp.where(below > row, first, 0.0) * upper
            lower = row_of(rows, row + 1) * inv_c
            groups[at] = rows - jnp.where(below > row + 1, second - ratio * first, 0.0) * lower
            for ahead in range(at, len(groups)):
                cols = columns[ahead]
                first = cols[i]
                second = cols[i + 1] - ratio * first
                for k, on_first, on_second in factors:
                    cols[k] = cols[k] - first * on_first - second * on_second
                if ahead > at:
                    groups[ahead] = groups[ahead] - first * upper - second * lower
                del cols[i], cols[i + 1]
        groups[at] = groups[at] * scale
    return groups


def scale_kernel(gram_ref, times_ref, plus_ref):
    gram = gram_ref[...]
    half, comps = gram.shape[0], gram.shape[1] // 2
    gram = jnp.concatenate([gram[:, :comps], gram[:, comps:]], axis=0)
    eye = lax.broadcasted_iota(jnp.int32, gram.shape, 0) == lax.broadcasted_iota(jnp.int32, gram.shape, 1)
    diagonal = jnp.where(eye, gram, 0.0)
    row_scale = lax.rsqrt(jnp.sum(diagonal, axis=1, keepdims=True))
    col_scale = lax.rsqrt(jnp.sum(diagonal, axis=0, keepdims=True))
    zeros = jnp.zeros_like(gram)
    times_ref[...] = jnp.concatenate([zeros, row_scale * col_scale], axis=1)
    plus_ref[...] = jnp.concatenate([jnp.where(eye, col_scale, 0.0), zeros], axis=1)


def scales(gram):
    half, lanes = gram.shape
    return pl.pallas_call(
        scale_kernel,
        out_shape=[jax.ShapeDtypeStruct((2 * half, lanes), F32)] * 2,
        in_specs=[WHOLE],
        out_specs=[WHOLE, WHOLE],
        compiler_params=PARAMS,
        name="scales",
    )(gram)


def basis_kernel(scale, *refs):
    grams, (times_ref, plus_ref, spread_ref, out_ref) = refs[:-4], refs[-4:]
    gram = tree_sum([ref[...] for ref in grams])
    comps = spread_ref.shape[0]
    gram = jnp.concatenate([pltpu.roll(gram, comps, 1), gram], axis=0)
    both = gram * times_ref[...] + plus_ref[...]
    groups = eliminate([both[at:at + 8] for at in range(0, comps, 8)], comps)
    inverse = jnp.concatenate(groups, axis=0)[:, :comps] * scale
    out_ref[...] = term_product(split_terms(inverse, 3), split_terms(spread_ref[...], 3), NN)


def orthonormal(grams, spread, scale):
    return pl.pallas_call(
        functools.partial(basis_kernel, scale),
        out_shape=jax.ShapeDtypeStruct(spread.shape, F32),
        in_specs=[WHOLE] * (len(grams) + 3),
        out_specs=WHOLE,
        compiler_params=PARAMS,
        name="orthonormal",
    )(*grams, *scales(grams[0]), spread)


def send(x, offset_cells, offset_genes):
    cells, genes = lax.axis_size("cells"), lax.axis_size("genes")
    pairs = []
    for c in range(cells):
        for g in range(genes):
            pairs.append((c * genes + g, (c ^ offset_cells) * genes + (g ^ offset_genes)))
    return lax.ppermute(x, ("cells", "genes"), pairs)


def gene_terms(x):
    x = x + send(x, 0, 1)
    return [x, send(x, 0, 3)]


def all_terms(x):
    x = x + send(x, 0, 1)
    across = [send(x, c, g) for c, g in ((1, 1), (1, 3), (0, 3))]
    x = (x + across[0]) + (across[1] + across[2])
    far, both, near = [send(x, c, 1) for c in (4, 6, 2)]
    return [x, near, both, far]


def scattered_spread(scores, high, low, occ, cell_total):
    comps = scores[0].shape[0]
    me = lax.axis_index("cells").astype(jnp.int32).reshape(1)
    make = functools.partial(spread_pieces, scores=scores, high=high, low=low, occ=occ)
    pair, first, across = make(me, picks=[[6, 2], [5], [7]])
    pair, me = lax.optimization_barrier((pair, me))
    pair, first = send(pair, 2, 0), send(first, 1, 0)
    across = send(across, 7, 0)
    far, own, *second = make(me, picks=[[4], [0], [3], [1]])
    first, second[0] = lax.optimization_barrier((first, second[0]))
    far, second[1] = lax.optimization_barrier((tree_sum([far, pair[:far.shape[0]], first]), second[1]))
    far = send(far, 4, 0)
    straight = [send(x, k, 0) for k, x in zip((3, 1), second)]
    return centered_gram([own, far, pair, across] + straight, comps, cell_total)


def all_alike(counts, occupancy, start_basis):
    tile_rows, tile_cols = occupancy.shape
    edge = counts.shape[0] // tile_rows
    logged = jnp.log(1.0 + counts.astype(F32)).reshape(tile_rows, edge, tile_cols, -1)
    logged = (logged * occupancy.astype(F32)[:, None, :, None]).reshape(counts.shape)
    high, low = split_terms(logged, 2)
    scores = lax.psum(dot(start_basis, high, NT) + dot(start_basis, low, NT), "genes")
    spread = term_product(split_terms(scores, 2), [high, low], NN)
    spread = lax.psum_scatter(spread, "cells", scatter_dimension=1, tiled=True)
    rows = lax.psum(jnp.sum(scores, axis=1, keepdims=True), "cells")
    sums = lax.psum_scatter(jnp.sum(logged, axis=0, keepdims=True), "cells", scatter_dimension=1, tiled=True)
    spread, gram = plain_gram(spread, rows, sums, counts.shape[0] * lax.axis_size("cells"))
    return [lax.psum(gram, ("cells", "genes"))], spread


def in_steps(counts, occupancy, start_basis):
    high, low = log_terms(counts)
    scores, occ = score_part(occupancy, start_basis, high, low)
    cell_total = counts.shape[0] * lax.axis_size("cells")
    spread, gram = scattered_spread(gene_terms(scores), high, low, occ, cell_total)
    return all_terms(gram), spread


def on_device(counts, occupancy, start_basis):
    gene_count = counts.shape[1]
    cells, genes = lax.axis_size("cells"), lax.axis_size("genes")
    halvings = cells == 1 << 3 and genes == 1 << 2
    tiles = occupancy.shape[0] == 1 and gene_count == occupancy.shape[1] * LANES
    work = in_steps if halvings and tiles and gene_count % (cells * LANES) == 0 else all_alike
    grams, spread = work(counts, occupancy, start_basis)
    return orthonormal(grams, spread, math.sqrt(gene_count * genes))


def solution(mesh):
    in_specs = (P("cells", "genes"), P("cells", "genes"), P(None, "genes"))
    out_specs = P(None, ("genes", "cells"))
    return jax.shard_map(
        on_device, mesh=mesh, in_specs=in_specs, out_specs=out_specs, check_vma=False
    )
```

```python
import functools
import math

import jax
import jax.numpy as jnp
from jax import lax
from jax.experimental import pallas as pl
from jax.experimental.pallas import tpu as pltpu
from jax.sharding import PartitionSpec as P

F32 = jnp.float32
BF16 = jnp.bfloat16
NN = (((1,), (0,)), ((), ()))
NT = (((1,), (1,)), ((), ()))
WHOLE = pl.BlockSpec(memory_space=pltpu.VMEM)
SCALARS = pl.BlockSpec(memory_space=pltpu.SMEM)
LANES = 128
PARAMS = pltpu.CompilerParams(vmem_limit_bytes=16 * 2**20)
LOG_PARAMS = pltpu.CompilerParams(vmem_limit_bytes=205 * 2**18)


def dot(a, b, dims):
    return lax.dot_general(a, b, dims, preferred_element_type=F32)


def split_terms(x, count):
    terms = []
    for _ in range(count):
        term = x.astype(BF16)
        terms.append(term)
        x = x - term.astype(F32)
    return terms


def tree_sum(parts):
    while len(parts) > 1:
        parts = [sum(parts[at + 1:at + 2], parts[at]) for at in range(0, len(parts), 2)]
    return parts[0]


def log_kernel(width, counts_hbm, high_ref, low_ref, counts_ref, counts_sem):
    cells, genes = high_ref.shape
    fetches = [
        pltpu.make_async_copy(
            counts_hbm.at[:, pl.ds(at * width, width)], counts_ref.at[:, pl.ds(at * width, width)], counts_sem.at[at]
        )
        for at in range(genes // width)
    ]
    for fetch in fetches:
        fetch.start()
    for at, fetch in enumerate(fetches):
        fetch.wait()
        for begin in range(at * width, (at + 1) * width, LANES):
            lanes = pl.ds(begin, LANES)
            logged = jnp.log(1.0 + counts_ref[:, lanes].astype(F32))
            high = logged.astype(BF16)
            high_ref[:, lanes] = high
            low_ref[:, lanes] = (logged - high.astype(F32)).astype(BF16)


def log_terms(counts):
    cells, genes = counts.shape
    width = genes // 8
    return pl.pallas_call(
        functools.partial(log_kernel, width),
        out_shape=(
            jax.ShapeDtypeStruct((cells, genes), BF16),
            jax.ShapeDtypeStruct((cells, genes), BF16),
        ),
        in_specs=[pl.BlockSpec(memory_space=pltpu.HBM)],
        out_specs=(WHOLE, WHOLE),
        scratch_shapes=[pltpu.VMEM(counts.shape, BF16), pltpu.SemaphoreType.DMA((genes // width,))],
        compiler_params=LOG_PARAMS,
        cost_estimate=pl.CostEstimate(flops=20 * cells * genes, bytes_accessed=8 * cells * genes, transcendentals=0),
        name="log_terms",
    )(counts)


def score_kernel(width, occ_ref, basis_ref, high_ref, low_ref, score_ref, lane_ref):
    comps, genes = basis_ref.shape
    edge = genes // occ_ref.shape[1]
    occupancy = occ_ref[...].astype(F32)
    scores = None
    for begin in range(0, genes, width):
        basis = []
        for at in range(begin, begin + width, edge):
            occ = jnp.broadcast_to(occupancy[:, at // edge:at // edge + 1], (1, edge))
            lane_ref[:, pl.ds(at, edge)] = occ
            basis.append(basis_ref[:, pl.ds(at, edge)] * occ.astype(BF16))
        basis = jnp.concatenate(basis, axis=1)
        lanes = pl.ds(begin, width)
        part = dot(basis, jnp.concatenate([high_ref[:, lanes], low_ref[:, lanes]], axis=0), NT)
        scores = part if scores is None else scores + part
    cells = score_ref.shape[1]
    score_ref[...] = scores[:, :cells] + scores[:, cells:]


def score_part(occupancy, basis, high, low):
    comps, genes = basis.shape
    cells = high.shape[0]
    return pl.pallas_call(
        functools.partial(score_kernel, genes // 4),
        out_shape=(jax.ShapeDtypeStruct((comps, cells), F32), jax.ShapeDtypeStruct((1, genes), F32)),
        in_specs=[WHOLE] * 4,
        out_specs=(WHOLE, WHOLE),
        compiler_params=PARAMS,
        name="scores",
    )(occupancy, basis, high, low)


def term_product(left, right, dims):
    rows = left[0].shape[0]
    left = jnp.concatenate([jnp.concatenate([term] * len(right), axis=1) for term in left], axis=0)
    out = dot(left, jnp.concatenate(right, axis=dims[0][1][0]), dims)
    parts = [out[at:at + rows] for at in range(0, out.shape[0], rows)]
    return functools.reduce(jnp.add, parts[::-1])


def spread_kernel(count, picks, me_ref, *refs):
    score_refs, outs = refs[:count], refs[count + 3:]
    high_ref, low_ref, occ_ref = refs[count:count + 3]
    scores = tree_sum([ref[...] for ref in score_refs])
    comps = scores.shape[0]
    terms = split_terms(scores, 2)
    scores = terms[0].astype(F32) + terms[1].astype(F32)
    terms = terms + [jnp.ones_like(scores, BF16)[:8]]
    eye = lax.broadcasted_iota(jnp.int32, (comps, LANES), 0) == lax.broadcasted_iota(jnp.int32, (comps, LANES), 1)
    row_sums = jnp.sum(jnp.where(eye, jnp.sum(scores, axis=1, keepdims=True), 0.0), axis=0, keepdims=True)
    chunks = high_ref.shape[1] // (LANES * lax.axis_size("cells"))
    width = chunks * LANES
    blocks = [(pick, out, at) for group, out in zip(picks, outs) for at, pick in enumerate(group)]
    rows = block_rows(comps, chunks)
    for pick, out, at_block in blocks:
        base = at_block * rows
        start = pl.multiple_of((me_ref[0] ^ pick) * width, width)
        lanes = pl.ds(start, width)
        left = jnp.concatenate([jnp.concatenate([term, term], axis=1) for term in terms], axis=0)
        out_all = dot(left, jnp.concatenate([high_ref[:, lanes], low_ref[:, lanes]], axis=0), NN) * occ_ref[:, lanes]
        piece = out_all[comps:2 * comps] + out_all[:comps]
        sums = out_all[2 * comps:2 * comps + 1]
        extra = [row_sums]
        for at in range(chunks):
            out[base + at * comps:base + (at + 1) * comps] = piece[:, at * LANES:(at + 1) * LANES]
            extra.append(sums[:, at * LANES:(at + 1) * LANES])
        extra.append(jnp.zeros((rows - chunks * comps - chunks - 1, LANES), F32))
        out[base + chunks * comps:base + rows] = jnp.concatenate(extra, axis=0)


def block_rows(comps, chunks):
    return comps * chunks + -(-(chunks + 1) // 8) * 8


def spread_pieces(me, scores, high, low, occ, picks):
    comps = scores[0].shape[0]
    chunks = high.shape[1] // (LANES * lax.axis_size("cells"))
    rows = block_rows(comps, chunks)
    count = sum(len(group) for group in picks)
    return pl.pallas_call(
        functools.partial(spread_kernel, len(scores), picks),
        out_shape=[jax.ShapeDtypeStruct((len(group) * rows, LANES), F32) for group in picks],
        in_specs=[SCALARS] + [WHOLE] * (len(scores) + 3),
        out_specs=[WHOLE] * len(picks),
        compiler_params=PARAMS,
        cost_estimate=pl.CostEstimate(
            flops=10 * comps * count * chunks * LANES * high.shape[0], bytes_accessed=2**21, transcendentals=0
        ),
        name="spread",
    )(me, *scores, high, low, occ)


def gram_kernel(scale, chunks, *refs):
    pieces, (spread_ref, gram_ref) = refs[:-2], refs[-2:]
    comps = spread_ref.shape[0]
    rows = block_rows(comps, chunks)
    total = tree_sum([ref[ref.shape[0] - rows:] for ref in pieces])
    extra = total[chunks * comps:chunks * comps + chunks + 1]
    eye = lax.broadcasted_iota(jnp.int32, (comps, LANES), 0) == lax.broadcasted_iota(jnp.int32, (comps, LANES), 1)
    row_sums = jnp.sum(jnp.where(eye, extra[:1], 0.0), axis=1, keepdims=True) * scale
    parts = [total[at * comps:(at + 1) * comps] - row_sums * extra[at + 1:at + 2] for at in range(chunks)]
    spread = jnp.concatenate(parts, axis=1)
    spread_ref[...] = spread
    gram_ref[...] = packed_gram(spread)


def packed_gram(spread):
    terms = split_terms(spread, 3)
    gram = term_product(terms, terms, NT)
    half = spread.shape[0] // 2
    return jnp.concatenate([gram[:half], gram[half:]], axis=1)


def centered_gram(pieces, comps, cell_total):
    chunks = pieces[0].shape[0] // comps
    return pl.pallas_call(
        functools.partial(gram_kernel, 1.0 / cell_total, chunks),
        out_shape=(
            jax.ShapeDtypeStruct((comps, chunks * LANES), F32),
            jax.ShapeDtypeStruct((comps // 2, comps * 2), F32),
        ),
        in_specs=[WHOLE] * len(pieces),
        out_specs=(WHOLE, WHOLE),
        compiler_params=PARAMS,
        name="gram",
    )(*pieces)


def plain_gram_kernel(scale, spread_ref, row_ref, sum_ref, out_ref, gram_ref):
    spread = spread_ref[...] - row_ref[...] * scale * sum_ref[...]
    out_ref[...] = spread
    gram_ref[...] = packed_gram(spread)


def plain_gram(spread, rows, sums, cell_total):
    comps, width = spread.shape
    return pl.pallas_call(
        functools.partial(plain_gram_kernel, 1.0 / cell_total),
        out_shape=(
            jax.ShapeDtypeStruct((comps, width), F32),
            jax.ShapeDtypeStruct((comps // 2, comps * 2), F32),
        ),
        in_specs=[WHOLE] * 3,
        out_specs=(WHOLE, WHOLE),
        compiler_params=PARAMS,
        name="plain_gram",
    )(spread, rows, sums)


def row_of(x, at):
    return jnp.broadcast_to(x[at:at + 1, :], x.shape)


def spread_column(rows, at):
    return jnp.broadcast_to(rows[:, at:at + 1], rows.shape)


def eliminate(groups, begin):
    groups = list(groups)
    edge = groups[0].shape[0]
    below = lax.broadcasted_iota(jnp.int32, groups[0].shape, 0)
    columns = [{c: spread_column(rows, begin + c) for c in range(edge)} for rows in groups]
    for at in range(len(groups)):
        scale = jnp.zeros_like(groups[0])
        later = (at + 1) * edge
        for i in range(at * edge, later, 2):
            if i == later - 4 and at + 1 < len(groups):
                for rows, cols in zip(groups[at:], columns[at:]):
                    cols.update({c: spread_column(rows, begin + c) for c in range(later, later + edge)})
            row = i - at * edge
            cols = columns[at]
            first, second = cols[i], cols[i + 1]
            a, b, c = row_of(first, row), row_of(second, row), row_of(second, row + 1)
            det = a * c - b * b
            inv_a = pl.reciprocal(a, approx=True)
            inv_c = a * pl.reciprocal(det, approx=True)
            ratio = b * inv_a
            scale = jnp.where(below == row, lax.rsqrt(a), jnp.where(below == row + 1, lax.rsqrt(det * inv_a), scale))
            factors = []
            for k in cols:
                if k > i + 1:
                    top = row_of(cols[k], row)
                    factors.append((k, top * inv_a, (row_of(cols[k], row + 1) - ratio * top) * inv_c))
            rows = groups[at]
            upper = row_of(rows, row) * inv_a
            rows = rows - jnp.where(below > row, first, 0.0) * upper
            lower = row_of(rows, row + 1) * inv_c
            groups[at] = rows - jnp.where(below > row + 1, second - ratio * first, 0.0) * lower
            for ahead in range(at, len(groups)):
                cols = columns[ahead]
                first = cols[i]
                second = cols[i + 1] - ratio * first
                for k, on_first, on_second in factors:
                    cols[k] = cols[k] - first * on_first - second * on_second
                if ahead > at:
                    groups[ahead] = groups[ahead] - first * upper - second * lower
                del cols[i], cols[i + 1]
        groups[at] = groups[at] * scale
    return groups


def scale_kernel(gram_ref, times_ref, plus_ref):
    gram = gram_ref[...]
    half, comps = gram.shape[0], gram.shape[1] // 2
    gram = jnp.concatenate([gram[:, :comps], gram[:, comps:]], axis=0)
    eye = lax.broadcasted_iota(jnp.int32, gram.shape, 0) == lax.broadcasted_iota(jnp.int32, gram.shape, 1)
    diagonal = jnp.where(eye, gram, 0.0)
    row_scale = lax.rsqrt(jnp.sum(diagonal, axis=1, keepdims=True))
    col_scale = lax.rsqrt(jnp.sum(diagonal, axis=0, keepdims=True))
    zeros = jnp.zeros_like(gram)
    times_ref[...] = jnp.concatenate([zeros, row_scale * col_scale], axis=1)
    plus_ref[...] = jnp.concatenate([jnp.where(eye, col_scale, 0.0), zeros], axis=1)


def scales(gram):
    half, lanes = gram.shape
    return pl.pallas_call(
        scale_kernel,
        out_shape=[jax.ShapeDtypeStruct((2 * half, lanes), F32)] * 2,
        in_specs=[WHOLE],
        out_specs=[WHOLE, WHOLE],
        compiler_params=PARAMS,
        name="scales",
    )(gram)


def basis_kernel(scale, *refs):
    grams, (times_ref, plus_ref, spread_ref, out_ref) = refs[:-4], refs[-4:]
    gram = tree_sum([ref[...] for ref in grams])
    comps = spread_ref.shape[0]
    gram = jnp.concatenate([pltpu.roll(gram, comps, 1), gram], axis=0)
    both = gram * times_ref[...] + plus_ref[...]
    groups = eliminate([both[at:at + 8] for at in range(0, comps, 8)], comps)
    inverse = jnp.concatenate(groups, axis=0)[:, :comps] * scale
    out_ref[...] = term_product(split_terms(inverse, 3), split_terms(spread_ref[...], 3), NN)


def orthonormal(grams, spread, scale):
    return pl.pallas_call(
        functools.partial(basis_kernel, scale),
        out_shape=jax.ShapeDtypeStruct(spread.shape, F32),
        in_specs=[WHOLE] * (len(grams) + 3),
        out_specs=WHOLE,
        compiler_params=PARAMS,
        name="orthonormal",
    )(*grams, *scales(grams[0]), spread)


def send(x, offset_cells, offset_genes):
    cells, genes = lax.axis_size("cells"), lax.axis_size("genes")
    pairs = []
    for c in range(cells):
        for g in range(genes):
            pairs.append((c * genes + g, (c ^ offset_cells) * genes + (g ^ offset_genes)))
    return lax.ppermute(x, ("cells", "genes"), pairs)


def gene_terms(x):
    x = x + send(x, 0, 1)
    return [x, send(x, 0, 3)]


def all_terms(x):
    x = x + send(x, 0, 1)
    across = [send(x, c, g) for c, g in ((0, 3), (1, 3), (1, 1))]
    x = (x + across[0]) + (across[1] + across[2])
    far, both, near = [send(x, c, 1) for c in (4, 6, 2)]
    return [x, near, both, far]


def scattered_spread(scores, high, low, occ, cell_total):
    comps = scores[0].shape[0]
    me = lax.axis_index("cells").astype(jnp.int32).reshape(1)
    make = functools.partial(spread_pieces, scores=scores, high=high, low=low, occ=occ)
    pair, first, across = make(me, picks=[[6, 2], [5], [7]])
    pair, me = lax.optimization_barrier((pair, me))
    pair, first = send(pair, 2, 0), send(first, 1, 0)
    across = send(across, 7, 0)
    far, own, *second = make(me, picks=[[4], [0], [3], [1]])
    first, second[0] = lax.optimization_barrier((first, second[0]))
    far, second[1] = lax.optimization_barrier((tree_sum([far, pair[:far.shape[0]], first]), second[1]))
    far = send(far, 4, 0)
    straight = [send(x, k, 0) for k, x in zip((3, 1), second)]
    return centered_gram([own, far, pair, across] + straight, comps, cell_total)


def all_alike(counts, occupancy, start_basis):
    tile_rows, tile_cols = occupancy.shape
    edge = counts.shape[0] // tile_rows
    logged = jnp.log(1.0 + counts.astype(F32)).reshape(tile_rows, edge, tile_cols, -1)
    logged = (logged * occupancy.astype(F32)[:, None, :, None]).reshape(counts.shape)
    high, low = split_terms(logged, 2)
    scores = lax.psum(dot(start_basis, high, NT) + dot(start_basis, low, NT), "genes")
    spread = term_product(split_terms(scores, 2), [high, low], NN)
    spread = lax.psum_scatter(spread, "cells", scatter_dimension=1, tiled=True)
    rows = lax.psum(jnp.sum(scores, axis=1, keepdims=True), "cells")
    sums = lax.psum_scatter(jnp.sum(logged, axis=0, keepdims=True), "cells", scatter_dimension=1, tiled=True)
    spread, gram = plain_gram(spread, rows, sums, counts.shape[0] * lax.axis_size("cells"))
    return [lax.psum(gram, ("cells", "genes"))], spread


def in_steps(counts, occupancy, start_basis):
    high, low = log_terms(counts)
    scores, occ = score_part(occupancy, start_basis, high, low)
    cell_total = counts.shape[0] * lax.axis_size("cells")
    spread, gram = scattered_spread(gene_terms(scores), high, low, occ, cell_total)
    return all_terms(gram), spread


def on_device(counts, occupancy, start_basis):
    gene_count = counts.shape[1]
    cells, genes = lax.axis_size("cells"), lax.axis_size("genes")
    halvings = cells == 1 << 3 and genes == 1 << 2
    tiles = occupancy.shape[0] == 1 and gene_count == occupancy.shape[1] * LANES
    work = in_steps if halvings and tiles and gene_count % (cells * LANES) == 0 else all_alike
    grams, spread = work(counts, occupancy, start_basis)
    return orthonormal(grams, spread, math.sqrt(gene_count * genes))


def solution(mesh):
    in_specs = (P("cells", "genes"), P("cells", "genes"), P(None, "genes"))
    out_specs = P(None, ("genes", "cells"))
    return jax.shard_map(
        on_device, mesh=mesh, in_specs=in_specs, out_specs=out_specs, check_vma=False
    )
```
